32 devices in a mesh: dp: 8 (over y, x, core), seq: 4 (over z).
Axes of the slice: x: 2, y: 2, z: 4, core: 2. Of those that a mesh axis runs over, the one named last changes fastest.
Arguments:
- block_input: float32 [12288, 768], P(('dp', 'seq')), may hold values from -6 to 6
- embedding: float32 [12288, 768], P(('dp', 'seq')), may hold values from -6 to 6
- earlier_outs: float32 [3, 12288, 768], P(None, ('dp', 'seq')), may hold values from -6 to 6
- dwa_weights: float32 [5], replicated, may hold values from 0.3 to 1.2
- ln1_gain: float32 [768], replicated, may hold values from 0.5 to 1.5
- ln1_bias: float32 [768], replicated, may hold values from -2 to 2
- w_qkv: float32 [768, 2304], P('dp'), may hold values from -0.21875 to 0.21875
- w_out: float32 [768, 768], P('dp'), may hold values from -1.75 to 1.75
- ln2_gain: float32 [768], replicated, may hold values from 0.5 to 1.5
- ln2_bias: float32 [768], replicated, may hold values from -2 to 2
- w_up: float32 [768, 3072], P('dp'), may hold values from -0.21875 to 0.21875
- w_down: float32 [3072, 768], P('dp'), may hold values from -0.109375 to 0.109375
- segments: int32 [8, 1536], P('dp', 'seq'), may hold values from 0 to 11, never falling along the last dimension, each value on 1 to 768 neighbouring positions
- cotangent: float32 [12288, 768], P(('dp', 'seq')), may hold values from -6 to 6
Outputs:
- output: float32 [12288, 768], P(('dp', 'seq'))
- grad_input: float32 [12288, 768], P(('dp', 'seq'))
- grad_dwa: float32 [5], replicated
- grad_ln1_gain: float32 [768], replicated
- grad_ln1_bias: float32 [768], replicated
- grad_qkv: float32 [768, 2304], P('dp')
- grad_wout: float32 [768, 768], P('dp')
- grad_ln2_gain: float32 [768], replicated
- grad_ln2_bias: float32 [768], replicated
- grad_up: float32 [768, 3072], P('dp')
- grad_down: float32 [3072, 768], P('dp')
The draws below stay inside these ranges and needn't reach their ends.
Inputs may be any that keep to these rules, and one draw needn't show every extreme that they name: `segments`: within a sequence the numbers never fall; equal numbers mark one document, of at most 768 tokens.
All inputs are finite; a program needn't handle non-finite values.
Results may differ from the reference program's by a relative error of at most 0.0003.
Values sent between devices are 32-bit elements; how exact they have to be, the bound alone decides.
No kernel may reach another device: no remote copies, remote signals or barrier semaphores. Data moves between devices by JAX's collectives and lax.ppermute only.
A program may use at most 192 MiB of HBM per device.

```python
import math
import jax
import jax.numpy as jnp
import numpy as np
from jax import lax

D = 768
H = 12
HD = 64
FF = 3072
SEQS = 8
LEN = 1536
TOKENS = 12288
DOCS = 12
DOC_MOST = 768


def block_levels(own_key, shape, split, least, high):
    level = 1.0
    for axis_at, shards_of in split:
        draws = jax.random.uniform(jax.random.fold_in(jax.random.fold_in(own_key, 6), axis_at), (shards_of,), jnp.float32, least / len(split), high / len(split))
        level = level * jnp.repeat(jnp.exp(draws), shape[axis_at] // shards_of).reshape((-1,) + (1,) * (len(shape) - 1 - axis_at))
    return level


def length_profile(number_of, total, most, lean):
    loads = [(1 << 20) // math.isqrt(grade ** lean) + 1 for grade in range(2, number_of + 1)]
    surplus, given = total - most - (number_of - 1), [1] * (number_of - 1)
    while surplus > 0:
        movable = [i for i in range(number_of - 1) if given[i] < most]
        whole, left = sum([loads[i] for i in movable]), surplus
        for i in movable:
            extra = min(most - given[i], max(1, left * loads[i] // whole), surplus)
            given[i] = given[i] + extra
            surplus = surplus - extra
    return np.array([most] + given)


def uneven_parts(key, count, total, limit, lean):
    if count == 2:
        one = jax.random.randint(key, (), max(1, total - limit), min(limit, total - 1) + 1)
        return jnp.stack([one, total - one])
    lengths = jnp.asarray(length_profile(count, total, limit, lean), jnp.int32)
    twos = (count - 1) // 2
    donor, sink = lengths[1:1 + 2 * twos:2], lengths[2:2 + 2 * twos:2]
    slack = jnp.minimum(donor - 1, limit - sink)
    shifted = jax.random.randint(jax.random.fold_in(key, 1), (twos,), 0, 1 << 20) % (slack + 1)
    lengths = lengths.at[1:1 + 2 * twos:2].set(donor - shifted).at[2:2 + 2 * twos:2].set(sink + shifted)
    return lengths[jax.random.permutation(jax.random.fold_in(key, 2), count)]


def bell_draw(stream_key, shape, scale, bound, shards=(), held_as=jnp.bfloat16):
    drawn = jax.random.normal(stream_key, shape, jnp.float32) * scale
    if len(shards) > 0:
        drawn = block_levels(stream_key, shape, shards, -0.22, 0.18) * drawn
    return jnp.clip(drawn, min=-bound, max=bound).astype(held_as)


def setup_inputs(seed: int = 0) -> dict:
    key_of = jax.random.split(jax.random.key(seed), 15)
    return {
        "block_input": bell_draw(key_of[0], (TOKENS, D), 1.0, 6.0, ((0, 32),), jnp.float32),
        "embedding": bell_draw(key_of[1], (TOKENS, D), 1.0, 6.0, ((0, 32),), jnp.float32),
        "earlier_outs": bell_draw(key_of[2], (3, TOKENS, D), 1.0, 6.0, ((1, 32),), jnp.float32),
        "dwa_weights": jnp.clip(jax.random.uniform(key_of[3], (5,), jnp.float32, 0.3, 1.2), 0.3, 1.2),
        "ln1_gain": jnp.clip(1.0 + 0.1 * jax.random.normal(key_of[4], (D,), jnp.float32), 0.5, 1.5),
        "ln1_bias": bell_draw(key_of[5], (D,), 0.3, 2.0, (), jnp.float32),
        "w_qkv": bell_draw(key_of[6], (D, 3 * D), D ** -0.5, 0.21875, ((0, 8),), jnp.float32),
        "w_out": bell_draw(key_of[7], (D, D), (D // 64) ** -0.5, 1.75, ((0, 8),), jnp.float32),
        "ln2_gain": jnp.clip(1.0 + 0.1 * jax.random.normal(key_of[8], (D,), jnp.float32), 0.5, 1.5),
        "ln2_bias": bell_draw(key_of[9], (D,), 0.3, 2.0, (), jnp.float32),
        "w_up": bell_draw(key_of[10], (D, FF), D ** -0.5, 0.21875, ((0, 8),), jnp.float32),
        "w_down": bell_draw(key_of[11], (FF, D), FF ** -0.5, 0.109375, ((0, 8),), jnp.float32),
        "segments": jax.vmap(lambda own: jnp.searchsorted(jnp.cumsum(uneven_parts(own, DOCS, LEN, DOC_MOST, 2)), jnp.arange(LEN), side="right"))(jax.random.split(key_of[12], SEQS)).reshape((SEQS, LEN)).astype(jnp.int32),
        "cotangent": bell_draw(key_of[13], (TOKENS, D), 1.0, 6.0, ((0, 32),), jnp.float32),
    }


@jax.custom_vjp
def low(v):
    return lax.optimization_barrier(v.astype(jnp.bfloat16)).astype(jnp.float32)

@jax.custom_vjp
def low_back(v):
    return v

def low_keep(v):
    return (low(v), None)

def low_pass(kept, grad):
    return (grad,)

def back_keep(v):
    return (v, None)

def back_low(kept, grad):
    return (low(grad),)
low.defvjp(low_keep, low_pass)
low_back.defvjp(back_keep, back_low)
precise = lax.Precision.HIGHEST

def layer_norm(values, gain, bias):
    row_mean = lax.optimization_barrier(jnp.mean(values, axis=-1, keepdims=True))
    centred = values - row_mean
    row_var = lax.optimization_barrier(jnp.mean(centred * centred, axis=-1, keepdims=True))
    return centred * lax.rsqrt(row_var + 1e-05) * gain + bias

def gelu_tanh(values):
    return 0.5 * values * (1.0 + jnp.tanh(0.7978845608028654 * (values + 0.044715 * values * values * values)))

def rotary_tables(length, head_dim):
    half_dim = head_dim // 2
    inv_freq = 10000.0 ** (-(jnp.arange(half_dim, dtype=jnp.float32) * 2.0 / head_dim))
    angles = jnp.arange(length, dtype=jnp.float32)[:, None] * inv_freq[None, :]
    angles = jnp.concatenate([angles, angles], axis=1)
    return (jnp.cos(angles), jnp.sin(angles))

def rotate(values, cosine_tab, sine_tab):
    half_dim = values.shape[-1] // 2
    turned = jnp.concatenate([-values[..., half_dim:], values[..., :half_dim]], axis=-1)
    return values * cosine_tab[:, None, :] + turned * sine_tab[:, None, :]

def one_sequence(weights, seq_input, seq_segments):
    ln1_gain, ln1_bias, w_qkv, w_out, ln2_gain, ln2_bias, w_up, w_down = weights
    length = seq_input.shape[0]
    normed_one = layer_norm(seq_input, ln1_gain, ln1_bias)
    packed = jnp.dot(normed_one, w_qkv, precision=precise)
    queries = packed[:, :D].reshape(length, H, HD)
    keys_all = packed[:, D:2 * D].reshape(length, H, HD)
    values_all = packed[:, 2 * D:].reshape(length, H, HD)
    cosine_tab, sine_tab = rotary_tables(length, HD)
    queries = rotate(queries, cosine_tab, sine_tab)
    keys_all = rotate(keys_all, cosine_tab, sine_tab)
    scores = jnp.einsum('qhd,khd->hqk', queries, keys_all, precision=precise) / jnp.sqrt(jnp.float32(HD))
    position = jnp.arange(length, dtype=jnp.int32)
    allowed = (position[None, :] <= position[:, None]) & (seq_segments[None, :] == seq_segments[:, None])
    scores = jnp.where(allowed[None], scores, -1e+30)
    probs = jax.nn.softmax(scores, axis=-1)
    attended = jnp.einsum('hqk,khd->qhd', probs, values_all, precision=precise).reshape(length, D)
    resid = seq_input + jnp.dot(attended, w_out, precision=precise)
    normed_two = layer_norm(resid, ln2_gain, ln2_bias)
    up_pre = jnp.dot(normed_two, w_up, precision=precise)
    return resid + jnp.dot(gelu_tanh(up_pre), w_down, precision=precise)

def forward(block_input, embedding, earlier_outs, dwa_weights, ln1_gain, ln1_bias, w_qkv, w_out, ln2_gain, ln2_bias, w_up, w_down, segments):
    weights = (ln1_gain, ln1_bias, w_qkv, w_out, ln2_gain, ln2_bias, w_up, w_down)
    per_seq = jax.checkpoint(one_sequence)
    seq_inputs = block_input.reshape(SEQS, LEN, D)
    block_out = lax.map(lambda pair: per_seq(weights, pair[0], pair[1]), (seq_inputs, segments))
    block_out = block_out.reshape(SEQS * LEN, D)
    return dwa_weights[0] * embedding + dwa_weights[1] * earlier_outs[0] + dwa_weights[2] * earlier_outs[1] + dwa_weights[3] * earlier_outs[2] + dwa_weights[4] * block_out

def reference(block_input, embedding, earlier_outs, dwa_weights, ln1_gain, ln1_bias, w_qkv, w_out, ln2_gain, ln2_bias, w_up, w_down, segments, cotangent):

    def wrapped(*floats):
        return forward(*floats, segments)
    output, pullback = jax.vjp(wrapped, block_input, embedding, earlier_outs, dwa_weights, ln1_gain, ln1_bias, w_qkv, w_out, ln2_gain, ln2_bias, w_up, w_down)
    grads = pullback(cotangent)
    return (output, grads[0], grads[3], grads[4], grads[5], grads[6], grads[7], grads[8], grads[9], grads[10], grads[11])
```

```python
import functools
import math

import jax
import jax.numpy as jnp
import numpy as np
from jax import lax
from jax.experimental import pallas as pl
from jax.experimental.pallas import tpu as pltpu
from jax.sharding import PartitionSpec as P

HD = 64
DOC_MOST = 768
LOG2E = math.log2(math.e)
SCALE = 1.0 / math.sqrt(HD)
NEG = -1e30
F32 = jnp.float32
BF16 = jnp.bfloat16
HIGH = lax.Precision.HIGH
VMEM_LIMIT = 56 * 1024 * 1024
BLK = 128


def params():
    return pltpu.CompilerParams(
        dimension_semantics=("arbitrary",), vmem_limit_bytes=VMEM_LIMIT
    )


def split(values):
    high = values.astype(BF16)
    return high, (values - high.astype(F32)).astype(BF16)


def dot_nn(left, right):
    return lax.dot_general(left, right, (((1,), (0,)), ((), ())), preferred_element_type=F32)


def dot_nt(left, right):
    return lax.dot_general(left, right, (((1,), (1,)), ((), ())), preferred_element_type=F32)


def dot_tn(left, right):
    return lax.dot_general(left, right, (((0,), (0,)), ((), ())), preferred_element_type=F32)


def three(dot, left, right):
    return (
        dot(left[0], right[0]) + dot(left[0], right[1]) + dot(left[1], right[0])
    )


def norm_stats(values):
    row_mean = jnp.mean(values, axis=-1, keepdims=True)
    centred = values - row_mean
    row_var = jnp.mean(centred * centred, axis=-1, keepdims=True)
    rate = lax.rsqrt(row_var + 1e-05)
    return centred * rate, rate


def turned(values):
    lane = lax.broadcasted_iota(jnp.int32, values.shape, 1)
    return jnp.where(
        (lane & 63) < 32, pltpu.roll(values, 96, 1), pltpu.roll(values, 32, 1)
    )


def rotate(values, cosine, sine):
    return values * cosine + turned(values) * sine


def unrotate(values, cosine, sine):
    return values * cosine - turned(values) * sine


def rotary_tables(length, halo):
    half = HD // 2
    inv_freq = (10000.0 ** (-(np.arange(half, dtype=np.float32) * 2.0 / HD))).astype(np.float32)
    place = np.arange(-halo, length, dtype=np.float32)
    angles = place[:, None] * inv_freq[None, :]
    cosine = np.cos(angles.astype(np.float64)).astype(np.float32)
    sine = np.sin(angles.astype(np.float64)).astype(np.float32)
    return (
        np.concatenate([cosine] * 4, axis=1),
        np.concatenate([-sine, sine, -sine, sine], axis=1),
    )


def qkv_kernel(far_ref, near_ref, own_ref, gain_ref, bias_ref, w_ref, cos_ref, sin_ref,
               q_ref, kv_ref, hi_ref, lo_ref):
    step = pl.program_id(0)
    rows = own_ref.shape[0]
    third = pl.num_programs(0) // 3
    halo = hi_ref.shape[0] - rows

    @pl.when(step == 0)
    def _():
        for at, ref in enumerate((far_ref, near_ref, own_ref)):
            xhat, _ = norm_stats(ref[...])
            high, low = split(xhat * gain_ref[...] + bias_ref[...])
            hi_ref[at * rows:(at + 1) * rows] = high
            lo_ref[at * rows:(at + 1) * rows] = low

    weights = split(w_ref[...])

    @pl.when(step < third)
    def _():
        got = three(dot_nn, (hi_ref[halo:], lo_ref[halo:]), weights)
        for at in range(0, got.shape[1], 128):
            q_ref[:, at:at + 128] = rotate(got[:, at:at + 128], cos_ref[halo:], sin_ref[halo:])

    @pl.when((step >= third) & (step < 2 * third))
    def _():
        got = three(dot_nn, (hi_ref[...], lo_ref[...]), weights)
        for at in range(0, got.shape[1], 128):
            kv_ref[:, at:at + 128] = rotate(got[:, at:at + 128], cos_ref[...], sin_ref[...])

    @pl.when(step >= 2 * third)
    def _():
        kv_ref[...] = three(dot_nn, (hi_ref[...], lo_ref[...]), weights)


def project(far, near, own, gain, bias, w_full, cosine, sine):
    rows, model = own.shape
    total = 3 * rows
    wide = 256
    third = model // wide
    whole = lambda shape: pl.BlockSpec(shape, lambda j: (0, 0))
    return pl.pallas_call(
        qkv_kernel,
        grid=(3 * third,),
        in_specs=[
            whole((rows, model)), whole((rows, model)), whole((rows, model)),
            whole((1, model)), whole((1, model)),
            pl.BlockSpec((model, wide), lambda j: (0, j)),
            whole((total, 128)), whole((total, 128)),
        ],
        out_specs=[
            pl.BlockSpec((rows, wide), lambda j: (0, jnp.minimum(j, third - 1))),
            pl.BlockSpec((total, wide), lambda j: (0, jnp.maximum(j - third, 0))),
            whole((total, model)), whole((total, model)),
        ],
        out_shape=[
            jax.ShapeDtypeStruct((rows, model), F32),
            jax.ShapeDtypeStruct((total, 2 * model), F32),
            jax.ShapeDtypeStruct((total, model), BF16),
            jax.ShapeDtypeStruct((total, model), BF16),
        ],
        compiler_params=params(),
    )(far, near, own, gain, bias, w_full, cosine, sine)


def own_pair(values, head):
    lane = lax.broadcasted_iota(jnp.int32, values.shape, 1)
    other = pltpu.roll(values, 64, 1)
    return jnp.where((lane < 64) == (head == 0), values, other)


def outer_form(values, head):
    high, low = split(own_pair(values, head))
    return jnp.concatenate([high, low], axis=1)


def mixed(values, head):
    pair = own_pair(values, head)
    lane = lax.broadcasted_iota(jnp.int32, pair.shape, 1)
    high = pair.astype(BF16).astype(F32)
    return jnp.where(lane < 64, high, pair - high).astype(BF16)


def inner_form(values, head):
    half = mixed(values, head)
    return jnp.concatenate([half, half], axis=1)


def fold(values):
    return values + pltpu.roll(values, 64, 1)


def attend_kernel(q_ref, k_ref, v_ref, segq_ref, segk_ref, out_ref, bias_ref):
    rows = q_ref.shape[0]
    halo = k_ref.shape[0] - rows
    span = halo + BLK

    @pl.when(pl.program_id(0) == 0)
    def _():
        for at in range(0, rows, BLK):
            row = lax.broadcasted_iota(jnp.int32, (BLK, span), 0)
            col = lax.broadcasted_iota(jnp.int32, (BLK, span), 1)
            same = segq_ref[at:at + BLK, :1] == segk_ref[:1, at:at + span]
            bias_ref[at:at + BLK] = jnp.where(same & (col - halo <= row), 0.0, NEG)

    lane = lax.broadcasted_iota(jnp.int32, (BLK, 128), 1)
    scaled = q_ref[...] * (SCALE * LOG2E)
    results = []
    for head in range(2):
        left = inner_form(scaled, head)
        right = outer_form(k_ref[...], head)
        vals = mixed(v_ref[...], head)
        outs = []
        for at in range(0, rows, BLK):
            scores = dot_nt(left[at:at + BLK], right[at:at + span]) + bias_ref[at:at + BLK]
            top = jnp.max(scores, axis=1, keepdims=True)
            expo = jnp.exp2(scores - top)
            total = jnp.sum(expo, axis=1, keepdims=True)
            high, low = split(expo)
            got = dot_nn(high, vals[at:at + span]) + dot_nn(low, vals[at:at + span])
            outs.append(fold(got) / total)
        results.append(outs)
    for at in range(0, rows, BLK):
        out_ref[at:at + BLK] = jnp.where(
            lane < 64, results[0][at // BLK], results[1][at // BLK]
        )


def attend(q_rot, kv, seg_q, seg_k):
    rows, model = q_rot.shape
    total = kv.shape[0]
    pairs = model // 128
    return pl.pallas_call(
        attend_kernel,
        grid=(pairs,),
        in_specs=[
            pl.BlockSpec((rows, 128), lambda p: (0, p)),
            pl.BlockSpec((total, 128), lambda p: (0, p)),
            pl.BlockSpec((total, 128), lambda p: (0, pairs + p)),
            pl.BlockSpec((rows, 128), lambda p: (0, 0)),
            pl.BlockSpec((8, total), lambda p: (0, 0)),
        ],
        out_specs=pl.BlockSpec((rows, 128), lambda p: (0, p)),
        out_shape=jax.ShapeDtypeStruct((rows, model), F32),
        scratch_shapes=[pltpu.VMEM((rows, total - rows + BLK), F32)],
        compiler_params=params(),
    )(q_rot, kv, kv, seg_q, seg_k)


def attend_back_kernel(q_ref, k_ref, v_ref, g_ref, segq_ref, segk_ref, cos_ref, sin_ref,
                       dq_ref, dk_ref, dv_ref, bias_ref):
    rows = q_ref.shape[0]
    halo = k_ref.shape[0] - rows
    span = halo + BLK

    @pl.when(pl.program_id(0) == 0)
    def _():
        for at in range(0, rows, BLK):
            key = lax.broadcasted_iota(jnp.int32, (span, BLK), 0)
            query = lax.broadcasted_iota(jnp.int32, (span, BLK), 1)
            same = segk_ref[at:at + span, :1] == segq_ref[:1, at:at + BLK]
            bias_ref[:, at:at + BLK] = jnp.where(same & (key - halo <= query), 0.0, NEG)

    scaled = q_ref[...] * (SCALE * LOG2E)
    dq, dk, dv = [], [], []
    for head in range(2):
        q_in = inner_form(scaled, head)
        g_in = inner_form(g_ref[...], head)
        k_out = outer_form(k_ref[...], head)
        v_out = outer_form(v_ref[...], head)
        q_mix = mixed(q_ref[...], head)
        g_mix = mixed(g_ref[...], head)
        k_mix = mixed(k_ref[...], head)
        dq_head = []
        dk_head = jnp.zeros((halo + rows, 128), F32)
        dv_head = jnp.zeros((halo + rows, 128), F32)
        dk_parts, dv_parts = [], []
        for at in range(0, rows, BLK):
            scores = dot_nt(k_out[at:at + span], q_in[at:at + BLK]) + bias_ref[:, at:at + BLK]
            top = jnp.max(scores, axis=0, keepdims=True)
            expo = jnp.exp2(scores - top)
            inverse = 1.0 / jnp.sum(expo, axis=0, keepdims=True)
            grad_probs = dot_nt(v_out[at:at + span], g_in[at:at + BLK])
            probs = expo * inverse
            delta = jnp.sum(probs * grad_probs, axis=0, keepdims=True)
            grad_scores = probs * (grad_probs - delta)
            probs_cat = jnp.concatenate(split(probs), axis=1)
            scores_cat = jnp.concatenate(split(grad_scores), axis=1)
            g_two = jnp.concatenate([g_mix[at:at + BLK]] * 2, axis=0)
            q_two = jnp.concatenate([q_mix[at:at + BLK]] * 2, axis=0)
            dv_parts.append(dot_nn(probs_cat, g_two))
            dk_parts.append(dot_nn(scores_cat, q_two))
            got = dot_tn(scores_cat, k_mix[at:at + span])
            dq_head.append(fold(got[:BLK] + got[BLK:]))
        for parts, full in ((dk_parts, dk), (dv_parts, dv)):
            pieces = []
            for kb in range((halo + rows) // BLK):
                terms = [
                    parts[qb][(kb - qb) * BLK:(kb - qb + 1) * BLK]
                    for qb in range(rows // BLK)
                    if 0 <= kb - qb < span // BLK
                ]
                pieces.append(fold(functools.reduce(lambda a, b: a + b, terms)))
            full.append(pieces)
        dq.append(dq_head)
    lane = lax.broadcasted_iota(jnp.int32, (BLK, 128), 1)
    for qb in range(rows // BLK):
        rng = slice(qb * BLK, (qb + 1) * BLK)
        far = slice(halo + qb * BLK, halo + (qb + 1) * BLK)
        both = jnp.where(lane < 64, dq[0][qb], dq[1][qb]) * SCALE
        dq_ref[rng] = unrotate(both, cos_ref[far], sin_ref[far])
    for kb in range((halo + rows) // BLK):
        rng = slice(kb * BLK, (kb + 1) * BLK)
        both = jnp.where(lane < 64, dk[0][kb], dk[1][kb]) * SCALE
        dk_ref[rng] = unrotate(both, cos_ref[rng], sin_ref[rng])
        dv_ref[rng] = jnp.where(lane < 64, dv[0][kb], dv[1][kb])


def attend_back(q_rot, kv, grad, seg_q, seg_k, cosine, sine):
    rows, model = q_rot.shape
    total = kv.shape[0]
    pairs = model // 128
    fixed = lambda shape: pl.BlockSpec(shape, lambda p: (0, 0))
    dq, dk, dv = pl.pallas_call(
        attend_back_kernel,
        grid=(pairs,),
        in_specs=[
            pl.BlockSpec((rows, 128), lambda p: (0, p)),
            pl.BlockSpec((total, 128), lambda p: (0, p)),
            pl.BlockSpec((total, 128), lambda p: (0, pairs + p)),
            pl.BlockSpec((rows, 128), lambda p: (0, p)),
            fixed((8, rows)), fixed((total, 128)),
            fixed((total, 128)), fixed((total, 128)),
        ],
        out_specs=[
            pl.BlockSpec((rows, 128), lambda p: (0, p)),
            pl.BlockSpec((total, 128), lambda p: (0, p)),
            pl.BlockSpec((total, 128), lambda p: (0, p)),
        ],
        out_shape=[
            jax.ShapeDtypeStruct((rows, model), F32),
            jax.ShapeDtypeStruct((total, model), F32),
            jax.ShapeDtypeStruct((total, model), F32),
        ],
        scratch_shapes=[pltpu.VMEM((total - rows + BLK, rows), F32)],
        compiler_params=params(),
    )(q_rot, kv, kv, grad, seg_q, seg_k, cosine, sine)
    return dq, dk, dv


def mlp_kernel(resid_ref, cot_ref, gain_ref, bias_ref, scale_ref, up_ref, down_ref,
               out_ref, gnorm_ref, gup_ref, gdown_ref,
               x_hi, x_lo, xt_hi, xt_lo, g_hi, g_lo):
    step = pl.program_id(0)

    @pl.when(step == 0)
    def _():
        xhat, _ = norm_stats(resid_ref[...])
        normed = xhat * gain_ref[...] + bias_ref[...]
        x_hi[...], x_lo[...] = split(normed)
        xt_hi[...], xt_lo[...] = split(normed.T)
        g_hi[...], g_lo[...] = split(cot_ref[...] * scale_ref[0, 0])
        out_ref[...] = jnp.zeros_like(out_ref)
        gnorm_ref[...] = jnp.zeros_like(gnorm_ref)

    up = split(up_ref[...])
    down = split(down_ref[...])
    normed = (x_hi[...], x_lo[...])
    normed_t = (xt_hi[...], xt_lo[...])
    grad_block = (g_hi[...], g_lo[...])
    pre = three(dot_nn, normed, up)
    grad_act = three(dot_nt, grad_block, down)
    inner = 0.7978845608028654 * (pre + 0.044715 * pre * pre * pre)
    bent = jnp.tanh(inner)
    act = 0.5 * pre * (1.0 + bent)
    slope = 0.5 * (1.0 + bent) + 0.5 * pre * (1.0 - bent * bent) * (
        0.7978845608028654 * (1.0 + 3.0 * 0.044715 * pre * pre)
    )
    act2 = split(act)
    grad_pre = split(grad_act * slope)
    out_ref[...] += three(dot_nn, act2, down)
    gnorm_ref[...] += three(dot_nt, grad_pre, up)
    gdown_ref[...] = three(dot_tn, act2, grad_block)
    gup_ref[...] = three(dot_nn, normed_t, grad_pre)


def mlp(resid, cotangent, gain, bias, scale, up_full, down_full):
    rows, model = resid.shape
    hidden = up_full.shape[1]
    wide = 256
    fixed = lambda shape: pl.BlockSpec(shape, lambda j: (0, 0))
    return pl.pallas_call(
        mlp_kernel,
        grid=(hidden // wide,),
        in_specs=[
            fixed((rows, model)), fixed((rows, model)),
            fixed((1, model)), fixed((1, model)),
            pl.BlockSpec(memory_space=pltpu.SMEM),
            pl.BlockSpec((model, wide), lambda j: (0, j)),
            pl.BlockSpec((wide, model), lambda j: (j, 0)),
        ],
        out_specs=[
            fixed((rows, model)), fixed((rows, model)),
            pl.BlockSpec((model, wide), lambda j: (0, j)),
            pl.BlockSpec((wide, model), lambda j: (j, 0)),
        ],
        out_shape=[
            jax.ShapeDtypeStruct((rows, model), F32),
            jax.ShapeDtypeStruct((rows, model), F32),
            jax.ShapeDtypeStruct((model, hidden), F32),
            jax.ShapeDtypeStruct((hidden, model), F32),
        ],
        scratch_shapes=[
            pltpu.VMEM((rows, model), BF16), pltpu.VMEM((rows, model), BF16),
            pltpu.VMEM((model, rows), BF16), pltpu.VMEM((model, rows), BF16),
            pltpu.VMEM((rows, model), BF16), pltpu.VMEM((rows, model), BF16),
        ],
        compiler_params=params(),
    )(resid, cotangent, gain, bias, scale, up_full, down_full)


def norm_back(grad, gain, xhat, rate):
    scaled = grad * gain
    return rate * (
        scaled
        - jnp.mean(scaled, axis=-1, keepdims=True)
        - xhat * jnp.mean(scaled * xhat, axis=-1, keepdims=True)
    )


def matmul(left, right):
    return jnp.dot(left, right, precision=HIGH)


def inner_rows(left, right):
    return lax.dot_general(left, right, (((0,), (0,)), ((), ())), precision=HIGH)


def outer_cols(left, right):
    return lax.dot_general(left, right, (((1,), (1,)), ((), ())), precision=HIGH)


def body(
    block_input,
    embedding,
    earlier_outs,
    dwa_weights,
    ln1_gain,
    ln1_bias,
    w_qkv,
    w_out,
    ln2_gain,
    ln2_bias,
    w_up,
    w_down,
    segments,
    cotangent,
):
    groups = lax.axis_size("seq")
    rows, model = block_input.shape
    length = rows * groups
    halo = 2 * rows
    place = lax.axis_index("seq")
    ahead = [(i, i + 1) for i in range(groups - 1)]
    behind = [(i + 1, i) for i in range(groups - 1)]
    gain1, bias1 = ln1_gain[None], ln1_bias[None]
    gain2, bias2 = ln2_gain[None], ln2_bias[None]

    gather = lambda v: lax.all_gather(v, "dp", axis=0, tiled=True)
    qkv_full = gather(w_qkv)
    seg_own = segments + 1
    near = lax.ppermute(block_input, "seq", ahead)
    seg_near = lax.ppermute(seg_own, "seq", ahead)
    far = lax.ppermute(near, "seq", ahead)
    seg_far = lax.ppermute(seg_near, "seq", ahead)
    seg_all = jnp.concatenate([seg_far, seg_near, seg_own], axis=1)
    seg_k_row = jnp.broadcast_to(seg_all, (8, halo + rows))
    seg_k_col = jnp.broadcast_to(seg_all.reshape(-1, 1), (halo + rows, 128))
    seg_q_row = seg_k_row[:, halo:]
    seg_q_col = seg_k_col[halo:]

    cos_all, sin_all = rotary_tables(length, halo)
    cosine = lax.dynamic_slice_in_dim(jnp.asarray(cos_all), place * rows, halo + rows, 0)
    sine = lax.dynamic_slice_in_dim(jnp.asarray(sin_all), place * rows, halo + rows, 0)

    q_rot, kv, normed_hi, normed_lo = project(
        far, near, block_input, gain1, bias1, qkv_full, cosine, sine
    )
    attended = attend(q_rot, kv, seg_q_col, seg_k_row)

    out_full = gather(w_out)
    up_full = gather(w_up)
    down_full = gather(w_down)
    resid = block_input + matmul(attended, out_full)
    mlp_out, grad_normed_two, grad_up_part, grad_down_part = mlp(
        resid, cotangent, gain2, bias2, dwa_weights[4].reshape(1, 1), up_full, down_full
    )
    scatter = lambda v: lax.psum_scatter(v, "dp", scatter_dimension=0, tiled=True)
    up_shard, down_shard = scatter(grad_up_part), scatter(grad_down_part)

    block_out = resid + mlp_out
    output = (
        dwa_weights[0] * embedding
        + dwa_weights[1] * earlier_outs[0]
        + dwa_weights[2] * earlier_outs[1]
        + dwa_weights[3] * earlier_outs[2]
        + dwa_weights[4] * block_out
    )
    dwa_local = jnp.stack(
        [
            jnp.sum(cotangent * embedding),
            jnp.sum(cotangent * earlier_outs[0]),
            jnp.sum(cotangent * earlier_outs[1]),
            jnp.sum(cotangent * earlier_outs[2]),
            jnp.sum(cotangent * block_out),
        ]
    )
    xhat2, rate2 = norm_stats(resid)
    grad_resid = dwa_weights[4] * cotangent + norm_back(grad_normed_two, gain2, xhat2, rate2)
    grad_gain_two = jnp.sum(grad_normed_two * xhat2, axis=0)
    grad_bias_two = jnp.sum(grad_normed_two, axis=0)
    grad_attended = outer_cols(grad_resid, out_full)
    grad_wout_part = inner_rows(attended, grad_resid)

    dq, dk, dv = attend_back(
        q_rot, kv, grad_attended, seg_q_row, seg_k_col, cosine, sine
    )
    normed_one = normed_hi.astype(F32) + normed_lo.astype(F32)
    dkv = jnp.concatenate([dk, dv], axis=1)
    grad_qkv_part = jnp.concatenate(
        [inner_rows(normed_one[halo:], dq), inner_rows(normed_one, dkv)], axis=1
    )
    wout_shard, qkv_shard = scatter(grad_wout_part), scatter(grad_qkv_part)

    wq, wkv = qkv_full[:, :model], qkv_full[:, model:]
    partial = outer_cols(dkv, wkv)
    own_part = partial[halo:] + outer_cols(dq, wq)
    back_near = partial[rows:halo] + lax.ppermute(partial[:rows], "seq", behind)
    grad_normed_one = own_part + lax.ppermute(back_near, "seq", behind)
    xhat1, rate1 = norm_stats(block_input)
    grad_input = grad_resid + norm_back(grad_normed_one, gain1, xhat1, rate1)
    grad_gain_one = jnp.sum(grad_normed_one * xhat1, axis=0)
    grad_bias_one = jnp.sum(grad_normed_one, axis=0)

    grad_up, grad_down = lax.psum((up_shard, down_shard), "seq")
    grad_qkv, grad_wout = lax.psum((qkv_shard, wout_shard), "seq")
    gain_one, bias_one, gain_two, bias_two, grad_dwa = lax.psum(
        (grad_gain_one, grad_bias_one, grad_gain_two, grad_bias_two, dwa_local), ("dp", "seq")
    )
    return (
        output,
        grad_input,
        grad_dwa,
        gain_one,
        bias_one,
        grad_qkv,
        grad_wout,
        gain_two,
        bias_two,
        grad_up,
        grad_down,
    )


def solution(mesh):
    in_specs = (
        P(("dp", "seq"), None),
        P(("dp", "seq"), None),
        P(None, ("dp", "seq"), None),
        P(),
        P(),
        P(),
        P("dp", None),
        P("dp", None),
        P(),
        P(),
        P("dp", None),
        P("dp", None),
        P("dp", "seq"),
        P(("dp", "seq"), None),
    )
    out_specs = (
        P(("dp", "seq"), None),
        P(("dp", "seq"), None),
        P(),
        P(),
        P(),
        P("dp", None),
        P("dp", None),
        P(),
        P(),
        P("dp", None),
        P("dp", None),
    )
    return jax.shard_map(body, mesh=mesh, in_specs=in_specs, out_specs=out_specs, check_vma=False)
```

```python
import functools
import math

import jax
import jax.numpy as jnp
import numpy as np
from jax import lax
from jax.experimental import pallas as pl
from jax.experimental.pallas import tpu as pltpu
from jax.sharding import PartitionSpec as P

HD = 64
DOC_MOST = 768
LOG2E = math.log2(math.e)
SCALE = 1.0 / math.sqrt(HD)
NEG = -1e30
F32 = jnp.float32
BF16 = jnp.bfloat16
HIGH = lax.Precision.HIGH
VMEM_LIMIT = 56 * 1024 * 1024
BLK = 128


def params():
    return pltpu.CompilerParams(
        dimension_semantics=("arbitrary",), vmem_limit_bytes=VMEM_LIMIT
    )


def split(values):
    high = values.astype(BF16)
    return high, (values - high.astype(F32)).astype(BF16)


def dot_nn(left, right):
    return lax.dot_general(left, right, (((1,), (0,)), ((), ())), preferred_element_type=F32)


def dot_nt(left, right):
    return lax.dot_general(left, right, (((1,), (1,)), ((), ())), preferred_element_type=F32)


def dot_tn(left, right):
    return lax.dot_general(left, right, (((0,), (0,)), ((), ())), preferred_element_type=F32)


def three(dot, left, right):
    return (
        dot(left[0], right[0]) + dot(left[0], right[1]) + dot(left[1], right[0])
    )


def norm_stats(values):
    row_mean = jnp.mean(values, axis=-1, keepdims=True)
    centred = values - row_mean
    row_var = jnp.mean(centred * centred, axis=-1, keepdims=True)
    rate = lax.rsqrt(row_var + 1e-05)
    return centred * rate, rate


def turned(values):
    lane = lax.broadcasted_iota(jnp.int32, values.shape, 1)
    return jnp.where(
        (lane & 63) < 32, pltpu.roll(values, 96, 1), pltpu.roll(values, 32, 1)
    )


def rotate(values, cosine, sine):
    return values * cosine + turned(values) * sine


def unrotate(values, cosine, sine):
    return values * cosine - turned(values) * sine


def rotary_tables(length, halo):
    half = HD // 2
    inv_freq = (10000.0 ** (-(np.arange(half, dtype=np.float32) * 2.0 / HD))).astype(np.float32)
    place = np.arange(-halo, length, dtype=np.float32)
    angles = place[:, None] * inv_freq[None, :]
    cosine = np.cos(angles.astype(np.float64)).astype(np.float32)
    sine = np.sin(angles.astype(np.float64)).astype(np.float32)
    return (
        np.concatenate([cosine] * 4, axis=1),
        np.concatenate([-sine, sine, -sine, sine], axis=1),
    )


def qkv_kernel(far_ref, near_ref, own_ref, gain_ref, bias_ref, w_ref, cos_ref, sin_ref,
               q_ref, kv_ref, hi_ref, lo_ref):
    step = pl.program_id(0)
    rows = own_ref.shape[0]
    third = pl.num_programs(0) // 3
    halo = hi_ref.shape[0] - rows

    @pl.when(step == 0)
    def _():
        for at, ref in enumerate((far_ref, near_ref, own_ref)):
            xhat, _ = norm_stats(ref[...])
            high, low = split(xhat * gain_ref[...] + bias_ref[...])
            hi_ref[at * rows:(at + 1) * rows] = high
            lo_ref[at * rows:(at + 1) * rows] = low

    weights = split(w_ref[...])

    @pl.when(step < third)
    def _():
        got = three(dot_nn, (hi_ref[halo:], lo_ref[halo:]), weights)
        for at in range(0, got.shape[1], 128):
            q_ref[:, at:at + 128] = rotate(got[:, at:at + 128], cos_ref[halo:], sin_ref[halo:])

    @pl.when((step >= third) & (step < 2 * third))
    def _():
        got = three(dot_nn, (hi_ref[...], lo_ref[...]), weights)
        for at in range(0, got.shape[1], 128):
            kv_ref[:, at:at + 128] = rotate(got[:, at:at + 128], cos_ref[...], sin_ref[...])

    @pl.when(step >= 2 * third)
    def _():
        kv_ref[...] = three(dot_nn, (hi_ref[...], lo_ref[...]), weights)


def project(far, near, own, gain, bias, w_full, cosine, sine):
    rows, model = own.shape
    total = 3 * rows
    wide = 256
    third = model // wide
    whole = lambda shape: pl.BlockSpec(shape, lambda j: (0, 0))
    return pl.pallas_call(
        qkv_kernel,
        grid=(3 * third,),
        in_specs=[
            whole((rows, model)), whole((rows, model)), whole((rows, model)),
            whole((1, model)), whole((1, model)),
            pl.BlockSpec((model, wide), lambda j: (0, j)),
            whole((total, 128)), whole((total, 128)),
        ],
        out_specs=[
            pl.BlockSpec((rows, wide), lambda j: (0, jnp.minimum(j, third - 1))),
            pl.BlockSpec((total, wide), lambda j: (0, jnp.maximum(j - third, 0))),
            whole((total, model)), whole((total, model)),
        ],
        out_shape=[
            jax.ShapeDtypeStruct((rows, model), F32),
            jax.ShapeDtypeStruct((total, 2 * model), F32),
            jax.ShapeDtypeStruct((total, model), BF16),
            jax.ShapeDtypeStruct((total, model), BF16),
        ],
        compiler_params=params(),
    )(far, near, own, gain, bias, w_full, cosine, sine)


def own_pair(values, head):
    lane = lax.broadcasted_iota(jnp.int32, values.shape, 1)
    other = pltpu.roll(values, 64, 1)
    return jnp.where((lane < 64) == (head == 0), values, other)


def outer_form(values, head):
    high, low = split(own_pair(values, head))
    return jnp.concatenate([high, low], axis=1)


def mixed(values, head):
    pair = own_pair(values, head)
    lane = lax.broadcasted_iota(jnp.int32, pair.shape, 1)
    high = pair.astype(BF16).astype(F32)
    return jnp.where(lane < 64, high, pair - high).astype(BF16)


def inner_form(values, head):
    half = mixed(values, head)
    return jnp.concatenate([half, half], axis=1)


def fold(values):
    return values + pltpu.roll(values, 64, 1)


def attend_kernel(q_ref, k_ref, v_ref, segq_ref, segk_ref, out_ref, bias_ref):
    rows = q_ref.shape[0]
    halo = k_ref.shape[0] - rows
    span = halo + BLK

    @pl.when(pl.program_id(0) == 0)
    def _():
        for at in range(0, rows, BLK):
            row = lax.broadcasted_iota(jnp.int32, (BLK, span), 0)
            col = lax.broadcasted_iota(jnp.int32, (BLK, span), 1)
            same = segq_ref[at:at + BLK, :1] == segk_ref[:1, at:at + span]
            bias_ref[at:at + BLK] = jnp.where(same & (col - halo <= row), 0.0, NEG)

    lane = lax.broadcasted_iota(jnp.int32, (BLK, 128), 1)
    scaled = q_ref[...] * (SCALE * LOG2E)
    results = []
    for head in range(2):
        left = inner_form(scaled, head)
        right = outer_form(k_ref[...], head)
        vals = mixed(v_ref[...], head)
        outs = []
        for at in range(0, rows, BLK):
            scores = dot_nt(left[at:at + BLK], right[at:at + span]) + bias_ref[at:at + BLK]
            top = jnp.max(scores, axis=1, keepdims=True)
            expo = jnp.exp2(scores - top)
            total = jnp.sum(expo, axis=1, keepdims=True)
            high, low = split(expo)
            got = dot_nn(high, vals[at:at + span]) + dot_nn(low, vals[at:at + span])
            outs.append(fold(got) / total)
        results.append(outs)
    for at in range(0, rows, BLK):
        out_ref[at:at + BLK] = jnp.where(
            lane < 64, results[0][at // BLK], results[1][at // BLK]
        )


def attend(q_rot, kv, seg_q, seg_k):
    rows, model = q_rot.shape
    total = kv.shape[0]
    pairs = model // 128
    return pl.pallas_call(
        attend_kernel,
        grid=(pairs,),
        in_specs=[
            pl.BlockSpec((rows, 128), lambda p: (0, p)),
            pl.BlockSpec((total, 128), lambda p: (0, p)),
            pl.BlockSpec((total, 128), lambda p: (0, pairs + p)),
            pl.BlockSpec((rows, 128), lambda p: (0, 0)),
            pl.BlockSpec((8, total), lambda p: (0, 0)),
        ],
        out_specs=pl.BlockSpec((rows, 128), lambda p: (0, p)),
        out_shape=jax.ShapeDtypeStruct((rows, model), F32),
        scratch_shapes=[pltpu.VMEM((rows, total - rows + BLK), F32)],
        compiler_params=params(),
    )(q_rot, kv, kv, seg_q, seg_k)


def attend_back_kernel(q_ref, k_ref, v_ref, g_ref, segq_ref, segk_ref, cos_ref, sin_ref,
                       dq_ref, dk_ref, dv_ref, bias_ref):
    rows = q_ref.shape[0]
    halo = k_ref.shape[0] - rows
    span = halo + BLK

    @pl.when(pl.program_id(0) == 0)
    def _():
        for at in range(0, rows, BLK):
            key = lax.broadcasted_iota(jnp.int32, (span, BLK), 0)
            query = lax.broadcasted_iota(jnp.int32, (span, BLK), 1)
            same = segk_ref[at:at + span, :1] == segq_ref[:1, at:at + BLK]
            bias_ref[:, at:at + BLK] = jnp.where(same & (key - halo <= query), 0.0, NEG)

    scaled = q_ref[...] * (SCALE * LOG2E)
    dq, dk, dv = [], [], []
    for head in range(2):
        q_in = inner_form(scaled, head)
        g_in = inner_form(g_ref[...], head)
        k_out = outer_form(k_ref[...], head)
        v_out = outer_form(v_ref[...], head)
        q_mix = mixed(q_ref[...], head)
        g_mix = mixed(g_ref[...], head)
        k_mix = mixed(k_ref[...], head)
        dq_head = []
        dk_head = jnp.zeros((halo + rows, 128), F32)
        dv_head = jnp.zeros((halo + rows, 128), F32)
        dk_parts, dv_parts = [], []
        for at in range(0, rows, BLK):
            scores = dot_nt(k_out[at:at + span], q_in[at:at + BLK]) + bias_ref[:, at:at + BLK]
            top = jnp.max(scores, axis=0, keepdims=True)
            expo = jnp.exp2(scores - top)
            inverse = 1.0 / jnp.sum(expo, axis=0, keepdims=True)
            grad_probs = dot_nt(v_out[at:at + span], g_in[at:at + BLK])
            probs = expo * inverse
            delta = jnp.sum(probs * grad_probs, axis=0, keepdims=True)
            grad_scores = probs * (grad_probs - delta)
            probs_cat = jnp.concatenate(split(probs), axis=1)
            scores_cat = jnp.concatenate(split(grad_scores), axis=1)
            g_two = jnp.concatenate([g_mix[at:at + BLK]] * 2, axis=0)
            q_two = jnp.concatenate([q_mix[at:at + BLK]] * 2, axis=0)
            dv_parts.append(dot_nn(probs_cat, g_two))
            dk_parts.append(dot_nn(scores_cat, q_two))
            got = dot_tn(scores_cat, k_mix[at:at + span])
            dq_head.append(fold(got[:BLK] + got[BLK:]))
        for parts, full in ((dk_parts, dk), (dv_parts, dv)):
            pieces = []
            for kb in range((halo + rows) // BLK):
                terms = [
                    parts[qb][(kb - qb) * BLK:(kb - qb + 1) * BLK]
                    for qb in range(rows // BLK)
                    if 0 <= kb - qb < span // BLK
                ]
                pieces.append(fold(functools.reduce(lambda a, b: a + b, terms)))
            full.append(pieces)
        dq.append(dq_head)
    lane = lax.broadcasted_iota(jnp.int32, (BLK, 128), 1)
    for qb in range(rows // BLK):
        rng = slice(qb * BLK, (qb + 1) * BLK)
        far = slice(halo + qb * BLK, halo + (qb + 1) * BLK)
        both = jnp.where(lane < 64, dq[0][qb], dq[1][qb]) * SCALE
        dq_ref[rng] = unrotate(both, cos_ref[far], sin_ref[far])
    for kb in range((halo + rows) // BLK):
        rng = slice(kb * BLK, (kb + 1) * BLK)
        both = jnp.where(lane < 64, dk[0][kb], dk[1][kb]) * SCALE
        dk_ref[rng] = unrotate(both, cos_ref[rng], sin_ref[rng])
        dv_ref[rng] = jnp.where(lane < 64, dv[0][kb], dv[1][kb])


def attend_back(q_rot, kv, grad, seg_q, seg_k, cosine, sine):
    rows, model = q_rot.shape
    total = kv.shape[0]
    pairs = model // 128
    fixed = lambda shape: pl.BlockSpec(shape, lambda p: (0, 0))
    dq, dk, dv = pl.pallas_call(
        attend_back_kernel,
        grid=(pairs,),
        in_specs=[
            pl.BlockSpec((rows, 128), lambda p: (0, p)),
            pl.BlockSpec((total, 128), lambda p: (0, p)),
            pl.BlockSpec((total, 128), lambda p: (0, pairs + p)),
            pl.BlockSpec((rows, 128), lambda p: (0, p)),
            fixed((8, rows)), fixed((total, 128)),
            fixed((total, 128)), fixed((total, 128)),
        ],
        out_specs=[
            pl.BlockSpec((rows, 128), lambda p: (0, p)),
            pl.BlockSpec((total, 128), lambda p: (0, p)),
            pl.BlockSpec((total, 128), lambda p: (0, p)),
        ],
        out_shape=[
            jax.ShapeDtypeStruct((rows, model), F32),
            jax.ShapeDtypeStruct((total, model), F32),
            jax.ShapeDtypeStruct((total, model), F32),
        ],
        scratch_shapes=[pltpu.VMEM((total - rows + BLK, rows), F32)],
        compiler_params=params(),
    )(q_rot, kv, kv, grad, seg_q, seg_k, cosine, sine)
    return dq, dk, dv


def mlp_kernel(count, chip_ref, resid_ref, other_ref, cot_ref, cot_other_ref, gain_ref, bias_ref,
               scale_ref, *refs):
    up_refs, down_refs = refs[:count], refs[count:2 * count]
    out_ref, gnorm_ref, grad_ref = refs[2 * count:2 * count + 3]
    (x_hi, x_lo, xt_hi, xt_lo, g_hi, g_lo, up_hi, up_lo, down_hi, down_lo) = refs[2 * count + 3:]
    step = pl.program_id(0)
    rows = resid_ref.shape[0]

    @pl.when(step == 0)
    def _():
        for at, source, cot in ((0, resid_ref, cot_ref), (rows, other_ref, cot_other_ref)):
            xhat, _ = norm_stats(source[...])
            normed = xhat * gain_ref[...] + bias_ref[...]
            x_hi[at:at + rows], x_lo[at:at + rows] = split(normed)
            xt_hi[:, at:at + rows], xt_lo[:, at:at + rows] = split(normed.T)
            g_hi[at:at + rows], g_lo[at:at + rows] = split(cot[...] * scale_ref[0, 0])
        out_ref[...] = jnp.zeros_like(out_ref)
        gnorm_ref[...] = jnp.zeros_like(gnorm_ref)

    for at in range(count):
        spot = (chip_ref[0] ^ at) if count > 1 else 0
        up_rows = up_refs[at].shape[0]
        high, low = split(up_refs[at][...])
        here = pl.ds(pl.multiple_of(spot * up_rows, up_rows), up_rows)
        up_hi[here], up_lo[here] = high, low
        block = down_refs[at][...]
        block = block.reshape(-1, block.shape[-1])
        high, low = split(block)
        here = pl.ds(pl.multiple_of(spot * block.shape[0], block.shape[0]), block.shape[0])
        down_hi[here], down_lo[here] = high, low

    chips, _, tall, width = grad_ref.shape
    up_tall = up_hi.shape[0] // chips
    deep = down_hi.shape[0] // chips
    up = (up_hi[...], up_lo[...])
    down = (down_hi[...], down_lo[...])
    normed = (x_hi[...], x_lo[...])
    normed_t = (xt_hi[...], xt_lo[...])
    grad_block = (g_hi[...], g_lo[...])
    pre = three(dot_nn, normed, up)
    grad_act = three(dot_nt, grad_block, down)
    inner = 0.7978845608028654 * (pre + 0.044715 * pre * pre * pre)
    bent = jnp.tanh(inner)
    act = 0.5 * pre * (1.0 + bent)
    slope = 0.5 * (1.0 + bent) + 0.5 * pre * (1.0 - bent * bent) * (
        0.7978845608028654 * (1.0 + 3.0 * 0.044715 * pre * pre)
    )
    act2 = split(act)
    grad_pre = split(grad_act * slope)
    out_ref[...] += three(dot_nn, act2, down)
    gnorm_ref[...] += three(dot_nt, grad_pre, up)
    gup = three(dot_nn, normed_t, grad_pre)
    gdown = three(dot_tn, act2, grad_block)
    half = deep // 2
    for chip in range(chips):
        grad_ref[chip, 0, :up_tall] = gup[chip * up_tall:(chip + 1) * up_tall]
        part = gdown[chip * deep:(chip + 1) * deep]
        grad_ref[chip, 0, up_tall:up_tall + deep] = part[:, :width]
        grad_ref[chip, 0, up_tall + deep:] = jnp.concatenate(
            [part[:half, width:], part[half:, width:]], axis=1
        )


def mlp(first, steps, chip, chips, resid, other, cot, cot_other, gain, bias, scale, ups, downs):
    rows, model = resid.shape
    width = 512
    up_tall = model // chips
    deep = width // chips
    fixed = lambda shape: pl.BlockSpec(shape, lambda j, c: (0, 0))
    if len(ups) > 1:
        down_spec = pl.BlockSpec((deep, model), lambda j, c: (first + j, 0))
    else:
        downs = [downs[0].reshape(chips, -1, model)]
        down_spec = pl.BlockSpec((chips, deep, model), lambda j, c: (0, first + j, 0))
    tall = up_tall + deep + deep // 2
    grid_spec = pltpu.PrefetchScalarGridSpec(
        num_scalar_prefetch=1,
        grid=(steps,),
        in_specs=[fixed((rows, model))] * 4 + [fixed((1, model))] * 2
        + [pl.BlockSpec(memory_space=pltpu.SMEM)]
        + [pl.BlockSpec((up.shape[0], width), lambda j, c: (0, first + j)) for up in ups]
        + [down_spec] * len(downs),
        out_specs=[
            fixed((2 * rows, model)), fixed((2 * rows, model)),
            pl.BlockSpec((chips, 1, tall, width), lambda j, c: (0, j, 0, 0)),
        ],
        scratch_shapes=[
            pltpu.VMEM((2 * rows, model), BF16), pltpu.VMEM((2 * rows, model), BF16),
            pltpu.VMEM((model, 2 * rows), BF16), pltpu.VMEM((model, 2 * rows), BF16),
            pltpu.VMEM((2 * rows, model), BF16), pltpu.VMEM((2 * rows, model), BF16),
            pltpu.VMEM((model, width), BF16), pltpu.VMEM((model, width), BF16),
            pltpu.VMEM((width, model), BF16), pltpu.VMEM((width, model), BF16),
        ],
    )
    return pl.pallas_call(
        functools.partial(mlp_kernel, len(ups)),
        grid_spec=grid_spec,
        out_shape=[
            jax.ShapeDtypeStruct((2 * rows, model), F32),
            jax.ShapeDtypeStruct((2 * rows, model), F32),
            jax.ShapeDtypeStruct((chips, steps, tall, width), F32),
        ],
        compiler_params=params(),
    )(chip, resid, other, cot, cot_other, gain, bias, scale, *ups, *downs)


def unpack_grads(summed, sibling_swap, core, chips):
    steps, tall, width = summed.shape
    up_tall = tall // 2
    deep = up_tall * 2 // 3
    half = up_tall // 2
    up = summed[:, :up_tall]
    mine = jnp.where(core == 0, up[:, :half], up[:, half:])
    other = sibling_swap(jnp.where(core == 0, up[:, half:], up[:, :half]))
    by_core = jnp.stack(
        [jnp.where(core == 0, mine, other), jnp.where(core == 0, other, mine)], axis=0
    )
    by_core = by_core.reshape(2, steps, half, chips, width // chips)
    grad_up = jnp.transpose(by_core, (2, 3, 0, 1, 4))
    left = summed[:, up_tall:up_tall + deep]
    tail = summed[:, up_tall + deep:]
    quarter = width // 2
    right = jnp.concatenate([tail[:, :, :quarter], tail[:, :, quarter:]], axis=1)
    grad_down = jnp.concatenate([left, right], axis=2).reshape(steps * deep, -1)
    return grad_up, grad_down


def norm_back(grad, gain, xhat, rate):
    scaled = grad * gain
    return rate * (
        scaled
        - jnp.mean(scaled, axis=-1, keepdims=True)
        - xhat * jnp.mean(scaled * xhat, axis=-1, keepdims=True)
    )


def matmul(left, right):
    return jnp.dot(left, right, precision=HIGH)


def inner_rows(left, right):
    return lax.dot_general(left, right, (((0,), (0,)), ((), ())), precision=HIGH)


def outer_cols(left, right):
    return lax.dot_general(left, right, (((1,), (1,)), ((), ())), precision=HIGH)


def body(
    block_input,
    embedding,
    earlier_outs,
    dwa_weights,
    ln1_gain,
    ln1_bias,
    w_qkv,
    w_out,
    ln2_gain,
    ln2_bias,
    w_up,
    w_down,
    segments,
    cotangent,
):
    groups = lax.axis_size("seq")
    rows, model = block_input.shape
    length = rows * groups
    halo = 2 * rows
    place = lax.axis_index("seq")
    ahead = [(i, i + 1) for i in range(groups - 1)]
    behind = [(i + 1, i) for i in range(groups - 1)]
    gain1, bias1 = ln1_gain[None], ln1_bias[None]
    gain2, bias2 = ln2_gain[None], ln2_bias[None]

    devices = lax.axis_size("dp")
    chips = devices // 2
    spot = lax.axis_index("dp")
    core = spot % 2
    chip = (spot // 2).reshape(1).astype(jnp.int32)
    same_core = [[2 * i + c for i in range(chips)] for c in range(2)]
    exchange = lambda v, bit: lax.ppermute(v, "dp", [(i, i ^ bit) for i in range(devices)])
    swap = lambda v: exchange(v, 1)

    gather = lambda v: lax.all_gather(v, "dp", axis=0, tiled=True)
    qkv_full = gather(w_qkv)

    shard = w_down.shape[0]
    third = shard // 3
    by_core = w_up.reshape(w_up.shape[0], chips, 2, 3, third)
    by_core = jnp.transpose(by_core, (2, 0, 3, 1, 4)).reshape(2, w_up.shape[0], -1)
    mine = jnp.where(core == 0, by_core[0], by_core[1])
    given = swap(jnp.where(core == 0, by_core[1], by_core[0]))
    up_chip = jnp.concatenate(
        [jnp.where(core == 0, mine, given), jnp.where(core == 0, given, mine)], axis=0
    )
    if chips == 4:
        up_x, down_x = exchange(up_chip, 2), exchange(w_down, 2)
        up_y, down_y = exchange(up_chip, 4), exchange(w_down, 4)
        ups = [up_chip, up_x, up_y, exchange(up_y, 2)]
        downs = [w_down, down_x, down_y, exchange(down_x, 4)]
    else:
        ups, downs = (
            [lax.all_gather(v, "dp", axis=0, tiled=True, axis_index_groups=same_core)]
            for v in (up_chip, w_down)
        )

    seg_own = segments + 1
    near = lax.ppermute(block_input, "seq", ahead)
    seg_near = lax.ppermute(seg_own, "seq", ahead)
    far = lax.ppermute(near, "seq", ahead)
    seg_far = lax.ppermute(seg_near, "seq", ahead)
    seg_all = jnp.concatenate([seg_far, seg_near, seg_own], axis=1)
    seg_k_row = jnp.broadcast_to(seg_all, (8, halo + rows))
    seg_k_col = jnp.broadcast_to(seg_all.reshape(-1, 1), (halo + rows, 128))
    seg_q_row = seg_k_row[:, halo:]
    seg_q_col = seg_k_col[halo:]

    cos_all, sin_all = rotary_tables(length, halo)
    cosine = lax.dynamic_slice_in_dim(jnp.asarray(cos_all), place * rows, halo + rows, 0)
    sine = lax.dynamic_slice_in_dim(jnp.asarray(sin_all), place * rows, halo + rows, 0)

    q_rot, kv, normed_hi, normed_lo = project(
        far, near, block_input, gain1, bias1, qkv_full, cosine, sine
    )
    attended = attend(q_rot, kv, seg_q_col, seg_k_row)

    out_full = gather(w_out)
    resid = block_input + matmul(attended, out_full)
    resid_other = swap(resid)
    cot_other = swap(cotangent)
    scale = dwa_weights[4].reshape(1, 1)
    call = functools.partial(
        mlp, chip=chip, chips=chips, resid=resid, other=resid_other, cot=cotangent,
        cot_other=cot_other, gain=gain2, bias=bias2, scale=scale, ups=ups, downs=downs,
    )
    scatter = lambda v: lax.psum_scatter(v, "dp", scatter_dimension=0, tiled=True)
    scatter_chips = lambda v: lax.psum_scatter(
        v, "dp", scatter_dimension=0, tiled=True, axis_index_groups=same_core
    )
    out_a, gnorm_a, grads_a = call(0, 1)
    shard_a = scatter_chips(grads_a)[0]
    out_b, gnorm_b, grads_b = call(1, 2)
    shard_b = scatter_chips(grads_b)[0]
    grad_normed_two = gnorm_a[:rows] + gnorm_b[:rows] + swap(gnorm_a[rows:] + gnorm_b[rows:])
    mlp_out = out_a[:rows] + out_b[:rows] + swap(out_a[rows:] + out_b[rows:])

    block_out = resid + mlp_out
    output = (
        dwa_weights[0] * embedding
        + dwa_weights[1] * earlier_outs[0]
        + dwa_weights[2] * earlier_outs[1]
        + dwa_weights[3] * earlier_outs[2]
        + dwa_weights[4] * block_out
    )
    dwa_local = jnp.stack(
        [
            jnp.sum(cotangent * embedding),
            jnp.sum(cotangent * earlier_outs[0]),
            jnp.sum(cotangent * earlier_outs[1]),
            jnp.sum(cotangent * earlier_outs[2]),
            jnp.sum(cotangent * block_out),
        ]
    )
    xhat2, rate2 = norm_stats(resid)
    grad_resid = dwa_weights[4] * cotangent + norm_back(grad_normed_two, gain2, xhat2, rate2)
    grad_gain_two = jnp.sum(grad_normed_two * xhat2, axis=0)
    grad_bias_two = jnp.sum(grad_normed_two, axis=0)
    grad_attended = outer_cols(grad_resid, out_full)
    grad_wout_part = inner_rows(attended, grad_resid)

    dq, dk, dv = attend_back(
        q_rot, kv, grad_attended, seg_q_row, seg_k_col, cosine, sine
    )
    normed_one = normed_hi.astype(F32) + normed_lo.astype(F32)
    dkv = jnp.concatenate([dk, dv], axis=1)
    shard_c = scatter(
        jnp.concatenate(
            [inner_rows(normed_one[halo:], dq), inner_rows(normed_one, dkv), grad_wout_part],
            axis=1,
        )
    )

    wq, wkv = qkv_full[:, :model], qkv_full[:, model:]
    partial = outer_cols(dkv, wkv)
    own_part = partial[halo:] + outer_cols(dq, wq)
    back_near = partial[rows:halo] + lax.ppermute(partial[:rows], "seq", behind)
    grad_normed_one = own_part + lax.ppermute(back_near, "seq", behind)
    xhat1, rate1 = norm_stats(block_input)
    grad_input = grad_resid + norm_back(grad_normed_one, gain1, xhat1, rate1)
    grad_gain_one = jnp.sum(grad_normed_one * xhat1, axis=0)
    grad_bias_one = jnp.sum(grad_normed_one, axis=0)

    sum_a = lax.psum(shard_a, "seq")
    shard_b, sum_a = lax.optimization_barrier((shard_b, sum_a))
    sum_b = lax.psum(shard_b, "seq")
    shard_c, sum_b = lax.optimization_barrier((shard_c, sum_b))
    sum_c = lax.psum(shard_c, "seq")
    up_a, down_a = unpack_grads(sum_a, swap, core, chips)
    up_b, down_b = unpack_grads(sum_b, swap, core, chips)
    grad_up = jnp.concatenate([up_a, up_b], axis=3).reshape(w_up.shape)
    grad_down = jnp.concatenate([down_a, down_b], axis=0)
    grad_qkv, grad_wout = sum_c[:, :3 * model], sum_c[:, 3 * model:]
    gain_one, bias_one, gain_two, bias_two, grad_dwa = lax.psum(
        (grad_gain_one, grad_bias_one, grad_gain_two, grad_bias_two, dwa_local), ("dp", "seq")
    )
    return (
        output,
        grad_input,
        grad_dwa,
        gain_one,
        bias_one,
        grad_qkv,
        grad_wout,
        gain_two,
        bias_two,
        grad_up,
        grad_down,
    )


def solution(mesh):
    in_specs = (
        P(("dp", "seq"), None),
        P(("dp", "seq"), None),
        P(None, ("dp", "seq"), None),
        P(),
        P(),
        P(),
        P("dp", None),
        P("dp", None),
        P(),
        P(),
        P("dp", None),
        P("dp", None),
        P("dp", "seq"),
        P(("dp", "seq"), None),
    )
    out_specs = (
        P(("dp", "seq"), None),
        P(("dp", "seq"), None),
        P(),
        P(),
        P(),
        P("dp", None),
        P("dp", None),
        P(),
        P(),
        P("dp", None),
        P("dp", None),
    )
    return jax.shard_map(body, mesh=mesh, in_specs=in_specs, out_specs=out_specs, check_vma=False)
```

```python
import functools
import math

import jax
import jax.numpy as jnp
import numpy as np
from jax import lax
from jax.experimental import pallas as pl
from jax.experimental.pallas import tpu as pltpu
from jax.sharding import PartitionSpec as P

HD = 64
DOC_MOST = 768
LOG2E = math.log2(math.e)
SCALE = 1.0 / math.sqrt(HD)
NEG = -1e30
F32 = jnp.float32
BF16 = jnp.bfloat16
HIGH = lax.Precision.HIGH
VMEM_LIMIT = 56 * 1024 * 1024
BLK = 128


def cost(micros):
    return pl.CostEstimate(
        flops=int(micros * 1.1e9), bytes_accessed=1 << 20, transcendentals=0
    )


def params():
    return pltpu.CompilerParams(
        dimension_semantics=("arbitrary",), vmem_limit_bytes=VMEM_LIMIT
    )


def split(values):
    high = values.astype(BF16)
    return high, (values - high.astype(F32)).astype(BF16)


def dot_nn(left, right):
    return lax.dot_general(left, right, (((1,), (0,)), ((), ())), preferred_element_type=F32)


def dot_nt(left, right):
    return lax.dot_general(left, right, (((1,), (1,)), ((), ())), preferred_element_type=F32)


def dot_tn(left, right):
    return lax.dot_general(left, right, (((0,), (0,)), ((), ())), preferred_element_type=F32)


def three(dot, left, right):
    return (
        dot(left[0], right[0]) + dot(left[0], right[1]) + dot(left[1], right[0])
    )


def norm_stats(values):
    row_mean = jnp.mean(values, axis=-1, keepdims=True)
    centred = values - row_mean
    row_var = jnp.mean(centred * centred, axis=-1, keepdims=True)
    rate = lax.rsqrt(row_var + 1e-05)
    return centred * rate, rate


def turned(values):
    lane = lax.broadcasted_iota(jnp.int32, values.shape, 1)
    return jnp.where(
        (lane & 63) < 32, pltpu.roll(values, 96, 1), pltpu.roll(values, 32, 1)
    )


def rotate(values, cosine, sine):
    return values * cosine + turned(values) * sine


def unrotate(values, cosine, sine):
    return values * cosine - turned(values) * sine


def rotary_tables(length, halo):
    half = HD // 2
    inv_freq = (10000.0 ** (-(np.arange(half, dtype=np.float32) * 2.0 / HD))).astype(np.float32)
    place = np.arange(-halo, length, dtype=np.float32)
    angles = place[:, None] * inv_freq[None, :]
    cosine = np.cos(angles.astype(np.float64)).astype(np.float32)
    sine = np.sin(angles.astype(np.float64)).astype(np.float32)
    return (
        np.concatenate([cosine] * 4, axis=1),
        np.concatenate([-sine, sine, -sine, sine], axis=1),
    )


def qkv_kernel(far_ref, near_ref, own_ref, gain_ref, bias_ref, w_ref, cos_ref, sin_ref,
               q_ref, kv_ref, hi_ref, lo_ref):
    step = pl.program_id(0)
    rows = own_ref.shape[0]
    third = pl.num_programs(0) // 3
    halo = hi_ref.shape[0] - rows

    @pl.when(step == 0)
    def _():
        for at, ref in enumerate((far_ref, near_ref, own_ref)):
            xhat, _ = norm_stats(ref[...])
            high, low = split(xhat * gain_ref[...] + bias_ref[...])
            hi_ref[at * rows:(at + 1) * rows] = high
            lo_ref[at * rows:(at + 1) * rows] = low

    weights = split(w_ref[...])

    @pl.when(step < third)
    def _():
        got = three(dot_nn, (hi_ref[halo:], lo_ref[halo:]), weights)
        for at in range(0, got.shape[1], 128):
            q_ref[:, at:at + 128] = rotate(got[:, at:at + 128], cos_ref[halo:], sin_ref[halo:])

    @pl.when((step >= third) & (step < 2 * third))
    def _():
        got = three(dot_nn, (hi_ref[...], lo_ref[...]), weights)
        for at in range(0, got.shape[1], 128):
            kv_ref[:, at:at + 128] = rotate(got[:, at:at + 128], cos_ref[...], sin_ref[...])

    @pl.when(step >= 2 * third)
    def _():
        kv_ref[...] = three(dot_nn, (hi_ref[...], lo_ref[...]), weights)


def project(far, near, own, gain, bias, w_full, cosine, sine):
    rows, model = own.shape
    total = 3 * rows
    wide = 256
    third = model // wide
    whole = lambda shape: pl.BlockSpec(shape, lambda j: (0, 0))
    return pl.pallas_call(
        qkv_kernel,
        grid=(3 * third,),
        in_specs=[
            whole((rows, model)), whole((rows, model)), whole((rows, model)),
            whole((1, model)), whole((1, model)),
            pl.BlockSpec((model, wide), lambda j: (0, j)),
            whole((total, 128)), whole((total, 128)),
        ],
        out_specs=[
            pl.BlockSpec((rows, wide), lambda j: (0, jnp.minimum(j, third - 1))),
            pl.BlockSpec((total, wide), lambda j: (0, jnp.maximum(j - third, 0))),
            whole((total, model)), whole((total, model)),
        ],
        out_shape=[
            jax.ShapeDtypeStruct((rows, model), F32),
            jax.ShapeDtypeStruct((total, 2 * model), F32),
            jax.ShapeDtypeStruct((total, model), BF16),
            jax.ShapeDtypeStruct((total, model), BF16),
        ],
        cost_estimate=cost(20),
        compiler_params=params(),
    )(far, near, own, gain, bias, w_full, cosine, sine)


def own_pair(values, head):
    lane = lax.broadcasted_iota(jnp.int32, values.shape, 1)
    other = pltpu.roll(values, 64, 1)
    return jnp.where((lane < 64) == (head == 0), values, other)


def outer_form(values, head):
    high, low = split(own_pair(values, head))
    return jnp.concatenate([high, low], axis=1)


def mixed(values, head):
    pair = own_pair(values, head)
    lane = lax.broadcasted_iota(jnp.int32, pair.shape, 1)
    high = pair.astype(BF16).astype(F32)
    return jnp.where(lane < 64, high, pair - high).astype(BF16)


def inner_form(values, head):
    half = mixed(values, head)
    return jnp.concatenate([half, half], axis=1)


def fold(values):
    return values + pltpu.roll(values, 64, 1)


def attend_kernel(q_ref, k_ref, v_ref, segq_ref, segk_ref, out_ref, bias_ref):
    rows = q_ref.shape[0]
    halo = k_ref.shape[0] - rows
    span = halo + BLK

    @pl.when(pl.program_id(0) == 0)
    def _():
        for at in range(0, rows, BLK):
            row = lax.broadcasted_iota(jnp.int32, (BLK, span), 0)
            col = lax.broadcasted_iota(jnp.int32, (BLK, span), 1)
            same = segq_ref[at:at + BLK, :1] == segk_ref[:1, at:at + span]
            bias_ref[at:at + BLK] = jnp.where(same & (col - halo <= row), 0.0, NEG)

    lane = lax.broadcasted_iota(jnp.int32, (BLK, 128), 1)
    scaled = q_ref[...] * (SCALE * LOG2E)
    results = []
    for head in range(2):
        left = inner_form(scaled, head)
        right = outer_form(k_ref[...], head)
        vals = mixed(v_ref[...], head)
        outs = []
        for at in range(0, rows, BLK):
            scores = dot_nt(left[at:at + BLK], right[at:at + span]) + bias_ref[at:at + BLK]
            top = jnp.max(scores, axis=1, keepdims=True)
            expo = jnp.exp2(scores - top)
            total = jnp.sum(expo, axis=1, keepdims=True)
            high, low = split(expo)
            got = dot_nn(high, vals[at:at + span]) + dot_nn(low, vals[at:at + span])
            outs.append(fold(got) / total)
        results.append(outs)
    for at in range(0, rows, BLK):
        out_ref[at:at + BLK] = jnp.where(
            lane < 64, results[0][at // BLK], results[1][at // BLK]
        )


def attend(q_rot, kv, seg_q, seg_k):
    rows, model = q_rot.shape
    total = kv.shape[0]
    pairs = model // 128
    return pl.pallas_call(
        attend_kernel,
        grid=(pairs,),
        in_specs=[
            pl.BlockSpec((rows, 128), lambda p: (0, p)),
            pl.BlockSpec((total, 128), lambda p: (0, p)),
            pl.BlockSpec((total, 128), lambda p: (0, pairs + p)),
            pl.BlockSpec((rows, 128), lambda p: (0, 0)),
            pl.BlockSpec((8, total), lambda p: (0, 0)),
        ],
        out_specs=pl.BlockSpec((rows, 128), lambda p: (0, p)),
        out_shape=jax.ShapeDtypeStruct((rows, model), F32),
        scratch_shapes=[pltpu.VMEM((rows, total - rows + BLK), F32)],
        cost_estimate=cost(24),
        compiler_params=params(),
    )(q_rot, kv, kv, seg_q, seg_k)


def attend_back_kernel(q_ref, k_ref, v_ref, g_ref, segq_ref, segk_ref, cos_ref, sin_ref,
                       dq_ref, dk_ref, dv_ref, bias_ref):
    rows = q_ref.shape[0]
    halo = k_ref.shape[0] - rows
    span = halo + BLK

    @pl.when(pl.program_id(0) == 0)
    def _():
        for at in range(0, rows, BLK):
            key = lax.broadcasted_iota(jnp.int32, (span, BLK), 0)
            query = lax.broadcasted_iota(jnp.int32, (span, BLK), 1)
            same = segk_ref[at:at + span, :1] == segq_ref[:1, at:at + BLK]
            bias_ref[:, at:at + BLK] = jnp.where(same & (key - halo <= query), 0.0, NEG)

    scaled = q_ref[...] * (SCALE * LOG2E)
    dq, dk, dv = [], [], []
    for head in range(2):
        q_in = inner_form(scaled, head)
        g_in = inner_form(g_ref[...], head)
        k_out = outer_form(k_ref[...], head)
        v_out = outer_form(v_ref[...], head)
        q_mix = mixed(q_ref[...], head)
        g_mix = mixed(g_ref[...], head)
        k_mix = mixed(k_ref[...], head)
        dq_head = []
        dk_head = jnp.zeros((halo + rows, 128), F32)
        dv_head = jnp.zeros((halo + rows, 128), F32)
        dk_parts, dv_parts = [], []
        for at in range(0, rows, BLK):
            scores = dot_nt(k_out[at:at + span], q_in[at:at + BLK]) + bias_ref[:, at:at + BLK]
            top = jnp.max(scores, axis=0, keepdims=True)
            expo = jnp.exp2(scores - top)
            inverse = 1.0 / jnp.sum(expo, axis=0, keepdims=True)
            grad_probs = dot_nt(v_out[at:at + span], g_in[at:at + BLK])
            probs = expo * inverse
            delta = jnp.sum(probs * grad_probs, axis=0, keepdims=True)
            grad_scores = probs * (grad_probs - delta)
            probs_cat = jnp.concatenate(split(probs), axis=1)
            scores_cat = jnp.concatenate(split(grad_scores), axis=1)
            g_two = jnp.concatenate([g_mix[at:at + BLK]] * 2, axis=0)
            q_two = jnp.concatenate([q_mix[at:at + BLK]] * 2, axis=0)
            dv_parts.append(dot_nn(probs_cat, g_two))
            dk_parts.append(dot_nn(scores_cat, q_two))
            got = dot_tn(scores_cat, k_mix[at:at + span])
            dq_head.append(fold(got[:BLK] + got[BLK:]))
        for parts, full in ((dk_parts, dk), (dv_parts, dv)):
            pieces = []
            for kb in range((halo + rows) // BLK):
                terms = [
                    parts[qb][(kb - qb) * BLK:(kb - qb + 1) * BLK]
                    for qb in range(rows // BLK)
                    if 0 <= kb - qb < span // BLK
                ]
                pieces.append(fold(functools.reduce(lambda a, b: a + b, terms)))
            full.append(pieces)
        dq.append(dq_head)
    lane = lax.broadcasted_iota(jnp.int32, (BLK, 128), 1)
    for qb in range(rows // BLK):
        rng = slice(qb * BLK, (qb + 1) * BLK)
        far = slice(halo + qb * BLK, halo + (qb + 1) * BLK)
        both = jnp.where(lane < 64, dq[0][qb], dq[1][qb]) * SCALE
        dq_ref[rng] = unrotate(both, cos_ref[far], sin_ref[far])
    for kb in range((halo + rows) // BLK):
        rng = slice(kb * BLK, (kb + 1) * BLK)
        both = jnp.where(lane < 64, dk[0][kb], dk[1][kb]) * SCALE
        dk_ref[rng] = unrotate(both, cos_ref[rng], sin_ref[rng])
        dv_ref[rng] = jnp.where(lane < 64, dv[0][kb], dv[1][kb])


def attend_back(q_rot, kv, grad, seg_q, seg_k, cosine, sine):
    rows, model = q_rot.shape
    total = kv.shape[0]
    pairs = model // 128
    fixed = lambda shape: pl.BlockSpec(shape, lambda p: (0, 0))
    dq, dk, dv = pl.pallas_call(
        attend_back_kernel,
        grid=(pairs,),
        in_specs=[
            pl.BlockSpec((rows, 128), lambda p: (0, p)),
            pl.BlockSpec((total, 128), lambda p: (0, p)),
            pl.BlockSpec((total, 128), lambda p: (0, pairs + p)),
            pl.BlockSpec((rows, 128), lambda p: (0, p)),
            fixed((8, rows)), fixed((total, 128)),
            fixed((total, 128)), fixed((total, 128)),
        ],
        out_specs=[
            pl.BlockSpec((rows, 128), lambda p: (0, p)),
            pl.BlockSpec((total, 128), lambda p: (0, p)),
            pl.BlockSpec((total, 128), lambda p: (0, p)),
        ],
        out_shape=[
            jax.ShapeDtypeStruct((rows, model), F32),
            jax.ShapeDtypeStruct((total, model), F32),
            jax.ShapeDtypeStruct((total, model), F32),
        ],
        scratch_shapes=[pltpu.VMEM((total - rows + BLK, rows), F32)],
        cost_estimate=cost(42),
        compiler_params=params(),
    )(q_rot, kv, kv, grad, seg_q, seg_k, cosine, sine)
    return dq, dk, dv


def mlp_kernel(count, chip_ref, resid_ref, other_ref, cot_ref, cot_other_ref, gain_ref, bias_ref,
               scale_ref, *refs):
    up_refs, down_refs = refs[:count], refs[count:2 * count]
    out_ref, gnorm_ref, grad_ref = refs[2 * count:2 * count + 3]
    (x_hi, x_lo, xt_hi, xt_lo, g_hi, g_lo, up_hi, up_lo, down_hi, down_lo) = refs[2 * count + 3:]
    step = pl.program_id(0)
    rows = resid_ref.shape[0]

    @pl.when(step == 0)
    def _():
        for at, source, cot in ((0, resid_ref, cot_ref), (rows, other_ref, cot_other_ref)):
            xhat, _ = norm_stats(source[...])
            normed = xhat * gain_ref[...] + bias_ref[...]
            x_hi[at:at + rows], x_lo[at:at + rows] = split(normed)
            xt_hi[:, at:at + rows], xt_lo[:, at:at + rows] = split(normed.T)
            g_hi[at:at + rows], g_lo[at:at + rows] = split(cot[...] * scale_ref[0, 0])
        out_ref[...] = jnp.zeros_like(out_ref)
        gnorm_ref[...] = jnp.zeros_like(gnorm_ref)

    for at in range(count):
        spot = (chip_ref[0] ^ at) if count > 1 else 0
        up_rows = up_refs[at].shape[0]
        high, low = split(up_refs[at][...])
        here = pl.ds(pl.multiple_of(spot * up_rows, up_rows), up_rows)
        up_hi[here], up_lo[here] = high, low
        block = down_refs[at][...]
        block = block.reshape(-1, block.shape[-1])
        high, low = split(block)
        here = pl.ds(pl.multiple_of(spot * block.shape[0], block.shape[0]), block.shape[0])
        down_hi[here], down_lo[here] = high, low

    chips, _, tall, width = grad_ref.shape
    up_tall = up_hi.shape[0] // chips
    deep = down_hi.shape[0] // chips
    up = (up_hi[...], up_lo[...])
    down = (down_hi[...], down_lo[...])
    normed = (x_hi[...], x_lo[...])
    normed_t = (xt_hi[...], xt_lo[...])
    grad_block = (g_hi[...], g_lo[...])
    pre = three(dot_nn, normed, up)
    grad_act = three(dot_nt, grad_block, down)
    inner = 0.7978845608028654 * (pre + 0.044715 * pre * pre * pre)
    bent = jnp.tanh(inner)
    act = 0.5 * pre * (1.0 + bent)
    slope = 0.5 * (1.0 + bent) + 0.5 * pre * (1.0 - bent * bent) * (
        0.7978845608028654 * (1.0 + 3.0 * 0.044715 * pre * pre)
    )
    act2 = split(act)
    grad_pre = split(grad_act * slope)
    out_ref[...] += three(dot_nn, act2, down)
    gnorm_ref[...] += three(dot_nt, grad_pre, up)
    gup = three(dot_nn, normed_t, grad_pre)
    gdown = three(dot_tn, act2, grad_block)
    half = deep // 2
    for chip in range(chips):
        grad_ref[chip, 0, :up_tall] = gup[chip * up_tall:(chip + 1) * up_tall]
        part = gdown[chip * deep:(chip + 1) * deep]
        grad_ref[chip, 0, up_tall:up_tall + deep] = part[:, :width]
        grad_ref[chip, 0, up_tall + deep:] = jnp.concatenate(
            [part[:half, width:], part[half:, width:]], axis=1
        )


def mlp(first, steps, chip, chips, resid, other, cot, cot_other, gain, bias, scale, ups, downs):
    rows, model = resid.shape
    width = 512
    up_tall = model // chips
    deep = width // chips
    fixed = lambda shape: pl.BlockSpec(shape, lambda j, c: (0, 0))
    if len(ups) > 1:
        down_spec = pl.BlockSpec((deep, model), lambda j, c: (first + j, 0))
    else:
        downs = [downs[0].reshape(chips, -1, model)]
        down_spec = pl.BlockSpec((chips, deep, model), lambda j, c: (0, first + j, 0))
    tall = up_tall + deep + deep // 2
    grid_spec = pltpu.PrefetchScalarGridSpec(
        num_scalar_prefetch=1,
        grid=(steps,),
        in_specs=[fixed((rows, model))] * 4 + [fixed((1, model))] * 2
        + [pl.BlockSpec(memory_space=pltpu.SMEM)]
        + [pl.BlockSpec((up.shape[0], width), lambda j, c: (0, first + j)) for up in ups]
        + [down_spec] * len(downs),
        out_specs=[
            fixed((2 * rows, model)), fixed((2 * rows, model)),
            pl.BlockSpec((chips, 1, tall, width), lambda j, c: (0, j, 0, 0)),
        ],
        scratch_shapes=[
            pltpu.VMEM((2 * rows, model), BF16), pltpu.VMEM((2 * rows, model), BF16),
            pltpu.VMEM((model, 2 * rows), BF16), pltpu.VMEM((model, 2 * rows), BF16),
            pltpu.VMEM((2 * rows, model), BF16), pltpu.VMEM((2 * rows, model), BF16),
            pltpu.VMEM((model, width), BF16), pltpu.VMEM((model, width), BF16),
            pltpu.VMEM((width, model), BF16), pltpu.VMEM((width, model), BF16),
        ],
    )
    return pl.pallas_call(
        functools.partial(mlp_kernel, len(ups)),
        grid_spec=grid_spec,
        out_shape=[
            jax.ShapeDtypeStruct((2 * rows, model), F32),
            jax.ShapeDtypeStruct((2 * rows, model), F32),
            jax.ShapeDtypeStruct((chips, steps, tall, width), F32),
        ],
        cost_estimate=cost(18 * steps),
        compiler_params=params(),
    )(chip, resid, other, cot, cot_other, gain, bias, scale, *ups, *downs)


def unpack_grads(up, down, sibling_swap, core, chips):
    steps, up_tall, width = up.shape
    deep = up_tall * 2 // 3
    half = up_tall // 2
    mine = jnp.where(core == 0, up[:, :half], up[:, half:])
    other = sibling_swap(jnp.where(core == 0, up[:, half:], up[:, :half]))
    by_core = jnp.stack(
        [jnp.where(core == 0, mine, other), jnp.where(core == 0, other, mine)], axis=0
    )
    by_core = by_core.reshape(2, steps, half, chips, width // chips)
    grad_up = jnp.transpose(by_core, (2, 3, 0, 1, 4)).reshape(half, -1)
    quarter = width // 2
    tail = down[:, deep:]
    right = jnp.concatenate([tail[:, :, :quarter], tail[:, :, quarter:]], axis=1)
    grad_down = jnp.concatenate([down[:, :deep], right], axis=2).reshape(steps * deep, -1)
    return grad_up, grad_down


def weights_kernel(hi_ref, lo_ref, dq_ref, dk_ref, dv_ref, att_ref, res_ref, out_ref,
                   nt_hi, nt_lo, at_hi, at_lo):
    step = pl.program_id(0)
    part = pl.num_programs(0) // 4
    halo = hi_ref.shape[0] - dq_ref.shape[0]

    @pl.when(step == 0)
    def _():
        nt_hi[...] = hi_ref[...].T
        nt_lo[...] = lo_ref[...].T
        at_hi[...], at_lo[...] = split(att_ref[...].T)

    @pl.when(step < part)
    def _():
        out_ref[...] = three(dot_nn, (nt_hi[:, halo:], nt_lo[:, halo:]), split(dq_ref[...]))

    @pl.when((step >= part) & (step < 2 * part))
    def _():
        out_ref[...] = three(dot_nn, (nt_hi[...], nt_lo[...]), split(dk_ref[...]))

    @pl.when((step >= 2 * part) & (step < 3 * part))
    def _():
        out_ref[...] = three(dot_nn, (nt_hi[...], nt_lo[...]), split(dv_ref[...]))

    @pl.when(step >= 3 * part)
    def _():
        out_ref[...] = three(dot_nn, (at_hi[...], at_lo[...]), split(res_ref[...]))


def weight_grads(normed_hi, normed_lo, dq, dk, dv, attended, grad_resid):
    rows, model = dq.shape
    total = dk.shape[0]
    wide = 256
    part = model // wide
    fixed = lambda shape: pl.BlockSpec(shape, lambda j: (0, 0))
    piece = lambda tall, at: pl.BlockSpec(
        (tall, wide), lambda j: (0, jnp.clip(j - at * part, 0, part - 1))
    )
    return pl.pallas_call(
        weights_kernel,
        grid=(4 * part,),
        in_specs=[
            fixed((total, model)), fixed((total, model)),
            piece(rows, 0), piece(total, 1), piece(total, 2),
            fixed((rows, model)), piece(rows, 3),
        ],
        out_specs=pl.BlockSpec((model, wide), lambda j: (0, j)),
        out_shape=jax.ShapeDtypeStruct((model, 4 * model), F32),
        scratch_shapes=[
            pltpu.VMEM((model, total), BF16), pltpu.VMEM((model, total), BF16),
            pltpu.VMEM((model, rows), BF16), pltpu.VMEM((model, rows), BF16),
        ],
        cost_estimate=cost(15),
        compiler_params=params(),
    )(normed_hi, normed_lo, dq, dk, dv, attended, grad_resid)


def norm_back(grad, gain, xhat, rate):
    scaled = grad * gain
    return rate * (
        scaled
        - jnp.mean(scaled, axis=-1, keepdims=True)
        - xhat * jnp.mean(scaled * xhat, axis=-1, keepdims=True)
    )


def matmul(left, right):
    return jnp.dot(left, right, precision=HIGH)


def inner_rows(left, right):
    return lax.dot_general(left, right, (((0,), (0,)), ((), ())), precision=HIGH)


def outer_cols(left, right):
    return lax.dot_general(left, right, (((1,), (1,)), ((), ())), precision=HIGH)


def body(
    block_input,
    embedding,
    earlier_outs,
    dwa_weights,
    ln1_gain,
    ln1_bias,
    w_qkv,
    w_out,
    ln2_gain,
    ln2_bias,
    w_up,
    w_down,
    segments,
    cotangent,
):
    groups = lax.axis_size("seq")
    rows, model = block_input.shape
    length = rows * groups
    halo = 2 * rows
    place = lax.axis_index("seq")
    ahead = [(i, i + 1) for i in range(groups - 1)]
    behind = [(i + 1, i) for i in range(groups - 1)]
    gain1, bias1 = ln1_gain[None], ln1_bias[None]
    gain2, bias2 = ln2_gain[None], ln2_bias[None]

    devices = lax.axis_size("dp")
    chips = devices // 2
    spot = lax.axis_index("dp")
    core = spot % 2
    chip = (spot // 2).reshape(1).astype(jnp.int32)
    same_core = [[2 * i + c for i in range(chips)] for c in range(2)]
    exchange = lambda v, bit: lax.ppermute(v, "dp", [(i, i ^ bit) for i in range(devices)])
    swap = lambda v: exchange(v, 1)

    gather = lambda v: lax.all_gather(v, "dp", axis=0, tiled=True)
    qkv_full = gather(w_qkv)

    shard = w_down.shape[0]
    third = shard // 3
    by_core = w_up.reshape(w_up.shape[0], chips, 2, 3, third)
    by_core = jnp.transpose(by_core, (2, 0, 3, 1, 4)).reshape(2, w_up.shape[0], -1)
    mine = jnp.where(core == 0, by_core[0], by_core[1])
    given = swap(jnp.where(core == 0, by_core[1], by_core[0]))
    up_chip = jnp.concatenate(
        [jnp.where(core == 0, mine, given), jnp.where(core == 0, given, mine)], axis=0
    )
    if chips == 4:
        up_x, down_x = exchange(up_chip, 2), exchange(w_down, 2)
        up_y, down_y = exchange(up_chip, 4), exchange(w_down, 4)
        ups = [up_chip, up_x, up_y, exchange(up_y, 2)]
        downs = [w_down, down_x, down_y, exchange(down_x, 4)]
    else:
        ups, downs = (
            [lax.all_gather(v, "dp", axis=0, tiled=True, axis_index_groups=same_core)]
            for v in (up_chip, w_down)
        )

    seg_own = segments + 1
    near = lax.ppermute(block_input, "seq", ahead)
    seg_near = lax.ppermute(seg_own, "seq", ahead)
    far = lax.ppermute(near, "seq", ahead)
    seg_far = lax.ppermute(seg_near, "seq", ahead)
    seg_all = jnp.concatenate([seg_far, seg_near, seg_own], axis=1)
    seg_k_row = jnp.broadcast_to(seg_all, (8, halo + rows))
    seg_k_col = jnp.broadcast_to(seg_all.reshape(-1, 1), (halo + rows, 128))
    seg_q_row = seg_k_row[:, halo:]
    seg_q_col = seg_k_col[halo:]

    cos_all, sin_all = rotary_tables(length, halo)
    cosine = lax.dynamic_slice_in_dim(jnp.asarray(cos_all), place * rows, halo + rows, 0)
    sine = lax.dynamic_slice_in_dim(jnp.asarray(sin_all), place * rows, halo + rows, 0)

    q_rot, kv, normed_hi, normed_lo = project(
        far, near, block_input, gain1, bias1, qkv_full, cosine, sine
    )
    attended = attend(q_rot, kv, seg_q_col, seg_k_row)

    out_full = gather(w_out)
    resid = block_input + matmul(attended, out_full)
    resid_other = swap(resid)
    cot_other = swap(cotangent)
    scale = dwa_weights[4].reshape(1, 1)
    call = functools.partial(
        mlp, chip=chip, chips=chips, resid=resid, other=resid_other, cot=cotangent,
        cot_other=cot_other, gain=gain2, bias=bias2, scale=scale, ups=ups, downs=downs,
    )
    scatter = lambda v: lax.psum_scatter(v, "dp", scatter_dimension=0, tiled=True)
    scatter_chips = lambda v: lax.psum_scatter(
        v, "dp", scatter_dimension=0, tiled=True, axis_index_groups=same_core
    )
    out_a, gnorm_a, grads_a = call(0, 1)
    shard_a = scatter_chips(grads_a)[0]
    out_b, gnorm_b, grads_b = call(1, 2)
    shard_b = scatter_chips(grads_b)[0]
    grad_normed_two = gnorm_a[:rows] + gnorm_b[:rows] + swap(gnorm_a[rows:] + gnorm_b[rows:])
    mlp_out = out_a[:rows] + out_b[:rows] + swap(out_a[rows:] + out_b[rows:])

    block_out = resid + mlp_out
    output = (
        dwa_weights[0] * embedding
        + dwa_weights[1] * earlier_outs[0]
        + dwa_weights[2] * earlier_outs[1]
        + dwa_weights[3] * earlier_outs[2]
        + dwa_weights[4] * block_out
    )
    dwa_local = jnp.stack(
        [
            jnp.sum(cotangent * embedding),
            jnp.sum(cotangent * earlier_outs[0]),
            jnp.sum(cotangent * earlier_outs[1]),
            jnp.sum(cotangent * earlier_outs[2]),
            jnp.sum(cotangent * block_out),
        ]
    )
    xhat2, rate2 = norm_stats(resid)
    grad_resid = dwa_weights[4] * cotangent + norm_back(grad_normed_two, gain2, xhat2, rate2)
    grad_gain_two = jnp.sum(grad_normed_two * xhat2, axis=0)
    grad_bias_two = jnp.sum(grad_normed_two, axis=0)
    grad_attended = outer_cols(grad_resid, out_full)

    dq, dk, dv = attend_back(
        q_rot, kv, grad_attended, seg_q_row, seg_k_col, cosine, sine
    )
    shard_c = scatter(
        weight_grads(normed_hi, normed_lo, dq, dk, dv, attended, grad_resid)
    )
    dkv = jnp.concatenate([dk, dv], axis=1)

    wq, wkv = qkv_full[:, :model], qkv_full[:, model:]
    partial = outer_cols(dkv, wkv)
    own_part = partial[halo:] + outer_cols(dq, wq)
    back_near = partial[rows:halo] + lax.ppermute(partial[:rows], "seq", behind)
    grad_normed_one = own_part + lax.ppermute(back_near, "seq", behind)
    xhat1, rate1 = norm_stats(block_input)
    grad_input = grad_resid + norm_back(grad_normed_one, gain1, xhat1, rate1)
    grad_gain_one = jnp.sum(grad_normed_one * xhat1, axis=0)
    grad_bias_one = jnp.sum(grad_normed_one, axis=0)

    shard = jnp.concatenate([shard_a, shard_b], axis=0)
    tall = shard.shape[1] // 2
    halves = (shard[:, :tall], shard[:, tall:])
    even = place % 2 == 0
    shift = lambda v, bit: lax.ppermute(v, "seq", [(i, i ^ bit) for i in range(groups)])
    kept = jnp.where(even, halves[0], halves[1])
    kept = kept + shift(jnp.where(even, halves[1], halves[0]), 1)
    bit = 2
    while bit < groups:
        kept = kept + shift(kept, bit)
        bit *= 2
    other = shift(kept, 1)
    grad_up, grad_down = unpack_grads(
        jnp.where(even, kept, other), jnp.where(even, other, kept), swap, core, chips
    )
    sum_c = lax.psum(shard_c, "seq")
    grad_qkv, grad_wout = sum_c[:, :3 * model], sum_c[:, 3 * model:]

    small = jnp.concatenate(
        [
            grad_gain_one[None], grad_bias_one[None], grad_gain_two[None], grad_bias_two[None],
            jnp.pad(dwa_local, (0, model - 5))[None], jnp.zeros((3, model), F32),
        ],
        axis=0,
    )
    bit = 1
    while bit < devices:
        small = small + exchange(small, bit)
        bit *= 2
    bit = 1
    while bit < groups:
        small = small + shift(small, bit)
        bit *= 2
    gain_one, bias_one, gain_two, bias_two = small[0], small[1], small[2], small[3]
    grad_dwa = small[4, :5]
    return (
        output,
        grad_input,
        grad_dwa,
        gain_one,
        bias_one,
        grad_qkv,
        grad_wout,
        gain_two,
        bias_two,
        grad_up,
        grad_down,
    )


def solution(mesh):
    in_specs = (
        P(("dp", "seq"), None),
        P(("dp", "seq"), None),
        P(None, ("dp", "seq"), None),
        P(),
        P(),
        P(),
        P("dp", None),
        P("dp", None),
        P(),
        P(),
        P("dp", None),
        P("dp", None),
        P("dp", "seq"),
        P(("dp", "seq"), None),
    )
    out_specs = (
        P(("dp", "seq"), None),
        P(("dp", "seq"), None),
        P(),
        P(),
        P(),
        P("dp", None),
        P("dp", None),
        P(),
        P(),
        P("dp", None),
        P("dp", None),
    )
    return jax.shard_map(body, mesh=mesh, in_specs=in_specs, out_specs=out_specs, check_vma=False)
```

```python
import functools
import math

import jax
import jax.numpy as jnp
import numpy as np
from jax import lax
from jax.experimental import pallas as pl
from jax.experimental.pallas import tpu as pltpu
from jax.sharding import PartitionSpec as P

HD = 64
DOC_MOST = 768
LOG2E = math.log2(math.e)
SCALE = 1.0 / math.sqrt(HD)
NEG = -1e30
F32 = jnp.float32
BF16 = jnp.bfloat16
HIGH = lax.Precision.HIGH
VMEM_LIMIT = 56 * 1024 * 1024
BLK = 128


def cost(micros):
    return pl.CostEstimate(
        flops=int(micros * 1.1e9), bytes_accessed=1 << 20, transcendentals=0
    )


def params():
    return pltpu.CompilerParams(
        dimension_semantics=("arbitrary",), vmem_limit_bytes=VMEM_LIMIT
    )


def split(values):
    high = values.astype(BF16)
    return high, (values - high.astype(F32)).astype(BF16)


def dot_nn(left, right):
    return lax.dot_general(left, right, (((1,), (0,)), ((), ())), preferred_element_type=F32)


def dot_nt(left, right):
    return lax.dot_general(left, right, (((1,), (1,)), ((), ())), preferred_element_type=F32)


def dot_tn(left, right):
    return lax.dot_general(left, right, (((0,), (0,)), ((), ())), preferred_element_type=F32)


def three(dot, left, right):
    return (
        dot(left[0], right[0]) + dot(left[0], right[1]) + dot(left[1], right[0])
    )


def norm_stats(values):
    row_mean = jnp.mean(values, axis=-1, keepdims=True)
    centred = values - row_mean
    row_var = jnp.mean(centred * centred, axis=-1, keepdims=True)
    rate = lax.rsqrt(row_var + 1e-05)
    return centred * rate, rate


def turned(values):
    lane = lax.broadcasted_iota(jnp.int32, values.shape, 1)
    return jnp.where(
        (lane & 63) < 32, pltpu.roll(values, 96, 1), pltpu.roll(values, 32, 1)
    )


def rotate(values, cosine, sine):
    return values * cosine + turned(values) * sine


def unrotate(values, cosine, sine):
    return values * cosine - turned(values) * sine


def rotary_tables(length, halo):
    half = HD // 2
    inv_freq = (10000.0 ** (-(np.arange(half, dtype=np.float32) * 2.0 / HD))).astype(np.float32)
    place = np.arange(-halo, length, dtype=np.float32)
    angles = place[:, None] * inv_freq[None, :]
    cosine = np.cos(angles.astype(np.float64)).astype(np.float32)
    sine = np.sin(angles.astype(np.float64)).astype(np.float32)
    return (
        np.concatenate([cosine] * 4, axis=1),
        np.concatenate([-sine, sine, -sine, sine], axis=1),
    )


def qkv_kernel(far_ref, near_ref, own_ref, gain_ref, bias_ref, w_ref, cos_ref, sin_ref,
               q_ref, kv_ref, hi_ref, lo_ref):
    step = pl.program_id(0)
    rows = own_ref.shape[0]
    third = pl.num_programs(0) // 3
    halo = hi_ref.shape[0] - rows

    @pl.when(step == 0)
    def _():
        for at, ref in enumerate((far_ref, near_ref, own_ref)):
            xhat, _ = norm_stats(ref[...])
            high, low = split(xhat * gain_ref[...] + bias_ref[...])
            hi_ref[at * rows:(at + 1) * rows] = high
            lo_ref[at * rows:(at + 1) * rows] = low

    weights = split(w_ref[...])

    @pl.when(step < third)
    def _():
        got = three(dot_nn, (hi_ref[halo:], lo_ref[halo:]), weights)
        for at in range(0, got.shape[1], 128):
            q_ref[:, at:at + 128] = rotate(got[:, at:at + 128], cos_ref[halo:], sin_ref[halo:])

    @pl.when((step >= third) & (step < 2 * third))
    def _():
        got = three(dot_nn, (hi_ref[...], lo_ref[...]), weights)
        for at in range(0, got.shape[1], 128):
            kv_ref[:, at:at + 128] = rotate(got[:, at:at + 128], cos_ref[...], sin_ref[...])

    @pl.when(step >= 2 * third)
    def _():
        kv_ref[...] = three(dot_nn, (hi_ref[...], lo_ref[...]), weights)


def project(far, near, own, gain, bias, w_full, cosine, sine):
    rows, model = own.shape
    total = 3 * rows
    wide = 256
    third = model // wide
    whole = lambda shape: pl.BlockSpec(shape, lambda j: (0, 0))
    return pl.pallas_call(
        qkv_kernel,
        grid=(3 * third,),
        in_specs=[
            whole((rows, model)), whole((rows, model)), whole((rows, model)),
            whole((1, model)), whole((1, model)),
            pl.BlockSpec((model, wide), lambda j: (0, j)),
            whole((total, 128)), whole((total, 128)),
        ],
        out_specs=[
            pl.BlockSpec((rows, wide), lambda j: (0, jnp.minimum(j, third - 1))),
            pl.BlockSpec((total, wide), lambda j: (0, jnp.maximum(j - third, 0))),
            whole((total, model)), whole((total, model)),
        ],
        out_shape=[
            jax.ShapeDtypeStruct((rows, model), F32),
            jax.ShapeDtypeStruct((total, 2 * model), F32),
            jax.ShapeDtypeStruct((total, model), BF16),
            jax.ShapeDtypeStruct((total, model), BF16),
        ],
        cost_estimate=cost(20),
        compiler_params=params(),
    )(far, near, own, gain, bias, w_full, cosine, sine)


def own_pair(values, head):
    lane = lax.broadcasted_iota(jnp.int32, values.shape, 1)
    other = pltpu.roll(values, 64, 1)
    return jnp.where((lane < 64) == (head == 0), values, other)


def outer_form(values, head):
    high, low = split(own_pair(values, head))
    return jnp.concatenate([high, low], axis=1)


def mixed(values, head):
    pair = own_pair(values, head)
    lane = lax.broadcasted_iota(jnp.int32, pair.shape, 1)
    high = pair.astype(BF16).astype(F32)
    return jnp.where(lane < 64, high, pair - high).astype(BF16)


def inner_form(values, head):
    half = mixed(values, head)
    return jnp.concatenate([half, half], axis=1)


def fold(values):
    return values + pltpu.roll(values, 64, 1)


def attend_kernel(q_ref, k_ref, v_ref, segq_ref, segk_ref, out_ref, bias_ref):
    rows = q_ref.shape[0]
    halo = k_ref.shape[0] - rows
    span = halo + BLK

    @pl.when(pl.program_id(0) == 0)
    def _():
        for at in range(0, rows, BLK):
            row = lax.broadcasted_iota(jnp.int32, (BLK, span), 0)
            col = lax.broadcasted_iota(jnp.int32, (BLK, span), 1)
            same = segq_ref[at:at + BLK, :1] == segk_ref[:1, at:at + span]
            bias_ref[at:at + BLK] = jnp.where(same & (col - halo <= row), 0.0, NEG)

    lane = lax.broadcasted_iota(jnp.int32, (BLK, 128), 1)
    scaled = q_ref[...] * (SCALE * LOG2E)
    results = []
    for head in range(2):
        left = inner_form(scaled, head)
        right = outer_form(k_ref[...], head)
        vals = mixed(v_ref[...], head)
        outs = []
        for at in range(0, rows, BLK):
            scores = dot_nt(left[at:at + BLK], right[at:at + span]) + bias_ref[at:at + BLK]
            top = jnp.max(scores, axis=1, keepdims=True)
            expo = jnp.exp2(scores - top)
            total = jnp.sum(expo, axis=1, keepdims=True)
            high, low = split(expo)
            got = dot_nn(high, vals[at:at + span]) + dot_nn(low, vals[at:at + span])
            outs.append(fold(got) / total)
        results.append(outs)
    for at in range(0, rows, BLK):
        out_ref[at:at + BLK] = jnp.where(
            lane < 64, results[0][at // BLK], results[1][at // BLK]
        )


def attend(q_rot, kv, seg_q, seg_k):
    rows, model = q_rot.shape
    total = kv.shape[0]
    pairs = model // 128
    return pl.pallas_call(
        attend_kernel,
        grid=(pairs,),
        in_specs=[
            pl.BlockSpec((rows, 128), lambda p: (0, p)),
            pl.BlockSpec((total, 128), lambda p: (0, p)),
            pl.BlockSpec((total, 128), lambda p: (0, pairs + p)),
            pl.BlockSpec((rows, 128), lambda p: (0, 0)),
            pl.BlockSpec((8, total), lambda p: (0, 0)),
        ],
        out_specs=pl.BlockSpec((rows, 128), lambda p: (0, p)),
        out_shape=jax.ShapeDtypeStruct((rows, model), F32),
        scratch_shapes=[pltpu.VMEM((rows, total - rows + BLK), F32)],
        cost_estimate=cost(24),
        compiler_params=params(),
    )(q_rot, kv, kv, seg_q, seg_k)


def attend_back_kernel(q_ref, k_ref, v_ref, g_ref, segq_ref, segk_ref, cos_ref, sin_ref, *refs):
    dq_ref, dk_ref, dv_ref, bias_ref = refs[-4:]
    rows = q_ref.shape[0]
    halo = k_ref.shape[0] - rows
    span = halo + BLK

    @pl.when(pl.program_id(0) == 0)
    def _():
        for at in range(0, rows, BLK):
            key = lax.broadcasted_iota(jnp.int32, (span, BLK), 0)
            query = lax.broadcasted_iota(jnp.int32, (span, BLK), 1)
            same = segk_ref[at:at + span, :1] == segq_ref[:1, at:at + BLK]
            bias_ref[:, at:at + BLK] = jnp.where(same & (key - halo <= query), 0.0, NEG)

    scaled = q_ref[...] * (SCALE * LOG2E)
    dq, dk, dv = [], [], []
    for head in range(2):
        q_in = inner_form(scaled, head)
        g_in = inner_form(g_ref[...], head)
        k_out = outer_form(k_ref[...], head)
        v_out = outer_form(v_ref[...], head)
        q_mix = mixed(q_ref[...], head)
        g_mix = mixed(g_ref[...], head)
        k_mix = mixed(k_ref[...], head)
        dq_head = []
        dk_head = jnp.zeros((halo + rows, 128), F32)
        dv_head = jnp.zeros((halo + rows, 128), F32)
        dk_parts, dv_parts = [], []
        for at in range(0, rows, BLK):
            scores = dot_nt(k_out[at:at + span], q_in[at:at + BLK]) + bias_ref[:, at:at + BLK]
            top = jnp.max(scores, axis=0, keepdims=True)
            expo = jnp.exp2(scores - top)
            inverse = 1.0 / jnp.sum(expo, axis=0, keepdims=True)
            grad_probs = dot_nt(v_out[at:at + span], g_in[at:at + BLK])
            probs = expo * inverse
            delta = jnp.sum(probs * grad_probs, axis=0, keepdims=True)
            grad_scores = probs * (grad_probs - delta)
            probs_cat = jnp.concatenate(split(probs), axis=1)
            scores_cat = jnp.concatenate(split(grad_scores), axis=1)
            g_two = jnp.concatenate([g_mix[at:at + BLK]] * 2, axis=0)
            q_two = jnp.concatenate([q_mix[at:at + BLK]] * 2, axis=0)
            dv_parts.append(dot_nn(probs_cat, g_two))
            dk_parts.append(dot_nn(scores_cat, q_two))
            got = dot_tn(scores_cat, k_mix[at:at + span])
            dq_head.append(fold(got[:BLK] + got[BLK:]))
        for parts, full in ((dk_parts, dk), (dv_parts, dv)):
            pieces = []
            for kb in range((halo + rows) // BLK):
                terms = [
                    parts[qb][(kb - qb) * BLK:(kb - qb + 1) * BLK]
                    for qb in range(rows // BLK)
                    if 0 <= kb - qb < span // BLK
                ]
                pieces.append(fold(functools.reduce(lambda a, b: a + b, terms)))
            full.append(pieces)
        dq.append(dq_head)
    lane = lax.broadcasted_iota(jnp.int32, (BLK, 128), 1)
    for qb in range(rows // BLK):
        rng = slice(qb * BLK, (qb + 1) * BLK)
        far = slice(halo + qb * BLK, halo + (qb + 1) * BLK)
        both = jnp.where(lane < 64, dq[0][qb], dq[1][qb]) * SCALE
        dq_ref[rng] = unrotate(both, cos_ref[far], sin_ref[far])
    for kb in range((halo + rows) // BLK):
        rng = slice(kb * BLK, (kb + 1) * BLK)
        both = jnp.where(lane < 64, dk[0][kb], dk[1][kb]) * SCALE
        dk_ref[rng] = unrotate(both, cos_ref[rng], sin_ref[rng])
        dv_ref[rng] = jnp.where(lane < 64, dv[0][kb], dv[1][kb])


def attend_back(first, count, q_rot, kv, grad, seg_q, seg_k, cosine, sine, before=()):
    rows, model = q_rot.shape
    total = kv.shape[0]
    pairs = model // 128
    fixed = lambda shape: pl.BlockSpec(shape, lambda p: (0, 0))
    return pl.pallas_call(
        attend_back_kernel,
        grid=(count,),
        in_specs=[
            pl.BlockSpec((rows, 128), lambda p: (0, first + p)),
            pl.BlockSpec((total, 128), lambda p: (0, first + p)),
            pl.BlockSpec((total, 128), lambda p: (0, pairs + first + p)),
            pl.BlockSpec((rows, 128), lambda p: (0, first + p)),
            fixed((8, rows)), fixed((total, 128)),
            fixed((total, 128)), fixed((total, 128)),
        ] + [pl.BlockSpec(memory_space=pl.ANY)] * len(before),
        out_specs=[
            pl.BlockSpec((rows, 128), lambda p: (0, first + p)),
            pl.BlockSpec((total, 128), lambda p: (0, first + p)),
            pl.BlockSpec((total, 128), lambda p: (0, first + p)),
        ],
        out_shape=[
            jax.ShapeDtypeStruct((rows, model), F32),
            jax.ShapeDtypeStruct((total, model), F32),
            jax.ShapeDtypeStruct((total, model), F32),
        ],
        scratch_shapes=[pltpu.VMEM((total - rows + BLK, rows), F32)],
        input_output_aliases={8 + i: i for i in range(len(before))},
        cost_estimate=cost(7 * count),
        compiler_params=params(),
    )(q_rot, kv, kv, grad, seg_q, seg_k, cosine, sine, *before)


def mlp_kernel(count, begun, chip_ref, resid_ref, other_ref, cot_ref, cot_other_ref, gain_ref, bias_ref,
               scale_ref, *refs):
    up_refs, down_refs = refs[:count], refs[count:2 * count]
    refs = refs[2 * count:]
    so_far, refs = refs[:2 * begun], refs[2 * begun:]
    out_ref, gnorm_ref, grad_ref = refs[:3]
    (x_hi, x_lo, xt_hi, xt_lo, g_hi, g_lo, up_hi, up_lo, down_hi, down_lo) = refs[3:]
    step = pl.program_id(0)
    rows = resid_ref.shape[0]

    @pl.when(step == 0)
    def _():
        for at, source, cot in ((0, resid_ref, cot_ref), (rows, other_ref, cot_other_ref)):
            xhat, _ = norm_stats(source[...])
            normed = xhat * gain_ref[...] + bias_ref[...]
            x_hi[at:at + rows], x_lo[at:at + rows] = split(normed)
            xt_hi[:, at:at + rows], xt_lo[:, at:at + rows] = split(normed.T)
            g_hi[at:at + rows], g_lo[at:at + rows] = split(cot[...] * scale_ref[0, 0])
        if begun:
            out_ref[...] = so_far[0][...]
            gnorm_ref[...] = so_far[1][...]
        else:
            out_ref[...] = jnp.zeros_like(out_ref)
            gnorm_ref[...] = jnp.zeros_like(gnorm_ref)

    for at in range(count):
        spot = (chip_ref[0] ^ at) if count > 1 else 0
        up_rows = up_refs[at].shape[0]
        high, low = split(up_refs[at][...])
        here = pl.ds(pl.multiple_of(spot * up_rows, up_rows), up_rows)
        up_hi[here], up_lo[here] = high, low
        block = down_refs[at][...]
        block = block.reshape(-1, block.shape[-1])
        high, low = split(block)
        here = pl.ds(pl.multiple_of(spot * block.shape[0], block.shape[0]), block.shape[0])
        down_hi[here], down_lo[here] = high, low

    chips, _, tall, width = grad_ref.shape
    up_tall = up_hi.shape[0] // chips
    deep = down_hi.shape[0] // chips
    up = (up_hi[...], up_lo[...])
    down = (down_hi[...], down_lo[...])
    normed = (x_hi[...], x_lo[...])
    normed_t = (xt_hi[...], xt_lo[...])
    grad_block = (g_hi[...], g_lo[...])
    pre = three(dot_nn, normed, up)
    grad_act = three(dot_nt, grad_block, down)
    inner = 0.7978845608028654 * (pre + 0.044715 * pre * pre * pre)
    bent = jnp.tanh(inner)
    act = 0.5 * pre * (1.0 + bent)
    slope = 0.5 * (1.0 + bent) + 0.5 * pre * (1.0 - bent * bent) * (
        0.7978845608028654 * (1.0 + 3.0 * 0.044715 * pre * pre)
    )
    act2 = split(act)
    grad_pre = split(grad_act * slope)
    out_ref[...] += three(dot_nn, act2, down)
    gnorm_ref[...] += three(dot_nt, grad_pre, up)
    gup = three(dot_nn, normed_t, grad_pre)
    gdown = three(dot_tn, act2, grad_block)
    half = deep // 2
    for chip in range(chips):
        grad_ref[chip, 0, :up_tall] = gup[chip * up_tall:(chip + 1) * up_tall]
        part = gdown[chip * deep:(chip + 1) * deep]
        grad_ref[chip, 0, up_tall:up_tall + deep] = part[:, :width]
        grad_ref[chip, 0, up_tall + deep:] = jnp.concatenate(
            [part[:half, width:], part[half:, width:]], axis=1
        )


def mlp(first, steps, so_far, chip, chips, resid, other, cot, cot_other, gain, bias, scale, ups, downs):
    rows, model = resid.shape
    width = 512
    up_tall = model // chips
    deep = width // chips
    fixed = lambda shape: pl.BlockSpec(shape, lambda j, c: (0, 0))
    if len(ups) > 1:
        down_spec = pl.BlockSpec((deep, model), lambda j, c: (first + j, 0))
    else:
        downs = [downs[0].reshape(chips, -1, model)]
        down_spec = pl.BlockSpec((chips, deep, model), lambda j, c: (0, first + j, 0))
    tall = up_tall + deep + deep // 2
    grid_spec = pltpu.PrefetchScalarGridSpec(
        num_scalar_prefetch=1,
        grid=(steps,),
        in_specs=[fixed((rows, model))] * 4 + [fixed((1, model))] * 2
        + [pl.BlockSpec(memory_space=pltpu.SMEM)]
        + [pl.BlockSpec((up.shape[0], width), lambda j, c: (0, first + j)) for up in ups]
        + [down_spec] * len(downs)
        + [fixed((2 * rows, model))] * len(so_far),
        out_specs=[
            fixed((2 * rows, model)), fixed((2 * rows, model)),
            pl.BlockSpec((chips, 1, tall, width), lambda j, c: (0, j, 0, 0)),
        ],
        scratch_shapes=[
            pltpu.VMEM((2 * rows, model), BF16), pltpu.VMEM((2 * rows, model), BF16),
            pltpu.VMEM((model, 2 * rows), BF16), pltpu.VMEM((model, 2 * rows), BF16),
            pltpu.VMEM((2 * rows, model), BF16), pltpu.VMEM((2 * rows, model), BF16),
            pltpu.VMEM((model, width), BF16), pltpu.VMEM((model, width), BF16),
            pltpu.VMEM((width, model), BF16), pltpu.VMEM((width, model), BF16),
        ],
    )
    return pl.pallas_call(
        functools.partial(mlp_kernel, len(ups), len(so_far) // 2),
        grid_spec=grid_spec,
        out_shape=[
            jax.ShapeDtypeStruct((2 * rows, model), F32),
            jax.ShapeDtypeStruct((2 * rows, model), F32),
            jax.ShapeDtypeStruct((chips, steps, tall, width), F32),
        ],
        cost_estimate=cost(18 * steps),
        compiler_params=params(),
    )(chip, resid, other, cot, cot_other, gain, bias, scale, *ups, *downs, *so_far)


def unpack_grads(up, down, sibling_swap, core, chips):
    steps, up_tall, width = up.shape
    deep = up_tall * 2 // 3
    half = up_tall // 2
    mine = jnp.where(core == 0, up[:, :half], up[:, half:])
    other = sibling_swap(jnp.where(core == 0, up[:, half:], up[:, :half]))
    by_core = jnp.stack(
        [jnp.where(core == 0, mine, other), jnp.where(core == 0, other, mine)], axis=0
    )
    by_core = by_core.reshape(2, steps, half, chips, width // chips)
    grad_up = jnp.transpose(by_core, (2, 3, 0, 1, 4)).reshape(half, -1)
    quarter = width // 2
    tail = down[:, deep:]
    right = jnp.concatenate([tail[:, :, :quarter], tail[:, :, quarter:]], axis=1)
    grad_down = jnp.concatenate([down[:, :deep], right], axis=2).reshape(steps * deep, -1)
    return grad_up, grad_down


def place_rows(core_ref, out_ref, got):
    chips = out_ref.shape[1]
    tall = out_ref.shape[2]
    for block in range(2 * chips):
        out_ref[(block & 1) ^ core_ref[0], block // 2] = got[block * tall:(block + 1) * tall]


def weights_qk_kernel(core_ref, hi_ref, lo_ref, dq_ref, dk_ref, out_ref, nt_hi, nt_lo):
    step = pl.program_id(0)
    part = pl.num_programs(0) // 2
    halo = hi_ref.shape[0] - dq_ref.shape[0]

    @pl.when(step == 0)
    def _():
        nt_hi[...] = hi_ref[...].T
        nt_lo[...] = lo_ref[...].T

    @pl.when(step < part)
    def _():
        left = (nt_hi[:, halo:], nt_lo[:, halo:])
        place_rows(core_ref, out_ref, three(dot_nn, left, split(dq_ref[...])))

    @pl.when(step >= part)
    def _():
        left = (nt_hi[...], nt_lo[...])
        place_rows(core_ref, out_ref, three(dot_nn, left, split(dk_ref[...])))


def weights_vo_kernel(core_ref, hi_ref, lo_ref, dv_ref, att_ref, res_ref, out_ref,
                      nt_hi, nt_lo, at_hi, at_lo):
    step = pl.program_id(0)
    part = pl.num_programs(0) // 2

    @pl.when(step == 0)
    def _():
        nt_hi[...] = hi_ref[...].T
        nt_lo[...] = lo_ref[...].T
        at_hi[...], at_lo[...] = split(att_ref[...].T)

    @pl.when(step < part)
    def _():
        left = (nt_hi[...], nt_lo[...])
        place_rows(core_ref, out_ref, three(dot_nn, left, split(dv_ref[...])))

    @pl.when(step >= part)
    def _():
        left = (at_hi[...], at_lo[...])
        place_rows(core_ref, out_ref, three(dot_nn, left, split(res_ref[...])))


def weight_call(kernel, micros, core, chips, fixed_args, pieces, scratch):
    model = fixed_args[0].shape[1]
    wide = 256
    part = model // wide
    tall = model // chips // 2
    fixed = lambda v: pl.BlockSpec(v.shape, lambda j, c: (0, 0))
    piece = lambda v, at: pl.BlockSpec(
        (v.shape[0], wide), lambda j, c: (0, jnp.clip(j - at * part, 0, part - 1))
    )
    specs, args = [], []
    for value, at in pieces:
        args.append(value)
        specs.append(fixed(value) if at is None else piece(value, at))
    return pl.pallas_call(
        kernel,
        grid_spec=pltpu.PrefetchScalarGridSpec(
            num_scalar_prefetch=1,
            grid=(2 * part,),
            in_specs=[fixed(v) for v in fixed_args] + specs,
            out_specs=pl.BlockSpec((2, chips, tall, wide), lambda j, c: (0, 0, 0, j)),
            scratch_shapes=[pltpu.VMEM((model, n), BF16) for n in scratch],
        ),
        out_shape=jax.ShapeDtypeStruct((2, chips, tall, 2 * model), F32),
        cost_estimate=cost(micros),
        compiler_params=params(),
    )(core, *fixed_args, *args)


def norm_back(grad, gain, xhat, rate):
    scaled = grad * gain
    return rate * (
        scaled
        - jnp.mean(scaled, axis=-1, keepdims=True)
        - xhat * jnp.mean(scaled * xhat, axis=-1, keepdims=True)
    )


def matmul(left, right):
    return jnp.dot(left, right, precision=HIGH)


def inner_rows(left, right):
    return lax.dot_general(left, right, (((0,), (0,)), ((), ())), precision=HIGH)


def outer_cols(left, right):
    return lax.dot_general(left, right, (((1,), (1,)), ((), ())), precision=HIGH)


def body(
    block_input,
    embedding,
    earlier_outs,
    dwa_weights,
    ln1_gain,
    ln1_bias,
    w_qkv,
    w_out,
    ln2_gain,
    ln2_bias,
    w_up,
    w_down,
    segments,
    cotangent,
):
    groups = lax.axis_size("seq")
    rows, model = block_input.shape
    length = rows * groups
    halo = 2 * rows
    place = lax.axis_index("seq")
    ahead = [(i, i + 1) for i in range(groups - 1)]
    behind = [(i + 1, i) for i in range(groups - 1)]
    gain1, bias1 = ln1_gain[None], ln1_bias[None]
    gain2, bias2 = ln2_gain[None], ln2_bias[None]

    devices = lax.axis_size("dp")
    chips = devices // 2
    spot = lax.axis_index("dp")
    core = spot % 2
    chip = (spot // 2).reshape(1).astype(jnp.int32)
    same_core = [[2 * i + c for i in range(chips)] for c in range(2)]
    exchange = lambda v, bit: lax.ppermute(v, "dp", [(i, i ^ bit) for i in range(devices)])
    swap = lambda v: exchange(v, 1)

    gather = lambda v: lax.all_gather(v, "dp", axis=0, tiled=True)
    qkv_full = gather(w_qkv)

    shard = w_down.shape[0]
    third = shard // 3
    by_core = w_up.reshape(w_up.shape[0], chips, 2, 3, third)
    by_core = jnp.transpose(by_core, (2, 0, 3, 1, 4)).reshape(2, w_up.shape[0], -1)
    mine = jnp.where(core == 0, by_core[0], by_core[1])
    given = swap(jnp.where(core == 0, by_core[1], by_core[0]))
    up_chip = jnp.concatenate(
        [jnp.where(core == 0, mine, given), jnp.where(core == 0, given, mine)], axis=0
    )
    if chips == 4:
        up_x, down_x = exchange(up_chip, 2), exchange(w_down, 2)
        up_y, down_y = exchange(up_chip, 4), exchange(w_down, 4)
        ups = [up_chip, up_x, up_y, exchange(up_y, 2)]
        downs = [w_down, down_x, down_y, exchange(down_x, 4)]
    else:
        ups, downs = (
            [lax.all_gather(v, "dp", axis=0, tiled=True, axis_index_groups=same_core)]
            for v in (up_chip, w_down)
        )

    seg_own = segments + 1
    near = lax.ppermute(block_input, "seq", ahead)
    seg_near = lax.ppermute(seg_own, "seq", ahead)
    far = lax.ppermute(near, "seq", ahead)
    seg_far = lax.ppermute(seg_near, "seq", ahead)
    seg_all = jnp.concatenate([seg_far, seg_near, seg_own], axis=1)
    seg_k_row = jnp.broadcast_to(seg_all, (8, halo + rows))
    seg_k_col = jnp.broadcast_to(seg_all.reshape(-1, 1), (halo + rows, 128))
    seg_q_row = seg_k_row[:, halo:]
    seg_q_col = seg_k_col[halo:]

    cos_all, sin_all = rotary_tables(length, halo)
    cosine = lax.dynamic_slice_in_dim(jnp.asarray(cos_all), place * rows, halo + rows, 0)
    sine = lax.dynamic_slice_in_dim(jnp.asarray(sin_all), place * rows, halo + rows, 0)

    q_rot, kv, normed_hi, normed_lo = project(
        far, near, block_input, gain1, bias1, qkv_full, cosine, sine
    )
    attended = attend(q_rot, kv, seg_q_col, seg_k_row)

    out_full = gather(w_out)
    resid = block_input + matmul(attended, out_full)
    resid_other = swap(resid)
    cot_other = swap(cotangent)
    scale = dwa_weights[4].reshape(1, 1)
    call = functools.partial(
        mlp, chip=chip, chips=chips, resid=resid, other=resid_other, cot=cotangent,
        cot_other=cot_other, gain=gain2, bias=bias2, scale=scale, ups=ups, downs=downs,
    )
    scatter = lambda v: lax.psum_scatter(v, "dp", scatter_dimension=0, tiled=True)
    scatter_chips = lambda v: lax.psum_scatter(
        v, "dp", scatter_dimension=0, tiled=True, axis_index_groups=same_core
    )
    out_part, gnorm_part, grads_a = call(0, 1, ())
    shard_a = scatter_chips(grads_a)[0]
    out_part, gnorm_part, grads_b = call(1, 2, (out_part, gnorm_part))
    shard_b = scatter_chips(grads_b)[0]
    grad_normed_two = gnorm_part[:rows] + swap(gnorm_part[rows:])
    mlp_out = out_part[:rows] + swap(out_part[rows:])

    block_out = resid + mlp_out
    output = (
        dwa_weights[0] * embedding
        + dwa_weights[1] * earlier_outs[0]
        + dwa_weights[2] * earlier_outs[1]
        + dwa_weights[3] * earlier_outs[2]
        + dwa_weights[4] * block_out
    )
    dwa_local = jnp.stack(
        [
            jnp.sum(cotangent * embedding),
            jnp.sum(cotangent * earlier_outs[0]),
            jnp.sum(cotangent * earlier_outs[1]),
            jnp.sum(cotangent * earlier_outs[2]),
            jnp.sum(cotangent * block_out),
        ]
    )
    xhat2, rate2 = norm_stats(resid)
    grad_resid = dwa_weights[4] * cotangent + norm_back(grad_normed_two, gain2, xhat2, rate2)
    grad_gain_two = jnp.sum(grad_normed_two * xhat2, axis=0)
    grad_bias_two = jnp.sum(grad_normed_two, axis=0)
    grad_attended = outer_cols(grad_resid, out_full)

    back_args = (q_rot, kv, grad_attended, seg_q_row, seg_k_col, cosine, sine)
    pairs = model // 128
    first_half = attend_back(0, pairs // 2, *back_args)
    shift = lambda v, bit: lax.ppermute(v, "seq", [(i, i ^ bit) for i in range(groups)])
    even = place % 2 == 0

    def line_start(shard):
        tall = shard.shape[1] // 2
        halves = (shard[:, :tall], shard[:, tall:])
        kept = jnp.where(even, halves[0], halves[1])
        return kept + shift(jnp.where(even, halves[1], halves[0]), 1)

    def line_middle(kept):
        bit = 2
        while bit < groups:
            kept = kept + shift(kept, bit)
            bit *= 2
        return kept

    def line_end(kept):
        other = shift(kept, 1)
        return jnp.where(even, kept, other), jnp.where(even, other, kept)

    line_sum = lambda shard: line_end(line_middle(line_start(shard)))

    kept_a = line_start(shard_a)
    kept_a, back_args, first_half = lax.optimization_barrier((kept_a, back_args, first_half))
    kept_a = line_middle(kept_a)
    dq, dk, dv = attend_back(pairs // 2, pairs - pairs // 2, *back_args, before=first_half)
    kept_a, dq, dk, dv = lax.optimization_barrier((kept_a, dq, dk, dv))
    core_at = core.reshape(1).astype(jnp.int32)
    normed_parts = (normed_hi, normed_lo)
    grads_qk = weight_call(
        weights_qk_kernel, 9, core_at, chips, normed_parts, [(dq, 0), (dk, 1)], [halo + rows] * 2
    )
    grads_vo = weight_call(
        weights_vo_kernel, 9, core_at, chips, normed_parts,
        [(dv, 0), (attended, None), (grad_resid, 1)], [halo + rows] * 2 + [rows] * 2,
    )
    shard_c = scatter_chips(
        jnp.concatenate(
            [grads_qk[0] + swap(grads_qk[1]), grads_vo[0] + swap(grads_vo[1])], axis=2
        )
    )[0]
    dkv = jnp.concatenate([dk, dv], axis=1)

    wq, wkv = qkv_full[:, :model], qkv_full[:, model:]
    partial = outer_cols(dkv, wkv)
    own_part = partial[halo:] + outer_cols(dq, wq)
    back_near = partial[rows:halo] + lax.ppermute(partial[:rows], "seq", behind)
    grad_normed_one = own_part + lax.ppermute(back_near, "seq", behind)
    xhat1, rate1 = norm_stats(block_input)
    grad_input = grad_resid + norm_back(grad_normed_one, gain1, xhat1, rate1)
    grad_gain_one = jnp.sum(grad_normed_one * xhat1, axis=0)
    grad_bias_one = jnp.sum(grad_normed_one, axis=0)

    grad_up, grad_down = unpack_grads(
        *(
            jnp.concatenate(parts, axis=0)
            for parts in zip(line_end(kept_a), line_sum(shard_b))
        ),
        swap, core, chips,
    )
    sum_c = lax.psum(shard_c, "seq")
    grad_qkv, grad_wout = sum_c[:, :3 * model], sum_c[:, 3 * model:]

    small = jnp.concatenate(
        [
            grad_gain_one[None], grad_bias_one[None], grad_gain_two[None], grad_bias_two[None],
            jnp.pad(dwa_local, (0, model - 5))[None], jnp.zeros((3, model), F32),
        ],
        axis=0,
    )
    bit = 1
    while bit < devices:
        small = small + exchange(small, bit)
        bit *= 2
    bit = 1
    while bit < groups:
        small = small + shift(small, bit)
        bit *= 2
    gain_one, bias_one, gain_two, bias_two = small[0], small[1], small[2], small[3]
    grad_dwa = small[4, :5]
    return (
        output,
        grad_input,
        grad_dwa,
        gain_one,
        bias_one,
        grad_qkv,
        grad_wout,
        gain_two,
        bias_two,
        grad_up,
        grad_down,
    )


def solution(mesh):
    in_specs = (
        P(("dp", "seq"), None),
        P(("dp", "seq"), None),
        P(None, ("dp", "seq"), None),
        P(),
        P(),
        P(),
        P("dp", None),
        P("dp", None),
        P(),
        P(),
        P("dp", None),
        P("dp", None),
        P("dp", "seq"),
        P(("dp", "seq"), None),
    )
    out_specs = (
        P(("dp", "seq"), None),
        P(("dp", "seq"), None),
        P(),
        P(),
        P(),
        P("dp", None),
        P("dp", None),
        P(),
        P(),
        P("dp", None),
        P("dp", None),
    )
    return jax.shard_map(body, mesh=mesh, in_specs=in_specs, out_specs=out_specs, check_vma=False)
```

```python
import functools
import math

import jax
import jax.numpy as jnp
import numpy as np
from jax import lax
from jax.experimental import pallas as pl
from jax.experimental.pallas import tpu as pltpu
from jax.sharding import PartitionSpec as P

HD = 64
DOC_MOST = 768
LOG2E = math.log2(math.e)
SCALE = 1.0 / math.sqrt(HD)
NEG = -1e30
F32 = jnp.float32
BF16 = jnp.bfloat16
HIGH = lax.Precision.HIGH
VMEM_LIMIT = 56 * 1024 * 1024
BLK = 128


def cost(micros):
    return pl.CostEstimate(
        flops=int(micros * 1.1e9), bytes_accessed=1 << 20, transcendentals=0
    )


def params():
    return pltpu.CompilerParams(
        dimension_semantics=("arbitrary",), vmem_limit_bytes=VMEM_LIMIT
    )


def split(values):
    high = values.astype(BF16)
    return high, (values - high.astype(F32)).astype(BF16)


def dot_nn(left, right):
    return lax.dot_general(left, right, (((1,), (0,)), ((), ())), preferred_element_type=F32)


def dot_nt(left, right):
    return lax.dot_general(left, right, (((1,), (1,)), ((), ())), preferred_element_type=F32)


def dot_tn(left, right):
    return lax.dot_general(left, right, (((0,), (0,)), ((), ())), preferred_element_type=F32)


def three(dot, left, right):
    return (
        dot(left[0], right[0]) + dot(left[0], right[1]) + dot(left[1], right[0])
    )


def norm_stats(values):
    row_mean = jnp.mean(values, axis=-1, keepdims=True)
    centred = values - row_mean
    row_var = jnp.mean(centred * centred, axis=-1, keepdims=True)
    rate = lax.rsqrt(row_var + 1e-05)
    return centred * rate, rate


def turned(values):
    lane = lax.broadcasted_iota(jnp.int32, values.shape, 1)
    return jnp.where(
        (lane & 63) < 32, pltpu.roll(values, 96, 1), pltpu.roll(values, 32, 1)
    )


def rotate(values, cosine, sine):
    return values * cosine + turned(values) * sine


def unrotate(values, cosine, sine):
    return values * cosine - turned(values) * sine


def rotary_tables(length, halo):
    half = HD // 2
    inv_freq = (10000.0 ** (-(np.arange(half, dtype=np.float32) * 2.0 / HD))).astype(np.float32)
    place = np.arange(-halo, length, dtype=np.float32)
    angles = place[:, None] * inv_freq[None, :]
    cosine = np.cos(angles.astype(np.float64)).astype(np.float32)
    sine = np.sin(angles.astype(np.float64)).astype(np.float32)
    return (
        np.concatenate([cosine] * 4, axis=1),
        np.concatenate([-sine, sine, -sine, sine], axis=1),
    )


def qkv_kernel(far_ref, near_ref, own_ref, gain_ref, bias_ref, w_ref, cos_ref, sin_ref,
               q_ref, kv_ref, hi_ref, lo_ref):
    step = pl.program_id(0)
    rows = own_ref.shape[0]
    third = pl.num_programs(0) // 3
    halo = hi_ref.shape[0] - rows

    @pl.when(step == 0)
    def _():
        for at, ref in enumerate((far_ref, near_ref, own_ref)):
            xhat, _ = norm_stats(ref[...])
            high, low = split(xhat * gain_ref[...] + bias_ref[...])
            hi_ref[at * rows:(at + 1) * rows] = high
            lo_ref[at * rows:(at + 1) * rows] = low

    weights = split(w_ref[...])

    @pl.when(step < third)
    def _():
        got = three(dot_nn, (hi_ref[halo:], lo_ref[halo:]), weights)
        for at in range(0, got.shape[1], 128):
            q_ref[:, at:at + 128] = rotate(got[:, at:at + 128], cos_ref[halo:], sin_ref[halo:])

    @pl.when((step >= third) & (step < 2 * third))
    def _():
        got = three(dot_nn, (hi_ref[...], lo_ref[...]), weights)
        for at in range(0, got.shape[1], 128):
            kv_ref[:, at:at + 128] = rotate(got[:, at:at + 128], cos_ref[...], sin_ref[...])

    @pl.when(step >= 2 * third)
    def _():
        kv_ref[...] = three(dot_nn, (hi_ref[...], lo_ref[...]), weights)


def project(far, near, own, gain, bias, w_full, cosine, sine):
    rows, model = own.shape
    total = 3 * rows
    wide = 256
    third = model // wide
    whole = lambda shape: pl.BlockSpec(shape, lambda j: (0, 0))
    return pl.pallas_call(
        qkv_kernel,
        grid=(3 * third,),
        in_specs=[
            whole((rows, model)), whole((rows, model)), whole((rows, model)),
            whole((1, model)), whole((1, model)),
            pl.BlockSpec((model, wide), lambda j: (0, j)),
            whole((total, 128)), whole((total, 128)),
        ],
        out_specs=[
            pl.BlockSpec((rows, wide), lambda j: (0, jnp.minimum(j, third - 1))),
            pl.BlockSpec((total, wide), lambda j: (0, jnp.maximum(j - third, 0))),
            whole((total, model)), whole((total, model)),
        ],
        out_shape=[
            jax.ShapeDtypeStruct((rows, model), F32),
            jax.ShapeDtypeStruct((total, 2 * model), F32),
            jax.ShapeDtypeStruct((total, model), BF16),
            jax.ShapeDtypeStruct((total, model), BF16),
        ],
        cost_estimate=cost(20),
        compiler_params=params(),
    )(far, near, own, gain, bias, w_full, cosine, sine)


def own_pair(values, head):
    lane = lax.broadcasted_iota(jnp.int32, values.shape, 1)
    other = pltpu.roll(values, 64, 1)
    return jnp.where((lane < 64) == (head == 0), values, other)


def outer_form(values, head):
    high, low = split(own_pair(values, head))
    return jnp.concatenate([high, low], axis=1)


def mixed(values, head):
    pair = own_pair(values, head)
    lane = lax.broadcasted_iota(jnp.int32, pair.shape, 1)
    high = pair.astype(BF16).astype(F32)
    return jnp.where(lane < 64, high, pair - high).astype(BF16)


def inner_form(values, head):
    half = mixed(values, head)
    return jnp.concatenate([half, half], axis=1)


def fold(values):
    return values + pltpu.roll(values, 64, 1)


def attend_kernel(q_ref, k_ref, v_ref, segq_ref, segk_ref, out_ref, bias_ref):
    rows = q_ref.shape[0]
    halo = k_ref.shape[0] - rows
    span = halo + BLK

    @pl.when(pl.program_id(0) == 0)
    def _():
        for at in range(0, rows, BLK):
            row = lax.broadcasted_iota(jnp.int32, (BLK, span), 0)
            col = lax.broadcasted_iota(jnp.int32, (BLK, span), 1)
            same = segq_ref[at:at + BLK, :1] == segk_ref[:1, at:at + span]
            bias_ref[at:at + BLK] = jnp.where(same & (col - halo <= row), 0.0, NEG)

    lane = lax.broadcasted_iota(jnp.int32, (BLK, 128), 1)
    scaled = q_ref[...] * (SCALE * LOG2E)
    results = []
    for head in range(2):
        left = inner_form(scaled, head)
        right = outer_form(k_ref[...], head)
        vals = mixed(v_ref[...], head)
        outs = []
        for at in range(0, rows, BLK):
            scores = dot_nt(left[at:at + BLK], right[at:at + span]) + bias_ref[at:at + BLK]
            top = jnp.max(scores, axis=1, keepdims=True)
            expo = jnp.exp2(scores - top)
            total = jnp.sum(expo, axis=1, keepdims=True)
            high, low = split(expo)
            got = dot_nn(high, vals[at:at + span]) + dot_nn(low, vals[at:at + span])
            outs.append(fold(got) / total)
        results.append(outs)
    for at in range(0, rows, BLK):
        out_ref[at:at + BLK] = jnp.where(
            lane < 64, results[0][at // BLK], results[1][at // BLK]
        )


def attend(q_rot, kv, seg_q, seg_k):
    rows, model = q_rot.shape
    total = kv.shape[0]
    pairs = model // 128
    return pl.pallas_call(
        attend_kernel,
        grid=(pairs,),
        in_specs=[
            pl.BlockSpec((rows, 128), lambda p: (0, p)),
            pl.BlockSpec((total, 128), lambda p: (0, p)),
            pl.BlockSpec((total, 128), lambda p: (0, pairs + p)),
            pl.BlockSpec((rows, 128), lambda p: (0, 0)),
            pl.BlockSpec((8, total), lambda p: (0, 0)),
        ],
        out_specs=pl.BlockSpec((rows, 128), lambda p: (0, p)),
        out_shape=jax.ShapeDtypeStruct((rows, model), F32),
        scratch_shapes=[pltpu.VMEM((rows, total - rows + BLK), F32)],
        cost_estimate=cost(24),
        compiler_params=params(),
    )(q_rot, kv, kv, seg_q, seg_k)


def attend_back_kernel(q_ref, k_ref, v_ref, g_ref, segq_ref, segk_ref, cos_ref, sin_ref, *refs):
    dq_ref, dk_ref, dv_ref, bias_ref = refs[-4:]
    rows = q_ref.shape[0]
    halo = k_ref.shape[0] - rows
    span = halo + BLK

    @pl.when(pl.program_id(0) == 0)
    def _():
        for at in range(0, rows, BLK):
            key = lax.broadcasted_iota(jnp.int32, (span, BLK), 0)
            query = lax.broadcasted_iota(jnp.int32, (span, BLK), 1)
            same = segk_ref[at:at + span, :1] == segq_ref[:1, at:at + BLK]
            bias_ref[:, at:at + BLK] = jnp.where(same & (key - halo <= query), 0.0, NEG)

    scaled = q_ref[...] * (SCALE * LOG2E)
    dq, dk, dv = [], [], []
    for head in range(2):
        q_in = inner_form(scaled, head)
        g_in = inner_form(g_ref[...], head)
        k_out = outer_form(k_ref[...], head)
        v_out = outer_form(v_ref[...], head)
        q_mix = mixed(q_ref[...], head)
        g_mix = mixed(g_ref[...], head)
        k_mix = mixed(k_ref[...], head)
        dq_head = []
        dk_head = jnp.zeros((halo + rows, 128), F32)
        dv_head = jnp.zeros((halo + rows, 128), F32)
        dk_parts, dv_parts = [], []
        for at in range(0, rows, BLK):
            scores = dot_nt(k_out[at:at + span], q_in[at:at + BLK]) + bias_ref[:, at:at + BLK]
            top = jnp.max(scores, axis=0, keepdims=True)
            expo = jnp.exp2(scores - top)
            inverse = 1.0 / jnp.sum(expo, axis=0, keepdims=True)
            grad_probs = dot_nt(v_out[at:at + span], g_in[at:at + BLK])
            probs = expo * inverse
            delta = jnp.sum(probs * grad_probs, axis=0, keepdims=True)
            grad_scores = probs * (grad_probs - delta)
            probs_cat = jnp.concatenate(split(probs), axis=1)
            scores_cat = jnp.concatenate(split(grad_scores), axis=1)
            g_two = jnp.concatenate([g_mix[at:at + BLK]] * 2, axis=0)
            q_two = jnp.concatenate([q_mix[at:at + BLK]] * 2, axis=0)
            dv_parts.append(dot_nn(probs_cat, g_two))
            dk_parts.append(dot_nn(scores_cat, q_two))
            got = dot_tn(scores_cat, k_mix[at:at + span])
            dq_head.append(fold(got[:BLK] + got[BLK:]))
        for parts, full in ((dk_parts, dk), (dv_parts, dv)):
            pieces = []
            for kb in range((halo + rows) // BLK):
                terms = [
                    parts[qb][(kb - qb) * BLK:(kb - qb + 1) * BLK]
                    for qb in range(rows // BLK)
                    if 0 <= kb - qb < span // BLK
                ]
                pieces.append(fold(functools.reduce(lambda a, b: a + b, terms)))
            full.append(pieces)
        dq.append(dq_head)
    lane = lax.broadcasted_iota(jnp.int32, (BLK, 128), 1)
    for qb in range(rows // BLK):
        rng = slice(qb * BLK, (qb + 1) * BLK)
        far = slice(halo + qb * BLK, halo + (qb + 1) * BLK)
        both = jnp.where(lane < 64, dq[0][qb], dq[1][qb]) * SCALE
        dq_ref[rng] = unrotate(both, cos_ref[far], sin_ref[far])
    for kb in range((halo + rows) // BLK):
        rng = slice(kb * BLK, (kb + 1) * BLK)
        both = jnp.where(lane < 64, dk[0][kb], dk[1][kb]) * SCALE
        dk_ref[rng] = unrotate(both, cos_ref[rng], sin_ref[rng])
        dv_ref[rng] = jnp.where(lane < 64, dv[0][kb], dv[1][kb])


def attend_back(first, count, q_rot, kv, grad, seg_q, seg_k, cosine, sine, before=()):
    rows, model = q_rot.shape
    total = kv.shape[0]
    pairs = model // 128
    fixed = lambda shape: pl.BlockSpec(shape, lambda p: (0, 0))
    return pl.pallas_call(
        attend_back_kernel,
        grid=(count,),
        in_specs=[
            pl.BlockSpec((rows, 128), lambda p: (0, first + p)),
            pl.BlockSpec((total, 128), lambda p: (0, first + p)),
            pl.BlockSpec((total, 128), lambda p: (0, pairs + first + p)),
            pl.BlockSpec((rows, 128), lambda p: (0, first + p)),
            fixed((8, rows)), fixed((total, 128)),
            fixed((total, 128)), fixed((total, 128)),
        ] + [pl.BlockSpec(memory_space=pl.ANY)] * len(before),
        out_specs=[
            pl.BlockSpec((rows, 128), lambda p: (0, first + p)),
            pl.BlockSpec((total, 128), lambda p: (0, first + p)),
            pl.BlockSpec((total, 128), lambda p: (0, first + p)),
        ],
        out_shape=[
            jax.ShapeDtypeStruct((rows, model), F32),
            jax.ShapeDtypeStruct((total, model), F32),
            jax.ShapeDtypeStruct((total, model), F32),
        ],
        scratch_shapes=[pltpu.VMEM((total - rows + BLK, rows), F32)],
        input_output_aliases={8 + i: i for i in range(len(before))},
        cost_estimate=cost(7 * count),
        compiler_params=params(),
    )(q_rot, kv, kv, grad, seg_q, seg_k, cosine, sine, *before)


def mlp_kernel(count, begun, chip_ref, resid_ref, other_ref, cot_ref, cot_other_ref, gain_ref, bias_ref,
               scale_ref, *refs):
    up_refs, down_refs = refs[:count], refs[count:2 * count]
    refs = refs[2 * count:]
    so_far, refs = refs[:2 * begun], refs[2 * begun:]
    out_ref, gnorm_ref, grad_ref = refs[:3]
    (x_hi, x_lo, xt_hi, xt_lo, g_hi, g_lo, up_hi, up_lo, down_hi, down_lo) = refs[3:]
    step = pl.program_id(0)
    rows = resid_ref.shape[0]

    @pl.when(step == 0)
    def _():
        for at, source, cot in ((0, resid_ref, cot_ref), (rows, other_ref, cot_other_ref)):
            xhat, _ = norm_stats(source[...])
            normed = xhat * gain_ref[...] + bias_ref[...]
            x_hi[at:at + rows], x_lo[at:at + rows] = split(normed)
            xt_hi[:, at:at + rows], xt_lo[:, at:at + rows] = split(normed.T)
            g_hi[at:at + rows], g_lo[at:at + rows] = split(cot[...] * scale_ref[0, 0])
        if begun:
            out_ref[...] = so_far[0][...]
            gnorm_ref[...] = so_far[1][...]
        else:
            out_ref[...] = jnp.zeros_like(out_ref)
            gnorm_ref[...] = jnp.zeros_like(gnorm_ref)

    for at in range(count):
        spot = (chip_ref[0] ^ at) if count > 1 else 0
        up_rows = up_refs[at].shape[0]
        high, low = split(up_refs[at][...])
        here = pl.ds(pl.multiple_of(spot * up_rows, up_rows), up_rows)
        up_hi[here], up_lo[here] = high, low
        block = down_refs[at][...]
        block = block.reshape(-1, block.shape[-1])
        high, low = split(block)
        here = pl.ds(pl.multiple_of(spot * block.shape[0], block.shape[0]), block.shape[0])
        down_hi[here], down_lo[here] = high, low

    chips, _, tall, width = grad_ref.shape
    up_tall = up_hi.shape[0] // chips
    deep = down_hi.shape[0] // chips
    up = (up_hi[...], up_lo[...])
    down = (down_hi[...], down_lo[...])
    normed = (x_hi[...], x_lo[...])
    normed_t = (xt_hi[...], xt_lo[...])
    grad_block = (g_hi[...], g_lo[...])
    pre = three(dot_nn, normed, up)
    grad_act = three(dot_nt, grad_block, down)
    inner = 0.7978845608028654 * (pre + 0.044715 * pre * pre * pre)
    bent = jnp.tanh(inner)
    act = 0.5 * pre * (1.0 + bent)
    slope = 0.5 * (1.0 + bent) + 0.5 * pre * (1.0 - bent * bent) * (
        0.7978845608028654 * (1.0 + 3.0 * 0.044715 * pre * pre)
    )
    act2 = split(act)
    grad_pre = split(grad_act * slope)
    out_ref[...] += three(dot_nn, act2, down)
    gnorm_ref[...] += three(dot_nt, grad_pre, up)
    gup = three(dot_nn, normed_t, grad_pre)
    gdown = three(dot_tn, act2, grad_block)
    half = deep // 2
    for chip in range(chips):
        grad_ref[chip, 0, :up_tall] = gup[chip * up_tall:(chip + 1) * up_tall]
        part = gdown[chip * deep:(chip + 1) * deep]
        grad_ref[chip, 0, up_tall:up_tall + deep] = part[:, :width]
        grad_ref[chip, 0, up_tall + deep:] = jnp.concatenate(
            [part[:half, width:], part[half:, width:]], axis=1
        )


def mlp(first, steps, so_far, chip, chips, resid, other, cot, cot_other, gain, bias, scale, ups, downs):
    rows, model = resid.shape
    width = 512
    up_tall = model // chips
    deep = width // chips
    fixed = lambda shape: pl.BlockSpec(shape, lambda j, c: (0, 0))
    if len(ups) > 1:
        down_spec = pl.BlockSpec((deep, model), lambda j, c: (first + j, 0))
    else:
        downs = [downs[0].reshape(chips, -1, model)]
        down_spec = pl.BlockSpec((chips, deep, model), lambda j, c: (0, first + j, 0))
    tall = up_tall + deep + deep // 2
    grid_spec = pltpu.PrefetchScalarGridSpec(
        num_scalar_prefetch=1,
        grid=(steps,),
        in_specs=[fixed((rows, model))] * 4 + [fixed((1, model))] * 2
        + [pl.BlockSpec(memory_space=pltpu.SMEM)]
        + [pl.BlockSpec((up.shape[0], width), lambda j, c: (0, first + j)) for up in ups]
        + [down_spec] * len(downs)
        + [fixed((2 * rows, model))] * len(so_far),
        out_specs=[
            fixed((2 * rows, model)), fixed((2 * rows, model)),
            pl.BlockSpec((chips, 1, tall, width), lambda j, c: (0, j, 0, 0)),
        ],
        scratch_shapes=[
            pltpu.VMEM((2 * rows, model), BF16), pltpu.VMEM((2 * rows, model), BF16),
            pltpu.VMEM((model, 2 * rows), BF16), pltpu.VMEM((model, 2 * rows), BF16),
            pltpu.VMEM((2 * rows, model), BF16), pltpu.VMEM((2 * rows, model), BF16),
            pltpu.VMEM((model, width), BF16), pltpu.VMEM((model, width), BF16),
            pltpu.VMEM((width, model), BF16), pltpu.VMEM((width, model), BF16),
        ],
    )
    return pl.pallas_call(
        functools.partial(mlp_kernel, len(ups), len(so_far) // 2),
        grid_spec=grid_spec,
        out_shape=[
            jax.ShapeDtypeStruct((2 * rows, model), F32),
            jax.ShapeDtypeStruct((2 * rows, model), F32),
            jax.ShapeDtypeStruct((chips, steps, tall, width), F32),
        ],
        cost_estimate=cost(18 * steps),
        compiler_params=params(),
    )(chip, resid, other, cot, cot_other, gain, bias, scale, *ups, *downs, *so_far)


def unpack_grads(up, down, sibling_swap, core, chips):
    steps, up_tall, width = up.shape
    deep = up_tall * 2 // 3
    half = up_tall // 2
    mine = jnp.where(core == 0, up[:, :half], up[:, half:])
    other = sibling_swap(jnp.where(core == 0, up[:, half:], up[:, :half]))
    by_core = jnp.stack(
        [jnp.where(core == 0, mine, other), jnp.where(core == 0, other, mine)], axis=0
    )
    by_core = by_core.reshape(2, steps, half, chips, width // chips)
    grad_up = jnp.transpose(by_core, (2, 3, 0, 1, 4)).reshape(half, -1)
    quarter = width // 2
    tail = down[:, deep:]
    right = jnp.concatenate([tail[:, :, :quarter], tail[:, :, quarter:]], axis=1)
    grad_down = jnp.concatenate([down[:, :deep], right], axis=2).reshape(steps * deep, -1)
    return grad_up, grad_down


def place_rows(core_ref, out_ref, got):
    chips = out_ref.shape[1]
    tall = out_ref.shape[2]
    for block in range(2 * chips):
        out_ref[(block & 1) ^ core_ref[0], block // 2] = got[block * tall:(block + 1) * tall]


def weights_qk_kernel(core_ref, hi_ref, lo_ref, dq_ref, dk_ref, out_ref, nt_hi, nt_lo):
    step = pl.program_id(0)
    part = pl.num_programs(0) // 2
    halo = hi_ref.shape[0] - dq_ref.shape[0]

    @pl.when(step == 0)
    def _():
        nt_hi[...] = hi_ref[...].T
        nt_lo[...] = lo_ref[...].T

    @pl.when(step < part)
    def _():
        left = (nt_hi[:, halo:], nt_lo[:, halo:])
        place_rows(core_ref, out_ref, three(dot_nn, left, split(dq_ref[...])))

    @pl.when(step >= part)
    def _():
        left = (nt_hi[...], nt_lo[...])
        place_rows(core_ref, out_ref, three(dot_nn, left, split(dk_ref[...])))


def weights_vo_kernel(core_ref, hi_ref, lo_ref, dv_ref, att_ref, res_ref, out_ref,
                      nt_hi, nt_lo, at_hi, at_lo):
    step = pl.program_id(0)
    part = pl.num_programs(0) // 2

    @pl.when(step == 0)
    def _():
        nt_hi[...] = hi_ref[...].T
        nt_lo[...] = lo_ref[...].T
        at_hi[...], at_lo[...] = split(att_ref[...].T)

    @pl.when(step < part)
    def _():
        left = (nt_hi[...], nt_lo[...])
        place_rows(core_ref, out_ref, three(dot_nn, left, split(dv_ref[...])))

    @pl.when(step >= part)
    def _():
        left = (at_hi[...], at_lo[...])
        place_rows(core_ref, out_ref, three(dot_nn, left, split(res_ref[...])))


def weight_call(kernel, micros, core, chips, fixed_args, pieces, scratch):
    model = fixed_args[0].shape[1]
    wide = 256
    part = model // wide
    tall = model // chips // 2
    fixed = lambda v: pl.BlockSpec(v.shape, lambda j, c: (0, 0))
    piece = lambda v, at: pl.BlockSpec(
        (v.shape[0], wide), lambda j, c: (0, jnp.clip(j - at * part, 0, part - 1))
    )
    specs, args = [], []
    for value, at in pieces:
        args.append(value)
        specs.append(fixed(value) if at is None else piece(value, at))
    return pl.pallas_call(
        kernel,
        grid_spec=pltpu.PrefetchScalarGridSpec(
            num_scalar_prefetch=1,
            grid=(2 * part,),
            in_specs=[fixed(v) for v in fixed_args] + specs,
            out_specs=pl.BlockSpec((2, chips, tall, wide), lambda j, c: (0, 0, 0, j)),
            scratch_shapes=[pltpu.VMEM((model, n), BF16) for n in scratch],
        ),
        out_shape=jax.ShapeDtypeStruct((2, chips, tall, 2 * model), F32),
        cost_estimate=cost(micros),
        compiler_params=params(),
    )(core, *fixed_args, *args)


def norm_back(grad, gain, xhat, rate):
    scaled = grad * gain
    return rate * (
        scaled
        - jnp.mean(scaled, axis=-1, keepdims=True)
        - xhat * jnp.mean(scaled * xhat, axis=-1, keepdims=True)
    )


def matmul(left, right):
    return jnp.dot(left, right, precision=HIGH)


def inner_rows(left, right):
    return lax.dot_general(left, right, (((0,), (0,)), ((), ())), precision=HIGH)


def outer_cols(left, right):
    return lax.dot_general(left, right, (((1,), (1,)), ((), ())), precision=HIGH)


def body(
    block_input,
    embedding,
    earlier_outs,
    dwa_weights,
    ln1_gain,
    ln1_bias,
    w_qkv,
    w_out,
    ln2_gain,
    ln2_bias,
    w_up,
    w_down,
    segments,
    cotangent,
):
    groups = lax.axis_size("seq")
    rows, model = block_input.shape
    length = rows * groups
    halo = 2 * rows
    place = lax.axis_index("seq")
    ahead = [(i, i + 1) for i in range(groups - 1)]
    behind = [(i + 1, i) for i in range(groups - 1)]
    gain1, bias1 = ln1_gain[None], ln1_bias[None]
    gain2, bias2 = ln2_gain[None], ln2_bias[None]

    devices = lax.axis_size("dp")
    chips = devices // 2
    spot = lax.axis_index("dp")
    core = spot % 2
    chip = (spot // 2).reshape(1).astype(jnp.int32)
    same_core = [[2 * i + c for i in range(chips)] for c in range(2)]
    exchange = lambda v, bit: lax.ppermute(v, "dp", [(i, i ^ bit) for i in range(devices)])
    swap = lambda v: exchange(v, 1)

    gather = lambda v: lax.all_gather(v, "dp", axis=0, tiled=True)
    qkv_full = gather(w_qkv)

    shard = w_down.shape[0]
    third = shard // 3
    by_core = w_up.reshape(w_up.shape[0], chips, 2, 3, third)
    by_core = jnp.transpose(by_core, (2, 0, 3, 1, 4)).reshape(2, w_up.shape[0], -1)
    mine = jnp.where(core == 0, by_core[0], by_core[1])
    given = swap(jnp.where(core == 0, by_core[1], by_core[0]))
    up_chip = jnp.concatenate(
        [jnp.where(core == 0, mine, given), jnp.where(core == 0, given, mine)], axis=0
    )
    if chips == 4:
        up_x, down_x = exchange(up_chip, 2), exchange(w_down, 2)
        up_y, down_y = exchange(up_chip, 4), exchange(w_down, 4)
        ups = [up_chip, up_x, up_y, exchange(up_y, 2)]
        downs = [w_down, down_x, down_y, exchange(down_x, 4)]
    else:
        ups, downs = (
            [lax.all_gather(v, "dp", axis=0, tiled=True, axis_index_groups=same_core)]
            for v in (up_chip, w_down)
        )

    seg_own = segments + 1
    near = lax.ppermute(block_input, "seq", ahead)
    seg_near = lax.ppermute(seg_own, "seq", ahead)
    far = lax.ppermute(near, "seq", ahead)
    seg_far = lax.ppermute(seg_near, "seq", ahead)
    seg_all = jnp.concatenate([seg_far, seg_near, seg_own], axis=1)
    seg_k_row = jnp.broadcast_to(seg_all, (8, halo + rows))
    seg_k_col = jnp.broadcast_to(seg_all.reshape(-1, 1), (halo + rows, 128))
    seg_q_row = seg_k_row[:, halo:]
    seg_q_col = seg_k_col[halo:]

    cos_all, sin_all = rotary_tables(length, halo)
    cosine = lax.dynamic_slice_in_dim(jnp.asarray(cos_all), place * rows, halo + rows, 0)
    sine = lax.dynamic_slice_in_dim(jnp.asarray(sin_all), place * rows, halo + rows, 0)

    q_rot, kv, normed_hi, normed_lo = project(
        far, near, block_input, gain1, bias1, qkv_full, cosine, sine
    )
    attended = attend(q_rot, kv, seg_q_col, seg_k_row)

    out_full = gather(w_out)
    resid = block_input + matmul(attended, out_full)
    resid_other = swap(resid)
    cot_other = swap(cotangent)
    scale = dwa_weights[4].reshape(1, 1)
    call = functools.partial(
        mlp, chip=chip, chips=chips, resid=resid, other=resid_other, cot=cotangent,
        cot_other=cot_other, gain=gain2, bias=bias2, scale=scale, ups=ups, downs=downs,
    )
    scatter = lambda v: lax.psum_scatter(v, "dp", scatter_dimension=0, tiled=True)
    scatter_chips = lambda v: lax.psum_scatter(
        v, "dp", scatter_dimension=0, tiled=True, axis_index_groups=same_core
    )
    out_part, gnorm_part, grads_a = call(0, 1, ())
    shard_a = scatter_chips(grads_a)[0]
    out_part, gnorm_part, grads_b = call(1, 2, (out_part, gnorm_part))
    shard_b = scatter_chips(grads_b)[0]
    grad_normed_two = gnorm_part[:rows] + swap(gnorm_part[rows:])
    mlp_out = out_part[:rows] + swap(out_part[rows:])

    block_out = resid + mlp_out
    output = (
        dwa_weights[0] * embedding
        + dwa_weights[1] * earlier_outs[0]
        + dwa_weights[2] * earlier_outs[1]
        + dwa_weights[3] * earlier_outs[2]
        + dwa_weights[4] * block_out
    )
    dwa_local = jnp.stack(
        [
            jnp.sum(cotangent * embedding),
            jnp.sum(cotangent * earlier_outs[0]),
            jnp.sum(cotangent * earlier_outs[1]),
            jnp.sum(cotangent * earlier_outs[2]),
            jnp.sum(cotangent * block_out),
        ]
    )
    xhat2, rate2 = norm_stats(resid)
    grad_resid = dwa_weights[4] * cotangent + norm_back(grad_normed_two, gain2, xhat2, rate2)
    grad_gain_two = jnp.sum(grad_normed_two * xhat2, axis=0)
    grad_bias_two = jnp.sum(grad_normed_two, axis=0)
    grad_attended = outer_cols(grad_resid, out_full)

    back_args = (q_rot, kv, grad_attended, seg_q_row, seg_k_col, cosine, sine)
    pairs = model // 128
    first_half = attend_back(0, pairs // 2, *back_args)
    shift = lambda v, bit: lax.ppermute(v, "seq", [(i, i ^ bit) for i in range(groups)])
    even = place % 2 == 0

    def line_start(shard):
        tall = shard.shape[1] // 2
        halves = (shard[:, :tall], shard[:, tall:])
        kept = jnp.where(even, halves[0], halves[1])
        return kept + shift(jnp.where(even, halves[1], halves[0]), 1)

    def line_middle(kept):
        bit = 2
        while bit < groups:
            kept = kept + shift(kept, bit)
            bit *= 2
        return kept

    def line_end(kept):
        other = shift(kept, 1)
        return jnp.where(even, kept, other), jnp.where(even, other, kept)

    kept_a = line_start(shard_a)
    kept_a, back_args, first_half = lax.optimization_barrier((kept_a, back_args, first_half))
    kept_a = line_middle(kept_a)
    dq, dk, dv = attend_back(pairs // 2, pairs - pairs // 2, *back_args, before=first_half)
    kept_a, dq, dk, dv = lax.optimization_barrier((kept_a, dq, dk, dv))
    core_at = core.reshape(1).astype(jnp.int32)
    normed_parts = (normed_hi, normed_lo)
    grads_qk = weight_call(
        weights_qk_kernel, 9, core_at, chips, normed_parts, [(dq, 0), (dk, 1)], [halo + rows] * 2
    )
    given_qk = swap(grads_qk[1])
    shard_b, dv = lax.optimization_barrier((shard_b, dv))
    kept_b = line_start(shard_b)
    grads_vo = weight_call(
        weights_vo_kernel, 9, core_at, chips, normed_parts,
        [(dv, 0), (attended, None), (grad_resid, 1)], [halo + rows] * 2 + [rows] * 2,
    )
    shard_c = scatter_chips(
        jnp.concatenate([grads_qk[0] + given_qk, grads_vo[0] + swap(grads_vo[1])], axis=2)
    )[0]
    kept_b, dk = lax.optimization_barrier((kept_b, dk))
    kept_b = line_middle(kept_b)
    dkv = jnp.concatenate([dk, dv], axis=1)

    wq, wkv = qkv_full[:, :model], qkv_full[:, model:]
    partial = outer_cols(dkv, wkv)
    own_part = partial[halo:] + outer_cols(dq, wq)
    back_near = partial[rows:halo] + lax.ppermute(partial[:rows], "seq", behind)

    xhat1, rate1 = norm_stats(block_input)
    terms = (
        (norm_stats(far)[0], partial[:rows]),
        (norm_stats(near)[0], partial[rows:halo]),
        (xhat1, own_part),
    )
    grad_gain_one = sum(jnp.sum(xhat * part, axis=0) for xhat, part in terms)
    grad_bias_one = sum(jnp.sum(part, axis=0) for _, part in terms)

    small = jnp.concatenate(
        [
            grad_gain_one[None], grad_bias_one[None], grad_gain_two[None], grad_bias_two[None],
            jnp.pad(dwa_local, (0, model - 5))[None], jnp.zeros((3, model), F32),
        ],
        axis=0,
    )
    bit = 1
    while bit < devices:
        small = small + exchange(small, bit)
        bit *= 2
    bit = 1
    while bit < groups:
        small = small + shift(small, bit)
        bit *= 2
    ends_a = line_end(kept_a)
    shard_c, back_near, ends_a, kept_b, small = lax.optimization_barrier(
        (shard_c, back_near, ends_a, kept_b, small)
    )
    gain_one, bias_one, gain_two, bias_two = small[0], small[1], small[2], small[3]
    grad_dwa = small[4, :5]
    sum_c = lax.psum(shard_c, "seq")
    grad_qkv, grad_wout = sum_c[:, :3 * model], sum_c[:, 3 * model:]
    grad_normed_one = own_part + lax.ppermute(back_near, "seq", behind)
    grad_input = grad_resid + norm_back(grad_normed_one, gain1, xhat1, rate1)
    grad_up, grad_down = unpack_grads(
        *(
            jnp.concatenate(parts, axis=0)
            for parts in zip(ends_a, line_end(kept_b))
        ),
        swap, core, chips,
    )
    return (
        output,
        grad_input,
        grad_dwa,
        gain_one,
        bias_one,
        grad_qkv,
        grad_wout,
        gain_two,
        bias_two,
        grad_up,
        grad_down,
    )


def solution(mesh):
    in_specs = (
        P(("dp", "seq"), None),
        P(("dp", "seq"), None),
        P(None, ("dp", "seq"), None),
        P(),
        P(),
        P(),
        P("dp", None),
        P("dp", None),
        P(),
        P(),
        P("dp", None),
        P("dp", None),
        P("dp", "seq"),
        P(("dp", "seq"), None),
    )
    out_specs = (
        P(("dp", "seq"), None),
        P(("dp", "seq"), None),
        P(),
        P(),
        P(),
        P("dp", None),
        P("dp", None),
        P(),
        P(),
        P("dp", None),
        P("dp", None),
    )
    return jax.shard_map(body, mesh=mesh, in_specs=in_specs, out_specs=out_specs, check_vma=False)
```

```python
import functools
import math

import jax
import jax.numpy as jnp
import numpy as np
from jax import lax
from jax.experimental import pallas as pl
from jax.experimental.pallas import tpu as pltpu
from jax.sharding import PartitionSpec as P

HD = 64
DOC_MOST = 768
LOG2E = math.log2(math.e)
SCALE = 1.0 / math.sqrt(HD)
NEG = -1e30
F32 = jnp.float32
BF16 = jnp.bfloat16
HIGH = lax.Precision.HIGH
VMEM_LIMIT = 56 * 1024 * 1024
BLK = 128


def cost(micros):
    return pl.CostEstimate(
        flops=int(micros * 1.1e9), bytes_accessed=1 << 20, transcendentals=0
    )


def params():
    return pltpu.CompilerParams(
        dimension_semantics=("arbitrary",), vmem_limit_bytes=VMEM_LIMIT
    )


def split(values):
    high = values.astype(BF16)
    return high, (values - high.astype(F32)).astype(BF16)


def dot_nn(left, right):
    return lax.dot_general(left, right, (((1,), (0,)), ((), ())), preferred_element_type=F32)


def dot_nt(left, right):
    return lax.dot_general(left, right, (((1,), (1,)), ((), ())), preferred_element_type=F32)


def dot_tn(left, right):
    return lax.dot_general(left, right, (((0,), (0,)), ((), ())), preferred_element_type=F32)


def three(dot, left, right):
    return (
        dot(left[0], right[0]) + dot(left[0], right[1]) + dot(left[1], right[0])
    )


def norm_stats(values):
    row_mean = jnp.mean(values, axis=-1, keepdims=True)
    centred = values - row_mean
    row_var = jnp.mean(centred * centred, axis=-1, keepdims=True)
    rate = lax.rsqrt(row_var + 1e-05)
    return centred * rate, rate


def norm_back(grad, gain, xhat, rate):
    scaled = grad * gain
    return rate * (
        scaled
        - jnp.mean(scaled, axis=-1, keepdims=True)
        - xhat * jnp.mean(scaled * xhat, axis=-1, keepdims=True)
    )


def turned(values):
    lane = lax.broadcasted_iota(jnp.int32, values.shape, 1)
    return jnp.where(
        (lane & 63) < 32, pltpu.roll(values, 96, 1), pltpu.roll(values, 32, 1)
    )


def rotate(values, cosine, sine):
    return values * cosine + turned(values) * sine


def unrotate(values, cosine, sine):
    return values * cosine - turned(values) * sine


def rotary_tables(length, halo):
    half = HD // 2
    inv_freq = (10000.0 ** (-(np.arange(half, dtype=np.float32) * 2.0 / HD))).astype(np.float32)
    place = np.arange(-halo, length, dtype=np.float32)
    angles = place[:, None] * inv_freq[None, :]
    cosine = np.cos(angles.astype(np.float64)).astype(np.float32)
    sine = np.sin(angles.astype(np.float64)).astype(np.float32)
    return (
        np.concatenate([cosine] * 4, axis=1),
        np.concatenate([-sine, sine, -sine, sine], axis=1),
    )


def qkv_kernel(far_ref, near_ref, own_ref, gain_ref, bias_ref, w_ref, cos_ref, sin_ref,
               q_ref, kv_ref, hi_ref, lo_ref):
    step = pl.program_id(0)
    rows = own_ref.shape[0]
    third = pl.num_programs(0) // 3
    halo = hi_ref.shape[0] - rows

    @pl.when(step == 0)
    def _():
        for at, ref in enumerate((far_ref, near_ref, own_ref)):
            xhat, _ = norm_stats(ref[...])
            high, low = split(xhat * gain_ref[...] + bias_ref[...])
            hi_ref[at * rows:(at + 1) * rows] = high
            lo_ref[at * rows:(at + 1) * rows] = low

    weights = split(w_ref[...])

    @pl.when(step < third)
    def _():
        got = three(dot_nn, (hi_ref[halo:], lo_ref[halo:]), weights)
        for at in range(0, got.shape[1], 128):
            q_ref[:, at:at + 128] = rotate(got[:, at:at + 128], cos_ref[halo:], sin_ref[halo:])

    @pl.when((step >= third) & (step < 2 * third))
    def _():
        got = three(dot_nn, (hi_ref[...], lo_ref[...]), weights)
        for at in range(0, got.shape[1], 128):
            kv_ref[:, at:at + 128] = rotate(got[:, at:at + 128], cos_ref[...], sin_ref[...])

    @pl.when(step >= 2 * third)
    def _():
        kv_ref[...] = three(dot_nn, (hi_ref[...], lo_ref[...]), weights)


def project(far, near, own, gain, bias, w_full, cosine, sine):
    rows, model = own.shape
    total = 3 * rows
    wide = 256
    third = model // wide
    whole = lambda shape: pl.BlockSpec(shape, lambda j: (0, 0))
    return pl.pallas_call(
        qkv_kernel,
        grid=(3 * third,),
        in_specs=[
            whole((rows, model)), whole((rows, model)), whole((rows, model)),
            whole((1, model)), whole((1, model)),
            pl.BlockSpec((model, wide), lambda j: (0, j)),
            whole((total, 128)), whole((total, 128)),
        ],
        out_specs=[
            pl.BlockSpec((rows, wide), lambda j: (0, jnp.minimum(j, third - 1))),
            pl.BlockSpec((total, wide), lambda j: (0, jnp.maximum(j - third, 0))),
            whole((total, model)), whole((total, model)),
        ],
        out_shape=[
            jax.ShapeDtypeStruct((rows, model), F32),
            jax.ShapeDtypeStruct((total, 2 * model), F32),
            jax.ShapeDtypeStruct((total, model), BF16),
            jax.ShapeDtypeStruct((total, model), BF16),
        ],
        cost_estimate=cost(20),
        compiler_params=params(),
    )(far, near, own, gain, bias, w_full, cosine, sine)


def own_pair(values, head):
    lane = lax.broadcasted_iota(jnp.int32, values.shape, 1)
    other = pltpu.roll(values, 64, 1)
    return jnp.where((lane < 64) == (head == 0), values, other)


def outer_form(values, head):
    high, low = split(own_pair(values, head))
    return jnp.concatenate([high, low], axis=1)


def mixed(values, head):
    pair = own_pair(values, head)
    lane = lax.broadcasted_iota(jnp.int32, pair.shape, 1)
    high = pair.astype(BF16).astype(F32)
    return jnp.where(lane < 64, high, pair - high).astype(BF16)


def inner_form(values, head):
    half = mixed(values, head)
    return jnp.concatenate([half, half], axis=1)


def fold(values):
    return values + pltpu.roll(values, 64, 1)


def attend_kernel(q_ref, k_ref, v_ref, segq_ref, segk_ref, out_ref, bias_ref):
    rows = q_ref.shape[0]
    halo = k_ref.shape[0] - rows
    span = halo + BLK

    @pl.when(pl.program_id(0) == 0)
    def _():
        for at in range(0, rows, BLK):
            row = lax.broadcasted_iota(jnp.int32, (BLK, span), 0)
            col = lax.broadcasted_iota(jnp.int32, (BLK, span), 1)
            same = segq_ref[at:at + BLK, :1] == segk_ref[:1, at:at + span]
            bias_ref[at:at + BLK] = jnp.where(same & (col - halo <= row), 0.0, NEG)

    lane = lax.broadcasted_iota(jnp.int32, (BLK, 128), 1)
    scaled = q_ref[...] * (SCALE * LOG2E)
    results = []
    for head in range(2):
        left = inner_form(scaled, head)
        right = outer_form(k_ref[...], head)
        vals = mixed(v_ref[...], head)
        outs = []
        for at in range(0, rows, BLK):
            scores = dot_nt(left[at:at + BLK], right[at:at + span]) + bias_ref[at:at + BLK]
            top = jnp.max(scores, axis=1, keepdims=True)
            expo = jnp.exp2(scores - top)
            total = jnp.sum(expo, axis=1, keepdims=True)
            high, low = split(expo)
            got = dot_nn(high, vals[at:at + span]) + dot_nn(low, vals[at:at + span])
            outs.append(fold(got) / total)
        results.append(outs)
    for at in range(0, rows, BLK):
        out_ref[at:at + BLK] = jnp.where(
            lane < 64, results[0][at // BLK], results[1][at // BLK]
        )


def attend(q_rot, kv, seg_q, seg_k):
    rows, model = q_rot.shape
    total = kv.shape[0]
    pairs = model // 128
    return pl.pallas_call(
        attend_kernel,
        grid=(pairs,),
        in_specs=[
            pl.BlockSpec((rows, 128), lambda p: (0, p)),
            pl.BlockSpec((total, 128), lambda p: (0, p)),
            pl.BlockSpec((total, 128), lambda p: (0, pairs + p)),
            pl.BlockSpec((rows, 128), lambda p: (0, 0)),
            pl.BlockSpec((8, total), lambda p: (0, 0)),
        ],
        out_specs=pl.BlockSpec((rows, 128), lambda p: (0, p)),
        out_shape=jax.ShapeDtypeStruct((rows, model), F32),
        scratch_shapes=[pltpu.VMEM((rows, total - rows + BLK), F32)],
        cost_estimate=cost(24),
        compiler_params=params(),
    )(q_rot, kv, kv, seg_q, seg_k)


def attend_back_kernel(q_ref, k_ref, v_ref, g_ref, segq_ref, segk_ref, cos_ref, sin_ref, *refs):
    dq_ref, dk_ref, dv_ref, bias_ref = refs[-4:]
    rows = q_ref.shape[0]
    halo = k_ref.shape[0] - rows
    span = halo + BLK

    @pl.when(pl.program_id(0) == 0)
    def _():
        for at in range(0, rows, BLK):
            key = lax.broadcasted_iota(jnp.int32, (span, BLK), 0)
            query = lax.broadcasted_iota(jnp.int32, (span, BLK), 1)
            same = segk_ref[at:at + span, :1] == segq_ref[:1, at:at + BLK]
            bias_ref[:, at:at + BLK] = jnp.where(same & (key - halo <= query), 0.0, NEG)

    scaled = q_ref[...] * (SCALE * LOG2E)
    dq, dk, dv = [], [], []
    for head in range(2):
        q_in = inner_form(scaled, head)
        g_in = inner_form(g_ref[...], head)
        k_out = outer_form(k_ref[...], head)
        v_out = outer_form(v_ref[...], head)
        q_mix = mixed(q_ref[...], head)
        g_mix = mixed(g_ref[...], head)
        k_mix = mixed(k_ref[...], head)
        dq_head = []
        dk_head = jnp.zeros((halo + rows, 128), F32)
        dv_head = jnp.zeros((halo + rows, 128), F32)
        dk_parts, dv_parts = [], []
        for at in range(0, rows, BLK):
            scores = dot_nt(k_out[at:at + span], q_in[at:at + BLK]) + bias_ref[:, at:at + BLK]
            top = jnp.max(scores, axis=0, keepdims=True)
            expo = jnp.exp2(scores - top)
            inverse = 1.0 / jnp.sum(expo, axis=0, keepdims=True)
            grad_probs = dot_nt(v_out[at:at + span], g_in[at:at + BLK])
            probs = expo * inverse
            delta = jnp.sum(probs * grad_probs, axis=0, keepdims=True)
            grad_scores = probs * (grad_probs - delta)
            probs_cat = jnp.concatenate(split(probs), axis=1)
            scores_cat = jnp.concatenate(split(grad_scores), axis=1)
            g_two = jnp.concatenate([g_mix[at:at + BLK]] * 2, axis=0)
            q_two = jnp.concatenate([q_mix[at:at + BLK]] * 2, axis=0)
            dv_parts.append(dot_nn(probs_cat, g_two))
            dk_parts.append(dot_nn(scores_cat, q_two))
            got = dot_tn(scores_cat, k_mix[at:at + span])
            dq_head.append(fold(got[:BLK] + got[BLK:]))
        for parts, full in ((dk_parts, dk), (dv_parts, dv)):
            pieces = []
            for kb in range((halo + rows) // BLK):
                terms = [
                    parts[qb][(kb - qb) * BLK:(kb - qb + 1) * BLK]
                    for qb in range(rows // BLK)
                    if 0 <= kb - qb < span // BLK
                ]
                pieces.append(fold(functools.reduce(lambda a, b: a + b, terms)))
            full.append(pieces)
        dq.append(dq_head)
    lane = lax.broadcasted_iota(jnp.int32, (BLK, 128), 1)
    for qb in range(rows // BLK):
        rng = slice(qb * BLK, (qb + 1) * BLK)
        far = slice(halo + qb * BLK, halo + (qb + 1) * BLK)
        both = jnp.where(lane < 64, dq[0][qb], dq[1][qb]) * SCALE
        dq_ref[rng] = unrotate(both, cos_ref[far], sin_ref[far])
    for kb in range((halo + rows) // BLK):
        rng = slice(kb * BLK, (kb + 1) * BLK)
        both = jnp.where(lane < 64, dk[0][kb], dk[1][kb]) * SCALE
        dk_ref[rng] = unrotate(both, cos_ref[rng], sin_ref[rng])
        dv_ref[rng] = jnp.where(lane < 64, dv[0][kb], dv[1][kb])


def attend_back(first, count, q_rot, kv, grad, seg_q, seg_k, cosine, sine, before=()):
    rows, model = q_rot.shape
    total = kv.shape[0]
    pairs = model // 128
    fixed = lambda shape: pl.BlockSpec(shape, lambda p: (0, 0))
    return pl.pallas_call(
        attend_back_kernel,
        grid=(count,),
        in_specs=[
            pl.BlockSpec((rows, 128), lambda p: (0, first + p)),
            pl.BlockSpec((total, 128), lambda p: (0, first + p)),
            pl.BlockSpec((total, 128), lambda p: (0, pairs + first + p)),
            pl.BlockSpec((rows, 128), lambda p: (0, first + p)),
            fixed((8, rows)), fixed((total, 128)),
            fixed((total, 128)), fixed((total, 128)),
        ] + [pl.BlockSpec(memory_space=pl.ANY)] * len(before),
        out_specs=[
            pl.BlockSpec((rows, 128), lambda p: (0, first + p)),
            pl.BlockSpec((total, 128), lambda p: (0, first + p)),
            pl.BlockSpec((total, 128), lambda p: (0, first + p)),
        ],
        out_shape=[
            jax.ShapeDtypeStruct((rows, model), F32),
            jax.ShapeDtypeStruct((total, model), F32),
            jax.ShapeDtypeStruct((total, model), F32),
        ],
        scratch_shapes=[pltpu.VMEM((total - rows + BLK, rows), F32)],
        input_output_aliases={8 + i: i for i in range(len(before))},
        cost_estimate=cost(7 * count),
        compiler_params=params(),
    )(q_rot, kv, kv, grad, seg_q, seg_k, cosine, sine, *before)


def mlp_kernel(count, begun, chip_ref, resid_ref, other_ref, cot_ref, cot_other_ref, gain_ref, bias_ref,
               scale_ref, *refs):
    up_refs, down_refs = refs[:count], refs[count:2 * count]
    refs = refs[2 * count:]
    so_far, refs = refs[:2 * begun], refs[2 * begun:]
    out_ref, gnorm_ref, grad_ref = refs[:3]
    (x_hi, x_lo, xt_hi, xt_lo, g_hi, g_lo, up_hi, up_lo, down_hi, down_lo) = refs[3:]
    step = pl.program_id(0)
    rows = resid_ref.shape[0]

    @pl.when(step == 0)
    def _():
        for at, source, cot in ((0, resid_ref, cot_ref), (rows, other_ref, cot_other_ref)):
            xhat, _ = norm_stats(source[...])
            normed = xhat * gain_ref[...] + bias_ref[...]
            x_hi[at:at + rows], x_lo[at:at + rows] = split(normed)
            xt_hi[:, at:at + rows], xt_lo[:, at:at + rows] = split(normed.T)
            g_hi[at:at + rows], g_lo[at:at + rows] = split(cot[...] * scale_ref[0, 0])
        if begun:
            out_ref[...] = so_far[0][...]
            gnorm_ref[...] = so_far[1][...]
        else:
            out_ref[...] = jnp.zeros_like(out_ref)
            gnorm_ref[...] = jnp.zeros_like(gnorm_ref)

    for at in range(count):
        spot = (chip_ref[0] ^ at) if count > 1 else 0
        up_rows = up_refs[at].shape[0]
        high, low = split(up_refs[at][...])
        here = pl.ds(pl.multiple_of(spot * up_rows, up_rows), up_rows)
        up_hi[here], up_lo[here] = high, low
        block = down_refs[at][...]
        block = block.reshape(-1, block.shape[-1])
        high, low = split(block)
        here = pl.ds(pl.multiple_of(spot * block.shape[0], block.shape[0]), block.shape[0])
        down_hi[here], down_lo[here] = high, low

    chips, _, tall, width = grad_ref.shape
    up_tall = up_hi.shape[0] // chips
    deep = down_hi.shape[0] // chips
    up = (up_hi[...], up_lo[...])
    down = (down_hi[...], down_lo[...])
    normed = (x_hi[...], x_lo[...])
    normed_t = (xt_hi[...], xt_lo[...])
    grad_block = (g_hi[...], g_lo[...])
    pre = three(dot_nn, normed, up)
    grad_act = three(dot_nt, grad_block, down)
    inner = 0.7978845608028654 * (pre + 0.044715 * pre * pre * pre)
    bent = jnp.tanh(inner)
    act = 0.5 * pre * (1.0 + bent)
    slope = 0.5 * (1.0 + bent) + 0.5 * pre * (1.0 - bent * bent) * (
        0.7978845608028654 * (1.0 + 3.0 * 0.044715 * pre * pre)
    )
    act2 = split(act)
    grad_pre = split(grad_act * slope)
    out_ref[...] += three(dot_nn, act2, down)
    gnorm_ref[...] += three(dot_nt, grad_pre, up)
    gup = three(dot_nn, normed_t, grad_pre)
    gdown = three(dot_tn, act2, grad_block)
    half = deep // 2
    for chip in range(chips):
        grad_ref[chip, 0, :up_tall] = gup[chip * up_tall:(chip + 1) * up_tall]
        part = gdown[chip * deep:(chip + 1) * deep]
        grad_ref[chip, 0, up_tall:up_tall + deep] = part[:, :width]
        grad_ref[chip, 0, up_tall + deep:] = jnp.concatenate(
            [part[:half, width:], part[half:, width:]], axis=1
        )


def mlp(first, steps, so_far, chip, chips, resid, other, cot, cot_other, gain, bias, scale, ups, downs):
    rows, model = resid.shape
    width = 512
    up_tall = model // chips
    deep = width // chips
    fixed = lambda shape: pl.BlockSpec(shape, lambda j, c: (0, 0))
    if len(ups) > 1:
        down_spec = pl.BlockSpec((deep, model), lambda j, c: (first + j, 0))
    else:
        downs = [downs[0].reshape(chips, -1, model)]
        down_spec = pl.BlockSpec((chips, deep, model), lambda j, c: (0, first + j, 0))
    tall = up_tall + deep + deep // 2
    grid_spec = pltpu.PrefetchScalarGridSpec(
        num_scalar_prefetch=1,
        grid=(steps,),
        in_specs=[fixed((rows, model))] * 4 + [fixed((1, model))] * 2
        + [pl.BlockSpec(memory_space=pltpu.SMEM)]
        + [pl.BlockSpec((up.shape[0], width), lambda j, c: (0, first + j)) for up in ups]
        + [down_spec] * len(downs)
        + [fixed((2 * rows, model))] * len(so_far),
        out_specs=[
            fixed((2 * rows, model)), fixed((2 * rows, model)),
            pl.BlockSpec((chips, 1, tall, width), lambda j, c: (0, j, 0, 0)),
        ],
        scratch_shapes=[
            pltpu.VMEM((2 * rows, model), BF16), pltpu.VMEM((2 * rows, model), BF16),
            pltpu.VMEM((model, 2 * rows), BF16), pltpu.VMEM((model, 2 * rows), BF16),
            pltpu.VMEM((2 * rows, model), BF16), pltpu.VMEM((2 * rows, model), BF16),
            pltpu.VMEM((model, width), BF16), pltpu.VMEM((model, width), BF16),
            pltpu.VMEM((width, model), BF16), pltpu.VMEM((width, model), BF16),
        ],
    )
    return pl.pallas_call(
        functools.partial(mlp_kernel, len(ups), len(so_far) // 2),
        grid_spec=grid_spec,
        out_shape=[
            jax.ShapeDtypeStruct((2 * rows, model), F32),
            jax.ShapeDtypeStruct((2 * rows, model), F32),
            jax.ShapeDtypeStruct((chips, steps, tall, width), F32),
        ],
        cost_estimate=cost(18 * steps),
        compiler_params=params(),
    )(chip, resid, other, cot, cot_other, gain, bias, scale, *ups, *downs, *so_far)


def unpack_grads(up, down, sibling_swap, core, chips):
    steps, up_tall, width = up.shape
    deep = up_tall * 2 // 3
    half = up_tall // 2
    mine = jnp.where(core == 0, up[:, :half], up[:, half:])
    other = sibling_swap(jnp.where(core == 0, up[:, half:], up[:, :half]))
    by_core = jnp.stack(
        [jnp.where(core == 0, mine, other), jnp.where(core == 0, other, mine)], axis=0
    )
    by_core = by_core.reshape(2, steps, half, chips, width // chips)
    grad_up = jnp.transpose(by_core, (2, 3, 0, 1, 4)).reshape(half, -1)
    quarter = width // 2
    tail = down[:, deep:]
    right = jnp.concatenate([tail[:, :, :quarter], tail[:, :, quarter:]], axis=1)
    grad_down = jnp.concatenate([down[:, :deep], right], axis=2).reshape(steps * deep, -1)
    return grad_up, grad_down


def resid_back_kernel(part_ref, given_ref, resid_ref, cot_ref, gain_ref, scale_ref, w_ref,
                      grad_ref, att_ref, sums_ref):
    grad = part_ref[...] + given_ref[...]
    xhat, rate = norm_stats(resid_ref[...])
    grad_resid = cot_ref[...] * scale_ref[0, 0] + norm_back(grad, gain_ref[...], xhat, rate)
    grad_ref[...] = grad_resid
    att_ref[...] = three(dot_nt, split(grad_resid), split(w_ref[...]))
    gain_sum = jnp.sum(grad * xhat, axis=0, keepdims=True)
    bias_sum = jnp.sum(grad, axis=0, keepdims=True)
    sums_ref[...] = jnp.concatenate(
        [gain_sum, bias_sum, jnp.zeros((6, gain_sum.shape[1]), F32)], axis=0
    )


def resid_back(part, given, resid, cot, gain, scale, w_full):
    rows, model = resid.shape
    fixed = lambda shape: pl.BlockSpec(shape, lambda j: (0, 0))
    return pl.pallas_call(
        resid_back_kernel,
        grid=(1,),
        in_specs=[fixed((rows, model))] * 4 + [fixed((1, model))]
        + [pl.BlockSpec(memory_space=pltpu.SMEM), fixed((model, model))],
        out_specs=[fixed((rows, model)), fixed((rows, model)), fixed((8, model))],
        out_shape=[
            jax.ShapeDtypeStruct((rows, model), F32),
            jax.ShapeDtypeStruct((rows, model), F32),
            jax.ShapeDtypeStruct((8, model), F32),
        ],
        cost_estimate=cost(6),
        compiler_params=params(),
    )(part, given, resid, cot, gain, scale, w_full)


def place_rows(core_ref, out_ref, got):
    chips = out_ref.shape[1]
    tall = out_ref.shape[2]
    for block in range(2 * chips):
        out_ref[(block & 1) ^ core_ref[0], block // 2] = got[block * tall:(block + 1) * tall]


def weights_qk_kernel(core_ref, hi_ref, lo_ref, dq_ref, dk_ref, out_ref, nt_hi, nt_lo):
    step = pl.program_id(0)
    part = pl.num_programs(0) // 2
    halo = hi_ref.shape[0] - dq_ref.shape[0]

    @pl.when(step == 0)
    def _():
        nt_hi[...] = hi_ref[...].T
        nt_lo[...] = lo_ref[...].T

    @pl.when(step < part)
    def _():
        left = (nt_hi[:, halo:], nt_lo[:, halo:])
        place_rows(core_ref, out_ref, three(dot_nn, left, split(dq_ref[...])))

    @pl.when(step >= part)
    def _():
        left = (nt_hi[...], nt_lo[...])
        place_rows(core_ref, out_ref, three(dot_nn, left, split(dk_ref[...])))


def weights_vo_kernel(core_ref, hi_ref, lo_ref, dv_ref, att_ref, res_ref, out_ref,
                      nt_hi, nt_lo, at_hi, at_lo):
    step = pl.program_id(0)
    part = pl.num_programs(0) // 2

    @pl.when(step == 0)
    def _():
        nt_hi[...] = hi_ref[...].T
        nt_lo[...] = lo_ref[...].T
        at_hi[...], at_lo[...] = split(att_ref[...].T)

    @pl.when(step < part)
    def _():
        left = (nt_hi[...], nt_lo[...])
        place_rows(core_ref, out_ref, three(dot_nn, left, split(dv_ref[...])))

    @pl.when(step >= part)
    def _():
        left = (at_hi[...], at_lo[...])
        place_rows(core_ref, out_ref, three(dot_nn, left, split(res_ref[...])))


def weight_call(kernel, micros, core, chips, fixed_args, pieces, scratch):
    model = fixed_args[0].shape[1]
    wide = 256
    part = model // wide
    tall = model // chips // 2
    fixed = lambda v: pl.BlockSpec(v.shape, lambda j, c: (0, 0))
    piece = lambda v, at: pl.BlockSpec(
        (v.shape[0], wide), lambda j, c: (0, jnp.clip(j - at * part, 0, part - 1))
    )
    specs, args = [], []
    for value, at in pieces:
        args.append(value)
        specs.append(fixed(value) if at is None else piece(value, at))
    return pl.pallas_call(
        kernel,
        grid_spec=pltpu.PrefetchScalarGridSpec(
            num_scalar_prefetch=1,
            grid=(2 * part,),
            in_specs=[fixed(v) for v in fixed_args] + specs,
            out_specs=pl.BlockSpec((2, chips, tall, wide), lambda j, c: (0, 0, 0, j)),
            scratch_shapes=[pltpu.VMEM((model, n), BF16) for n in scratch],
        ),
        out_shape=jax.ShapeDtypeStruct((2, chips, tall, 2 * model), F32),
        cost_estimate=cost(micros),
        compiler_params=params(),
    )(core, *fixed_args, *args)


def matmul(left, right):
    return jnp.dot(left, right, precision=HIGH)


def inner_rows(left, right):
    return lax.dot_general(left, right, (((0,), (0,)), ((), ())), precision=HIGH)


def outer_cols(left, right):
    return lax.dot_general(left, right, (((1,), (1,)), ((), ())), precision=HIGH)


def body(
    block_input,
    embedding,
    earlier_outs,
    dwa_weights,
    ln1_gain,
    ln1_bias,
    w_qkv,
    w_out,
    ln2_gain,
    ln2_bias,
    w_up,
    w_down,
    segments,
    cotangent,
):
    groups = lax.axis_size("seq")
    rows, model = block_input.shape
    length = rows * groups
    halo = 2 * rows
    place = lax.axis_index("seq")
    ahead = [(i, i + 1) for i in range(groups - 1)]
    behind = [(i + 1, i) for i in range(groups - 1)]
    gain1, bias1 = ln1_gain[None], ln1_bias[None]
    gain2, bias2 = ln2_gain[None], ln2_bias[None]

    devices = lax.axis_size("dp")
    chips = devices // 2
    spot = lax.axis_index("dp")
    core = spot % 2
    chip = (spot // 2).reshape(1).astype(jnp.int32)
    same_core = [[2 * i + c for i in range(chips)] for c in range(2)]
    exchange = lambda v, bit: lax.ppermute(v, "dp", [(i, i ^ bit) for i in range(devices)])
    swap = lambda v: exchange(v, 1)

    gather = lambda v: lax.all_gather(v, "dp", axis=0, tiled=True)
    qkv_full = gather(w_qkv)

    shard = w_down.shape[0]
    third = shard // 3
    by_core = w_up.reshape(w_up.shape[0], chips, 2, 3, third)
    by_core = jnp.transpose(by_core, (2, 0, 3, 1, 4)).reshape(2, w_up.shape[0], -1)
    mine = jnp.where(core == 0, by_core[0], by_core[1])
    given = swap(jnp.where(core == 0, by_core[1], by_core[0]))
    up_chip = jnp.concatenate(
        [jnp.where(core == 0, mine, given), jnp.where(core == 0, given, mine)], axis=0
    )
    if chips == 4:
        up_x, down_x = exchange(up_chip, 2), exchange(w_down, 2)
        up_y, down_y = exchange(up_chip, 4), exchange(w_down, 4)
        ups = [up_chip, up_x, up_y, exchange(up_y, 2)]
        downs = [w_down, down_x, down_y, exchange(down_x, 4)]
    else:
        ups, downs = (
            [lax.all_gather(v, "dp", axis=0, tiled=True, axis_index_groups=same_core)]
            for v in (up_chip, w_down)
        )

    seg_own = segments + 1
    near = lax.ppermute(block_input, "seq", ahead)
    seg_near = lax.ppermute(seg_own, "seq", ahead)
    far = lax.ppermute(near, "seq", ahead)
    seg_far = lax.ppermute(seg_near, "seq", ahead)
    seg_all = jnp.concatenate([seg_far, seg_near, seg_own], axis=1)
    seg_k_row = jnp.broadcast_to(seg_all, (8, halo + rows))
    seg_k_col = jnp.broadcast_to(seg_all.reshape(-1, 1), (halo + rows, 128))
    seg_q_row = seg_k_row[:, halo:]
    seg_q_col = seg_k_col[halo:]

    cos_all, sin_all = rotary_tables(length, halo)
    cosine = lax.dynamic_slice_in_dim(jnp.asarray(cos_all), place * rows, halo + rows, 0)
    sine = lax.dynamic_slice_in_dim(jnp.asarray(sin_all), place * rows, halo + rows, 0)

    earlier = (embedding, earlier_outs[0], earlier_outs[1], earlier_outs[2])
    base = sum(dwa_weights[i] * value for i, value in enumerate(earlier))
    dots = jnp.stack([jnp.sum(cotangent * value) for value in earlier])
    far, base, dots = lax.optimization_barrier((far, base, dots))

    q_rot, kv, normed_hi, normed_lo = project(
        far, near, block_input, gain1, bias1, qkv_full, cosine, sine
    )
    attended = attend(q_rot, kv, seg_q_col, seg_k_row)

    out_full = gather(w_out)
    resid = block_input + matmul(attended, out_full)
    resid_other = swap(resid)
    cot_other = swap(cotangent)
    scale = dwa_weights[4].reshape(1, 1)
    call = functools.partial(
        mlp, chip=chip, chips=chips, resid=resid, other=resid_other, cot=cotangent,
        cot_other=cot_other, gain=gain2, bias=bias2, scale=scale, ups=ups, downs=downs,
    )
    scatter = lambda v: lax.psum_scatter(v, "dp", scatter_dimension=0, tiled=True)
    scatter_chips = lambda v: lax.psum_scatter(
        v, "dp", scatter_dimension=0, tiled=True, axis_index_groups=same_core
    )
    so_far, shards = (), []
    for third_at in range(3):
        out_part, gnorm_part, grads = call(third_at, 1, so_far)
        so_far = (out_part, gnorm_part)
        shards.append(scatter_chips(grads)[0])
    given = swap(gnorm_part[rows:])

    shift = lambda v, bit: lax.ppermute(v, "seq", [(i, i ^ bit) for i in range(groups)])
    even = place % 2 == 0

    def line_start(shard):
        tall = shard.shape[1] // 2
        halves = (shard[:, :tall], shard[:, tall:])
        kept = jnp.where(even, halves[0], halves[1])
        return kept + shift(jnp.where(even, halves[1], halves[0]), 1)

    def line_middle(kept):
        bit = 2
        while bit < groups:
            kept = kept + shift(kept, bit)
            bit *= 2
        return kept

    def line_end(kept):
        other = shift(kept, 1)
        return jnp.where(even, kept, other), jnp.where(even, other, kept)

    together = lax.optimization_barrier
    shards[0], given = together((shards[0], given))
    line_a = line_start(shards[0])
    grad_resid, grad_attended, sums_two = resid_back(
        gnorm_part, given, resid, cotangent, gain2, scale, out_full
    )

    back_args = (q_rot, kv, grad_attended, seg_q_row, seg_k_col, cosine, sine)
    pairs = model // 128
    line_a, back_args = together((line_a, back_args))
    line_a = line_middle(line_a)
    first_half = attend_back(0, pairs // 2, *back_args)
    line_a, shards[1], back_args, first_half = together(
        (line_a, shards[1], back_args, first_half)
    )
    line_b = line_start(shards[1])
    ends_a = line_end(line_a)
    dq, dk, dv = attend_back(pairs // 2, pairs - pairs // 2, *back_args, before=first_half)
    line_b, ends_a, dq, dk, dv = together((line_b, ends_a, dq, dk, dv))
    line_b = line_middle(line_b)
    core_at = core.reshape(1).astype(jnp.int32)
    normed_parts = (normed_hi, normed_lo)
    grads_qk = weight_call(
        weights_qk_kernel, 9, core_at, chips, normed_parts, [(dq, 0), (dk, 1)], [halo + rows] * 2
    )
    given_qk = swap(grads_qk[1])
    line_b, dv, grad_resid = together((line_b, dv, grad_resid))
    ends_b = line_end(line_b)
    grads_vo = weight_call(
        weights_vo_kernel, 9, core_at, chips, normed_parts,
        [(dv, 0), (attended, None), (grad_resid, 1)], [halo + rows] * 2 + [rows] * 2,
    )
    grads_c = jnp.concatenate([grads_qk[0] + given_qk, grads_vo[0] + swap(grads_vo[1])], axis=2)
    grads_c, shards[2], out_part = together((grads_c, shards[2], out_part))
    shard_c = scatter_chips(grads_c)[0]
    line_c = line_start(shards[2])
    out_sib = swap(out_part[rows:])
    line_c, ends_b, dk, dv = together((line_c, ends_b, dk, dv))
    line_c = line_middle(line_c)
    dkv = jnp.concatenate([dk, dv], axis=1)

    block_out = resid + out_part[:rows] + out_sib
    output = base + dwa_weights[4] * block_out
    dwa_local = jnp.concatenate([dots, jnp.sum(cotangent * block_out)[None]])

    wq, wkv = qkv_full[:, :model], qkv_full[:, model:]
    partial = outer_cols(dkv, wkv)
    own_part = partial[halo:] + outer_cols(dq, wq)
    (sent,) = together((partial,))
    back_near = sent[rows:halo] + lax.ppermute(sent[:rows], "seq", behind)

    xhat1, rate1 = norm_stats(block_input)
    terms = (
        (norm_stats(far)[0], partial[:rows]),
        (norm_stats(near)[0], partial[rows:halo]),
        (xhat1, own_part),
    )
    grad_gain_one = sum(jnp.sum(xhat * part, axis=0) for xhat, part in terms)
    grad_bias_one = sum(jnp.sum(part, axis=0) for _, part in terms)

    small = jnp.concatenate(
        [
            grad_gain_one[None], grad_bias_one[None], sums_two[:2],
            jnp.pad(dwa_local, (0, model - 5))[None], jnp.zeros((3, model), F32),
        ],
        axis=0,
    )
    bit = 1
    while bit < devices:
        small = small + exchange(small, bit)
        bit *= 2
    tall = shard_c.shape[0]
    payload = jnp.concatenate([shard_c, small.reshape(-1, shard_c.shape[1])], axis=0)
    ends_c = line_end(line_c)
    payload, back_near, ends_c = together((payload, back_near, ends_c))
    summed = lax.psum(payload, "seq")
    grad_qkv, grad_wout = summed[:tall, :3 * model], summed[:tall, 3 * model:]
    small = summed[tall:].reshape(-1, model)
    gain_one, bias_one, gain_two, bias_two = small[0], small[1], small[2], small[3]
    grad_dwa = small[4, :5]
    grad_normed_one = own_part + lax.ppermute(back_near, "seq", behind)
    grad_input = grad_resid + norm_back(grad_normed_one, gain1, xhat1, rate1)
    grad_up, grad_down = unpack_grads(
        *(
            jnp.concatenate(parts, axis=0)
            for parts in zip(ends_a, ends_b, ends_c)
        ),
        swap, core, chips,
    )
    return (
        output,
        grad_input,
        grad_dwa,
        gain_one,
        bias_one,
        grad_qkv,
        grad_wout,
        gain_two,
        bias_two,
        grad_up,
        grad_down,
    )


def solution(mesh):
    in_specs = (
        P(("dp", "seq"), None),
        P(("dp", "seq"), None),
        P(None, ("dp", "seq"), None),
        P(),
        P(),
        P(),
        P("dp", None),
        P("dp", None),
        P(),
        P(),
        P("dp", None),
        P("dp", None),
        P("dp", "seq"),
        P(("dp", "seq"), None),
    )
    out_specs = (
        P(("dp", "seq"), None),
        P(("dp", "seq"), None),
        P(),
        P(),
        P(),
        P("dp", None),
        P("dp", None),
        P(),
        P(),
        P("dp", None),
        P("dp", None),
    )
    return jax.shard_map(body, mesh=mesh, in_specs=in_specs, out_specs=out_specs, check_vma=False)
```

```python
import functools
import math

import jax
import jax.numpy as jnp
import numpy as np
from jax import lax
from jax.experimental import pallas as pl
from jax.experimental.pallas import tpu as pltpu
from jax.sharding import PartitionSpec as P

HD = 64
DOC_MOST = 768
LOG2E = math.log2(math.e)
SCALE = 1.0 / math.sqrt(HD)
NEG = -1e30
F32 = jnp.float32
BF16 = jnp.bfloat16
HIGH = lax.Precision.HIGH
VMEM_LIMIT = 56 * 1024 * 1024
BLK = 128


def cost(micros):
    return pl.CostEstimate(
        flops=int(micros * 1.1e9), bytes_accessed=1 << 20, transcendentals=0
    )


def params():
    return pltpu.CompilerParams(
        dimension_semantics=("arbitrary",), vmem_limit_bytes=VMEM_LIMIT
    )


def split(values):
    high = values.astype(BF16)
    return high, (values - high.astype(F32)).astype(BF16)


def dot_nn(left, right):
    return lax.dot_general(left, right, (((1,), (0,)), ((), ())), preferred_element_type=F32)


def dot_nt(left, right):
    return lax.dot_general(left, right, (((1,), (1,)), ((), ())), preferred_element_type=F32)


def dot_tn(left, right):
    return lax.dot_general(left, right, (((0,), (0,)), ((), ())), preferred_element_type=F32)


def three(dot, left, right):
    return (
        dot(left[0], right[0]) + dot(left[0], right[1]) + dot(left[1], right[0])
    )


def norm_stats(values):
    row_mean = jnp.mean(values, axis=-1, keepdims=True)
    centred = values - row_mean
    row_var = jnp.mean(centred * centred, axis=-1, keepdims=True)
    rate = lax.rsqrt(row_var + 1e-05)
    return centred * rate, rate


def norm_back(grad, gain, xhat, rate):
    scaled = grad * gain
    return rate * (
        scaled
        - jnp.mean(scaled, axis=-1, keepdims=True)
        - xhat * jnp.mean(scaled * xhat, axis=-1, keepdims=True)
    )


def turned(values):
    lane = lax.broadcasted_iota(jnp.int32, values.shape, 1)
    return jnp.where(
        (lane & 63) < 32, pltpu.roll(values, 96, 1), pltpu.roll(values, 32, 1)
    )


def rotate(values, cosine, sine):
    return values * cosine + turned(values) * sine


def unrotate(values, cosine, sine):
    return values * cosine - turned(values) * sine


def rotary_tables(length, halo):
    half = HD // 2
    inv_freq = (10000.0 ** (-(np.arange(half, dtype=np.float32) * 2.0 / HD))).astype(np.float32)
    place = np.arange(-halo, length, dtype=np.float32)
    angles = place[:, None] * inv_freq[None, :]
    cosine = np.cos(angles.astype(np.float64)).astype(np.float32)
    sine = np.sin(angles.astype(np.float64)).astype(np.float32)
    return (
        np.concatenate([cosine] * 4, axis=1),
        np.concatenate([-sine, sine, -sine, sine], axis=1),
    )


def qkv_kernel(far_ref, near_ref, own_ref, gain_ref, bias_ref, w_ref, cos_ref, sin_ref,
               q_ref, kv_ref, hi_ref, lo_ref):
    step = pl.program_id(0)
    rows = own_ref.shape[0]
    third = pl.num_programs(0) // 3
    halo = hi_ref.shape[0] - rows

    @pl.when(step == 0)
    def _():
        for at, ref in enumerate((far_ref, near_ref, own_ref)):
            xhat, _ = norm_stats(ref[...])
            high, low = split(xhat * gain_ref[...] + bias_ref[...])
            hi_ref[at * rows:(at + 1) * rows] = high
            lo_ref[at * rows:(at + 1) * rows] = low

    weights = split(w_ref[...])

    @pl.when(step < third)
    def _():
        got = three(dot_nn, (hi_ref[halo:], lo_ref[halo:]), weights)
        for at in range(0, got.shape[1], 128):
            q_ref[:, at:at + 128] = rotate(got[:, at:at + 128], cos_ref[halo:], sin_ref[halo:])

    @pl.when((step >= third) & (step < 2 * third))
    def _():
        got = three(dot_nn, (hi_ref[...], lo_ref[...]), weights)
        for at in range(0, got.shape[1], 128):
            kv_ref[:, at:at + 128] = rotate(got[:, at:at + 128], cos_ref[...], sin_ref[...])

    @pl.when(step >= 2 * third)
    def _():
        kv_ref[...] = three(dot_nn, (hi_ref[...], lo_ref[...]), weights)


def project(far, near, own, gain, bias, w_full, cosine, sine):
    rows, model = own.shape
    total = 3 * rows
    wide = 256
    third = model // wide
    whole = lambda shape: pl.BlockSpec(shape, lambda j: (0, 0))
    return pl.pallas_call(
        qkv_kernel,
        grid=(3 * third,),
        in_specs=[
            whole((rows, model)), whole((rows, model)), whole((rows, model)),
            whole((1, model)), whole((1, model)),
            pl.BlockSpec((model, wide), lambda j: (0, j)),
            whole((total, 128)), whole((total, 128)),
        ],
        out_specs=[
            pl.BlockSpec((rows, wide), lambda j: (0, jnp.minimum(j, third - 1))),
            pl.BlockSpec((total, wide), lambda j: (0, jnp.maximum(j - third, 0))),
            whole((total, model)), whole((total, model)),
        ],
        out_shape=[
            jax.ShapeDtypeStruct((rows, model), F32),
            jax.ShapeDtypeStruct((total, 2 * model), F32),
            jax.ShapeDtypeStruct((total, model), BF16),
            jax.ShapeDtypeStruct((total, model), BF16),
        ],
        cost_estimate=cost(20),
        compiler_params=params(),
    )(far, near, own, gain, bias, w_full, cosine, sine)


def own_pair(values, head):
    lane = lax.broadcasted_iota(jnp.int32, values.shape, 1)
    other = pltpu.roll(values, 64, 1)
    return jnp.where((lane < 64) == (head == 0), values, other)


def outer_form(values, head):
    high, low = split(own_pair(values, head))
    return jnp.concatenate([high, low], axis=1)


def mixed(values, head):
    pair = own_pair(values, head)
    lane = lax.broadcasted_iota(jnp.int32, pair.shape, 1)
    high = pair.astype(BF16).astype(F32)
    return jnp.where(lane < 64, high, pair - high).astype(BF16)


def inner_form(values, head):
    half = mixed(values, head)
    return jnp.concatenate([half, half], axis=1)


def fold(values):
    return values + pltpu.roll(values, 64, 1)


def attend_kernel(q_ref, k_ref, v_ref, segq_ref, segk_ref, out_ref, bias_ref):
    rows = q_ref.shape[0]
    halo = k_ref.shape[0] - rows
    span = halo + BLK

    @pl.when(pl.program_id(0) == 0)
    def _():
        for at in range(0, rows, BLK):
            row = lax.broadcasted_iota(jnp.int32, (BLK, span), 0)
            col = lax.broadcasted_iota(jnp.int32, (BLK, span), 1)
            same = segq_ref[at:at + BLK, :1] == segk_ref[:1, at:at + span]
            bias_ref[at:at + BLK] = jnp.where(same & (col - halo <= row), 0.0, NEG)

    lane = lax.broadcasted_iota(jnp.int32, (BLK, 128), 1)
    scaled = q_ref[...] * (SCALE * LOG2E)
    results = []
    for head in range(2):
        left = inner_form(scaled, head)
        right = outer_form(k_ref[...], head)
        vals = mixed(v_ref[...], head)
        outs = []
        for at in range(0, rows, BLK):
            scores = dot_nt(left[at:at + BLK], right[at:at + span]) + bias_ref[at:at + BLK]
            top = jnp.max(scores, axis=1, keepdims=True)
            expo = jnp.exp2(scores - top)
            total = jnp.sum(expo, axis=1, keepdims=True)
            high, low = split(expo)
            got = dot_nn(high, vals[at:at + span]) + dot_nn(low, vals[at:at + span])
            outs.append(fold(got) / total)
        results.append(outs)
    for at in range(0, rows, BLK):
        out_ref[at:at + BLK] = jnp.where(
            lane < 64, results[0][at // BLK], results[1][at // BLK]
        )


def attend(q_rot, kv, seg_q, seg_k):
    rows, model = q_rot.shape
    total = kv.shape[0]
    pairs = model // 128
    return pl.pallas_call(
        attend_kernel,
        grid=(pairs,),
        in_specs=[
            pl.BlockSpec((rows, 128), lambda p: (0, p)),
            pl.BlockSpec((total, 128), lambda p: (0, p)),
            pl.BlockSpec((total, 128), lambda p: (0, pairs + p)),
            pl.BlockSpec((rows, 128), lambda p: (0, 0)),
            pl.BlockSpec((8, total), lambda p: (0, 0)),
        ],
        out_specs=pl.BlockSpec((rows, 128), lambda p: (0, p)),
        out_shape=jax.ShapeDtypeStruct((rows, model), F32),
        scratch_shapes=[pltpu.VMEM((rows, total - rows + BLK), F32)],
        cost_estimate=cost(24),
        compiler_params=params(),
    )(q_rot, kv, kv, seg_q, seg_k)


def attend_back_kernel(q_ref, k_ref, v_ref, g_ref, segq_ref, segk_ref, cos_ref, sin_ref, *refs):
    dq_ref, dk_ref, dv_ref, bias_ref = refs[-4:]
    rows = q_ref.shape[0]
    halo = k_ref.shape[0] - rows
    span = halo + BLK

    @pl.when(pl.program_id(0) == 0)
    def _():
        for at in range(0, rows, BLK):
            key = lax.broadcasted_iota(jnp.int32, (span, BLK), 0)
            query = lax.broadcasted_iota(jnp.int32, (span, BLK), 1)
            same = segk_ref[at:at + span, :1] == segq_ref[:1, at:at + BLK]
            bias_ref[:, at:at + BLK] = jnp.where(same & (key - halo <= query), 0.0, NEG)

    scaled = q_ref[...] * (SCALE * LOG2E)
    dq, dk, dv = [], [], []
    for head in range(2):
        q_in = inner_form(scaled, head)
        g_in = inner_form(g_ref[...], head)
        k_out = outer_form(k_ref[...], head)
        v_out = outer_form(v_ref[...], head)
        q_mix = mixed(q_ref[...], head)
        g_mix = mixed(g_ref[...], head)
        k_mix = mixed(k_ref[...], head)
        dq_head = []
        dk_head = jnp.zeros((halo + rows, 128), F32)
        dv_head = jnp.zeros((halo + rows, 128), F32)
        dk_parts, dv_parts = [], []
        for at in range(0, rows, BLK):
            scores = dot_nt(k_out[at:at + span], q_in[at:at + BLK]) + bias_ref[:, at:at + BLK]
            top = jnp.max(scores, axis=0, keepdims=True)
            expo = jnp.exp2(scores - top)
            inverse = 1.0 / jnp.sum(expo, axis=0, keepdims=True)
            grad_probs = dot_nt(v_out[at:at + span], g_in[at:at + BLK])
            probs = expo * inverse
            delta = jnp.sum(probs * grad_probs, axis=0, keepdims=True)
            grad_scores = probs * (grad_probs - delta)
            probs_cat = jnp.concatenate(split(probs), axis=1)
            scores_cat = jnp.concatenate(split(grad_scores), axis=1)
            g_two = jnp.concatenate([g_mix[at:at + BLK]] * 2, axis=0)
            q_two = jnp.concatenate([q_mix[at:at + BLK]] * 2, axis=0)
            dv_parts.append(dot_nn(probs_cat, g_two))
            dk_parts.append(dot_nn(scores_cat, q_two))
            got = dot_tn(scores_cat, k_mix[at:at + span])
            dq_head.append(fold(got[:BLK] + got[BLK:]))
        for parts, full in ((dk_parts, dk), (dv_parts, dv)):
            pieces = []
            for kb in range((halo + rows) // BLK):
                terms = [
                    parts[qb][(kb - qb) * BLK:(kb - qb + 1) * BLK]
                    for qb in range(rows // BLK)
                    if 0 <= kb - qb < span // BLK
                ]
                pieces.append(fold(functools.reduce(lambda a, b: a + b, terms)))
            full.append(pieces)
        dq.append(dq_head)
    lane = lax.broadcasted_iota(jnp.int32, (BLK, 128), 1)
    for qb in range(rows // BLK):
        rng = slice(qb * BLK, (qb + 1) * BLK)
        far = slice(halo + qb * BLK, halo + (qb + 1) * BLK)
        both = jnp.where(lane < 64, dq[0][qb], dq[1][qb]) * SCALE
        dq_ref[rng] = unrotate(both, cos_ref[far], sin_ref[far])
    for kb in range((halo + rows) // BLK):
        rng = slice(kb * BLK, (kb + 1) * BLK)
        both = jnp.where(lane < 64, dk[0][kb], dk[1][kb]) * SCALE
        dk_ref[rng] = unrotate(both, cos_ref[rng], sin_ref[rng])
        dv_ref[rng] = jnp.where(lane < 64, dv[0][kb], dv[1][kb])


def attend_back(first, count, q_rot, kv, grad, seg_q, seg_k, cosine, sine, before=()):
    rows, model = q_rot.shape
    total = kv.shape[0]
    pairs = model // 128
    fixed = lambda shape: pl.BlockSpec(shape, lambda p: (0, 0))
    return pl.pallas_call(
        attend_back_kernel,
        grid=(count,),
        in_specs=[
            pl.BlockSpec((rows, 128), lambda p: (0, first + p)),
            pl.BlockSpec((total, 128), lambda p: (0, first + p)),
            pl.BlockSpec((total, 128), lambda p: (0, pairs + first + p)),
            pl.BlockSpec((rows, 128), lambda p: (0, first + p)),
            fixed((8, rows)), fixed((total, 128)),
            fixed((total, 128)), fixed((total, 128)),
        ] + [pl.BlockSpec(memory_space=pl.ANY)] * len(before),
        out_specs=[
            pl.BlockSpec((rows, 128), lambda p: (0, first + p)),
            pl.BlockSpec((total, 128), lambda p: (0, first + p)),
            pl.BlockSpec((total, 128), lambda p: (0, first + p)),
        ],
        out_shape=[
            jax.ShapeDtypeStruct((rows, model), F32),
            jax.ShapeDtypeStruct((total, model), F32),
            jax.ShapeDtypeStruct((total, model), F32),
        ],
        scratch_shapes=[pltpu.VMEM((total - rows + BLK, rows), F32)],
        input_output_aliases={8 + i: i for i in range(len(before))},
        cost_estimate=cost(7 * count),
        compiler_params=params(),
    )(q_rot, kv, kv, grad, seg_q, seg_k, cosine, sine, *before)


def mlp_kernel(count, begun, chip_ref, resid_ref, other_ref, cot_ref, cot_other_ref, gain_ref, bias_ref,
               scale_ref, *refs):
    up_refs, down_refs = refs[:count], refs[count:2 * count]
    refs = refs[2 * count:]
    so_far, refs = refs[:2 * begun], refs[2 * begun:]
    out_ref, gnorm_ref, grad_ref = refs[:3]
    (x_hi, x_lo, xt_hi, xt_lo, g_hi, g_lo, up_hi, up_lo, down_hi, down_lo) = refs[3:]
    step = pl.program_id(0)
    rows = resid_ref.shape[0]

    @pl.when(step == 0)
    def _():
        for at, source, cot in ((0, resid_ref, cot_ref), (rows, other_ref, cot_other_ref)):
            xhat, _ = norm_stats(source[...])
            normed = xhat * gain_ref[...] + bias_ref[...]
            x_hi[at:at + rows], x_lo[at:at + rows] = split(normed)
            xt_hi[:, at:at + rows], xt_lo[:, at:at + rows] = split(normed.T)
            g_hi[at:at + rows], g_lo[at:at + rows] = split(cot[...] * scale_ref[0, 0])
        if begun:
            out_ref[...] = so_far[0][...]
            gnorm_ref[...] = so_far[1][...]
        else:
            out_ref[...] = jnp.zeros_like(out_ref)
            gnorm_ref[...] = jnp.zeros_like(gnorm_ref)

    for at in range(count):
        spot = (chip_ref[0] ^ at) if count > 1 else 0
        up_rows = up_refs[at].shape[0]
        high, low = split(up_refs[at][...])
        here = pl.ds(pl.multiple_of(spot * up_rows, up_rows), up_rows)
        up_hi[here], up_lo[here] = high, low
        block = down_refs[at][...]
        block = block.reshape(-1, block.shape[-1])
        high, low = split(block)
        here = pl.ds(pl.multiple_of(spot * block.shape[0], block.shape[0]), block.shape[0])
        down_hi[here], down_lo[here] = high, low

    chips, _, tall, width = grad_ref.shape
    up_tall = up_hi.shape[0] // chips
    deep = down_hi.shape[0] // chips
    up = (up_hi[...], up_lo[...])
    down = (down_hi[...], down_lo[...])
    normed = (x_hi[...], x_lo[...])
    normed_t = (xt_hi[...], xt_lo[...])
    grad_block = (g_hi[...], g_lo[...])
    pre = three(dot_nn, normed, up)
    grad_act = three(dot_nt, grad_block, down)
    inner = 0.7978845608028654 * (pre + 0.044715 * pre * pre * pre)
    bent = jnp.tanh(inner)
    act = 0.5 * pre * (1.0 + bent)
    slope = 0.5 * (1.0 + bent) + 0.5 * pre * (1.0 - bent * bent) * (
        0.7978845608028654 * (1.0 + 3.0 * 0.044715 * pre * pre)
    )
    act2 = split(act)
    grad_pre = split(grad_act * slope)
    out_ref[...] += three(dot_nn, act2, down)
    gnorm_ref[...] += three(dot_nt, grad_pre, up)
    gup = three(dot_nn, normed_t, grad_pre)
    gdown = three(dot_tn, act2, grad_block)
    half = deep // 2
    for chip in range(chips):
        grad_ref[chip, 0, :up_tall] = gup[chip * up_tall:(chip + 1) * up_tall]
        part = gdown[chip * deep:(chip + 1) * deep]
        grad_ref[chip, 0, up_tall:up_tall + deep] = part[:, :width]
        grad_ref[chip, 0, up_tall + deep:] = jnp.concatenate(
            [part[:half, width:], part[half:, width:]], axis=1
        )


def mlp(first, steps, so_far, chip, chips, resid, other, cot, cot_other, gain, bias, scale, ups, downs):
    rows, model = resid.shape
    width = 512
    up_tall = model // chips
    deep = width // chips
    fixed = lambda shape: pl.BlockSpec(shape, lambda j, c: (0, 0))
    if len(ups) > 1:
        down_spec = pl.BlockSpec((deep, model), lambda j, c: (first + j, 0))
    else:
        downs = [downs[0].reshape(chips, -1, model)]
        down_spec = pl.BlockSpec((chips, deep, model), lambda j, c: (0, first + j, 0))
    tall = up_tall + deep + deep // 2
    grid_spec = pltpu.PrefetchScalarGridSpec(
        num_scalar_prefetch=1,
        grid=(steps,),
        in_specs=[fixed((rows, model))] * 4 + [fixed((1, model))] * 2
        + [pl.BlockSpec(memory_space=pltpu.SMEM)]
        + [pl.BlockSpec((up.shape[0], width), lambda j, c: (0, first + j)) for up in ups]
        + [down_spec] * len(downs)
        + [fixed((2 * rows, model))] * len(so_far),
        out_specs=[
            fixed((2 * rows, model)), fixed((2 * rows, model)),
            pl.BlockSpec((chips, 1, tall, width), lambda j, c: (0, j, 0, 0)),
        ],
        scratch_shapes=[
            pltpu.VMEM((2 * rows, model), BF16), pltpu.VMEM((2 * rows, model), BF16),
            pltpu.VMEM((model, 2 * rows), BF16), pltpu.VMEM((model, 2 * rows), BF16),
            pltpu.VMEM((2 * rows, model), BF16), pltpu.VMEM((2 * rows, model), BF16),
            pltpu.VMEM((model, width), BF16), pltpu.VMEM((model, width), BF16),
            pltpu.VMEM((width, model), BF16), pltpu.VMEM((width, model), BF16),
        ],
    )
    return pl.pallas_call(
        functools.partial(mlp_kernel, len(ups), len(so_far) // 2),
        grid_spec=grid_spec,
        out_shape=[
            jax.ShapeDtypeStruct((2 * rows, model), F32),
            jax.ShapeDtypeStruct((2 * rows, model), F32),
            jax.ShapeDtypeStruct((chips, steps, tall, width), F32),
        ],
        cost_estimate=cost(18 * steps),
        compiler_params=params(),
    )(chip, resid, other, cot, cot_other, gain, bias, scale, *ups, *downs, *so_far)


def unpack_grads(up, down, sibling_swap, core, chips):
    steps, up_tall, width = up.shape
    deep = up_tall * 2 // 3
    half = up_tall // 2
    mine = jnp.where(core == 0, up[:, :half], up[:, half:])
    other = sibling_swap(jnp.where(core == 0, up[:, half:], up[:, :half]))
    by_core = jnp.stack(
        [jnp.where(core == 0, mine, other), jnp.where(core == 0, other, mine)], axis=0
    )
    by_core = by_core.reshape(2, steps, half, chips, width // chips)
    grad_up = jnp.transpose(by_core, (2, 3, 0, 1, 4)).reshape(half, -1)
    quarter = width // 2
    tail = down[:, deep:]
    right = jnp.concatenate([tail[:, :, :quarter], tail[:, :, quarter:]], axis=1)
    grad_down = jnp.concatenate([down[:, :deep], right], axis=2).reshape(steps * deep, -1)
    return grad_up, grad_down


def resid_back_kernel(part_ref, given_ref, resid_ref, cot_ref, gain_ref, scale_ref, w_ref,
                      grad_ref, att_ref, sums_ref):
    grad = part_ref[...] + given_ref[...]
    xhat, rate = norm_stats(resid_ref[...])
    grad_resid = cot_ref[...] * scale_ref[0, 0] + norm_back(grad, gain_ref[...], xhat, rate)
    grad_ref[...] = grad_resid
    att_ref[...] = three(dot_nt, split(grad_resid), split(w_ref[...]))
    gain_sum = jnp.sum(grad * xhat, axis=0, keepdims=True)
    bias_sum = jnp.sum(grad, axis=0, keepdims=True)
    sums_ref[...] = jnp.concatenate(
        [gain_sum, bias_sum, jnp.zeros((6, gain_sum.shape[1]), F32)], axis=0
    )


def resid_back(part, given, resid, cot, gain, scale, w_full):
    rows, model = resid.shape
    fixed = lambda shape: pl.BlockSpec(shape, lambda j: (0, 0))
    return pl.pallas_call(
        resid_back_kernel,
        grid=(1,),
        in_specs=[fixed((rows, model))] * 4 + [fixed((1, model))]
        + [pl.BlockSpec(memory_space=pltpu.SMEM), fixed((model, model))],
        out_specs=[fixed((rows, model)), fixed((rows, model)), fixed((8, model))],
        out_shape=[
            jax.ShapeDtypeStruct((rows, model), F32),
            jax.ShapeDtypeStruct((rows, model), F32),
            jax.ShapeDtypeStruct((8, model), F32),
        ],
        cost_estimate=cost(6),
        compiler_params=params(),
    )(part, given, resid, cot, gain, scale, w_full)


def place_rows(core_ref, out_ref, got):
    chips = out_ref.shape[1]
    tall = out_ref.shape[2]
    for block in range(2 * chips):
        out_ref[(block & 1) ^ core_ref[0], block // 2] = got[block * tall:(block + 1) * tall]


def weights_qk_kernel(core_ref, hi_ref, lo_ref, dq_ref, dk_ref, out_ref, nt_hi, nt_lo):
    step = pl.program_id(0)
    part = pl.num_programs(0) // 2
    halo = hi_ref.shape[0] - dq_ref.shape[0]

    @pl.when(step == 0)
    def _():
        nt_hi[...] = hi_ref[...].T
        nt_lo[...] = lo_ref[...].T

    @pl.when(step < part)
    def _():
        left = (nt_hi[:, halo:], nt_lo[:, halo:])
        place_rows(core_ref, out_ref, three(dot_nn, left, split(dq_ref[...])))

    @pl.when(step >= part)
    def _():
        left = (nt_hi[...], nt_lo[...])
        place_rows(core_ref, out_ref, three(dot_nn, left, split(dk_ref[...])))


def weights_vo_kernel(core_ref, hi_ref, lo_ref, dv_ref, att_ref, res_ref, out_ref,
                      nt_hi, nt_lo, at_hi, at_lo):
    step = pl.program_id(0)
    part = pl.num_programs(0) // 2

    @pl.when(step == 0)
    def _():
        nt_hi[...] = hi_ref[...].T
        nt_lo[...] = lo_ref[...].T
        at_hi[...], at_lo[...] = split(att_ref[...].T)

    @pl.when(step < part)
    def _():
        left = (nt_hi[...], nt_lo[...])
        place_rows(core_ref, out_ref, three(dot_nn, left, split(dv_ref[...])))

    @pl.when(step >= part)
    def _():
        left = (at_hi[...], at_lo[...])
        place_rows(core_ref, out_ref, three(dot_nn, left, split(res_ref[...])))


def weight_call(kernel, micros, core, chips, fixed_args, pieces, scratch):
    model = fixed_args[0].shape[1]
    wide = 256
    part = model // wide
    tall = model // chips // 2
    fixed = lambda v: pl.BlockSpec(v.shape, lambda j, c: (0, 0))
    piece = lambda v, at: pl.BlockSpec(
        (v.shape[0], wide), lambda j, c: (0, jnp.clip(j - at * part, 0, part - 1))
    )
    specs, args = [], []
    for value, at in pieces:
        args.append(value)
        specs.append(fixed(value) if at is None else piece(value, at))
    return pl.pallas_call(
        kernel,
        grid_spec=pltpu.PrefetchScalarGridSpec(
            num_scalar_prefetch=1,
            grid=(2 * part,),
            in_specs=[fixed(v) for v in fixed_args] + specs,
            out_specs=pl.BlockSpec((2, chips, tall, wide), lambda j, c: (0, 0, 0, j)),
            scratch_shapes=[pltpu.VMEM((model, n), BF16) for n in scratch],
        ),
        out_shape=jax.ShapeDtypeStruct((2, chips, tall, 2 * model), F32),
        cost_estimate=cost(micros),
        compiler_params=params(),
    )(core, *fixed_args, *args)


def matmul(left, right):
    return jnp.dot(left, right, precision=HIGH)


def inner_rows(left, right):
    return lax.dot_general(left, right, (((0,), (0,)), ((), ())), precision=HIGH)


def outer_cols(left, right):
    return lax.dot_general(left, right, (((1,), (1,)), ((), ())), precision=HIGH)


def body(
    block_input,
    embedding,
    earlier_outs,
    dwa_weights,
    ln1_gain,
    ln1_bias,
    w_qkv,
    w_out,
    ln2_gain,
    ln2_bias,
    w_up,
    w_down,
    segments,
    cotangent,
):
    groups = lax.axis_size("seq")
    rows, model = block_input.shape
    length = rows * groups
    halo = 2 * rows
    place = lax.axis_index("seq")
    ahead = [(i, i + 1) for i in range(groups - 1)]
    behind = [(i + 1, i) for i in range(groups - 1)]
    gain1, bias1 = ln1_gain[None], ln1_bias[None]
    gain2, bias2 = ln2_gain[None], ln2_bias[None]

    devices = lax.axis_size("dp")
    chips = devices // 2
    spot = lax.axis_index("dp")
    core = spot % 2
    chip = (spot // 2).reshape(1).astype(jnp.int32)
    same_core = [[2 * i + c for i in range(chips)] for c in range(2)]
    exchange = lambda v, bit: lax.ppermute(v, "dp", [(i, i ^ bit) for i in range(devices)])
    swap = lambda v: exchange(v, 1)

    gather = lambda v: lax.all_gather(v, "dp", axis=0, tiled=True)
    qkv_full = gather(w_qkv)

    shard = w_down.shape[0]
    third = shard // 3
    by_core = w_up.reshape(w_up.shape[0], chips, 2, 3, third)
    by_core = jnp.transpose(by_core, (2, 0, 3, 1, 4)).reshape(2, w_up.shape[0], -1)
    mine = jnp.where(core == 0, by_core[0], by_core[1])
    given = swap(jnp.where(core == 0, by_core[1], by_core[0]))
    up_chip = jnp.concatenate(
        [jnp.where(core == 0, mine, given), jnp.where(core == 0, given, mine)], axis=0
    )
    if chips == 4:
        up_x, down_x = exchange(up_chip, 2), exchange(w_down, 2)
        up_y, down_y = exchange(up_chip, 4), exchange(w_down, 4)
        ups = [up_chip, up_x, up_y, exchange(up_y, 2)]
        downs = [w_down, down_x, down_y, exchange(down_x, 4)]
    else:
        ups, downs = (
            [lax.all_gather(v, "dp", axis=0, tiled=True, axis_index_groups=same_core)]
            for v in (up_chip, w_down)
        )

    seg_own = segments + 1
    near = lax.ppermute(block_input, "seq", ahead)
    seg_near = lax.ppermute(seg_own, "seq", ahead)
    far = lax.ppermute(near, "seq", ahead)
    seg_far = lax.ppermute(seg_near, "seq", ahead)
    seg_all = jnp.concatenate([seg_far, seg_near, seg_own], axis=1)
    seg_k_row = jnp.broadcast_to(seg_all, (8, halo + rows))
    seg_k_col = jnp.broadcast_to(seg_all.reshape(-1, 1), (halo + rows, 128))
    seg_q_row = seg_k_row[:, halo:]
    seg_q_col = seg_k_col[halo:]

    cos_all, sin_all = rotary_tables(length, halo)
    cosine = lax.dynamic_slice_in_dim(jnp.asarray(cos_all), place * rows, halo + rows, 0)
    sine = lax.dynamic_slice_in_dim(jnp.asarray(sin_all), place * rows, halo + rows, 0)

    earlier = (embedding, earlier_outs[0], earlier_outs[1], earlier_outs[2])
    base = sum(dwa_weights[i] * value for i, value in enumerate(earlier))
    dots = jnp.stack([jnp.sum(cotangent * value) for value in earlier])
    far, base, dots = lax.optimization_barrier((far, base, dots))

    q_rot, kv, normed_hi, normed_lo = project(
        far, near, block_input, gain1, bias1, qkv_full, cosine, sine
    )
    attended = attend(q_rot, kv, seg_q_col, seg_k_row)

    out_full = gather(w_out)
    resid = block_input + matmul(attended, out_full)
    resid_other = swap(resid)
    cot_other = swap(cotangent)
    scale = dwa_weights[4].reshape(1, 1)
    call = functools.partial(
        mlp, chip=chip, chips=chips, resid=resid, other=resid_other, cot=cotangent,
        cot_other=cot_other, gain=gain2, bias=bias2, scale=scale, ups=ups, downs=downs,
    )
    scatter = lambda v: lax.psum_scatter(v, "dp", scatter_dimension=0, tiled=True)
    scatter_chips = lambda v: lax.psum_scatter(
        v, "dp", scatter_dimension=0, tiled=True, axis_index_groups=same_core
    )
    so_far, shards = (), []
    for third_at in range(3):
        out_part, gnorm_part, grads = call(third_at, 1, so_far)
        so_far = (out_part, gnorm_part)
        shards.append(scatter_chips(grads)[0])
    given = swap(gnorm_part[rows:])

    shift = lambda v, bit: lax.ppermute(v, "seq", [(i, i ^ bit) for i in range(groups)])
    even = place % 2 == 0

    def line_start(shard):
        tall = shard.shape[1] // 2
        halves = (shard[:, :tall], shard[:, tall:])
        kept = jnp.where(even, halves[0], halves[1])
        return kept + shift(jnp.where(even, halves[1], halves[0]), 1)

    def line_middle(kept):
        bit = 2
        while bit < groups:
            kept = kept + shift(kept, bit)
            bit *= 2
        return kept

    def line_end(kept):
        other = shift(kept, 1)
        return jnp.where(even, kept, other), jnp.where(even, other, kept)

    together = lax.optimization_barrier
    shards[0], given = together((shards[0], given))
    line_a = line_start(shards[0])
    grad_resid, grad_attended, sums_two = resid_back(
        gnorm_part, given, resid, cotangent, gain2, scale, out_full
    )

    back_args = (q_rot, kv, grad_attended, seg_q_row, seg_k_col, cosine, sine)
    pairs = model // 128
    line_a, back_args = together((line_a, back_args))
    line_a = line_middle(line_a)
    first_half = attend_back(0, pairs // 2, *back_args)
    line_a, shards[1], back_args, first_half = together(
        (line_a, shards[1], back_args, first_half)
    )
    line_b = line_start(shards[1])
    ends_a = line_end(line_a)
    dq, dk, dv = attend_back(pairs // 2, pairs - pairs // 2, *back_args, before=first_half)
    line_b, ends_a, dq, dk, dv = together((line_b, ends_a, dq, dk, dv))
    line_b = line_middle(line_b)
    core_at = core.reshape(1).astype(jnp.int32)
    normed_parts = (normed_hi, normed_lo)
    grads_qk = weight_call(
        weights_qk_kernel, 9, core_at, chips, normed_parts, [(dq, 0), (dk, 1)], [halo + rows] * 2
    )
    given_qk = swap(grads_qk[1])
    line_b, dv, grad_resid = together((line_b, dv, grad_resid))
    ends_b = line_end(line_b)
    grads_vo = weight_call(
        weights_vo_kernel, 9, core_at, chips, normed_parts,
        [(dv, 0), (attended, None), (grad_resid, 1)], [halo + rows] * 2 + [rows] * 2,
    )
    grads_c = jnp.concatenate([grads_qk[0] + given_qk, grads_vo[0] + swap(grads_vo[1])], axis=2)
    grads_c, shards[2], out_part = together((grads_c, shards[2], out_part))
    shard_c = scatter_chips(grads_c)[0]
    line_c = line_start(shards[2])
    out_sib = swap(out_part[rows:])
    ends_b, dk, dv = together((ends_b, dk, dv))
    dkv = jnp.concatenate([dk, dv], axis=1)

    block_out = resid + out_part[:rows] + out_sib
    output = base + dwa_weights[4] * block_out
    dwa_local = jnp.concatenate([dots, jnp.sum(cotangent * block_out)[None]])

    wq, wkv = qkv_full[:, :model], qkv_full[:, model:]
    partial = outer_cols(dkv, wkv)
    line_c, partial = together((line_c, partial))
    line_c = line_middle(line_c)
    own_part = partial[halo:] + outer_cols(dq, wq)
    (sent,) = together((partial,))
    back_near = sent[rows:halo] + lax.ppermute(sent[:rows], "seq", behind)

    xhat1, rate1 = norm_stats(block_input)
    terms = (
        (norm_stats(far)[0], partial[:rows]),
        (norm_stats(near)[0], partial[rows:halo]),
        (xhat1, own_part),
    )
    grad_gain_one = sum(jnp.sum(xhat * part, axis=0) for xhat, part in terms)
    grad_bias_one = sum(jnp.sum(part, axis=0) for _, part in terms)

    small = jnp.concatenate(
        [
            grad_gain_one[None], grad_bias_one[None], sums_two[:2],
            jnp.pad(dwa_local, (0, model - 5))[None], jnp.zeros((3, model), F32),
        ],
        axis=0,
    )
    bit = 1
    while bit < devices:
        small = small + exchange(small, bit)
        bit *= 2
    shard_c, line_c, back_near, small = together((shard_c, line_c, back_near, small))
    last = line_middle(line_start(shard_c[None]))
    ends_c = line_end(line_c)
    last, ends_c, small, own_part = together((last, ends_c, small, own_part))
    bit = 1
    while bit < groups:
        small = small + shift(small, bit)
        bit *= 2
    gain_one, bias_one, gain_two, bias_two = small[0], small[1], small[2], small[3]
    grad_dwa = small[4, :5]
    last = jnp.concatenate(line_end(last), axis=1)[0]
    grad_qkv, grad_wout = last[:, :3 * model], last[:, 3 * model:]
    grad_normed_one = own_part + lax.ppermute(back_near, "seq", behind)
    grad_input = grad_resid + norm_back(grad_normed_one, gain1, xhat1, rate1)
    grad_up, grad_down = unpack_grads(
        *(
            jnp.concatenate(parts, axis=0)
            for parts in zip(ends_a, ends_b, ends_c)
        ),
        swap, core, chips,
    )
    return (
        output,
        grad_input,
        grad_dwa,
        gain_one,
        bias_one,
        grad_qkv,
        grad_wout,
        gain_two,
        bias_two,
        grad_up,
        grad_down,
    )


def solution(mesh):
    in_specs = (
        P(("dp", "seq"), None),
        P(("dp", "seq"), None),
        P(None, ("dp", "seq"), None),
        P(),
        P(),
        P(),
        P("dp", None),
        P("dp", None),
        P(),
        P(),
        P("dp", None),
        P("dp", None),
        P("dp", "seq"),
        P(("dp", "seq"), None),
    )
    out_specs = (
        P(("dp", "seq"), None),
        P(("dp", "seq"), None),
        P(),
        P(),
        P(),
        P("dp", None),
        P("dp", None),
        P(),
        P(),
        P("dp", None),
        P("dp", None),
    )
    return jax.shard_map(body, mesh=mesh, in_specs=in_specs, out_specs=out_specs, check_vma=False)
```

```python
import functools
import math

import jax
import jax.numpy as jnp
import numpy as np
from jax import lax
from jax.experimental import pallas as pl
from jax.experimental.pallas import tpu as pltpu
from jax.sharding import PartitionSpec as P

HD = 64
DOC_MOST = 768
LOG2E = math.log2(math.e)
SCALE = 1.0 / math.sqrt(HD)
NEG = -1e30
F32 = jnp.float32
BF16 = jnp.bfloat16
HIGH = lax.Precision.HIGH
VMEM_LIMIT = 56 * 1024 * 1024
BLK = 128


def cost(micros):
    return pl.CostEstimate(
        flops=int(micros * 1.1e9), bytes_accessed=1 << 20, transcendentals=0
    )


def params():
    return pltpu.CompilerParams(
        dimension_semantics=("arbitrary",), vmem_limit_bytes=VMEM_LIMIT
    )


def split(values):
    high = values.astype(BF16)
    return high, (values - high.astype(F32)).astype(BF16)


def dot_nn(left, right):
    return lax.dot_general(left, right, (((1,), (0,)), ((), ())), preferred_element_type=F32)


def dot_nt(left, right):
    return lax.dot_general(left, right, (((1,), (1,)), ((), ())), preferred_element_type=F32)


def dot_tn(left, right):
    return lax.dot_general(left, right, (((0,), (0,)), ((), ())), preferred_element_type=F32)


def three(dot, left, right):
    return (
        dot(left[0], right[0]) + dot(left[0], right[1]) + dot(left[1], right[0])
    )


def norm_stats(values):
    row_mean = jnp.mean(values, axis=-1, keepdims=True)
    centred = values - row_mean
    row_var = jnp.mean(centred * centred, axis=-1, keepdims=True)
    rate = lax.rsqrt(row_var + 1e-05)
    return centred * rate, rate


def norm_back(grad, gain, xhat, rate):
    scaled = grad * gain
    return rate * (
        scaled
        - jnp.mean(scaled, axis=-1, keepdims=True)
        - xhat * jnp.mean(scaled * xhat, axis=-1, keepdims=True)
    )


def turned(values):
    lane = lax.broadcasted_iota(jnp.int32, values.shape, 1)
    return jnp.where(
        (lane & 63) < 32, pltpu.roll(values, 96, 1), pltpu.roll(values, 32, 1)
    )


def rotate(values, cosine, sine):
    return values * cosine + turned(values) * sine


def unrotate(values, cosine, sine):
    return values * cosine - turned(values) * sine


def rotary_tables(length, halo):
    half = HD // 2
    inv_freq = (10000.0 ** (-(np.arange(half, dtype=np.float32) * 2.0 / HD))).astype(np.float32)
    place = np.arange(-halo, length, dtype=np.float32)
    angles = place[:, None] * inv_freq[None, :]
    cosine = np.cos(angles.astype(np.float64)).astype(np.float32)
    sine = np.sin(angles.astype(np.float64)).astype(np.float32)
    return (
        np.concatenate([cosine] * 4, axis=1),
        np.concatenate([-sine, sine, -sine, sine], axis=1),
    )


def qkv_kernel(far_ref, near_ref, own_ref, gain_ref, bias_ref, w_ref, cos_ref, sin_ref,
               q_ref, kv_ref, hi_ref, lo_ref):
    step = pl.program_id(0)
    rows = own_ref.shape[0]
    third = pl.num_programs(0) // 3
    halo = hi_ref.shape[0] - rows

    @pl.when(step == 0)
    def _():
        for at, ref in enumerate((far_ref, near_ref, own_ref)):
            xhat, _ = norm_stats(ref[...])
            high, low = split(xhat * gain_ref[...] + bias_ref[...])
            hi_ref[at * rows:(at + 1) * rows] = high
            lo_ref[at * rows:(at + 1) * rows] = low

    weights = split(w_ref[...])

    @pl.when(step < third)
    def _():
        got = three(dot_nn, (hi_ref[halo:], lo_ref[halo:]), weights)
        for at in range(0, got.shape[1], 128):
            q_ref[:, at:at + 128] = rotate(got[:, at:at + 128], cos_ref[halo:], sin_ref[halo:])

    @pl.when((step >= third) & (step < 2 * third))
    def _():
        got = three(dot_nn, (hi_ref[...], lo_ref[...]), weights)
        for at in range(0, got.shape[1], 128):
            kv_ref[:, at:at + 128] = rotate(got[:, at:at + 128], cos_ref[...], sin_ref[...])

    @pl.when(step >= 2 * third)
    def _():
        kv_ref[...] = three(dot_nn, (hi_ref[...], lo_ref[...]), weights)


def project(far, near, own, gain, bias, w_full, cosine, sine):
    rows, model = own.shape
    total = 3 * rows
    wide = 256
    third = model // wide
    whole = lambda shape: pl.BlockSpec(shape, lambda j: (0, 0))
    return pl.pallas_call(
        qkv_kernel,
        grid=(3 * third,),
        in_specs=[
            whole((rows, model)), whole((rows, model)), whole((rows, model)),
            whole((1, model)), whole((1, model)),
            pl.BlockSpec((model, wide), lambda j: (0, j)),
            whole((total, 128)), whole((total, 128)),
        ],
        out_specs=[
            pl.BlockSpec((rows, wide), lambda j: (0, jnp.minimum(j, third - 1))),
            pl.BlockSpec((total, wide), lambda j: (0, jnp.maximum(j - third, 0))),
            whole((total, model)), whole((total, model)),
        ],
        out_shape=[
            jax.ShapeDtypeStruct((rows, model), F32),
            jax.ShapeDtypeStruct((total, 2 * model), F32),
            jax.ShapeDtypeStruct((total, model), BF16),
            jax.ShapeDtypeStruct((total, model), BF16),
        ],
        cost_estimate=cost(20),
        compiler_params=params(),
    )(far, near, own, gain, bias, w_full, cosine, sine)


def own_pair(values, head):
    lane = lax.broadcasted_iota(jnp.int32, values.shape, 1)
    other = pltpu.roll(values, 64, 1)
    return jnp.where((lane < 64) == (head == 0), values, other)


def outer_form(values, head):
    high, low = split(own_pair(values, head))
    return jnp.concatenate([high, low], axis=1)


def mixed(values, head):
    pair = own_pair(values, head)
    lane = lax.broadcasted_iota(jnp.int32, pair.shape, 1)
    high = pair.astype(BF16).astype(F32)
    return jnp.where(lane < 64, high, pair - high).astype(BF16)


def inner_form(values, head):
    half = mixed(values, head)
    return jnp.concatenate([half, half], axis=1)


def fold(values):
    return values + pltpu.roll(values, 64, 1)


def attend_kernel(q_ref, k_ref, v_ref, segq_ref, segk_ref, out_ref, bias_ref):
    rows = q_ref.shape[0]
    halo = k_ref.shape[0] - rows
    span = halo + BLK

    @pl.when(pl.program_id(0) == 0)
    def _():
        for at in range(0, rows, BLK):
            row = lax.broadcasted_iota(jnp.int32, (BLK, span), 0)
            col = lax.broadcasted_iota(jnp.int32, (BLK, span), 1)
            same = segq_ref[at:at + BLK, :1] == segk_ref[:1, at:at + span]
            bias_ref[at:at + BLK] = jnp.where(same & (col - halo <= row), 0.0, NEG)

    lane = lax.broadcasted_iota(jnp.int32, (BLK, 128), 1)
    scaled = q_ref[...] * (SCALE * LOG2E)
    results = []
    for head in range(2):
        left = inner_form(scaled, head)
        right = outer_form(k_ref[...], head)
        vals = mixed(v_ref[...], head)
        outs = []
        for at in range(0, rows, BLK):
            scores = dot_nt(left[at:at + BLK], right[at:at + span]) + bias_ref[at:at + BLK]
            top = jnp.max(scores, axis=1, keepdims=True)
            expo = jnp.exp2(scores - top)
            total = jnp.sum(expo, axis=1, keepdims=True)
            high, low = split(expo)
            got = dot_nn(high, vals[at:at + span]) + dot_nn(low, vals[at:at + span])
            outs.append(fold(got) / total)
        results.append(outs)
    for at in range(0, rows, BLK):
        out_ref[at:at + BLK] = jnp.where(
            lane < 64, results[0][at // BLK], results[1][at // BLK]
        )


def attend(q_rot, kv, seg_q, seg_k):
    rows, model = q_rot.shape
    total = kv.shape[0]
    pairs = model // 128
    return pl.pallas_call(
        attend_kernel,
        grid=(pairs,),
        in_specs=[
            pl.BlockSpec((rows, 128), lambda p: (0, p)),
            pl.BlockSpec((total, 128), lambda p: (0, p)),
            pl.BlockSpec((total, 128), lambda p: (0, pairs + p)),
            pl.BlockSpec((rows, 128), lambda p: (0, 0)),
            pl.BlockSpec((8, total), lambda p: (0, 0)),
        ],
        out_specs=pl.BlockSpec((rows, 128), lambda p: (0, p)),
        out_shape=jax.ShapeDtypeStruct((rows, model), F32),
        scratch_shapes=[pltpu.VMEM((rows, total - rows + BLK), F32)],
        cost_estimate=cost(24),
        compiler_params=params(),
    )(q_rot, kv, kv, seg_q, seg_k)


def attend_back_kernel(q_ref, k_ref, v_ref, g_ref, segq_ref, segk_ref, cos_ref, sin_ref, *refs):
    dq_ref, dk_ref, dv_ref, bias_ref = refs[-4:]
    rows = q_ref.shape[0]
    halo = k_ref.shape[0] - rows
    span = halo + BLK

    @pl.when(pl.program_id(0) == 0)
    def _():
        for at in range(0, rows, BLK):
            key = lax.broadcasted_iota(jnp.int32, (span, BLK), 0)
            query = lax.broadcasted_iota(jnp.int32, (span, BLK), 1)
            same = segk_ref[at:at + span, :1] == segq_ref[:1, at:at + BLK]
            bias_ref[:, at:at + BLK] = jnp.where(same & (key - halo <= query), 0.0, NEG)

    scaled = q_ref[...] * (SCALE * LOG2E)
    dq, dk, dv = [], [], []
    for head in range(2):
        q_in = inner_form(scaled, head)
        g_in = inner_form(g_ref[...], head)
        k_out = outer_form(k_ref[...], head)
        v_out = outer_form(v_ref[...], head)
        q_mix = mixed(q_ref[...], head)
        g_mix = mixed(g_ref[...], head)
        k_mix = mixed(k_ref[...], head)
        dq_head = []
        dk_head = jnp.zeros((halo + rows, 128), F32)
        dv_head = jnp.zeros((halo + rows, 128), F32)
        dk_parts, dv_parts = [], []
        for at in range(0, rows, BLK):
            scores = dot_nt(k_out[at:at + span], q_in[at:at + BLK]) + bias_ref[:, at:at + BLK]
            top = jnp.max(scores, axis=0, keepdims=True)
            expo = jnp.exp2(scores - top)
            inverse = 1.0 / jnp.sum(expo, axis=0, keepdims=True)
            grad_probs = dot_nt(v_out[at:at + span], g_in[at:at + BLK])
            probs = expo * inverse
            delta = jnp.sum(probs * grad_probs, axis=0, keepdims=True)
            grad_scores = probs * (grad_probs - delta)
            probs_cat = jnp.concatenate(split(probs), axis=1)
            scores_cat = jnp.concatenate(split(grad_scores), axis=1)
            g_two = jnp.concatenate([g_mix[at:at + BLK]] * 2, axis=0)
            q_two = jnp.concatenate([q_mix[at:at + BLK]] * 2, axis=0)
            dv_parts.append(dot_nn(probs_cat, g_two))
            dk_parts.append(dot_nn(scores_cat, q_two))
            got = dot_tn(scores_cat, k_mix[at:at + span])
            dq_head.append(fold(got[:BLK] + got[BLK:]))
        for parts, full in ((dk_parts, dk), (dv_parts, dv)):
            pieces = []
            for kb in range((halo + rows) // BLK):
                terms = [
                    parts[qb][(kb - qb) * BLK:(kb - qb + 1) * BLK]
                    for qb in range(rows // BLK)
                    if 0 <= kb - qb < span // BLK
                ]
                pieces.append(fold(functools.reduce(lambda a, b: a + b, terms)))
            full.append(pieces)
        dq.append(dq_head)
    lane = lax.broadcasted_iota(jnp.int32, (BLK, 128), 1)
    for qb in range(rows // BLK):
        rng = slice(qb * BLK, (qb + 1) * BLK)
        far = slice(halo + qb * BLK, halo + (qb + 1) * BLK)
        both = jnp.where(lane < 64, dq[0][qb], dq[1][qb]) * SCALE
        dq_ref[rng] = unrotate(both, cos_ref[far], sin_ref[far])
    for kb in range((halo + rows) // BLK):
        rng = slice(kb * BLK, (kb + 1) * BLK)
        both = jnp.where(lane < 64, dk[0][kb], dk[1][kb]) * SCALE
        dk_ref[rng] = unrotate(both, cos_ref[rng], sin_ref[rng])
        dv_ref[rng] = jnp.where(lane < 64, dv[0][kb], dv[1][kb])


def attend_back(first, count, q_rot, kv, grad, seg_q, seg_k, cosine, sine, before=()):
    rows, model = q_rot.shape
    total = kv.shape[0]
    pairs = model // 128
    fixed = lambda shape: pl.BlockSpec(shape, lambda p: (0, 0))
    return pl.pallas_call(
        attend_back_kernel,
        grid=(count,),
        in_specs=[
            pl.BlockSpec((rows, 128), lambda p: (0, first + p)),
            pl.BlockSpec((total, 128), lambda p: (0, first + p)),
            pl.BlockSpec((total, 128), lambda p: (0, pairs + first + p)),
            pl.BlockSpec((rows, 128), lambda p: (0, first + p)),
            fixed((8, rows)), fixed((total, 128)),
            fixed((total, 128)), fixed((total, 128)),
        ] + [pl.BlockSpec(memory_space=pl.ANY)] * len(before),
        out_specs=[
            pl.BlockSpec((rows, 128), lambda p: (0, first + p)),
            pl.BlockSpec((total, 128), lambda p: (0, first + p)),
            pl.BlockSpec((total, 128), lambda p: (0, first + p)),
        ],
        out_shape=[
            jax.ShapeDtypeStruct((rows, model), F32),
            jax.ShapeDtypeStruct((total, model), F32),
            jax.ShapeDtypeStruct((total, model), F32),
        ],
        scratch_shapes=[pltpu.VMEM((total - rows + BLK, rows), F32)],
        input_output_aliases={8 + i: i for i in range(len(before))},
        cost_estimate=cost(7 * count),
        compiler_params=params(),
    )(q_rot, kv, kv, grad, seg_q, seg_k, cosine, sine, *before)


def mlp_kernel(count, begun, chip_ref, resid_ref, other_ref, cot_ref, cot_other_ref, gain_ref, bias_ref,
               scale_ref, *refs):
    up_refs, down_refs = refs[:count], refs[count:2 * count]
    refs = refs[2 * count:]
    so_far, refs = refs[:2 * begun], refs[2 * begun:]
    out_ref, gnorm_ref, grad_ref = refs[:3]
    (x_hi, x_lo, xt_hi, xt_lo, g_hi, g_lo, up_hi, up_lo, down_hi, down_lo) = refs[3:]
    step = pl.program_id(0)
    rows = resid_ref.shape[0]

    @pl.when(step == 0)
    def _():
        for at, source, cot in ((0, resid_ref, cot_ref), (rows, other_ref, cot_other_ref)):
            xhat, _ = norm_stats(source[...])
            normed = xhat * gain_ref[...] + bias_ref[...]
            x_hi[at:at + rows], x_lo[at:at + rows] = split(normed)
            xt_hi[:, at:at + rows], xt_lo[:, at:at + rows] = split(normed.T)
            g_hi[at:at + rows], g_lo[at:at + rows] = split(cot[...] * scale_ref[0, 0])
        if begun:
            out_ref[...] = so_far[0][...]
            gnorm_ref[...] = so_far[1][...]
        else:
            out_ref[...] = jnp.zeros_like(out_ref)
            gnorm_ref[...] = jnp.zeros_like(gnorm_ref)

    for at in range(count):
        spot = (chip_ref[0] ^ at) if count > 1 else 0
        up_rows = up_refs[at].shape[0]
        high, low = split(up_refs[at][...])
        here = pl.ds(pl.multiple_of(spot * up_rows, up_rows), up_rows)
        up_hi[here], up_lo[here] = high, low
        block = down_refs[at][...]
        block = block.reshape(-1, block.shape[-1])
        high, low = split(block)
        here = pl.ds(pl.multiple_of(spot * block.shape[0], block.shape[0]), block.shape[0])
        down_hi[here], down_lo[here] = high, low

    chips, _, tall, width = grad_ref.shape
    up_tall = up_hi.shape[0] // chips
    deep = down_hi.shape[0] // chips
    up = (up_hi[...], up_lo[...])
    down = (down_hi[...], down_lo[...])
    normed = (x_hi[...], x_lo[...])
    normed_t = (xt_hi[...], xt_lo[...])
    grad_block = (g_hi[...], g_lo[...])
    pre = three(dot_nn, normed, up)
    grad_act = three(dot_nt, grad_block, down)
    inner = 0.7978845608028654 * (pre + 0.044715 * pre * pre * pre)
    bent = jnp.tanh(inner)
    act = 0.5 * pre * (1.0 + bent)
    slope = 0.5 * (1.0 + bent) + 0.5 * pre * (1.0 - bent * bent) * (
        0.7978845608028654 * (1.0 + 3.0 * 0.044715 * pre * pre)
    )
    act2 = split(act)
    grad_pre = split(grad_act * slope)
    out_ref[...] += three(dot_nn, act2, down)
    gnorm_ref[...] += three(dot_nt, grad_pre, up)
    gup = three(dot_nn, normed_t, grad_pre)
    gdown = three(dot_tn, act2, grad_block)
    half = deep // 2
    for chip in range(chips):
        grad_ref[chip, 0, :up_tall] = gup[chip * up_tall:(chip + 1) * up_tall]
        part = gdown[chip * deep:(chip + 1) * deep]
        grad_ref[chip, 0, up_tall:up_tall + deep] = part[:, :width]
        grad_ref[chip, 0, up_tall + deep:] = jnp.concatenate(
            [part[:half, width:], part[half:, width:]], axis=1
        )


def mlp(first, steps, so_far, chip, chips, resid, other, cot, cot_other, gain, bias, scale, ups, downs):
    rows, model = resid.shape
    width = 512
    up_tall = model // chips
    deep = width // chips
    fixed = lambda shape: pl.BlockSpec(shape, lambda j, c: (0, 0))
    if len(ups) > 1:
        down_spec = pl.BlockSpec((deep, model), lambda j, c: (first + j, 0))
    else:
        downs = [downs[0].reshape(chips, -1, model)]
        down_spec = pl.BlockSpec((chips, deep, model), lambda j, c: (0, first + j, 0))
    tall = up_tall + deep + deep // 2
    grid_spec = pltpu.PrefetchScalarGridSpec(
        num_scalar_prefetch=1,
        grid=(steps,),
        in_specs=[fixed((rows, model))] * 4 + [fixed((1, model))] * 2
        + [pl.BlockSpec(memory_space=pltpu.SMEM)]
        + [pl.BlockSpec((up.shape[0], width), lambda j, c: (0, first + j)) for up in ups]
        + [down_spec] * len(downs)
        + [fixed((2 * rows, model))] * len(so_far),
        out_specs=[
            fixed((2 * rows, model)), fixed((2 * rows, model)),
            pl.BlockSpec((chips, 1, tall, width), lambda j, c: (0, j, 0, 0)),
        ],
        scratch_shapes=[
            pltpu.VMEM((2 * rows, model), BF16), pltpu.VMEM((2 * rows, model), BF16),
            pltpu.VMEM((model, 2 * rows), BF16), pltpu.VMEM((model, 2 * rows), BF16),
            pltpu.VMEM((2 * rows, model), BF16), pltpu.VMEM((2 * rows, model), BF16),
            pltpu.VMEM((model, width), BF16), pltpu.VMEM((model, width), BF16),
            pltpu.VMEM((width, model), BF16), pltpu.VMEM((width, model), BF16),
        ],
    )
    return pl.pallas_call(
        functools.partial(mlp_kernel, len(ups), len(so_far) // 2),
        grid_spec=grid_spec,
        out_shape=[
            jax.ShapeDtypeStruct((2 * rows, model), F32),
            jax.ShapeDtypeStruct((2 * rows, model), F32),
            jax.ShapeDtypeStruct((chips, steps, tall, width), F32),
        ],
        cost_estimate=cost(18 * steps),
        compiler_params=params(),
    )(chip, resid, other, cot, cot_other, gain, bias, scale, *ups, *downs, *so_far)


def unpack_grads(up, down, sibling_swap, core, chips):
    steps, up_tall, width = up.shape
    deep = up_tall * 2 // 3
    half = up_tall // 2
    mine = jnp.where(core == 0, up[:, :half], up[:, half:])
    other = sibling_swap(jnp.where(core == 0, up[:, half:], up[:, :half]))
    by_core = jnp.stack(
        [jnp.where(core == 0, mine, other), jnp.where(core == 0, other, mine)], axis=0
    )
    by_core = by_core.reshape(2, steps, half, chips, width // chips)
    grad_up = jnp.transpose(by_core, (2, 3, 0, 1, 4)).reshape(half, -1)
    quarter = width // 2
    tail = down[:, deep:]
    right = jnp.concatenate([tail[:, :, :quarter], tail[:, :, quarter:]], axis=1)
    grad_down = jnp.concatenate([down[:, :deep], right], axis=2).reshape(steps * deep, -1)
    return grad_up, grad_down


def resid_back_kernel(part_ref, given_ref, resid_ref, cot_ref, gain_ref, scale_ref, w_ref,
                      grad_ref, att_ref, sums_ref):
    grad = part_ref[...] + given_ref[...]
    xhat, rate = norm_stats(resid_ref[...])
    grad_resid = cot_ref[...] * scale_ref[0, 0] + norm_back(grad, gain_ref[...], xhat, rate)
    grad_ref[...] = grad_resid
    att_ref[...] = three(dot_nt, split(grad_resid), split(w_ref[...]))
    gain_sum = jnp.sum(grad * xhat, axis=0, keepdims=True)
    bias_sum = jnp.sum(grad, axis=0, keepdims=True)
    sums_ref[...] = jnp.concatenate(
        [gain_sum, bias_sum, jnp.zeros((6, gain_sum.shape[1]), F32)], axis=0
    )


def resid_back(part, given, resid, cot, gain, scale, w_full):
    rows, model = resid.shape
    fixed = lambda shape: pl.BlockSpec(shape, lambda j: (0, 0))
    return pl.pallas_call(
        resid_back_kernel,
        grid=(1,),
        in_specs=[fixed((rows, model))] * 4 + [fixed((1, model))]
        + [pl.BlockSpec(memory_space=pltpu.SMEM), fixed((model, model))],
        out_specs=[fixed((rows, model)), fixed((rows, model)), fixed((8, model))],
        out_shape=[
            jax.ShapeDtypeStruct((rows, model), F32),
            jax.ShapeDtypeStruct((rows, model), F32),
            jax.ShapeDtypeStruct((8, model), F32),
        ],
        cost_estimate=cost(6),
        compiler_params=params(),
    )(part, given, resid, cot, gain, scale, w_full)


def place_rows(core_ref, out_ref, got):
    chips = out_ref.shape[1]
    tall = out_ref.shape[2]
    for block in range(2 * chips):
        out_ref[(block & 1) ^ core_ref[0], block // 2] = got[block * tall:(block + 1) * tall]


def weights_qk_kernel(core_ref, hi_ref, lo_ref, dq_ref, dk_ref, out_ref, nt_hi, nt_lo):
    step = pl.program_id(0)
    part = pl.num_programs(0) // 2
    halo = hi_ref.shape[0] - dq_ref.shape[0]

    @pl.when(step == 0)
    def _():
        nt_hi[...] = hi_ref[...].T
        nt_lo[...] = lo_ref[...].T

    @pl.when(step < part)
    def _():
        left = (nt_hi[:, halo:], nt_lo[:, halo:])
        place_rows(core_ref, out_ref, three(dot_nn, left, split(dq_ref[...])))

    @pl.when(step >= part)
    def _():
        left = (nt_hi[...], nt_lo[...])
        place_rows(core_ref, out_ref, three(dot_nn, left, split(dk_ref[...])))


def weights_vo_kernel(core_ref, hi_ref, lo_ref, dv_ref, att_ref, res_ref, out_ref,
                      nt_hi, nt_lo, at_hi, at_lo):
    step = pl.program_id(0)
    part = pl.num_programs(0) // 2

    @pl.when(step == 0)
    def _():
        nt_hi[...] = hi_ref[...].T
        nt_lo[...] = lo_ref[...].T
        at_hi[...], at_lo[...] = split(att_ref[...].T)

    @pl.when(step < part)
    def _():
        left = (nt_hi[...], nt_lo[...])
        place_rows(core_ref, out_ref, three(dot_nn, left, split(dv_ref[...])))

    @pl.when(step >= part)
    def _():
        left = (at_hi[...], at_lo[...])
        place_rows(core_ref, out_ref, three(dot_nn, left, split(res_ref[...])))


def weight_call(kernel, micros, core, chips, fixed_args, pieces, scratch):
    model = fixed_args[0].shape[1]
    wide = 256
    part = model // wide
    tall = model // chips // 2
    fixed = lambda v: pl.BlockSpec(v.shape, lambda j, c: (0, 0))
    piece = lambda v, at: pl.BlockSpec(
        (v.shape[0], wide), lambda j, c: (0, jnp.clip(j - at * part, 0, part - 1))
    )
    specs, args = [], []
    for value, at in pieces:
        args.append(value)
        specs.append(fixed(value) if at is None else piece(value, at))
    return pl.pallas_call(
        kernel,
        grid_spec=pltpu.PrefetchScalarGridSpec(
            num_scalar_prefetch=1,
            grid=(2 * part,),
            in_specs=[fixed(v) for v in fixed_args] + specs,
            out_specs=pl.BlockSpec((2, chips, tall, wide), lambda j, c: (0, 0, 0, j)),
            scratch_shapes=[pltpu.VMEM((model, n), BF16) for n in scratch],
        ),
        out_shape=jax.ShapeDtypeStruct((2, chips, tall, 2 * model), F32),
        cost_estimate=cost(micros),
        compiler_params=params(),
    )(core, *fixed_args, *args)


def matmul(left, right):
    return jnp.dot(left, right, precision=HIGH)


def inner_rows(left, right):
    return lax.dot_general(left, right, (((0,), (0,)), ((), ())), precision=HIGH)


def outer_cols(left, right):
    return lax.dot_general(left, right, (((1,), (1,)), ((), ())), precision=HIGH)


def body(
    block_input,
    embedding,
    earlier_outs,
    dwa_weights,
    ln1_gain,
    ln1_bias,
    w_qkv,
    w_out,
    ln2_gain,
    ln2_bias,
    w_up,
    w_down,
    segments,
    cotangent,
):
    groups = lax.axis_size("seq")
    rows, model = block_input.shape
    length = rows * groups
    halo = 2 * rows
    place = lax.axis_index("seq")
    ahead = [(i, i + 1) for i in range(groups - 1)]
    behind = [(i + 1, i) for i in range(groups - 1)]
    gain1, bias1 = ln1_gain[None], ln1_bias[None]
    gain2, bias2 = ln2_gain[None], ln2_bias[None]

    devices = lax.axis_size("dp")
    chips = devices // 2
    spot = lax.axis_index("dp")
    core = spot % 2
    chip = (spot // 2).reshape(1).astype(jnp.int32)
    same_core = [[2 * i + c for i in range(chips)] for c in range(2)]
    exchange = lambda v, bit: lax.ppermute(v, "dp", [(i, i ^ bit) for i in range(devices)])
    swap = lambda v: exchange(v, 1)

    gather = lambda v: lax.all_gather(v, "dp", axis=0, tiled=True)
    qkv_full = gather(w_qkv)

    shard = w_down.shape[0]
    third = shard // 3
    by_core = w_up.reshape(w_up.shape[0], chips, 2, 3, third)
    by_core = jnp.transpose(by_core, (2, 0, 3, 1, 4)).reshape(2, w_up.shape[0], -1)
    mine = jnp.where(core == 0, by_core[0], by_core[1])
    given = swap(jnp.where(core == 0, by_core[1], by_core[0]))
    up_chip = jnp.concatenate(
        [jnp.where(core == 0, mine, given), jnp.where(core == 0, given, mine)], axis=0
    )
    if chips == 4:
        up_x, down_x = exchange(up_chip, 2), exchange(w_down, 2)
        up_y, down_y = exchange(up_chip, 4), exchange(w_down, 4)
        ups = [up_chip, up_x, up_y, exchange(up_y, 2)]
        downs = [w_down, down_x, down_y, exchange(down_x, 4)]
    else:
        ups, downs = (
            [lax.all_gather(v, "dp", axis=0, tiled=True, axis_index_groups=same_core)]
            for v in (up_chip, w_down)
        )

    seg_own = segments + 1
    near = lax.ppermute(block_input, "seq", ahead)
    seg_near = lax.ppermute(seg_own, "seq", ahead)
    far = lax.ppermute(near, "seq", ahead)
    seg_far = lax.ppermute(seg_near, "seq", ahead)
    seg_all = jnp.concatenate([seg_far, seg_near, seg_own], axis=1)
    seg_k_row = jnp.broadcast_to(seg_all, (8, halo + rows))
    seg_k_col = jnp.broadcast_to(seg_all.reshape(-1, 1), (halo + rows, 128))
    seg_q_row = seg_k_row[:, halo:]
    seg_q_col = seg_k_col[halo:]

    cos_all, sin_all = rotary_tables(length, halo)
    cosine = lax.dynamic_slice_in_dim(jnp.asarray(cos_all), place * rows, halo + rows, 0)
    sine = lax.dynamic_slice_in_dim(jnp.asarray(sin_all), place * rows, halo + rows, 0)

    earlier = (embedding, earlier_outs[0], earlier_outs[1], earlier_outs[2])
    base = sum(dwa_weights[i] * value for i, value in enumerate(earlier))
    dots = jnp.stack([jnp.sum(cotangent * value) for value in earlier])
    far, base, dots = lax.optimization_barrier((far, base, dots))

    q_rot, kv, normed_hi, normed_lo = project(
        far, near, block_input, gain1, bias1, qkv_full, cosine, sine
    )
    attended = attend(q_rot, kv, seg_q_col, seg_k_row)

    out_full = gather(w_out)
    resid = block_input + matmul(attended, out_full)
    resid_other = swap(resid)
    cot_other = swap(cotangent)
    scale = dwa_weights[4].reshape(1, 1)
    call = functools.partial(
        mlp, chip=chip, chips=chips, resid=resid, other=resid_other, cot=cotangent,
        cot_other=cot_other, gain=gain2, bias=bias2, scale=scale, ups=ups, downs=downs,
    )
    scatter = lambda v: lax.psum_scatter(v, "dp", scatter_dimension=0, tiled=True)
    scatter_chips = lambda v: lax.psum_scatter(
        v, "dp", scatter_dimension=0, tiled=True, axis_index_groups=same_core
    )
    so_far, shards = (), []
    for third_at in range(3):
        out_part, gnorm_part, grads = call(third_at, 1, so_far)
        so_far = (out_part, gnorm_part)
        shards.append(scatter_chips(grads)[0])
    given = swap(gnorm_part[rows:])

    shift = lambda v, bit: lax.ppermute(v, "seq", [(i, i ^ bit) for i in range(groups)])
    even = place % 2 == 0

    def line_start(shard):
        tall = shard.shape[1] // 2
        halves = (shard[:, :tall], shard[:, tall:])
        kept = jnp.where(even, halves[0], halves[1])
        return kept + shift(jnp.where(even, halves[1], halves[0]), 1)

    def line_middle(kept):
        bit = 2
        while bit < groups:
            kept = kept + shift(kept, bit)
            bit *= 2
        return kept

    def line_end(kept):
        other = shift(kept, 1)
        return jnp.where(even, kept, other), jnp.where(even, other, kept)

    together = lax.optimization_barrier
    shards[0], given = together((shards[0], given))
    line_a = line_start(shards[0])
    grad_resid, grad_attended, sums_two = resid_back(
        gnorm_part, given, resid, cotangent, gain2, scale, out_full
    )

    back_args = (q_rot, kv, grad_attended, seg_q_row, seg_k_col, cosine, sine)
    pairs = model // 128
    line_a, back_args = together((line_a, back_args))
    line_a = line_middle(line_a)
    first_half = attend_back(0, pairs // 2, *back_args)
    line_a, shards[1], back_args, first_half = together(
        (line_a, shards[1], back_args, first_half)
    )
    line_b = line_start(shards[1])
    ends_a = line_end(line_a)
    dq, dk, dv = attend_back(pairs // 2, pairs - pairs // 2, *back_args, before=first_half)
    line_b, ends_a, dq, dk, dv = together((line_b, ends_a, dq, dk, dv))
    line_b = line_middle(line_b)
    core_at = core.reshape(1).astype(jnp.int32)
    normed_parts = (normed_hi, normed_lo)
    grads_qk = weight_call(
        weights_qk_kernel, 9, core_at, chips, normed_parts, [(dq, 0), (dk, 1)], [halo + rows] * 2
    )
    given_qk = swap(grads_qk[1])
    line_b, shards[2], dv, grad_resid = together((line_b, shards[2], dv, grad_resid))
    ends_b = line_end(line_b)
    line_c = line_start(shards[2])
    grads_vo = weight_call(
        weights_vo_kernel, 9, core_at, chips, normed_parts,
        [(dv, 0), (attended, None), (grad_resid, 1)], [halo + rows] * 2 + [rows] * 2,
    )
    line_c, grads_vo = together((line_c, grads_vo))
    line_c = line_middle(line_c)
    grads_c = jnp.concatenate([grads_qk[0] + given_qk, grads_vo[0] + swap(grads_vo[1])], axis=2)
    grads_c, out_part = together((grads_c, out_part))
    shard_c = scatter_chips(grads_c)[0]
    out_sib = swap(out_part[rows:])
    ends_b, dk, dv = together((ends_b, dk, dv))
    dkv = jnp.concatenate([dk, dv], axis=1)

    block_out = resid + out_part[:rows] + out_sib
    output = base + dwa_weights[4] * block_out
    dwa_local = jnp.concatenate([dots, jnp.sum(cotangent * block_out)[None]])

    wq, wkv = qkv_full[:, :model], qkv_full[:, model:]
    partial = outer_cols(dkv, wkv)
    line_c, partial = together((line_c, partial))
    ends_c = line_end(line_c)
    own_part = partial[halo:] + outer_cols(dq, wq)
    (sent,) = together((partial,))
    back_near = sent[rows:halo] + lax.ppermute(sent[:rows], "seq", behind)

    xhat1, rate1 = norm_stats(block_input)
    terms = (
        (norm_stats(far)[0], partial[:rows]),
        (norm_stats(near)[0], partial[rows:halo]),
        (xhat1, own_part),
    )
    grad_gain_one = sum(jnp.sum(xhat * part, axis=0) for xhat, part in terms)
    grad_bias_one = sum(jnp.sum(part, axis=0) for _, part in terms)

    small = jnp.concatenate(
        [
            grad_gain_one[None], grad_bias_one[None], sums_two[:2],
            jnp.pad(dwa_local, (0, model - 5))[None], jnp.zeros((3, model), F32),
        ],
        axis=0,
    )
    bit = 1
    while bit < devices:
        small = small + exchange(small, bit)
        bit *= 2
    shard_c, ends_c, back_near, small = together((shard_c, ends_c, back_near, small))
    last = line_middle(line_start(shard_c[None]))
    given_back = lax.ppermute(back_near, "seq", behind)
    grad_up, grad_down = unpack_grads(
        *(
            jnp.concatenate(parts, axis=0)
            for parts in zip(ends_a, ends_b, ends_c)
        ),
        swap, core, chips,
    )
    last, grad_up, grad_down, small, given_back = together(
        (last, grad_up, grad_down, small, given_back)
    )
    bit = 1
    while bit < groups:
        small = small + shift(small, bit)
        bit *= 2
    gain_one, bias_one, gain_two, bias_two = small[0], small[1], small[2], small[3]
    grad_dwa = small[4, :5]
    last = jnp.concatenate(line_end(last), axis=1)[0]
    grad_qkv, grad_wout = last[:, :3 * model], last[:, 3 * model:]
    grad_normed_one = own_part + given_back
    grad_input = grad_resid + norm_back(grad_normed_one, gain1, xhat1, rate1)
    return (
        output,
        grad_input,
        grad_dwa,
        gain_one,
        bias_one,
        grad_qkv,
        grad_wout,
        gain_two,
        bias_two,
        grad_up,
        grad_down,
    )


def solution(mesh):
    in_specs = (
        P(("dp", "seq"), None),
        P(("dp", "seq"), None),
        P(None, ("dp", "seq"), None),
        P(),
        P(),
        P(),
        P("dp", None),
        P("dp", None),
        P(),
        P(),
        P("dp", None),
        P("dp", None),
        P("dp", "seq"),
        P(("dp", "seq"), None),
    )
    out_specs = (
        P(("dp", "seq"), None),
        P(("dp", "seq"), None),
        P(),
        P(),
        P(),
        P("dp", None),
        P("dp", None),
        P(),
        P(),
        P("dp", None),
        P("dp", None),
    )
    return jax.shard_map(body, mesh=mesh, in_specs=in_specs, out_specs=out_specs, check_vma=False)
```

```python
import functools
import math

import jax
import jax.numpy as jnp
import numpy as np
from jax import lax
from jax.experimental import pallas as pl
from jax.experimental.pallas import tpu as pltpu
from jax.sharding import PartitionSpec as P

HD = 64
DOC_MOST = 768
LOG2E = math.log2(math.e)
SCALE = 1.0 / math.sqrt(HD)
NEG = -1e30
F32 = jnp.float32
BF16 = jnp.bfloat16
HIGH = lax.Precision.HIGH
VMEM_LIMIT = 56 * 1024 * 1024
BLK = 128


def cost(micros):
    return pl.CostEstimate(
        flops=int(micros * 1.1e9), bytes_accessed=1 << 20, transcendentals=0
    )


def params():
    return pltpu.CompilerParams(
        dimension_semantics=("arbitrary",), vmem_limit_bytes=VMEM_LIMIT
    )


def split(values):
    high = values.astype(BF16)
    return high, (values - high.astype(F32)).astype(BF16)


def dot_nn(left, right):
    return lax.dot_general(left, right, (((1,), (0,)), ((), ())), preferred_element_type=F32)


def dot_nt(left, right):
    return lax.dot_general(left, right, (((1,), (1,)), ((), ())), preferred_element_type=F32)


def dot_tn(left, right):
    return lax.dot_general(left, right, (((0,), (0,)), ((), ())), preferred_element_type=F32)


def three(dot, left, right):
    return (
        dot(left[0], right[0]) + dot(left[0], right[1]) + dot(left[1], right[0])
    )


def norm_stats(values):
    row_mean = jnp.mean(values, axis=-1, keepdims=True)
    centred = values - row_mean
    row_var = jnp.mean(centred * centred, axis=-1, keepdims=True)
    rate = lax.rsqrt(row_var + 1e-05)
    return centred * rate, rate


def norm_back(grad, gain, xhat, rate):
    scaled = grad * gain
    return rate * (
        scaled
        - jnp.mean(scaled, axis=-1, keepdims=True)
        - xhat * jnp.mean(scaled * xhat, axis=-1, keepdims=True)
    )


def turned(values):
    lane = lax.broadcasted_iota(jnp.int32, values.shape, 1)
    return jnp.where(
        (lane & 63) < 32, pltpu.roll(values, 96, 1), pltpu.roll(values, 32, 1)
    )


def rotate(values, cosine, sine):
    return values * cosine + turned(values) * sine


def unrotate(values, cosine, sine):
    return values * cosine - turned(values) * sine


def rotary_tables(length, halo):
    half = HD // 2
    inv_freq = (10000.0 ** (-(np.arange(half, dtype=np.float32) * 2.0 / HD))).astype(np.float32)
    place = np.arange(-halo, length, dtype=np.float32)
    angles = place[:, None] * inv_freq[None, :]
    cosine = np.cos(angles.astype(np.float64)).astype(np.float32)
    sine = np.sin(angles.astype(np.float64)).astype(np.float32)
    return (
        np.concatenate([cosine] * 4, axis=1),
        np.concatenate([-sine, sine, -sine, sine], axis=1),
    )


def qkv_kernel(far_ref, near_ref, own_ref, gain_ref, bias_ref, w_ref, cos_ref, sin_ref,
               q_ref, kv_ref, hi_ref, lo_ref):
    step = pl.program_id(0)
    rows = own_ref.shape[0]
    third = pl.num_programs(0) // 3
    halo = hi_ref.shape[0] - rows

    @pl.when(step == 0)
    def _():
        for at, ref in enumerate((far_ref, near_ref, own_ref)):
            xhat, _ = norm_stats(ref[...])
            high, low = split(xhat * gain_ref[...] + bias_ref[...])
            hi_ref[at * rows:(at + 1) * rows] = high
            lo_ref[at * rows:(at + 1) * rows] = low

    weights = split(w_ref[...])

    @pl.when(step < third)
    def _():
        got = three(dot_nn, (hi_ref[halo:], lo_ref[halo:]), weights)
        for at in range(0, got.shape[1], 128):
            q_ref[:, at:at + 128] = rotate(got[:, at:at + 128], cos_ref[halo:], sin_ref[halo:])

    @pl.when((step >= third) & (step < 2 * third))
    def _():
        got = three(dot_nn, (hi_ref[...], lo_ref[...]), weights)
        for at in range(0, got.shape[1], 128):
            kv_ref[:, at:at + 128] = rotate(got[:, at:at + 128], cos_ref[...], sin_ref[...])

    @pl.when(step >= 2 * third)
    def _():
        kv_ref[...] = three(dot_nn, (hi_ref[...], lo_ref[...]), weights)


def project(far, near, own, gain, bias, w_full, cosine, sine):
    rows, model = own.shape
    total = 3 * rows
    wide = 256
    third = model // wide
    whole = lambda shape: pl.BlockSpec(shape, lambda j: (0, 0))
    return pl.pallas_call(
        qkv_kernel,
        grid=(3 * third,),
        in_specs=[
            whole((rows, model)), whole((rows, model)), whole((rows, model)),
            whole((1, model)), whole((1, model)),
            pl.BlockSpec((model, wide), lambda j: (0, j)),
            whole((total, 128)), whole((total, 128)),
        ],
        out_specs=[
            pl.BlockSpec((rows, wide), lambda j: (0, jnp.minimum(j, third - 1))),
            pl.BlockSpec((total, wide), lambda j: (0, jnp.maximum(j - third, 0))),
            whole((total, model)), whole((total, model)),
        ],
        out_shape=[
            jax.ShapeDtypeStruct((rows, model), F32),
            jax.ShapeDtypeStruct((total, 2 * model), F32),
            jax.ShapeDtypeStruct((total, model), BF16),
            jax.ShapeDtypeStruct((total, model), BF16),
        ],
        cost_estimate=cost(2),
        compiler_params=params(),
    )(far, near, own, gain, bias, w_full, cosine, sine)


def own_pair(values, head):
    lane = lax.broadcasted_iota(jnp.int32, values.shape, 1)
    other = pltpu.roll(values, 64, 1)
    return jnp.where((lane < 64) == (head == 0), values, other)


def outer_form(values, head):
    high, low = split(own_pair(values, head))
    return jnp.concatenate([high, low], axis=1)


def mixed(values, head):
    pair = own_pair(values, head)
    lane = lax.broadcasted_iota(jnp.int32, pair.shape, 1)
    high = pair.astype(BF16).astype(F32)
    return jnp.where(lane < 64, high, pair - high).astype(BF16)


def inner_form(values, head):
    half = mixed(values, head)
    return jnp.concatenate([half, half], axis=1)


def fold(values):
    return values + pltpu.roll(values, 64, 1)


def attend_kernel(q_ref, k_ref, v_ref, segq_ref, segk_ref, out_ref, bias_ref):
    rows = q_ref.shape[0]
    halo = k_ref.shape[0] - rows
    span = halo + BLK

    @pl.when(pl.program_id(0) == 0)
    def _():
        for at in range(0, rows, BLK):
            row = lax.broadcasted_iota(jnp.int32, (BLK, span), 0)
            col = lax.broadcasted_iota(jnp.int32, (BLK, span), 1)
            same = segq_ref[at:at + BLK, :1] == segk_ref[:1, at:at + span]
            bias_ref[at:at + BLK] = jnp.where(same & (col - halo <= row), 0.0, NEG)

    lane = lax.broadcasted_iota(jnp.int32, (BLK, 128), 1)
    scaled = q_ref[...] * (SCALE * LOG2E)
    results = []
    for head in range(2):
        left = inner_form(scaled, head)
        right = outer_form(k_ref[...], head)
        vals = mixed(v_ref[...], head)
        outs = []
        for at in range(0, rows, BLK):
            scores = dot_nt(left[at:at + BLK], right[at:at + span]) + bias_ref[at:at + BLK]
            top = jnp.max(scores, axis=1, keepdims=True)
            expo = jnp.exp2(scores - top)
            total = jnp.sum(expo, axis=1, keepdims=True)
            high, low = split(expo)
            got = dot_nn(high, vals[at:at + span]) + dot_nn(low, vals[at:at + span])
            outs.append(fold(got) / total)
        results.append(outs)
    for at in range(0, rows, BLK):
        out_ref[at:at + BLK] = jnp.where(
            lane < 64, results[0][at // BLK], results[1][at // BLK]
        )


def attend(q_rot, kv, seg_q, seg_k):
    rows, model = q_rot.shape
    total = kv.shape[0]
    pairs = model // 128
    return pl.pallas_call(
        attend_kernel,
        grid=(pairs,),
        in_specs=[
            pl.BlockSpec((rows, 128), lambda p: (0, p)),
            pl.BlockSpec((total, 128), lambda p: (0, p)),
            pl.BlockSpec((total, 128), lambda p: (0, pairs + p)),
            pl.BlockSpec((rows, 128), lambda p: (0, 0)),
            pl.BlockSpec((8, total), lambda p: (0, 0)),
        ],
        out_specs=pl.BlockSpec((rows, 128), lambda p: (0, p)),
        out_shape=jax.ShapeDtypeStruct((rows, model), F32),
        scratch_shapes=[pltpu.VMEM((rows, total - rows + BLK), F32)],
        cost_estimate=cost(2),
        compiler_params=params(),
    )(q_rot, kv, kv, seg_q, seg_k)


def attend_back_kernel(q_ref, k_ref, v_ref, g_ref, segq_ref, segk_ref, cos_ref, sin_ref, *refs):
    dq_ref, dk_ref, dv_ref, bias_ref = refs[-4:]
    rows = q_ref.shape[0]
    halo = k_ref.shape[0] - rows
    span = halo + BLK

    @pl.when(pl.program_id(0) == 0)
    def _():
        for at in range(0, rows, BLK):
            key = lax.broadcasted_iota(jnp.int32, (span, BLK), 0)
            query = lax.broadcasted_iota(jnp.int32, (span, BLK), 1)
            same = segk_ref[at:at + span, :1] == segq_ref[:1, at:at + BLK]
            bias_ref[:, at:at + BLK] = jnp.where(same & (key - halo <= query), 0.0, NEG)

    scaled = q_ref[...] * (SCALE * LOG2E)
    dq, dk, dv = [], [], []
    for head in range(2):
        q_in = inner_form(scaled, head)
        g_in = inner_form(g_ref[...], head)
        k_out = outer_form(k_ref[...], head)
        v_out = outer_form(v_ref[...], head)
        q_mix = mixed(q_ref[...], head)
        g_mix = mixed(g_ref[...], head)
        k_mix = mixed(k_ref[...], head)
        dq_head = []
        dk_head = jnp.zeros((halo + rows, 128), F32)
        dv_head = jnp.zeros((halo + rows, 128), F32)
        dk_parts, dv_parts = [], []
        for at in range(0, rows, BLK):
            scores = dot_nt(k_out[at:at + span], q_in[at:at + BLK]) + bias_ref[:, at:at + BLK]
            top = jnp.max(scores, axis=0, keepdims=True)
            expo = jnp.exp2(scores - top)
            inverse = 1.0 / jnp.sum(expo, axis=0, keepdims=True)
            grad_probs = dot_nt(v_out[at:at + span], g_in[at:at + BLK])
            probs = expo * inverse
            delta = jnp.sum(probs * grad_probs, axis=0, keepdims=True)
            grad_scores = probs * (grad_probs - delta)
            probs_cat = jnp.concatenate(split(probs), axis=1)
            scores_cat = jnp.concatenate(split(grad_scores), axis=1)
            g_two = jnp.concatenate([g_mix[at:at + BLK]] * 2, axis=0)
            q_two = jnp.concatenate([q_mix[at:at + BLK]] * 2, axis=0)
            dv_parts.append(dot_nn(probs_cat, g_two))
            dk_parts.append(dot_nn(scores_cat, q_two))
            got = dot_tn(scores_cat, k_mix[at:at + span])
            dq_head.append(fold(got[:BLK] + got[BLK:]))
        for parts, full in ((dk_parts, dk), (dv_parts, dv)):
            pieces = []
            for kb in range((halo + rows) // BLK):
                terms = [
                    parts[qb][(kb - qb) * BLK:(kb - qb + 1) * BLK]
                    for qb in range(rows // BLK)
                    if 0 <= kb - qb < span // BLK
                ]
                pieces.append(fold(functools.reduce(lambda a, b: a + b, terms)))
            full.append(pieces)
        dq.append(dq_head)
    lane = lax.broadcasted_iota(jnp.int32, (BLK, 128), 1)
    for qb in range(rows // BLK):
        rng = slice(qb * BLK, (qb + 1) * BLK)
        far = slice(halo + qb * BLK, halo + (qb + 1) * BLK)
        both = jnp.where(lane < 64, dq[0][qb], dq[1][qb]) * SCALE
        dq_ref[rng] = unrotate(both, cos_ref[far], sin_ref[far])
    for kb in range((halo + rows) // BLK):
        rng = slice(kb * BLK, (kb + 1) * BLK)
        both = jnp.where(lane < 64, dk[0][kb], dk[1][kb]) * SCALE
        dk_ref[rng] = unrotate(both, cos_ref[rng], sin_ref[rng])
        dv_ref[rng] = jnp.where(lane < 64, dv[0][kb], dv[1][kb])


def attend_back(first, count, q_rot, kv, grad, seg_q, seg_k, cosine, sine, before=()):
    rows, model = q_rot.shape
    total = kv.shape[0]
    pairs = model // 128
    fixed = lambda shape: pl.BlockSpec(shape, lambda p: (0, 0))
    return pl.pallas_call(
        attend_back_kernel,
        grid=(count,),
        in_specs=[
            pl.BlockSpec((rows, 128), lambda p: (0, first + p)),
            pl.BlockSpec((total, 128), lambda p: (0, first + p)),
            pl.BlockSpec((total, 128), lambda p: (0, pairs + first + p)),
            pl.BlockSpec((rows, 128), lambda p: (0, first + p)),
            fixed((8, rows)), fixed((total, 128)),
            fixed((total, 128)), fixed((total, 128)),
        ] + [pl.BlockSpec(memory_space=pl.ANY)] * len(before),
        out_specs=[
            pl.BlockSpec((rows, 128), lambda p: (0, first + p)),
            pl.BlockSpec((total, 128), lambda p: (0, first + p)),
            pl.BlockSpec((total, 128), lambda p: (0, first + p)),
        ],
        out_shape=[
            jax.ShapeDtypeStruct((rows, model), F32),
            jax.ShapeDtypeStruct((total, model), F32),
            jax.ShapeDtypeStruct((total, model), F32),
        ],
        scratch_shapes=[pltpu.VMEM((total - rows + BLK, rows), F32)],
        input_output_aliases={8 + i: i for i in range(len(before))},
        cost_estimate=cost(7 * count),
        compiler_params=params(),
    )(q_rot, kv, kv, grad, seg_q, seg_k, cosine, sine, *before)


def mlp_kernel(count, begun, chip_ref, resid_ref, other_ref, cot_ref, cot_other_ref, gain_ref, bias_ref,
               scale_ref, *refs):
    packed_ref, refs = (refs[:1], refs[1:]) if count == 0 else ((), refs)
    up_refs, down_refs = refs[:count], refs[count:2 * count]
    refs = refs[2 * count:]
    so_far, refs = refs[:2 * begun], refs[2 * begun:]
    out_ref, gnorm_ref, grad_ref = refs[:3]
    (x_hi, x_lo, xt_hi, xt_lo, g_hi, g_lo, up_hi, up_lo, down_hi, down_lo) = refs[3:]
    step = pl.program_id(0)
    rows = resid_ref.shape[0]

    @pl.when(step == 0)
    def _():
        for at, source, cot in ((0, resid_ref, cot_ref), (rows, other_ref, cot_other_ref)):
            xhat, _ = norm_stats(source[...])
            normed = xhat * gain_ref[...] + bias_ref[...]
            x_hi[at:at + rows], x_lo[at:at + rows] = split(normed)
            xt_hi[:, at:at + rows], xt_lo[:, at:at + rows] = split(normed.T)
            g_hi[at:at + rows], g_lo[at:at + rows] = split(cot[...] * scale_ref[0, 0])
        if begun:
            out_ref[...] = so_far[0][...]
            gnorm_ref[...] = so_far[1][...]
        else:
            out_ref[...] = jnp.zeros_like(out_ref)
            gnorm_ref[...] = jnp.zeros_like(gnorm_ref)

    for at in range(count):
        spot = (chip_ref[0] ^ at) if count > 1 else 0
        up_rows = up_refs[at].shape[0]
        high, low = split(up_refs[at][...])
        here = pl.ds(pl.multiple_of(spot * up_rows, up_rows), up_rows)
        up_hi[here], up_lo[here] = high, low
        block = down_refs[at][...]
        block = block.reshape(-1, block.shape[-1])
        high, low = split(block)
        here = pl.ds(pl.multiple_of(spot * block.shape[0], block.shape[0]), block.shape[0])
        down_hi[here], down_lo[here] = high, low

    chips, _, tall, width = grad_ref.shape
    up_tall = up_hi.shape[0] // chips
    deep = down_hi.shape[0] // chips
    half = deep // 2
    for ref in packed_ref:
        for at in range(chips):
            high, low = split(ref[at])
            here = slice(at * up_tall, (at + 1) * up_tall)
            up_hi[here], up_lo[here] = high[:up_tall], low[:up_tall]
            here = slice(at * deep, (at + 1) * deep)
            for part, target in ((high, down_hi), (low, down_lo)):
                target[here, :width] = part[up_tall:up_tall + deep]
                right = part[up_tall + deep:]
                target[here, width:] = jnp.concatenate(
                    [right[:, :width // 2], right[:, width // 2:]], axis=0
                )
    up = (up_hi[...], up_lo[...])
    down = (down_hi[...], down_lo[...])
    normed = (x_hi[...], x_lo[...])
    normed_t = (xt_hi[...], xt_lo[...])
    grad_block = (g_hi[...], g_lo[...])
    pre = three(dot_nn, normed, up)
    grad_act = three(dot_nt, grad_block, down)
    inner = 0.7978845608028654 * (pre + 0.044715 * pre * pre * pre)
    bent = jnp.tanh(inner)
    act = 0.5 * pre * (1.0 + bent)
    slope = 0.5 * (1.0 + bent) + 0.5 * pre * (1.0 - bent * bent) * (
        0.7978845608028654 * (1.0 + 3.0 * 0.044715 * pre * pre)
    )
    act2 = split(act)
    grad_pre = split(grad_act * slope)
    out_ref[...] += three(dot_nn, act2, down)
    gnorm_ref[...] += three(dot_nt, grad_pre, up)
    gup = three(dot_nn, normed_t, grad_pre)
    gdown = three(dot_tn, act2, grad_block)
    for chip in range(chips):
        grad_ref[chip, 0, :up_tall] = gup[chip * up_tall:(chip + 1) * up_tall]
        part = gdown[chip * deep:(chip + 1) * deep]
        grad_ref[chip, 0, up_tall:up_tall + deep] = part[:, :width]
        grad_ref[chip, 0, up_tall + deep:] = jnp.concatenate(
            [part[:half, width:], part[half:, width:]], axis=1
        )


def mlp(first, steps, so_far, chip, chips, resid, other, cot, cot_other, gain, bias, scale, ups, downs):
    rows, model = resid.shape
    width = 512
    up_tall = model // chips
    deep = width // chips
    fixed = lambda shape: pl.BlockSpec(shape, lambda j, c: (0, 0))
    pieces = len(downs)
    if pieces == 0:
        up_specs = [pl.BlockSpec(ups[0].shape, lambda j, c: (0, 0, 0))]
    else:
        up_specs = [
            pl.BlockSpec((up.shape[0], width), lambda j, c: (0, first + j)) for up in ups
        ]
    if pieces != 1:
        down_spec = pl.BlockSpec((deep, model), lambda j, c: (first + j, 0))
    else:
        downs = [downs[0].reshape(chips, -1, model)]
        down_spec = pl.BlockSpec((chips, deep, model), lambda j, c: (0, first + j, 0))
    tall = up_tall + deep + deep // 2
    grid_spec = pltpu.PrefetchScalarGridSpec(
        num_scalar_prefetch=1,
        grid=(steps,),
        in_specs=[fixed((rows, model))] * 4 + [fixed((1, model))] * 2
        + [pl.BlockSpec(memory_space=pltpu.SMEM)]
        + up_specs
        + [down_spec] * len(downs)
        + [fixed((2 * rows, model))] * len(so_far),
        out_specs=[
            fixed((2 * rows, model)), fixed((2 * rows, model)),
            pl.BlockSpec((chips, 1, tall, width), lambda j, c: (0, j, 0, 0)),
        ],
        scratch_shapes=[
            pltpu.VMEM((2 * rows, model), BF16), pltpu.VMEM((2 * rows, model), BF16),
            pltpu.VMEM((model, 2 * rows), BF16), pltpu.VMEM((model, 2 * rows), BF16),
            pltpu.VMEM((2 * rows, model), BF16), pltpu.VMEM((2 * rows, model), BF16),
            pltpu.VMEM((model, width), BF16), pltpu.VMEM((model, width), BF16),
            pltpu.VMEM((width, model), BF16), pltpu.VMEM((width, model), BF16),
        ],
    )
    return pl.pallas_call(
        functools.partial(mlp_kernel, pieces, len(so_far) // 2),
        grid_spec=grid_spec,
        out_shape=[
            jax.ShapeDtypeStruct((2 * rows, model), F32),
            jax.ShapeDtypeStruct((2 * rows, model), F32),
            jax.ShapeDtypeStruct((chips, steps, tall, width), F32),
        ],
        cost_estimate=cost(18 * steps),
        compiler_params=params(),
    )(chip, resid, other, cot, cot_other, gain, bias, scale, *ups, *downs, *so_far)


def fold_rows(values, width):
    rows = values.shape[0]
    right = values[:, width:]
    return jnp.concatenate(
        [
            values[:, :width],
            jnp.concatenate([right[:rows // 2], right[rows // 2:]], axis=1),
        ],
        axis=0,
    )


def unpack_grads(up, down, sibling_swap, core, chips):
    steps, up_tall, width = up.shape
    deep = up_tall * 2 // 3
    half = up_tall // 2
    mine = jnp.where(core == 0, up[:, :half], up[:, half:])
    other = sibling_swap(jnp.where(core == 0, up[:, half:], up[:, :half]))
    by_core = jnp.stack(
        [jnp.where(core == 0, mine, other), jnp.where(core == 0, other, mine)], axis=0
    )
    by_core = by_core.reshape(2, steps, half, chips, width // chips)
    grad_up = jnp.transpose(by_core, (2, 3, 0, 1, 4)).reshape(half, -1)
    quarter = width // 2
    tail = down[:, deep:]
    right = jnp.concatenate([tail[:, :, :quarter], tail[:, :, quarter:]], axis=1)
    grad_down = jnp.concatenate([down[:, :deep], right], axis=2).reshape(steps * deep, -1)
    return grad_up, grad_down


def resid_back_kernel(part_ref, given_ref, resid_ref, cot_ref, gain_ref, scale_ref, w_ref,
                      grad_ref, att_ref, sums_ref):
    grad = part_ref[...] + given_ref[...]
    xhat, rate = norm_stats(resid_ref[...])
    grad_resid = cot_ref[...] * scale_ref[0, 0] + norm_back(grad, gain_ref[...], xhat, rate)
    grad_ref[...] = grad_resid
    att_ref[...] = three(dot_nt, split(grad_resid), split(w_ref[...]))
    gain_sum = jnp.sum(grad * xhat, axis=0, keepdims=True)
    bias_sum = jnp.sum(grad, axis=0, keepdims=True)
    sums_ref[...] = jnp.concatenate(
        [gain_sum, bias_sum, jnp.zeros((6, gain_sum.shape[1]), F32)], axis=0
    )


def resid_back(part, given, resid, cot, gain, scale, w_full):
    rows, model = resid.shape
    fixed = lambda shape: pl.BlockSpec(shape, lambda j: (0, 0))
    return pl.pallas_call(
        resid_back_kernel,
        grid=(1,),
        in_specs=[fixed((rows, model))] * 4 + [fixed((1, model))]
        + [pl.BlockSpec(memory_space=pltpu.SMEM), fixed((model, model))],
        out_specs=[fixed((rows, model)), fixed((rows, model)), fixed((8, model))],
        out_shape=[
            jax.ShapeDtypeStruct((rows, model), F32),
            jax.ShapeDtypeStruct((rows, model), F32),
            jax.ShapeDtypeStruct((8, model), F32),
        ],
        cost_estimate=cost(6),
        compiler_params=params(),
    )(part, given, resid, cot, gain, scale, w_full)


def place_rows(core_ref, out_ref, got):
    chips = out_ref.shape[1]
    tall = out_ref.shape[2]
    for block in range(2 * chips):
        out_ref[(block & 1) ^ core_ref[0], block // 2] = got[block * tall:(block + 1) * tall]


def weights_qk_kernel(core_ref, hi_ref, lo_ref, dq_ref, dk_ref, out_ref, nt_hi, nt_lo):
    step = pl.program_id(0)
    part = pl.num_programs(0) // 2
    halo = hi_ref.shape[0] - dq_ref.shape[0]

    @pl.when(step == 0)
    def _():
        nt_hi[...] = hi_ref[...].T
        nt_lo[...] = lo_ref[...].T

    @pl.when(step < part)
    def _():
        left = (nt_hi[:, halo:], nt_lo[:, halo:])
        place_rows(core_ref, out_ref, three(dot_nn, left, split(dq_ref[...])))

    @pl.when(step >= part)
    def _():
        left = (nt_hi[...], nt_lo[...])
        place_rows(core_ref, out_ref, three(dot_nn, left, split(dk_ref[...])))


def weights_vo_kernel(core_ref, hi_ref, lo_ref, dv_ref, att_ref, res_ref, out_ref,
                      nt_hi, nt_lo, at_hi, at_lo):
    step = pl.program_id(0)
    part = pl.num_programs(0) // 2

    @pl.when(step == 0)
    def _():
        nt_hi[...] = hi_ref[...].T
        nt_lo[...] = lo_ref[...].T
        at_hi[...], at_lo[...] = split(att_ref[...].T)

    @pl.when(step < part)
    def _():
        left = (nt_hi[...], nt_lo[...])
        place_rows(core_ref, out_ref, three(dot_nn, left, split(dv_ref[...])))

    @pl.when(step >= part)
    def _():
        left = (at_hi[...], at_lo[...])
        place_rows(core_ref, out_ref, three(dot_nn, left, split(res_ref[...])))


def weight_call(kernel, micros, core, chips, fixed_args, pieces, scratch):
    model = fixed_args[0].shape[1]
    wide = 256
    part = model // wide
    tall = model // chips // 2
    fixed = lambda v: pl.BlockSpec(v.shape, lambda j, c: (0, 0))
    piece = lambda v, at: pl.BlockSpec(
        (v.shape[0], wide), lambda j, c: (0, jnp.clip(j - at * part, 0, part - 1))
    )
    specs, args = [], []
    for value, at in pieces:
        args.append(value)
        specs.append(fixed(value) if at is None else piece(value, at))
    return pl.pallas_call(
        kernel,
        grid_spec=pltpu.PrefetchScalarGridSpec(
            num_scalar_prefetch=1,
            grid=(2 * part,),
            in_specs=[fixed(v) for v in fixed_args] + specs,
            out_specs=pl.BlockSpec((2, chips, tall, wide), lambda j, c: (0, 0, 0, j)),
            scratch_shapes=[pltpu.VMEM((model, n), BF16) for n in scratch],
        ),
        out_shape=jax.ShapeDtypeStruct((2, chips, tall, 2 * model), F32),
        cost_estimate=cost(micros),
        compiler_params=params(),
    )(core, *fixed_args, *args)


def matmul(left, right):
    return jnp.dot(left, right, precision=HIGH)


def inner_rows(left, right):
    return lax.dot_general(left, right, (((0,), (0,)), ((), ())), precision=HIGH)


def outer_cols(left, right):
    return lax.dot_general(left, right, (((1,), (1,)), ((), ())), precision=HIGH)


def body(
    block_input,
    embedding,
    earlier_outs,
    dwa_weights,
    ln1_gain,
    ln1_bias,
    w_qkv,
    w_out,
    ln2_gain,
    ln2_bias,
    w_up,
    w_down,
    segments,
    cotangent,
):
    groups = lax.axis_size("seq")
    rows, model = block_input.shape
    length = rows * groups
    halo = 2 * rows
    place = lax.axis_index("seq")
    ahead = [(i, i + 1) for i in range(groups - 1)]
    behind = [(i + 1, i) for i in range(groups - 1)]
    gain1, bias1 = ln1_gain[None], ln1_bias[None]
    gain2, bias2 = ln2_gain[None], ln2_bias[None]

    devices = lax.axis_size("dp")
    chips = devices // 2
    spot = lax.axis_index("dp")
    core = spot % 2
    chip = (spot // 2).reshape(1).astype(jnp.int32)
    same_core = [[2 * i + c for i in range(chips)] for c in range(2)]
    exchange = lambda v, bit: lax.ppermute(v, "dp", [(i, i ^ bit) for i in range(devices)])
    swap = lambda v: exchange(v, 1)

    gather = lambda v: lax.all_gather(v, "dp", axis=0, tiled=True)
    qkv_full = gather(w_qkv)

    shard = w_down.shape[0]
    third = shard // 3
    by_core = w_up.reshape(w_up.shape[0], chips, 2, 3, third)
    by_core = jnp.transpose(by_core, (2, 0, 3, 1, 4)).reshape(2, w_up.shape[0], -1)
    mine = jnp.where(core == 0, by_core[0], by_core[1])
    given = swap(jnp.where(core == 0, by_core[1], by_core[0]))
    together = lax.optimization_barrier
    up_chip = jnp.concatenate(
        [jnp.where(core == 0, mine, given), jnp.where(core == 0, given, mine)], axis=0
    )
    width = up_chip.shape[1] // 3

    chip_gather = functools.partial(
        lax.all_gather, axis_name="dp", axis=0, axis_index_groups=same_core
    )

    up_near, down_near = up_chip[:, :2 * width], w_down[:2 * third]
    if chips == 4:
        sides = [
            exchange(up_near, 2), exchange(up_near, 4),
            exchange(down_near, 2), exchange(down_near, 4),
        ]
    else:
        sides = []
    packed = chip_gather(
        jnp.concatenate([up_chip[:, 2 * width:], fold_rows(w_down[2 * third:], width)], axis=0)
    )

    seg_own = segments + 1
    near = lax.ppermute(block_input, "seq", ahead)
    seg_near = lax.ppermute(seg_own, "seq", ahead)
    far = lax.ppermute(near, "seq", ahead)
    seg_far = lax.ppermute(seg_near, "seq", ahead)
    seg_all = jnp.concatenate([seg_far, seg_near, seg_own], axis=1)
    seg_k_row = jnp.broadcast_to(seg_all, (8, halo + rows))
    seg_k_col = jnp.broadcast_to(seg_all.reshape(-1, 1), (halo + rows, 128))
    seg_q_row = seg_k_row[:, halo:]
    seg_q_col = seg_k_col[halo:]

    cos_all, sin_all = rotary_tables(length, halo)
    cosine = lax.dynamic_slice_in_dim(jnp.asarray(cos_all), place * rows, halo + rows, 0)
    sine = lax.dynamic_slice_in_dim(jnp.asarray(sin_all), place * rows, halo + rows, 0)

    earlier = (embedding, earlier_outs[0], earlier_outs[1], earlier_outs[2])
    base = sum(dwa_weights[i] * value for i, value in enumerate(earlier))
    dots = jnp.stack([jnp.sum(cotangent * value) for value in earlier])
    far, base, dots, sides = together((far, base, dots, sides))

    q_rot, kv, normed_hi, normed_lo = project(
        far, near, block_input, gain1, bias1, qkv_full, cosine, sine
    )
    if chips == 4:
        diagonal = [exchange(sides[1], 2), exchange(sides[2], 4)]
        q_rot, diagonal = together((q_rot, diagonal))
        near_weights = (
            [up_near, sides[0], sides[1], diagonal[0]],
            [down_near, sides[2], sides[3], diagonal[1]],
        )
    else:
        near_weights = tuple([chip_gather(v, tiled=True)] for v in (up_near, down_near))
    attended = attend(q_rot, kv, seg_q_col, seg_k_row)

    out_full = gather(w_out)
    resid = block_input + matmul(attended, out_full)
    resid_other = swap(resid)
    cot_other = swap(cotangent)
    scale = dwa_weights[4].reshape(1, 1)
    call = functools.partial(
        mlp, chip=chip, chips=chips, resid=resid, other=resid_other, cot=cotangent,
        cot_other=cot_other, gain=gain2, bias=bias2, scale=scale,
    )
    scatter = lambda v: lax.psum_scatter(v, "dp", scatter_dimension=0, tiled=True)
    scatter_chips = lambda v: lax.psum_scatter(
        v, "dp", scatter_dimension=0, tiled=True, axis_index_groups=same_core
    )
    so_far, shards = (), []
    for third_at in range(3):
        ups, downs = near_weights if third_at < 2 else ([packed], [])
        out_part, gnorm_part, grads = call(third_at, 1, so_far, ups=ups, downs=downs)
        so_far = (out_part, gnorm_part)
        shards.append(scatter_chips(grads)[0])
    given = swap(gnorm_part[rows:])

    shift = lambda v, bit: lax.ppermute(v, "seq", [(i, i ^ bit) for i in range(groups)])
    even = place % 2 == 0

    def line_start(shard):
        tall = shard.shape[1] // 2
        halves = (shard[:, :tall], shard[:, tall:])
        kept = jnp.where(even, halves[0], halves[1])
        return kept + shift(jnp.where(even, halves[1], halves[0]), 1)

    def line_middle(kept):
        bit = 2
        while bit < groups:
            kept = kept + shift(kept, bit)
            bit *= 2
        return kept

    def line_end(kept):
        other = shift(kept, 1)
        return jnp.where(even, kept, other), jnp.where(even, other, kept)

    shards[0], given = together((shards[0], given))
    line_a = line_start(shards[0])
    grad_resid, grad_attended, sums_two = resid_back(
        gnorm_part, given, resid, cotangent, gain2, scale, out_full
    )

    back_args = (q_rot, kv, grad_attended, seg_q_row, seg_k_col, cosine, sine)
    pairs = model // 128
    line_a, back_args = together((line_a, back_args))
    line_a = line_middle(line_a)
    first_half = attend_back(0, pairs // 2, *back_args)
    line_a, shards[1], back_args, first_half = together(
        (line_a, shards[1], back_args, first_half)
    )
    line_b = line_start(shards[1])
    ends_a = line_end(line_a)
    dq, dk, dv = attend_back(pairs // 2, pairs - pairs // 2, *back_args, before=first_half)
    line_b, ends_a, dq, dk, dv = together((line_b, ends_a, dq, dk, dv))
    line_b = line_middle(line_b)
    core_at = core.reshape(1).astype(jnp.int32)
    normed_parts = (normed_hi, normed_lo)
    grads_qk = weight_call(
        weights_qk_kernel, 9, core_at, chips, normed_parts, [(dq, 0), (dk, 1)], [halo + rows] * 2
    )
    given_qk = swap(grads_qk[1])
    line_b, shards[2], dv, grad_resid = together((line_b, shards[2], dv, grad_resid))
    ends_b = line_end(line_b)
    line_c = line_start(shards[2])
    grads_vo = weight_call(
        weights_vo_kernel, 9, core_at, chips, normed_parts,
        [(dv, 0), (attended, None), (grad_resid, 1)], [halo + rows] * 2 + [rows] * 2,
    )
    line_c, grads_vo = together((line_c, grads_vo))
    line_c = line_middle(line_c)
    grads_c = jnp.concatenate([grads_qk[0] + given_qk, grads_vo[0] + swap(grads_vo[1])], axis=2)
    grads_c, out_part = together((grads_c, out_part))
    shard_c = scatter_chips(grads_c)[0]
    out_sib = swap(out_part[rows:])
    dkv = jnp.concatenate([dk, dv], axis=1)

    block_out = resid + out_part[:rows] + out_sib
    output = base + dwa_weights[4] * block_out
    dwa_local = jnp.concatenate([dots, jnp.sum(cotangent * block_out)[None]])

    wq, wkv = qkv_full[:, :model], qkv_full[:, model:]
    partial = outer_cols(dkv, wkv)
    line_c, ends_b, partial = together((line_c, ends_b, partial))
    ends_c = line_end(line_c)
    own_part = partial[halo:] + outer_cols(dq, wq)
    (sent,) = together((partial,))
    back_near = sent[rows:halo] + lax.ppermute(sent[:rows], "seq", behind)

    xhat1, rate1 = norm_stats(block_input)
    terms = (
        (norm_stats(far)[0], partial[:rows]),
        (norm_stats(near)[0], partial[rows:halo]),
        (xhat1, own_part),
    )
    grad_gain_one = sum(jnp.sum(xhat * part, axis=0) for xhat, part in terms)
    grad_bias_one = sum(jnp.sum(part, axis=0) for _, part in terms)

    small = jnp.concatenate(
        [
            grad_gain_one[None], grad_bias_one[None], sums_two[:2],
            jnp.pad(dwa_local, (0, model - 5))[None], jnp.zeros((3, model), F32),
        ],
        axis=0,
    )
    bit = 1
    while bit < devices:
        small = small + exchange(small, bit)
        bit *= 2
    given_back = lax.ppermute(back_near, "seq", behind)
    shard_c, ends_c, given_back, small = together((shard_c, ends_c, given_back, small))
    last = line_middle(line_start(shard_c[None]))
    grad_normed_one = own_part + given_back
    grad_input = grad_resid + norm_back(grad_normed_one, gain1, xhat1, rate1)
    grad_up, grad_down = unpack_grads(
        *(
            jnp.concatenate(parts, axis=0)
            for parts in zip(ends_a, ends_b, ends_c)
        ),
        swap, core, chips,
    )
    last, grad_up, grad_down, small, grad_input = together(
        (last, grad_up, grad_down, small, grad_input)
    )
    bit = 1
    while bit < groups:
        small = small + shift(small, bit)
        bit *= 2
    gain_one, bias_one, gain_two, bias_two = small[0], small[1], small[2], small[3]
    grad_dwa = small[4, :5]
    last = jnp.concatenate(line_end(last), axis=1)[0]
    grad_qkv, grad_wout = last[:, :3 * model], last[:, 3 * model:]
    return (
        output,
        grad_input,
        grad_dwa,
        gain_one,
        bias_one,
        grad_qkv,
        grad_wout,
        gain_two,
        bias_two,
        grad_up,
        grad_down,
    )


def solution(mesh):
    in_specs = (
        P(("dp", "seq"), None),
        P(("dp", "seq"), None),
        P(None, ("dp", "seq"), None),
        P(),
        P(),
        P(),
        P("dp", None),
        P("dp", None),
        P(),
        P(),
        P("dp", None),
        P("dp", None),
        P("dp", "seq"),
        P(("dp", "seq"), None),
    )
    out_specs = (
        P(("dp", "seq"), None),
        P(("dp", "seq"), None),
        P(),
        P(),
        P(),
        P("dp", None),
        P("dp", None),
        P(),
        P(),
        P("dp", None),
        P("dp", None),
    )
    return jax.shard_map(body, mesh=mesh, in_specs=in_specs, out_specs=out_specs, check_vma=False)
```

```python
import functools
import math

import jax
import jax.numpy as jnp
import numpy as np
from jax import lax
from jax.experimental import pallas as pl
from jax.experimental.pallas import tpu as pltpu
from jax.sharding import PartitionSpec as P

HD = 64
DOC_MOST = 768
LOG2E = math.log2(math.e)
SCALE = 1.0 / math.sqrt(HD)
NEG = -1e30
F32 = jnp.float32
BF16 = jnp.bfloat16
HIGH = lax.Precision.HIGH
VMEM_LIMIT = 56 * 1024 * 1024
BLK = 128


def cost(micros):
    return pl.CostEstimate(
        flops=int(micros * 1.1e9), bytes_accessed=1 << 20, transcendentals=0
    )


def params():
    return pltpu.CompilerParams(
        dimension_semantics=("arbitrary",), vmem_limit_bytes=VMEM_LIMIT
    )


def split(values):
    high = values.astype(BF16)
    return high, (values - high.astype(F32)).astype(BF16)


def dot_nn(left, right):
    return lax.dot_general(left, right, (((1,), (0,)), ((), ())), preferred_element_type=F32)


def dot_nt(left, right):
    return lax.dot_general(left, right, (((1,), (1,)), ((), ())), preferred_element_type=F32)


def dot_tn(left, right):
    return lax.dot_general(left, right, (((0,), (0,)), ((), ())), preferred_element_type=F32)


def three(dot, left, right):
    return (
        dot(left[0], right[0]) + dot(left[0], right[1]) + dot(left[1], right[0])
    )


def norm_stats(values):
    row_mean = jnp.mean(values, axis=-1, keepdims=True)
    centred = values - row_mean
    row_var = jnp.mean(centred * centred, axis=-1, keepdims=True)
    rate = lax.rsqrt(row_var + 1e-05)
    return centred * rate, rate


def norm_back(grad, gain, xhat, rate):
    scaled = grad * gain
    return rate * (
        scaled
        - jnp.mean(scaled, axis=-1, keepdims=True)
        - xhat * jnp.mean(scaled * xhat, axis=-1, keepdims=True)
    )


def turned(values):
    lane = lax.broadcasted_iota(jnp.int32, values.shape, 1)
    return jnp.where(
        (lane & 63) < 32, pltpu.roll(values, 96, 1), pltpu.roll(values, 32, 1)
    )


def rotate(values, cosine, sine):
    return values * cosine + turned(values) * sine


def unrotate(values, cosine, sine):
    return values * cosine - turned(values) * sine


def rotary_tables(length, halo):
    half = HD // 2
    inv_freq = (10000.0 ** (-(np.arange(half, dtype=np.float32) * 2.0 / HD))).astype(np.float32)
    place = np.arange(-halo, length, dtype=np.float32)
    angles = place[:, None] * inv_freq[None, :]
    cosine = np.cos(angles.astype(np.float64)).astype(np.float32)
    sine = np.sin(angles.astype(np.float64)).astype(np.float32)
    return (
        np.concatenate([cosine] * 4, axis=1),
        np.concatenate([-sine, sine, -sine, sine], axis=1),
    )


def qkv_kernel(far_ref, near_ref, own_ref, gain_ref, bias_ref, w_ref, cos_ref, sin_ref,
               q_ref, kv_ref, hi_ref, lo_ref):
    step = pl.program_id(0)
    rows = own_ref.shape[0]
    third = pl.num_programs(0) // 3
    halo = hi_ref.shape[0] - rows

    @pl.when(step == 0)
    def _():
        for at, ref in enumerate((far_ref, near_ref, own_ref)):
            xhat, _ = norm_stats(ref[...])
            high, low = split(xhat * gain_ref[...] + bias_ref[...])
            hi_ref[at * rows:(at + 1) * rows] = high
            lo_ref[at * rows:(at + 1) * rows] = low

    weights = split(w_ref[...])

    @pl.when(step < third)
    def _():
        got = three(dot_nn, (hi_ref[halo:], lo_ref[halo:]), weights)
        for at in range(0, got.shape[1], 128):
            q_ref[:, at:at + 128] = rotate(got[:, at:at + 128], cos_ref[halo:], sin_ref[halo:])

    @pl.when((step >= third) & (step < 2 * third))
    def _():
        got = three(dot_nn, (hi_ref[...], lo_ref[...]), weights)
        for at in range(0, got.shape[1], 128):
            kv_ref[:, at:at + 128] = rotate(got[:, at:at + 128], cos_ref[...], sin_ref[...])

    @pl.when(step >= 2 * third)
    def _():
        kv_ref[...] = three(dot_nn, (hi_ref[...], lo_ref[...]), weights)


def project(far, near, own, gain, bias, w_full, cosine, sine):
    rows, model = own.shape
    total = 3 * rows
    wide = 256
    third = model // wide
    whole = lambda shape: pl.BlockSpec(shape, lambda j: (0, 0))
    return pl.pallas_call(
        qkv_kernel,
        grid=(3 * third,),
        in_specs=[
            whole((rows, model)), whole((rows, model)), whole((rows, model)),
            whole((1, model)), whole((1, model)),
            pl.BlockSpec((model, wide), lambda j: (0, j)),
            whole((total, 128)), whole((total, 128)),
        ],
        out_specs=[
            pl.BlockSpec((rows, wide), lambda j: (0, jnp.minimum(j, third - 1))),
            pl.BlockSpec((total, wide), lambda j: (0, jnp.maximum(j - third, 0))),
            whole((total, model)), whole((total, model)),
        ],
        out_shape=[
            jax.ShapeDtypeStruct((rows, model), F32),
            jax.ShapeDtypeStruct((total, 2 * model), F32),
            jax.ShapeDtypeStruct((total, model), BF16),
            jax.ShapeDtypeStruct((total, model), BF16),
        ],
        cost_estimate=cost(0.5),
        compiler_params=params(),
    )(far, near, own, gain, bias, w_full, cosine, sine)


def own_pair(values, head):
    lane = lax.broadcasted_iota(jnp.int32, values.shape, 1)
    other = pltpu.roll(values, 64, 1)
    return jnp.where((lane < 64) == (head == 0), values, other)


def outer_form(values, head):
    high, low = split(own_pair(values, head))
    return jnp.concatenate([high, low], axis=1)


def mixed(values, head):
    pair = own_pair(values, head)
    lane = lax.broadcasted_iota(jnp.int32, pair.shape, 1)
    high = pair.astype(BF16).astype(F32)
    return jnp.where(lane < 64, high, pair - high).astype(BF16)


def inner_form(values, head):
    half = mixed(values, head)
    return jnp.concatenate([half, half], axis=1)


def fold(values):
    return values + pltpu.roll(values, 64, 1)


def attend_kernel(q_ref, k_ref, v_ref, segq_ref, segk_ref, out_ref, bias_ref):
    rows = q_ref.shape[0]
    halo = k_ref.shape[0] - rows
    span = halo + BLK

    @pl.when(pl.program_id(0) == 0)
    def _():
        for at in range(0, rows, BLK):
            row = lax.broadcasted_iota(jnp.int32, (BLK, span), 0)
            col = lax.broadcasted_iota(jnp.int32, (BLK, span), 1)
            same = segq_ref[at:at + BLK, :1] == segk_ref[:1, at:at + span]
            bias_ref[at:at + BLK] = jnp.where(same & (col - halo <= row), 0.0, NEG)

    lane = lax.broadcasted_iota(jnp.int32, (BLK, 128), 1)
    scaled = q_ref[...] * (SCALE * LOG2E)
    results = []
    for head in range(2):
        left = inner_form(scaled, head)
        right = outer_form(k_ref[...], head)
        vals = mixed(v_ref[...], head)
        outs = []
        for at in range(0, rows, BLK):
            scores = dot_nt(left[at:at + BLK], right[at:at + span]) + bias_ref[at:at + BLK]
            top = jnp.max(scores, axis=1, keepdims=True)
            expo = jnp.exp2(scores - top)
            total = jnp.sum(expo, axis=1, keepdims=True)
            high, low = split(expo)
            got = dot_nn(high, vals[at:at + span]) + dot_nn(low, vals[at:at + span])
            outs.append(fold(got) / total)
        results.append(outs)
    for at in range(0, rows, BLK):
        out_ref[at:at + BLK] = jnp.where(
            lane < 64, results[0][at // BLK], results[1][at // BLK]
        )


def attend(q_rot, kv, seg_q, seg_k):
    rows, model = q_rot.shape
    total = kv.shape[0]
    pairs = model // 128
    return pl.pallas_call(
        attend_kernel,
        grid=(pairs,),
        in_specs=[
            pl.BlockSpec((rows, 128), lambda p: (0, p)),
            pl.BlockSpec((total, 128), lambda p: (0, p)),
            pl.BlockSpec((total, 128), lambda p: (0, pairs + p)),
            pl.BlockSpec((rows, 128), lambda p: (0, 0)),
            pl.BlockSpec((8, total), lambda p: (0, 0)),
        ],
        out_specs=pl.BlockSpec((rows, 128), lambda p: (0, p)),
        out_shape=jax.ShapeDtypeStruct((rows, model), F32),
        scratch_shapes=[pltpu.VMEM((rows, total - rows + BLK), F32)],
        cost_estimate=cost(0.5),
        compiler_params=params(),
    )(q_rot, kv, kv, seg_q, seg_k)


def attend_back_kernel(q_ref, k_ref, v_ref, g_ref, segq_ref, segk_ref, cos_ref, sin_ref, *refs):
    dq_ref, dk_ref, dv_ref, bias_ref = refs[-4:]
    rows = q_ref.shape[0]
    halo = k_ref.shape[0] - rows
    span = halo + BLK

    @pl.when(pl.program_id(0) == 0)
    def _():
        for at in range(0, rows, BLK):
            key = lax.broadcasted_iota(jnp.int32, (span, BLK), 0)
            query = lax.broadcasted_iota(jnp.int32, (span, BLK), 1)
            same = segk_ref[at:at + span, :1] == segq_ref[:1, at:at + BLK]
            bias_ref[:, at:at + BLK] = jnp.where(same & (key - halo <= query), 0.0, NEG)

    scaled = q_ref[...] * (SCALE * LOG2E)
    dq, dk, dv = [], [], []
    for head in range(2):
        q_in = inner_form(scaled, head)
        g_in = inner_form(g_ref[...], head)
        k_out = outer_form(k_ref[...], head)
        v_out = outer_form(v_ref[...], head)
        q_mix = mixed(q_ref[...], head)
        g_mix = mixed(g_ref[...], head)
        k_mix = mixed(k_ref[...], head)
        dq_head = []
        dk_head = jnp.zeros((halo + rows, 128), F32)
        dv_head = jnp.zeros((halo + rows, 128), F32)
        dk_parts, dv_parts = [], []
        for at in range(0, rows, BLK):
            scores = dot_nt(k_out[at:at + span], q_in[at:at + BLK]) + bias_ref[:, at:at + BLK]
            top = jnp.max(scores, axis=0, keepdims=True)
            expo = jnp.exp2(scores - top)
            inverse = 1.0 / jnp.sum(expo, axis=0, keepdims=True)
            grad_probs = dot_nt(v_out[at:at + span], g_in[at:at + BLK])
            probs = expo * inverse
            delta = jnp.sum(probs * grad_probs, axis=0, keepdims=True)
            grad_scores = probs * (grad_probs - delta)
            probs_cat = jnp.concatenate(split(probs), axis=1)
            scores_cat = jnp.concatenate(split(grad_scores), axis=1)
            g_two = jnp.concatenate([g_mix[at:at + BLK]] * 2, axis=0)
            q_two = jnp.concatenate([q_mix[at:at + BLK]] * 2, axis=0)
            dv_parts.append(dot_nn(probs_cat, g_two))
            dk_parts.append(dot_nn(scores_cat, q_two))
            got = dot_tn(scores_cat, k_mix[at:at + span])
            dq_head.append(fold(got[:BLK] + got[BLK:]))
        for parts, full in ((dk_parts, dk), (dv_parts, dv)):
            pieces = []
            for kb in range((halo + rows) // BLK):
                terms = [
                    parts[qb][(kb - qb) * BLK:(kb - qb + 1) * BLK]
                    for qb in range(rows // BLK)
                    if 0 <= kb - qb < span // BLK
                ]
                pieces.append(fold(functools.reduce(lambda a, b: a + b, terms)))
            full.append(pieces)
        dq.append(dq_head)
    lane = lax.broadcasted_iota(jnp.int32, (BLK, 128), 1)
    for qb in range(rows // BLK):
        rng = slice(qb * BLK, (qb + 1) * BLK)
        far = slice(halo + qb * BLK, halo + (qb + 1) * BLK)
        both = jnp.where(lane < 64, dq[0][qb], dq[1][qb]) * SCALE
        dq_ref[rng] = unrotate(both, cos_ref[far], sin_ref[far])
    for kb in range((halo + rows) // BLK):
        rng = slice(kb * BLK, (kb + 1) * BLK)
        both = jnp.where(lane < 64, dk[0][kb], dk[1][kb]) * SCALE
        dk_ref[rng] = unrotate(both, cos_ref[rng], sin_ref[rng])
        dv_ref[rng] = jnp.where(lane < 64, dv[0][kb], dv[1][kb])


def attend_back(first, count, q_rot, kv, grad, seg_q, seg_k, cosine, sine, before=()):
    rows, model = q_rot.shape
    total = kv.shape[0]
    pairs = model // 128
    fixed = lambda shape: pl.BlockSpec(shape, lambda p: (0, 0))
    return pl.pallas_call(
        attend_back_kernel,
        grid=(count,),
        in_specs=[
            pl.BlockSpec((rows, 128), lambda p: (0, first + p)),
            pl.BlockSpec((total, 128), lambda p: (0, first + p)),
            pl.BlockSpec((total, 128), lambda p: (0, pairs + first + p)),
            pl.BlockSpec((rows, 128), lambda p: (0, first + p)),
            fixed((8, rows)), fixed((total, 128)),
            fixed((total, 128)), fixed((total, 128)),
        ] + [pl.BlockSpec(memory_space=pl.ANY)] * len(before),
        out_specs=[
            pl.BlockSpec((rows, 128), lambda p: (0, first + p)),
            pl.BlockSpec((total, 128), lambda p: (0, first + p)),
            pl.BlockSpec((total, 128), lambda p: (0, first + p)),
        ],
        out_shape=[
            jax.ShapeDtypeStruct((rows, model), F32),
            jax.ShapeDtypeStruct((total, model), F32),
            jax.ShapeDtypeStruct((total, model), F32),
        ],
        scratch_shapes=[pltpu.VMEM((total - rows + BLK, rows), F32)],
        input_output_aliases={8 + i: i for i in range(len(before))},
        cost_estimate=cost(7 * count),
        compiler_params=params(),
    )(q_rot, kv, kv, grad, seg_q, seg_k, cosine, sine, *before)


def mlp_kernel(count, begun, chip_ref, resid_ref, other_ref, cot_ref, cot_other_ref, gain_ref, bias_ref,
               scale_ref, *refs):
    weight_refs, refs = refs[:max(1, 2 * count)], refs[max(1, 2 * count):]
    so_far, refs = refs[:2 * begun], refs[2 * begun:]
    out_ref, gnorm_ref, grad_ref = refs[:3]
    (x_hi, x_lo, xt_hi, xt_lo, g_hi, g_lo, up_hi, up_lo, down_hi, down_lo) = refs[3:]
    step = pl.program_id(0)
    rows = resid_ref.shape[0]

    @pl.when(step == 0)
    def _():
        for at, source, cot in ((0, resid_ref, cot_ref), (rows, other_ref, cot_other_ref)):
            xhat, _ = norm_stats(source[...])
            normed = xhat * gain_ref[...] + bias_ref[...]
            x_hi[at:at + rows], x_lo[at:at + rows] = split(normed)
            xt_hi[:, at:at + rows], xt_lo[:, at:at + rows] = split(normed.T)
            g_hi[at:at + rows], g_lo[at:at + rows] = split(cot[...] * scale_ref[0, 0])
        if begun:
            out_ref[...] = so_far[0][...]
            gnorm_ref[...] = so_far[1][...]
        else:
            out_ref[...] = jnp.zeros_like(out_ref)
            gnorm_ref[...] = jnp.zeros_like(gnorm_ref)

    chips, _, tall, width = grad_ref.shape
    up_tall = up_hi.shape[0] // chips
    deep = down_hi.shape[0] // chips
    half = deep // 2

    def place(spot, values, targets, folded):
        for part, target in zip(split(values), targets):
            if folded:
                here = pl.ds(pl.multiple_of(spot * deep, deep), deep)
                target[here, :width] = part[:deep]
                target[here, width:] = jnp.concatenate(
                    [part[deep:, :width // 2], part[deep:, width // 2:]], axis=0
                )
            else:
                target[pl.ds(pl.multiple_of(spot * up_tall, up_tall), up_tall)] = part

    for at in range(count):
        place(chip_ref[0] ^ at, weight_refs[at][...], (up_hi, up_lo), False)
        place(chip_ref[0] ^ at, weight_refs[count + at][...], (down_hi, down_lo), True)
    if count == 0:
        for at in range(chips):
            place(at, weight_refs[0][at, :up_tall], (up_hi, up_lo), False)
            place(at, weight_refs[0][at, up_tall:], (down_hi, down_lo), True)
    up = (up_hi[...], up_lo[...])
    down = (down_hi[...], down_lo[...])
    normed = (x_hi[...], x_lo[...])
    normed_t = (xt_hi[...], xt_lo[...])
    grad_block = (g_hi[...], g_lo[...])
    pre = three(dot_nn, normed, up)
    grad_act = three(dot_nt, grad_block, down)
    inner = 0.7978845608028654 * (pre + 0.044715 * pre * pre * pre)
    bent = jnp.tanh(inner)
    act = 0.5 * pre * (1.0 + bent)
    slope = 0.5 * (1.0 + bent) + 0.5 * pre * (1.0 - bent * bent) * (
        0.7978845608028654 * (1.0 + 3.0 * 0.044715 * pre * pre)
    )
    act2 = split(act)
    grad_pre = split(grad_act * slope)
    out_ref[...] += three(dot_nn, act2, down)
    gnorm_ref[...] += three(dot_nt, grad_pre, up)
    gup = three(dot_nn, normed_t, grad_pre)
    gdown = three(dot_tn, act2, grad_block)
    for chip in range(chips):
        grad_ref[chip, 0, :up_tall] = gup[chip * up_tall:(chip + 1) * up_tall]
        part = gdown[chip * deep:(chip + 1) * deep]
        grad_ref[chip, 0, up_tall:up_tall + deep] = part[:, :width]
        grad_ref[chip, 0, up_tall + deep:] = jnp.concatenate(
            [part[:half, width:], part[half:, width:]], axis=1
        )


def mlp(so_far, weights, chip, chips, resid, other, cot, cot_other, gain, bias, scale):
    rows, model = resid.shape
    width = 512
    up_tall = model // chips
    deep = width // chips
    fixed = lambda shape: pl.BlockSpec(shape, lambda j, c: (0, 0))
    if len(weights) > 1:
        specs = [
            pl.BlockSpec((up_tall, width), lambda j, c, at=at: (at, 0)) for _, at in weights
        ]
        weights = [value for value, _ in weights]
    else:
        specs = [pl.BlockSpec(weights[0].shape, lambda j, c: (0, 0, 0))]
    count = len(weights) // 2
    tall = up_tall + deep + deep // 2
    grid_spec = pltpu.PrefetchScalarGridSpec(
        num_scalar_prefetch=1,
        grid=(1,),
        in_specs=[fixed((rows, model))] * 4 + [fixed((1, model))] * 2
        + [pl.BlockSpec(memory_space=pltpu.SMEM)]
        + specs
        + [fixed((2 * rows, model))] * len(so_far),
        out_specs=[
            fixed((2 * rows, model)), fixed((2 * rows, model)),
            pl.BlockSpec((chips, 1, tall, width), lambda j, c: (0, j, 0, 0)),
        ],
        scratch_shapes=[
            pltpu.VMEM((2 * rows, model), BF16), pltpu.VMEM((2 * rows, model), BF16),
            pltpu.VMEM((model, 2 * rows), BF16), pltpu.VMEM((model, 2 * rows), BF16),
            pltpu.VMEM((2 * rows, model), BF16), pltpu.VMEM((2 * rows, model), BF16),
            pltpu.VMEM((model, width), BF16), pltpu.VMEM((model, width), BF16),
            pltpu.VMEM((width, model), BF16), pltpu.VMEM((width, model), BF16),
        ],
    )
    return pl.pallas_call(
        functools.partial(mlp_kernel, count, len(so_far) // 2),
        grid_spec=grid_spec,
        out_shape=[
            jax.ShapeDtypeStruct((2 * rows, model), F32),
            jax.ShapeDtypeStruct((2 * rows, model), F32),
            jax.ShapeDtypeStruct((chips, 1, tall, width), F32),
        ],
        cost_estimate=cost(18),
        compiler_params=params(),
    )(chip, resid, other, cot, cot_other, gain, bias, scale, *weights, *so_far)


def fold_rows(values, width):
    rows = values.shape[0]
    right = values[:, width:]
    return jnp.concatenate(
        [
            values[:, :width],
            jnp.concatenate([right[:rows // 2], right[rows // 2:]], axis=1),
        ],
        axis=0,
    )


def unpack_grads(up, down, sibling_swap, core, chips):
    steps, up_tall, width = up.shape
    deep = up_tall * 2 // 3
    half = up_tall // 2
    mine = jnp.where(core == 0, up[:, :half], up[:, half:])
    other = sibling_swap(jnp.where(core == 0, up[:, half:], up[:, :half]))
    by_core = jnp.stack(
        [jnp.where(core == 0, mine, other), jnp.where(core == 0, other, mine)], axis=0
    )
    by_core = by_core.reshape(2, steps, half, chips, width // chips)
    grad_up = jnp.transpose(by_core, (2, 3, 0, 1, 4)).reshape(half, -1)
    quarter = width // 2
    tail = down[:, deep:]
    right = jnp.concatenate([tail[:, :, :quarter], tail[:, :, quarter:]], axis=1)
    grad_down = jnp.concatenate([down[:, :deep], right], axis=2).reshape(steps * deep, -1)
    return grad_up, grad_down


def resid_back_kernel(part_ref, given_ref, resid_ref, cot_ref, gain_ref, scale_ref, w_ref,
                      grad_ref, att_ref, sums_ref):
    grad = part_ref[...] + given_ref[...]
    xhat, rate = norm_stats(resid_ref[...])
    grad_resid = cot_ref[...] * scale_ref[0, 0] + norm_back(grad, gain_ref[...], xhat, rate)
    grad_ref[...] = grad_resid
    att_ref[...] = three(dot_nt, split(grad_resid), split(w_ref[...]))
    gain_sum = jnp.sum(grad * xhat, axis=0, keepdims=True)
    bias_sum = jnp.sum(grad, axis=0, keepdims=True)
    sums_ref[...] = jnp.concatenate(
        [gain_sum, bias_sum, jnp.zeros((6, gain_sum.shape[1]), F32)], axis=0
    )


def resid_back(part, given, resid, cot, gain, scale, w_full):
    rows, model = resid.shape
    fixed = lambda shape: pl.BlockSpec(shape, lambda j: (0, 0))
    return pl.pallas_call(
        resid_back_kernel,
        grid=(1,),
        in_specs=[fixed((rows, model))] * 4 + [fixed((1, model))]
        + [pl.BlockSpec(memory_space=pltpu.SMEM), fixed((model, model))],
        out_specs=[fixed((rows, model)), fixed((rows, model)), fixed((8, model))],
        out_shape=[
            jax.ShapeDtypeStruct((rows, model), F32),
            jax.ShapeDtypeStruct((rows, model), F32),
            jax.ShapeDtypeStruct((8, model), F32),
        ],
        cost_estimate=cost(6),
        compiler_params=params(),
    )(part, given, resid, cot, gain, scale, w_full)


def place_rows(core_ref, out_ref, got):
    chips = out_ref.shape[1]
    tall = out_ref.shape[2]
    for block in range(2 * chips):
        out_ref[(block & 1) ^ core_ref[0], block // 2] = got[block * tall:(block + 1) * tall]


def weights_qk_kernel(core_ref, hi_ref, lo_ref, dq_ref, dk_ref, out_ref, nt_hi, nt_lo):
    step = pl.program_id(0)
    part = pl.num_programs(0) // 2
    halo = hi_ref.shape[0] - dq_ref.shape[0]

    @pl.when(step == 0)
    def _():
        nt_hi[...] = hi_ref[...].T
        nt_lo[...] = lo_ref[...].T

    @pl.when(step < part)
    def _():
        left = (nt_hi[:, halo:], nt_lo[:, halo:])
        place_rows(core_ref, out_ref, three(dot_nn, left, split(dq_ref[...])))

    @pl.when(step >= part)
    def _():
        left = (nt_hi[...], nt_lo[...])
        place_rows(core_ref, out_ref, three(dot_nn, left, split(dk_ref[...])))


def weights_vo_kernel(core_ref, hi_ref, lo_ref, dv_ref, att_ref, res_ref, out_ref,
                      nt_hi, nt_lo, at_hi, at_lo):
    step = pl.program_id(0)
    part = pl.num_programs(0) // 2

    @pl.when(step == 0)
    def _():
        nt_hi[...] = hi_ref[...].T
        nt_lo[...] = lo_ref[...].T
        at_hi[...], at_lo[...] = split(att_ref[...].T)

    @pl.when(step < part)
    def _():
        left = (nt_hi[...], nt_lo[...])
        place_rows(core_ref, out_ref, three(dot_nn, left, split(dv_ref[...])))

    @pl.when(step >= part)
    def _():
        left = (at_hi[...], at_lo[...])
        place_rows(core_ref, out_ref, three(dot_nn, left, split(res_ref[...])))


def weight_call(kernel, micros, core, chips, fixed_args, pieces, scratch):
    model = fixed_args[0].shape[1]
    wide = 256
    part = model // wide
    tall = model // chips // 2
    fixed = lambda v: pl.BlockSpec(v.shape, lambda j, c: (0, 0))
    piece = lambda v, at: pl.BlockSpec(
        (v.shape[0], wide), lambda j, c: (0, jnp.clip(j - at * part, 0, part - 1))
    )
    specs, args = [], []
    for value, at in pieces:
        args.append(value)
        specs.append(fixed(value) if at is None else piece(value, at))
    return pl.pallas_call(
        kernel,
        grid_spec=pltpu.PrefetchScalarGridSpec(
            num_scalar_prefetch=1,
            grid=(2 * part,),
            in_specs=[fixed(v) for v in fixed_args] + specs,
            out_specs=pl.BlockSpec((2, chips, tall, wide), lambda j, c: (0, 0, 0, j)),
            scratch_shapes=[pltpu.VMEM((model, n), BF16) for n in scratch],
        ),
        out_shape=jax.ShapeDtypeStruct((2, chips, tall, 2 * model), F32),
        cost_estimate=cost(micros),
        compiler_params=params(),
    )(core, *fixed_args, *args)


def matmul(left, right):
    return jnp.dot(left, right, precision=HIGH)


def inner_rows(left, right):
    return lax.dot_general(left, right, (((0,), (0,)), ((), ())), precision=HIGH)


def outer_cols(left, right):
    return lax.dot_general(left, right, (((1,), (1,)), ((), ())), precision=HIGH)


def body(
    block_input,
    embedding,
    earlier_outs,
    dwa_weights,
    ln1_gain,
    ln1_bias,
    w_qkv,
    w_out,
    ln2_gain,
    ln2_bias,
    w_up,
    w_down,
    segments,
    cotangent,
):
    groups = lax.axis_size("seq")
    rows, model = block_input.shape
    length = rows * groups
    halo = 2 * rows
    place = lax.axis_index("seq")
    ahead = [(i, i + 1) for i in range(groups - 1)]
    behind = [(i + 1, i) for i in range(groups - 1)]
    gain1, bias1 = ln1_gain[None], ln1_bias[None]
    gain2, bias2 = ln2_gain[None], ln2_bias[None]

    devices = lax.axis_size("dp")
    chips = devices // 2
    spot = lax.axis_index("dp")
    core = spot % 2
    chip = (spot // 2).reshape(1).astype(jnp.int32)
    same_core = [[2 * i + c for i in range(chips)] for c in range(2)]
    exchange = lambda v, bit: lax.ppermute(v, "dp", [(i, i ^ bit) for i in range(devices)])
    swap = lambda v: exchange(v, 1)

    gather = lambda v: lax.all_gather(v, "dp", axis=0, tiled=True)
    qkv_full = gather(w_qkv)

    shard = w_down.shape[0]
    third = shard // 3
    by_core = w_up.reshape(w_up.shape[0], chips, 2, 3, third)
    by_core = jnp.transpose(by_core, (2, 0, 3, 1, 4)).reshape(2, w_up.shape[0], -1)
    mine = jnp.where(core == 0, by_core[0], by_core[1])
    given = swap(jnp.where(core == 0, by_core[1], by_core[0]))
    up_chip = jnp.concatenate(
        [jnp.where(core == 0, mine, given), jnp.where(core == 0, given, mine)], axis=0
    )
    width = up_chip.shape[1] // 3
    together = lax.optimization_barrier
    thirds = [
        (up_chip[:, i * width:(i + 1) * width], fold_rows(w_down[i * third:(i + 1) * third], width))
        for i in range(3)
    ]
    first_own = jnp.concatenate(thirds[0], axis=0)
    rest_own = jnp.concatenate([thirds[1][0], thirds[2][0], thirds[1][1], thirds[2][1]], axis=0)

    def sides_of(own):
        return [exchange(own, 2), exchange(own, 4)] if chips == 4 else []

    def diagonal_of(sides):
        if chips != 4:
            return []
        middle = sides[0].shape[0] // 2
        return [exchange(sides[1][:middle], 2), exchange(sides[0][middle:], 4)]

    def pieces(own, sides, diagonal, at):
        if chips != 4:
            own = own.reshape(2, -1, up_chip.shape[0], width)[:, at].reshape(-1, width)
            return [
                lax.all_gather(own, "dp", axis=0, axis_index_groups=same_core)
            ]
        below = own.shape[0] // up_chip.shape[0] // 2
        ups = [(own, at), (sides[0], at), (sides[1], at), (diagonal[0], at)]
        downs = [(value, below + at) for value in (own, *sides)] + [(diagonal[1], at)]
        return ups + downs

    first_sides = sides_of(first_own)
    first_diagonal = diagonal_of(first_sides)

    numbers = jnp.pad((segments + 1).astype(F32), ((0, 7), (0, model - rows)))
    near = lax.ppermute(jnp.concatenate([block_input, numbers], axis=0), "seq", ahead)
    far = lax.ppermute(near, "seq", ahead)
    seg_all = jnp.concatenate(
        [far[rows:rows + 1, :rows], near[rows:rows + 1, :rows], numbers[:1, :rows]], axis=1
    ).astype(jnp.int32)
    seg_k_row = jnp.broadcast_to(seg_all, (8, halo + rows))
    seg_k_col = jnp.broadcast_to(seg_all.reshape(-1, 1), (halo + rows, 128))
    seg_q_row = seg_k_row[:, halo:]
    seg_q_col = seg_k_col[halo:]

    cos_all, sin_all = rotary_tables(length, halo)
    cosine = lax.dynamic_slice_in_dim(jnp.asarray(cos_all), place * rows, halo + rows, 0)
    sine = lax.dynamic_slice_in_dim(jnp.asarray(sin_all), place * rows, halo + rows, 0)

    earlier = (embedding, earlier_outs[0], earlier_outs[1], earlier_outs[2])
    base = sum(dwa_weights[i] * value for i, value in enumerate(earlier))
    dots = jnp.stack([jnp.sum(cotangent * value) for value in earlier])
    qkv_full, rest_own, far, base, dots, first_sides, first_diagonal = together(
        (qkv_full, rest_own, far, base, dots, first_sides, first_diagonal)
    )
    rest_sides = sides_of(rest_own)

    q_rot, kv, normed_hi, normed_lo = project(
        far, near, block_input, gain1, bias1, qkv_full, cosine, sine
    )
    attended = attend(q_rot, kv, seg_q_col, seg_k_row)
    attended, rest_sides = together((attended, rest_sides))
    rest_diagonal = diagonal_of(rest_sides)

    out_full = gather(w_out)
    resid = block_input + matmul(attended, out_full)
    resid_other = swap(resid)
    resid_other, rest_diagonal = together((resid_other, rest_diagonal))
    cot_other = swap(cotangent)
    scale = dwa_weights[4].reshape(1, 1)
    call = functools.partial(
        mlp, chip=chip, chips=chips, resid=resid, other=resid_other, cot=cotangent,
        cot_other=cot_other, gain=gain2, bias=bias2, scale=scale,
    )
    scatter = lambda v: lax.psum_scatter(v, "dp", scatter_dimension=0, tiled=True)
    scatter_chips = lambda v: lax.psum_scatter(
        v, "dp", scatter_dimension=0, tiled=True, axis_index_groups=same_core
    )
    so_far, shards = (), []
    for third_at in range(3):
        if third_at == 0:
            weights = pieces(first_own, first_sides, first_diagonal, 0)
        else:
            weights = pieces(rest_own, rest_sides, rest_diagonal, third_at - 1)
        out_part, gnorm_part, grads = call(so_far, weights)
        so_far = (out_part, gnorm_part)
        shards.append(scatter_chips(grads)[0])
    given = swap(gnorm_part[rows:])

    shift = lambda v, bit: lax.ppermute(v, "seq", [(i, i ^ bit) for i in range(groups)])
    even = place % 2 == 0

    def line_start(shard):
        tall = shard.shape[1] // 2
        halves = (shard[:, :tall], shard[:, tall:])
        kept = jnp.where(even, halves[0], halves[1])
        return kept + shift(jnp.where(even, halves[1], halves[0]), 1)

    def line_middle(kept):
        bit = 2
        while bit < groups:
            kept = kept + shift(kept, bit)
            bit *= 2
        return kept

    def line_end(kept):
        other = shift(kept, 1)
        return jnp.where(even, kept, other), jnp.where(even, other, kept)

    shards[0], given = together((shards[0], given))
    line_a = line_start(shards[0])
    grad_resid, grad_attended, sums_two = resid_back(
        gnorm_part, given, resid, cotangent, gain2, scale, out_full
    )

    back_args = (q_rot, kv, grad_attended, seg_q_row, seg_k_col, cosine, sine)
    pairs = model // 128
    line_a, back_args = together((line_a, back_args))
    line_a = line_middle(line_a)
    first_half = attend_back(0, pairs // 2, *back_args)
    line_a, shards[1], back_args, first_half = together(
        (line_a, shards[1], back_args, first_half)
    )
    line_b = line_start(shards[1])
    ends_a = line_end(line_a)
    dq, dk, dv = attend_back(pairs // 2, pairs - pairs // 2, *back_args, before=first_half)
    line_b, ends_a, dq, dk, dv = together((line_b, ends_a, dq, dk, dv))
    line_b = line_middle(line_b)
    core_at = core.reshape(1).astype(jnp.int32)
    normed_parts = (normed_hi, normed_lo)
    grads_qk = weight_call(
        weights_qk_kernel, 9, core_at, chips, normed_parts, [(dq, 0), (dk, 1)], [halo + rows] * 2
    )
    given_qk = swap(grads_qk[1])
    line_b, shards[2], dv, grad_resid = together((line_b, shards[2], dv, grad_resid))
    ends_b = line_end(line_b)
    line_c = line_start(shards[2])
    grads_vo = weight_call(
        weights_vo_kernel, 9, core_at, chips, normed_parts,
        [(dv, 0), (attended, None), (grad_resid, 1)], [halo + rows] * 2 + [rows] * 2,
    )
    line_c, grads_vo = together((line_c, grads_vo))
    line_c = line_middle(line_c)
    grads_c = jnp.concatenate([grads_qk[0] + given_qk, grads_vo[0] + swap(grads_vo[1])], axis=2)
    grads_c, out_part = together((grads_c, out_part))
    shard_c = scatter_chips(grads_c)[0]
    out_sib = swap(out_part[rows:])

    block_out = resid + out_part[:rows] + out_sib
    output = base + dwa_weights[4] * block_out
    dwa_local = jnp.concatenate([dots, jnp.sum(cotangent * block_out)[None]])

    wq, wk, wv = (qkv_full[:, i * model:(i + 1) * model] for i in range(3))
    part_far = outer_cols(dk[:rows], wk) + outer_cols(dv[:rows], wv)
    dk_rest, dv_rest, far, near, part_far = together((dk[rows:], dv[rows:], far, near, part_far))
    given_near = lax.ppermute(part_far, "seq", behind)
    part_rest = outer_cols(dk_rest, wk) + outer_cols(dv_rest, wv)
    own_part = part_rest[rows:] + outer_cols(dq, wq)
    line_c, ends_b, part_rest, own_part = together((line_c, ends_b, part_rest, own_part))
    ends_c = line_end(line_c)
    back_near = part_rest[:rows] + given_near

    xhat1, rate1 = norm_stats(block_input)
    terms = (
        (norm_stats(far[:rows])[0], part_far),
        (norm_stats(near[:rows])[0], part_rest[:rows]),
        (xhat1, own_part),
    )
    grad_gain_one = sum(jnp.sum(xhat * part, axis=0) for xhat, part in terms)
    grad_bias_one = sum(jnp.sum(part, axis=0) for _, part in terms)

    small = jnp.concatenate(
        [
            grad_gain_one[None], grad_bias_one[None], sums_two[:2],
            jnp.pad(dwa_local, (0, model - 5))[None], jnp.zeros((3, model), F32),
        ],
        axis=0,
    )
    bit = 1
    while bit < devices:
        small = small + exchange(small, bit)
        bit *= 2
    shard_c, ends_c, back_near, small = together((shard_c, ends_c, back_near, small))
    last = line_middle(line_start(shard_c[None]))
    given_back = lax.ppermute(back_near, "seq", behind)
    grad_up, grad_down = unpack_grads(
        *(
            jnp.concatenate(parts, axis=0)
            for parts in zip(ends_a, ends_b, ends_c)
        ),
        swap, core, chips,
    )
    last, grad_up, grad_down, small, given_back = together(
        (last, grad_up, grad_down, small, given_back)
    )
    bit = 1
    while bit < groups:
        small = small + shift(small, bit)
        bit *= 2
    gain_one, bias_one, gain_two, bias_two = small[0], small[1], small[2], small[3]
    grad_dwa = small[4, :5]
    last = jnp.concatenate(line_end(last), axis=1)[0]
    grad_qkv, grad_wout = last[:, :3 * model], last[:, 3 * model:]
    grad_normed_one = own_part + given_back
    grad_input = grad_resid + norm_back(grad_normed_one, gain1, xhat1, rate1)
    return (
        output,
        grad_input,
        grad_dwa,
        gain_one,
        bias_one,
        grad_qkv,
        grad_wout,
        gain_two,
        bias_two,
        grad_up,
        grad_down,
    )


def solution(mesh):
    in_specs = (
        P(("dp", "seq"), None),
        P(("dp", "seq"), None),
        P(None, ("dp", "seq"), None),
        P(),
        P(),
        P(),
        P("dp", None),
        P("dp", None),
        P(),
        P(),
        P("dp", None),
        P("dp", None),
        P("dp", "seq"),
        P(("dp", "seq"), None),
    )
    out_specs = (
        P(("dp", "seq"), None),
        P(("dp", "seq"), None),
        P(),
        P(),
        P(),
        P("dp", None),
        P("dp", None),
        P(),
        P(),
        P("dp", None),
        P("dp", None),
    )
    return jax.shard_map(body, mesh=mesh, in_specs=in_specs, out_specs=out_specs, check_vma=False)
```

```python
import functools
import math

import jax
import jax.numpy as jnp
import numpy as np
from jax import lax
from jax.experimental import pallas as pl
from jax.experimental.pallas import tpu as pltpu
from jax.sharding import PartitionSpec as P

HD = 64
DOC_MOST = 768
LOG2E = math.log2(math.e)
SCALE = 1.0 / math.sqrt(HD)
NEG = -1e30
F32 = jnp.float32
BF16 = jnp.bfloat16
HIGH = lax.Precision.HIGH
VMEM_LIMIT = 56 * 1024 * 1024
BLK = 128


def cost(micros):
    return pl.CostEstimate(
        flops=int(micros * 1.1e9), bytes_accessed=1 << 20, transcendentals=0
    )


def params():
    return pltpu.CompilerParams(
        dimension_semantics=("arbitrary",), vmem_limit_bytes=VMEM_LIMIT
    )


def split(values):
    high = values.astype(BF16)
    return high, (values - high.astype(F32)).astype(BF16)


def dot_nn(left, right):
    return lax.dot_general(left, right, (((1,), (0,)), ((), ())), preferred_element_type=F32)


def dot_nt(left, right):
    return lax.dot_general(left, right, (((1,), (1,)), ((), ())), preferred_element_type=F32)


def dot_tn(left, right):
    return lax.dot_general(left, right, (((0,), (0,)), ((), ())), preferred_element_type=F32)


def three(dot, left, right):
    return (
        dot(left[0], right[0]) + dot(left[0], right[1]) + dot(left[1], right[0])
    )


def norm_stats(values):
    row_mean = jnp.mean(values, axis=-1, keepdims=True)
    centred = values - row_mean
    row_var = jnp.mean(centred * centred, axis=-1, keepdims=True)
    rate = lax.rsqrt(row_var + 1e-05)
    return centred * rate, rate


def norm_back(grad, gain, xhat, rate):
    scaled = grad * gain
    return rate * (
        scaled
        - jnp.mean(scaled, axis=-1, keepdims=True)
        - xhat * jnp.mean(scaled * xhat, axis=-1, keepdims=True)
    )


def turned(values):
    lane = lax.broadcasted_iota(jnp.int32, values.shape, 1)
    return jnp.where(
        (lane & 63) < 32, pltpu.roll(values, 96, 1), pltpu.roll(values, 32, 1)
    )


def rotate(values, cosine, sine):
    return values * cosine + turned(values) * sine


def unrotate(values, cosine, sine):
    return values * cosine - turned(values) * sine


def rotary_tables(length, halo):
    half = HD // 2
    inv_freq = (10000.0 ** (-(np.arange(half, dtype=np.float32) * 2.0 / HD))).astype(np.float32)
    place = np.arange(-halo, length, dtype=np.float32)
    angles = place[:, None] * inv_freq[None, :]
    cosine = np.cos(angles.astype(np.float64)).astype(np.float32)
    sine = np.sin(angles.astype(np.float64)).astype(np.float32)
    return (
        np.concatenate([cosine] * 4, axis=1),
        np.concatenate([-sine, sine, -sine, sine], axis=1),
    )


def qkv_kernel(far_ref, near_ref, own_ref, gain_ref, bias_ref, w_ref, cos_ref, sin_ref,
               q_ref, kv_ref, hi_ref, lo_ref):
    step = pl.program_id(0)
    rows = own_ref.shape[0]
    third = pl.num_programs(0) // 3
    halo = hi_ref.shape[0] - rows

    @pl.when(step == 0)
    def _():
        for at, ref in enumerate((far_ref, near_ref, own_ref)):
            xhat, _ = norm_stats(ref[...])
            high, low = split(xhat * gain_ref[...] + bias_ref[...])
            hi_ref[at * rows:(at + 1) * rows] = high
            lo_ref[at * rows:(at + 1) * rows] = low

    weights = split(w_ref[...])

    @pl.when(step < third)
    def _():
        got = three(dot_nn, (hi_ref[halo:], lo_ref[halo:]), weights)
        for at in range(0, got.shape[1], 128):
            q_ref[:, at:at + 128] = rotate(got[:, at:at + 128], cos_ref[halo:], sin_ref[halo:])

    @pl.when((step >= third) & (step < 2 * third))
    def _():
        got = three(dot_nn, (hi_ref[...], lo_ref[...]), weights)
        for at in range(0, got.shape[1], 128):
            kv_ref[:, at:at + 128] = rotate(got[:, at:at + 128], cos_ref[...], sin_ref[...])

    @pl.when(step >= 2 * third)
    def _():
        kv_ref[...] = three(dot_nn, (hi_ref[...], lo_ref[...]), weights)


def project(far, near, own, gain, bias, w_full, cosine, sine):
    rows, model = own.shape
    total = 3 * rows
    wide = 256
    third = model // wide
    whole = lambda shape: pl.BlockSpec(shape, lambda j: (0, 0))
    return pl.pallas_call(
        qkv_kernel,
        grid=(3 * third,),
        in_specs=[
            whole((rows, model)), whole((rows, model)), whole((rows, model)),
            whole((1, model)), whole((1, model)),
            pl.BlockSpec((model, wide), lambda j: (0, j)),
            whole((total, 128)), whole((total, 128)),
        ],
        out_specs=[
            pl.BlockSpec((rows, wide), lambda j: (0, jnp.minimum(j, third - 1))),
            pl.BlockSpec((total, wide), lambda j: (0, jnp.maximum(j - third, 0))),
            whole((total, model)), whole((total, model)),
        ],
        out_shape=[
            jax.ShapeDtypeStruct((rows, model), F32),
            jax.ShapeDtypeStruct((total, 2 * model), F32),
            jax.ShapeDtypeStruct((total, model), BF16),
            jax.ShapeDtypeStruct((total, model), BF16),
        ],
        cost_estimate=cost(0.3),
        compiler_params=params(),
    )(far, near, own, gain, bias, w_full, cosine, sine)


def own_pair(values, head):
    lane = lax.broadcasted_iota(jnp.int32, values.shape, 1)
    other = pltpu.roll(values, 64, 1)
    return jnp.where((lane < 64) == (head == 0), values, other)


def outer_form(values, head):
    high, low = split(own_pair(values, head))
    return jnp.concatenate([high, low], axis=1)


def mixed(values, head):
    pair = own_pair(values, head)
    lane = lax.broadcasted_iota(jnp.int32, pair.shape, 1)
    high = pair.astype(BF16).astype(F32)
    return jnp.where(lane < 64, high, pair - high).astype(BF16)


def inner_form(values, head):
    half = mixed(values, head)
    return jnp.concatenate([half, half], axis=1)


def fold(values):
    return values + pltpu.roll(values, 64, 1)


def attend_kernel(q_ref, k_ref, v_ref, segq_ref, segk_ref, out_ref, bias_ref):
    rows = q_ref.shape[0]
    halo = k_ref.shape[0] - rows
    span = halo + BLK

    @pl.when(pl.program_id(0) == 0)
    def _():
        for at in range(0, rows, BLK):
            row = lax.broadcasted_iota(jnp.int32, (BLK, span), 0)
            col = lax.broadcasted_iota(jnp.int32, (BLK, span), 1)
            same = segq_ref[at:at + BLK, :1] == segk_ref[:1, at:at + span]
            bias_ref[at:at + BLK] = jnp.where(same & (col - halo <= row), 0.0, NEG)

    lane = lax.broadcasted_iota(jnp.int32, (BLK, 128), 1)
    scaled = q_ref[...] * (SCALE * LOG2E)
    results = []
    for head in range(2):
        left = inner_form(scaled, head)
        right = outer_form(k_ref[...], head)
        vals = mixed(v_ref[...], head)
        outs = []
        for at in range(0, rows, BLK):
            scores = dot_nt(left[at:at + BLK], right[at:at + span]) + bias_ref[at:at + BLK]
            top = jnp.max(scores, axis=1, keepdims=True)
            expo = jnp.exp2(scores - top)
            total = jnp.sum(expo, axis=1, keepdims=True)
            high, low = split(expo)
            got = dot_nn(high, vals[at:at + span]) + dot_nn(low, vals[at:at + span])
            outs.append(fold(got) / total)
        results.append(outs)
    for at in range(0, rows, BLK):
        out_ref[at:at + BLK] = jnp.where(
            lane < 64, results[0][at // BLK], results[1][at // BLK]
        )


def attend(q_rot, kv, seg_q, seg_k):
    rows, model = q_rot.shape
    total = kv.shape[0]
    pairs = model // 128
    return pl.pallas_call(
        attend_kernel,
        grid=(pairs,),
        in_specs=[
            pl.BlockSpec((rows, 128), lambda p: (0, p)),
            pl.BlockSpec((total, 128), lambda p: (0, p)),
            pl.BlockSpec((total, 128), lambda p: (0, pairs + p)),
            pl.BlockSpec((rows, 128), lambda p: (0, 0)),
            pl.BlockSpec((8, total), lambda p: (0, 0)),
        ],
        out_specs=pl.BlockSpec((rows, 128), lambda p: (0, p)),
        out_shape=jax.ShapeDtypeStruct((rows, model), F32),
        scratch_shapes=[pltpu.VMEM((rows, total - rows + BLK), F32)],
        cost_estimate=cost(0.3),
        compiler_params=params(),
    )(q_rot, kv, kv, seg_q, seg_k)


def attend_back_kernel(q_ref, k_ref, v_ref, g_ref, segq_ref, segk_ref, cos_ref, sin_ref, *refs):
    dq_ref, dk_ref, dv_ref, bias_ref = refs[-4:]
    rows = q_ref.shape[0]
    halo = k_ref.shape[0] - rows
    span = halo + BLK

    @pl.when(pl.program_id(0) == 0)
    def _():
        for at in range(0, rows, BLK):
            key = lax.broadcasted_iota(jnp.int32, (span, BLK), 0)
            query = lax.broadcasted_iota(jnp.int32, (span, BLK), 1)
            same = segk_ref[at:at + span, :1] == segq_ref[:1, at:at + BLK]
            bias_ref[:, at:at + BLK] = jnp.where(same & (key - halo <= query), 0.0, NEG)

    scaled = q_ref[...] * (SCALE * LOG2E)
    dq, dk, dv = [], [], []
    for head in range(2):
        q_in = inner_form(scaled, head)
        g_in = inner_form(g_ref[...], head)
        k_out = outer_form(k_ref[...], head)
        v_out = outer_form(v_ref[...], head)
        q_mix = mixed(q_ref[...], head)
        g_mix = mixed(g_ref[...], head)
        k_mix = mixed(k_ref[...], head)
        dq_head = []
        dk_head = jnp.zeros((halo + rows, 128), F32)
        dv_head = jnp.zeros((halo + rows, 128), F32)
        dk_parts, dv_parts = [], []
        for at in range(0, rows, BLK):
            scores = dot_nt(k_out[at:at + span], q_in[at:at + BLK]) + bias_ref[:, at:at + BLK]
            top = jnp.max(scores, axis=0, keepdims=True)
            expo = jnp.exp2(scores - top)
            inverse = 1.0 / jnp.sum(expo, axis=0, keepdims=True)
            grad_probs = dot_nt(v_out[at:at + span], g_in[at:at + BLK])
            probs = expo * inverse
            delta = jnp.sum(probs * grad_probs, axis=0, keepdims=True)
            grad_scores = probs * (grad_probs - delta)
            probs_cat = jnp.concatenate(split(probs), axis=1)
            scores_cat = jnp.concatenate(split(grad_scores), axis=1)
            g_two = jnp.concatenate([g_mix[at:at + BLK]] * 2, axis=0)
            q_two = jnp.concatenate([q_mix[at:at + BLK]] * 2, axis=0)
            dv_parts.append(dot_nn(probs_cat, g_two))
            dk_parts.append(dot_nn(scores_cat, q_two))
            got = dot_tn(scores_cat, k_mix[at:at + span])
            dq_head.append(fold(got[:BLK] + got[BLK:]))
        for parts, full in ((dk_parts, dk), (dv_parts, dv)):
            pieces = []
            for kb in range((halo + rows) // BLK):
                terms = [
                    parts[qb][(kb - qb) * BLK:(kb - qb + 1) * BLK]
                    for qb in range(rows // BLK)
                    if 0 <= kb - qb < span // BLK
                ]
                pieces.append(fold(functools.reduce(lambda a, b: a + b, terms)))
            full.append(pieces)
        dq.append(dq_head)
    lane = lax.broadcasted_iota(jnp.int32, (BLK, 128), 1)
    for qb in range(rows // BLK):
        rng = slice(qb * BLK, (qb + 1) * BLK)
        far = slice(halo + qb * BLK, halo + (qb + 1) * BLK)
        both = jnp.where(lane < 64, dq[0][qb], dq[1][qb]) * SCALE
        dq_ref[rng] = unrotate(both, cos_ref[far], sin_ref[far])
    for kb in range((halo + rows) // BLK):
        rng = slice(kb * BLK, (kb + 1) * BLK)
        both = jnp.where(lane < 64, dk[0][kb], dk[1][kb]) * SCALE
        dk_ref[rng] = unrotate(both, cos_ref[rng], sin_ref[rng])
        dv_ref[rng] = jnp.where(lane < 64, dv[0][kb], dv[1][kb])


def attend_back(first, count, q_rot, kv, grad, seg_q, seg_k, cosine, sine, before=()):
    rows, model = q_rot.shape
    total = kv.shape[0]
    pairs = model // 128
    fixed = lambda shape: pl.BlockSpec(shape, lambda p: (0, 0))
    return pl.pallas_call(
        attend_back_kernel,
        grid=(count,),
        in_specs=[
            pl.BlockSpec((rows, 128), lambda p: (0, first + p)),
            pl.BlockSpec((total, 128), lambda p: (0, first + p)),
            pl.BlockSpec((total, 128), lambda p: (0, pairs + first + p)),
            pl.BlockSpec((rows, 128), lambda p: (0, first + p)),
            fixed((8, rows)), fixed((total, 128)),
            fixed((total, 128)), fixed((total, 128)),
        ] + [pl.BlockSpec(memory_space=pl.ANY)] * len(before),
        out_specs=[
            pl.BlockSpec((rows, 128), lambda p: (0, first + p)),
            pl.BlockSpec((total, 128), lambda p: (0, first + p)),
            pl.BlockSpec((total, 128), lambda p: (0, first + p)),
        ],
        out_shape=[
            jax.ShapeDtypeStruct((rows, model), F32),
            jax.ShapeDtypeStruct((total, model), F32),
            jax.ShapeDtypeStruct((total, model), F32),
        ],
        scratch_shapes=[pltpu.VMEM((total - rows + BLK, rows), F32)],
        input_output_aliases={8 + i: i for i in range(len(before))},
        cost_estimate=cost(0.3),
        compiler_params=params(),
    )(q_rot, kv, kv, grad, seg_q, seg_k, cosine, sine, *before)


def mlp_kernel(count, begun, chip_ref, resid_ref, other_ref, cot_ref, cot_other_ref, gain_ref, bias_ref,
               scale_ref, *refs):
    up_refs, down_refs = refs[:count], refs[count:2 * count]
    refs = refs[2 * count:]
    so_far, refs = refs[:4 * begun], refs[4 * begun:]
    sums, grad_refs = refs[:4], refs[4:-10]
    (x_hi, x_lo, xt_hi, xt_lo, g_hi, g_lo, up_hi, up_lo, down_hi, down_lo) = refs[-10:]
    step = pl.program_id(0)
    rows = resid_ref.shape[0]

    @pl.when(step == 0)
    def _():
        for at, source, cot in ((0, resid_ref, cot_ref), (rows, other_ref, cot_other_ref)):
            xhat, _ = norm_stats(source[...])
            normed = xhat * gain_ref[...] + bias_ref[...]
            x_hi[at:at + rows], x_lo[at:at + rows] = split(normed)
            xt_hi[:, at:at + rows], xt_lo[:, at:at + rows] = split(normed.T)
            g_hi[at:at + rows], g_lo[at:at + rows] = split(cot[...] * scale_ref[0, 0])
        for at, ref in enumerate(sums):
            ref[...] = so_far[at][...] if begun else jnp.zeros_like(ref)

    for at in range(count):
        spot = (chip_ref[0] ^ at) if count > 1 else 0
        up_rows = up_refs[at].shape[0]
        high, low = split(up_refs[at][...])
        here = pl.ds(pl.multiple_of(spot * up_rows, up_rows), up_rows)
        up_hi[here], up_lo[here] = high, low
        block = down_refs[at][...]
        block = block.reshape(-1, block.shape[-1])
        high, low = split(block)
        here = pl.ds(pl.multiple_of(spot * block.shape[0], block.shape[0]), block.shape[0])
        down_hi[here], down_lo[here] = high, low

    chips, tall, width = grad_refs[0].shape
    up_tall = up_hi.shape[0] // chips
    deep = down_hi.shape[0] // chips
    up = (up_hi[...], up_lo[...])
    down = (down_hi[...], down_lo[...])
    normed = (x_hi[...], x_lo[...])
    normed_t = (xt_hi[...], xt_lo[...])
    grad_block = (g_hi[...], g_lo[...])
    pre = three(dot_nn, normed, up)
    grad_act = three(dot_nt, grad_block, down)
    inner = 0.7978845608028654 * (pre + 0.044715 * pre * pre * pre)
    bent = jnp.tanh(inner)
    act = 0.5 * pre * (1.0 + bent)
    slope = 0.5 * (1.0 + bent) + 0.5 * pre * (1.0 - bent * bent) * (
        0.7978845608028654 * (1.0 + 3.0 * 0.044715 * pre * pre)
    )
    act2 = split(act)
    grad_pre = split(grad_act * slope)
    for at, total in enumerate((three(dot_nn, act2, down), three(dot_nt, grad_pre, up))):
        sums[2 * at][...] += total[:rows]
        sums[2 * at + 1][...] += total[rows:]
    gup = three(dot_nn, normed_t, grad_pre)
    gdown = three(dot_tn, act2, grad_block)
    half = deep // 2

    def store(grad_ref):
        for chip in range(chips):
            grad_ref[chip, :up_tall] = gup[chip * up_tall:(chip + 1) * up_tall]
            part = gdown[chip * deep:(chip + 1) * deep]
            grad_ref[chip, up_tall:up_tall + deep] = part[:, :width]
            grad_ref[chip, up_tall + deep:] = jnp.concatenate(
                [part[:half, width:], part[half:, width:]], axis=1
            )

    for at, ref in enumerate(grad_refs):
        pl.when(step == at)(functools.partial(store, ref))


def mlp(first, steps, so_far, chip, chips, resid, other, cot, cot_other, gain, bias, scale, ups, downs):
    rows, model = resid.shape
    width = 512
    up_tall = model // chips
    deep = width // chips
    fixed = lambda shape: pl.BlockSpec(shape, lambda j, c: (0, 0))
    if len(ups) > 1:
        down_spec = pl.BlockSpec((deep, model), lambda j, c: (first + j, 0))
    else:
        downs = [downs[0].reshape(chips, -1, model)]
        down_spec = pl.BlockSpec((chips, deep, model), lambda j, c: (0, first + j, 0))
    tall = up_tall + deep + deep // 2
    grid_spec = pltpu.PrefetchScalarGridSpec(
        num_scalar_prefetch=1,
        grid=(steps,),
        in_specs=[fixed((rows, model))] * 4 + [fixed((1, model))] * 2
        + [pl.BlockSpec(memory_space=pltpu.SMEM)]
        + [pl.BlockSpec((up.shape[0], width), lambda j, c: (0, first + j)) for up in ups]
        + [down_spec] * len(downs)
        + [fixed((rows, model))] * len(so_far),
        out_specs=[fixed((rows, model))] * 4
        + [pl.BlockSpec((chips, tall, width), lambda j, c: (0, 0, 0))] * steps,
        scratch_shapes=[
            pltpu.VMEM((2 * rows, model), BF16), pltpu.VMEM((2 * rows, model), BF16),
            pltpu.VMEM((model, 2 * rows), BF16), pltpu.VMEM((model, 2 * rows), BF16),
            pltpu.VMEM((2 * rows, model), BF16), pltpu.VMEM((2 * rows, model), BF16),
            pltpu.VMEM((model, width), BF16), pltpu.VMEM((model, width), BF16),
            pltpu.VMEM((width, model), BF16), pltpu.VMEM((width, model), BF16),
        ],
    )
    return pl.pallas_call(
        functools.partial(mlp_kernel, len(ups), len(so_far) // 4),
        grid_spec=grid_spec,
        out_shape=[
            *[jax.ShapeDtypeStruct((rows, model), F32)] * 4,
            *[jax.ShapeDtypeStruct((chips, tall, width), F32)] * steps,
        ],
        cost_estimate=cost(0.3),
        compiler_params=params(),
    )(chip, resid, other, cot, cot_other, gain, bias, scale, *ups, *downs, *so_far)


def unpack_grads(up, down, sibling_swap, core, chips):
    steps, up_tall, width = up.shape
    deep = up_tall * 2 // 3
    half = up_tall // 2
    mine = jnp.where(core == 0, up[:, :half], up[:, half:])
    other = sibling_swap(jnp.where(core == 0, up[:, half:], up[:, :half]))
    by_core = jnp.stack(
        [jnp.where(core == 0, mine, other), jnp.where(core == 0, other, mine)], axis=0
    )
    by_core = by_core.reshape(2, steps, half, chips, width // chips)
    grad_up = jnp.transpose(by_core, (2, 3, 0, 1, 4)).reshape(half, -1)
    quarter = width // 2
    tail = down[:, deep:]
    right = jnp.concatenate([tail[:, :, :quarter], tail[:, :, quarter:]], axis=1)
    grad_down = jnp.concatenate([down[:, :deep], right], axis=2).reshape(steps * deep, -1)
    return grad_up, grad_down


def resid_back_kernel(part_ref, given_ref, resid_ref, cot_ref, gain_ref, scale_ref, w_ref,
                      grad_ref, att_ref, sums_ref):
    grad = part_ref[...] + given_ref[...]
    xhat, rate = norm_stats(resid_ref[...])
    grad_resid = cot_ref[...] * scale_ref[0, 0] + norm_back(grad, gain_ref[...], xhat, rate)
    grad_ref[...] = grad_resid
    att_ref[...] = three(dot_nt, split(grad_resid), split(w_ref[...]))
    gain_sum = jnp.sum(grad * xhat, axis=0, keepdims=True)
    bias_sum = jnp.sum(grad, axis=0, keepdims=True)
    sums_ref[...] = jnp.concatenate(
        [gain_sum, bias_sum, jnp.zeros((6, gain_sum.shape[1]), F32)], axis=0
    )


def resid_back(part, given, resid, cot, gain, scale, w_full):
    rows, model = resid.shape
    fixed = lambda shape: pl.BlockSpec(shape, lambda j: (0, 0))
    return pl.pallas_call(
        resid_back_kernel,
        grid=(1,),
        in_specs=[fixed((rows, model))] * 4 + [fixed((1, model))]
        + [pl.BlockSpec(memory_space=pltpu.SMEM), fixed((model, model))],
        out_specs=[fixed((rows, model)), fixed((rows, model)), fixed((8, model))],
        out_shape=[
            jax.ShapeDtypeStruct((rows, model), F32),
            jax.ShapeDtypeStruct((rows, model), F32),
            jax.ShapeDtypeStruct((8, model), F32),
        ],
        cost_estimate=cost(0.3),
        compiler_params=params(),
    )(part, given, resid, cot, gain, scale, w_full)


def place_rows(core_ref, out_refs, got):
    chips, tall = out_refs[0].shape[:2]

    def store(core):
        for block in range(2 * chips):
            ref = out_refs[(block & 1) ^ core]
            ref[block // 2] = got[block * tall:(block + 1) * tall]

    for core in range(2):
        pl.when(core_ref[0] == core)(functools.partial(store, core))


def weights_qk_kernel(core_ref, hi_ref, lo_ref, dq_ref, dk_ref, own_ref, sib_ref, nt_hi, nt_lo):
    out_ref = (own_ref, sib_ref)
    step = pl.program_id(0)
    part = pl.num_programs(0) // 2
    halo = hi_ref.shape[0] - dq_ref.shape[0]

    @pl.when(step == 0)
    def _():
        nt_hi[...] = hi_ref[...].T
        nt_lo[...] = lo_ref[...].T

    @pl.when(step < part)
    def _():
        left = (nt_hi[:, halo:], nt_lo[:, halo:])
        place_rows(core_ref, out_ref, three(dot_nn, left, split(dq_ref[...])))

    @pl.when(step >= part)
    def _():
        left = (nt_hi[...], nt_lo[...])
        place_rows(core_ref, out_ref, three(dot_nn, left, split(dk_ref[...])))


def weights_vo_kernel(core_ref, hi_ref, lo_ref, dv_ref, att_ref, res_ref, own_ref, sib_ref,
                      nt_hi, nt_lo, at_hi, at_lo):
    out_ref = (own_ref, sib_ref)
    step = pl.program_id(0)
    part = pl.num_programs(0) // 2

    @pl.when(step == 0)
    def _():
        nt_hi[...] = hi_ref[...].T
        nt_lo[...] = lo_ref[...].T
        at_hi[...], at_lo[...] = split(att_ref[...].T)

    @pl.when(step < part)
    def _():
        left = (nt_hi[...], nt_lo[...])
        place_rows(core_ref, out_ref, three(dot_nn, left, split(dv_ref[...])))

    @pl.when(step >= part)
    def _():
        left = (at_hi[...], at_lo[...])
        place_rows(core_ref, out_ref, three(dot_nn, left, split(res_ref[...])))


def weight_call(kernel, micros, core, chips, fixed_args, pieces, scratch):
    model = fixed_args[0].shape[1]
    wide = 256
    part = model // wide
    tall = model // chips // 2
    fixed = lambda v: pl.BlockSpec(v.shape, lambda j, c: (0, 0))
    piece = lambda v, at: pl.BlockSpec(
        (v.shape[0], wide), lambda j, c: (0, jnp.clip(j - at * part, 0, part - 1))
    )
    specs, args = [], []
    for value, at in pieces:
        args.append(value)
        specs.append(fixed(value) if at is None else piece(value, at))
    return pl.pallas_call(
        kernel,
        grid_spec=pltpu.PrefetchScalarGridSpec(
            num_scalar_prefetch=1,
            grid=(2 * part,),
            in_specs=[fixed(v) for v in fixed_args] + specs,
            out_specs=[pl.BlockSpec((chips, tall, wide), lambda j, c: (0, 0, j))] * 2,
            scratch_shapes=[pltpu.VMEM((model, n), BF16) for n in scratch],
        ),
        out_shape=[jax.ShapeDtypeStruct((chips, tall, 2 * model), F32)] * 2,
        cost_estimate=cost(0.3),
        compiler_params=params(),
    )(core, *fixed_args, *args)


def matmul(left, right):
    return jnp.dot(left, right, precision=HIGH)


def inner_rows(left, right):
    return lax.dot_general(left, right, (((0,), (0,)), ((), ())), precision=HIGH)


def outer_cols(left, right):
    return lax.dot_general(left, right, (((1,), (1,)), ((), ())), precision=HIGH)


def body(
    block_input,
    embedding,
    earlier_outs,
    dwa_weights,
    ln1_gain,
    ln1_bias,
    w_qkv,
    w_out,
    ln2_gain,
    ln2_bias,
    w_up,
    w_down,
    segments,
    cotangent,
):
    groups = lax.axis_size("seq")
    rows, model = block_input.shape
    length = rows * groups
    halo = 2 * rows
    place = lax.axis_index("seq")
    ahead = [(i, i + 1) for i in range(groups - 1)]
    behind = [(i + 1, i) for i in range(groups - 1)]
    gain1, bias1 = ln1_gain[None], ln1_bias[None]
    gain2, bias2 = ln2_gain[None], ln2_bias[None]

    devices = lax.axis_size("dp")
    chips = devices // 2
    spot = lax.axis_index("dp")
    core = spot % 2
    chip = (spot // 2).reshape(1).astype(jnp.int32)
    same_core = [[2 * i + c for i in range(chips)] for c in range(2)]
    exchange = lambda v, bit: lax.ppermute(v, "dp", [(i, i ^ bit) for i in range(devices)])
    swap = lambda v: exchange(v, 1)

    gather = lambda v: lax.all_gather(v, "dp", axis=0, tiled=True)
    qkv_full = gather(w_qkv)

    shard = w_down.shape[0]
    third = shard // 3
    by_core = w_up.reshape(w_up.shape[0], chips, 2, 3, third)
    by_core = jnp.transpose(by_core, (2, 0, 3, 1, 4)).reshape(2, w_up.shape[0], -1)
    mine = jnp.where(core == 0, by_core[0], by_core[1])
    given = swap(jnp.where(core == 0, by_core[1], by_core[0]))
    up_chip = jnp.concatenate(
        [jnp.where(core == 0, mine, given), jnp.where(core == 0, given, mine)], axis=0
    )
    if chips == 4:
        up_x, down_x = exchange(up_chip, 2), exchange(w_down, 2)
        up_y, down_y = exchange(up_chip, 4), exchange(w_down, 4)
        ups = [up_chip, up_x, up_y, exchange(up_y, 2)]
        downs = [w_down, down_x, down_y, exchange(down_x, 4)]
    else:
        ups, downs = (
            [lax.all_gather(v, "dp", axis=0, tiled=True, axis_index_groups=same_core)]
            for v in (up_chip, w_down)
        )

    numbers = jnp.pad((segments + 1).astype(F32), ((0, 7), (0, model - rows)))
    near = lax.ppermute(jnp.concatenate([block_input, numbers], axis=0), "seq", ahead)
    far = lax.ppermute(near, "seq", ahead)
    seg_all = jnp.concatenate(
        [far[rows:rows + 1, :rows], near[rows:rows + 1, :rows], numbers[:1, :rows]], axis=1
    ).astype(jnp.int32)
    seg_k_row = jnp.broadcast_to(seg_all, (8, halo + rows))
    seg_k_col = jnp.broadcast_to(seg_all.reshape(-1, 1), (halo + rows, 128))
    seg_q_row = seg_k_row[:, halo:]
    seg_q_col = seg_k_col[halo:]

    cos_all, sin_all = rotary_tables(length, halo)
    cosine = lax.dynamic_slice_in_dim(jnp.asarray(cos_all), place * rows, halo + rows, 0)
    sine = lax.dynamic_slice_in_dim(jnp.asarray(sin_all), place * rows, halo + rows, 0)

    earlier = (embedding, earlier_outs[0], earlier_outs[1], earlier_outs[2])
    base = sum(dwa_weights[i] * value for i, value in enumerate(earlier))
    dots = jnp.stack([jnp.sum(cotangent * value) for value in earlier])
    far, base, dots = lax.optimization_barrier((far, base, dots))

    q_rot, kv, normed_hi, normed_lo = project(
        far, near, block_input, gain1, bias1, qkv_full, cosine, sine
    )
    attended = attend(q_rot, kv, seg_q_col, seg_k_row)

    out_full = gather(w_out)
    resid = block_input + matmul(attended, out_full)
    resid_other = swap(resid)
    cot_other = swap(cotangent)
    scale = dwa_weights[4].reshape(1, 1)
    call = functools.partial(
        mlp, chip=chip, chips=chips, resid=resid, other=resid_other, cot=cotangent,
        cot_other=cot_other, gain=gain2, bias=bias2, scale=scale, ups=ups, downs=downs,
    )
    scatter = lambda v: lax.psum_scatter(v, "dp", scatter_dimension=0, tiled=True)
    scatter_chips = lambda v: lax.psum_scatter(
        v, "dp", scatter_dimension=0, tiled=True, axis_index_groups=same_core
    )
    *so_far, grads = call(0, 1, ())
    *so_far, grads_next, grads_last = call(1, 2, tuple(so_far))
    out_own, out_part, gnorm_own, gnorm_part = so_far
    shards = [scatter_chips(value) for value in (grads, grads_next, grads_last)]
    given = swap(gnorm_part)

    shift = lambda v, bit: lax.ppermute(v, "seq", [(i, i ^ bit) for i in range(groups)])
    even = place % 2 == 0

    def line_start(shard):
        tall = shard.shape[1] // 2
        halves = (shard[:, :tall], shard[:, tall:])
        kept = jnp.where(even, halves[0], halves[1])
        return kept + shift(jnp.where(even, halves[1], halves[0]), 1)

    def line_middle(kept):
        bit = 2
        while bit < groups:
            kept = kept + shift(kept, bit)
            bit *= 2
        return kept

    def line_end(kept):
        other = shift(kept, 1)
        return jnp.where(even, kept, other), jnp.where(even, other, kept)

    together = lax.optimization_barrier
    shards[0], given = together((shards[0], given))
    line_a = line_start(shards[0])
    grad_resid, grad_attended, sums_two = resid_back(
        gnorm_own, given, resid, cotangent, gain2, scale, out_full
    )

    back_args = (q_rot, kv, grad_attended, seg_q_row, seg_k_col, cosine, sine)
    pairs = model // 128
    line_a, back_args = together((line_a, back_args))
    line_a = line_middle(line_a)
    first_half = attend_back(0, pairs // 2, *back_args)
    line_a, shards[1], back_args, first_half = together(
        (line_a, shards[1], back_args, first_half)
    )
    line_b = line_start(shards[1])
    ends_a = line_end(line_a)
    dq, dk, dv = attend_back(pairs // 2, pairs - pairs // 2, *back_args, before=first_half)
    line_b, ends_a, dq, dk, dv = together((line_b, ends_a, dq, dk, dv))
    line_b = line_middle(line_b)
    core_at = core.reshape(1).astype(jnp.int32)
    normed_parts = (normed_hi, normed_lo)
    grads_qk = weight_call(
        weights_qk_kernel, 9, core_at, chips, normed_parts, [(dq, 0), (dk, 1)], [halo + rows] * 2
    )
    given_qk = swap(grads_qk[1])
    line_b, shards[2], dv, grad_resid = together((line_b, shards[2], dv, grad_resid))
    ends_b = line_end(line_b)
    line_c = line_start(shards[2])
    grads_vo = weight_call(
        weights_vo_kernel, 9, core_at, chips, normed_parts,
        [(dv, 0), (attended, None), (grad_resid, 1)], [halo + rows] * 2 + [rows] * 2,
    )
    line_c, ends_b, grads_vo = together((line_c, ends_b, grads_vo))
    line_c = line_middle(line_c)
    grads_c = jnp.concatenate([grads_qk[0] + given_qk, grads_vo[0] + swap(grads_vo[1])], axis=2)
    grads_c, out_part = together((grads_c, out_part))
    shard_c = scatter_chips(grads_c)[0]
    out_sib = swap(out_part)

    block_out = resid + out_own + out_sib
    output = base + dwa_weights[4] * block_out
    dwa_local = jnp.concatenate([dots, jnp.sum(cotangent * block_out)[None]])

    wq, wk, wv = (qkv_full[:, i * model:(i + 1) * model] for i in range(3))
    part_far = outer_cols(dk[:rows], wk) + outer_cols(dv[:rows], wv)
    dk_rest, dv_rest, far, near, part_far, line_c = together(
        (dk[rows:], dv[rows:], far, near, part_far, line_c)
    )
    ends_c = line_end(line_c)
    given_near = lax.ppermute(part_far, "seq", behind)
    part_rest = outer_cols(dk_rest, wk) + outer_cols(dv_rest, wv)
    own_part = part_rest[rows:] + outer_cols(dq, wq)
    back_near = part_rest[:rows] + given_near

    xhat1, rate1 = norm_stats(block_input)
    terms = (
        (norm_stats(far[:rows])[0], part_far),
        (norm_stats(near[:rows])[0], part_rest[:rows]),
        (xhat1, own_part),
    )
    grad_gain_one = sum(jnp.sum(xhat * part, axis=0) for xhat, part in terms)
    grad_bias_one = sum(jnp.sum(part, axis=0) for _, part in terms)

    small = jnp.concatenate(
        [
            grad_gain_one[None], grad_bias_one[None], sums_two[:2],
            jnp.pad(dwa_local, (0, model - 5))[None], jnp.zeros((3, model), F32),
        ],
        axis=0,
    )
    bit = 1
    while bit < devices:
        small = small + exchange(small, bit)
        bit *= 2
    shard_c, ends_c, back_near, small = together((shard_c, ends_c, back_near, small))
    last = line_middle(line_start(shard_c[None]))
    given_back = lax.ppermute(back_near, "seq", behind)
    grad_up, grad_down = unpack_grads(
        *(
            jnp.concatenate(parts, axis=0)
            for parts in zip(ends_a, ends_b, ends_c)
        ),
        swap, core, chips,
    )
    last, grad_up, grad_down, small, given_back = together(
        (last, grad_up, grad_down, small, given_back)
    )
    bit = 1
    while bit < groups:
        small = small + shift(small, bit)
        bit *= 2
    gain_one, bias_one, gain_two, bias_two = small[0], small[1], small[2], small[3]
    grad_dwa = small[4, :5]
    last = jnp.concatenate(line_end(last), axis=1)[0]
    grad_qkv, grad_wout = last[:, :3 * model], last[:, 3 * model:]
    grad_normed_one = own_part + given_back
    grad_input = grad_resid + norm_back(grad_normed_one, gain1, xhat1, rate1)
    return (
        output,
        grad_input,
        grad_dwa,
        gain_one,
        bias_one,
        grad_qkv,
        grad_wout,
        gain_two,
        bias_two,
        grad_up,
        grad_down,
    )


def solution(mesh):
    in_specs = (
        P(("dp", "seq"), None),
        P(("dp", "seq"), None),
        P(None, ("dp", "seq"), None),
        P(),
        P(),
        P(),
        P("dp", None),
        P("dp", None),
        P(),
        P(),
        P("dp", None),
        P("dp", None),
        P("dp", "seq"),
        P(("dp", "seq"), None),
    )
    out_specs = (
        P(("dp", "seq"), None),
        P(("dp", "seq"), None),
        P(),
        P(),
        P(),
        P("dp", None),
        P("dp", None),
        P(),
        P(),
        P("dp", None),
        P("dp", None),
    )
    return jax.shard_map(body, mesh=mesh, in_specs=in_specs, out_specs=out_specs, check_vma=False)
```

```python
import functools
import math

import jax
import jax.numpy as jnp
import numpy as np
from jax import lax
from jax.experimental import pallas as pl
from jax.experimental.pallas import tpu as pltpu
from jax.sharding import PartitionSpec as P

HD = 64
DOC_MOST = 768
LOG2E = math.log2(math.e)
SCALE = 1.0 / math.sqrt(HD)
NEG = -1e30
F32 = jnp.float32
BF16 = jnp.bfloat16
HIGH = lax.Precision.HIGH
VMEM_LIMIT = 56 * 1024 * 1024
BLK = 128


def cost(micros):
    return pl.CostEstimate(
        flops=int(micros * 1.1e9), bytes_accessed=1 << 20, transcendentals=0
    )


def params():
    return pltpu.CompilerParams(
        dimension_semantics=("arbitrary",), vmem_limit_bytes=VMEM_LIMIT
    )


def split(values):
    high = values.astype(BF16)
    return high, (values - high.astype(F32)).astype(BF16)


def dot_nn(left, right):
    return lax.dot_general(left, right, (((1,), (0,)), ((), ())), preferred_element_type=F32)


def dot_nt(left, right):
    return lax.dot_general(left, right, (((1,), (1,)), ((), ())), preferred_element_type=F32)


def dot_tn(left, right):
    return lax.dot_general(left, right, (((0,), (0,)), ((), ())), preferred_element_type=F32)


def three(dot, left, right):
    return (
        dot(left[0], right[0]) + dot(left[0], right[1]) + dot(left[1], right[0])
    )


def norm_stats(values):
    row_mean = jnp.mean(values, axis=-1, keepdims=True)
    centred = values - row_mean
    row_var = jnp.mean(centred * centred, axis=-1, keepdims=True)
    rate = lax.rsqrt(row_var + 1e-05)
    return centred * rate, rate


def norm_back(grad, gain, xhat, rate):
    scaled = grad * gain
    return rate * (
        scaled
        - jnp.mean(scaled, axis=-1, keepdims=True)
        - xhat * jnp.mean(scaled * xhat, axis=-1, keepdims=True)
    )


def turned(values):
    lane = lax.broadcasted_iota(jnp.int32, values.shape, 1)
    return jnp.where(
        (lane & 63) < 32, pltpu.roll(values, 96, 1), pltpu.roll(values, 32, 1)
    )


def rotate(values, cosine, sine):
    return values * cosine + turned(values) * sine


def unrotate(values, cosine, sine):
    return values * cosine - turned(values) * sine


def rotary_tables(length, halo):
    half = HD // 2
    inv_freq = (10000.0 ** (-(np.arange(half, dtype=np.float32) * 2.0 / HD))).astype(np.float32)
    place = np.arange(-halo, length, dtype=np.float32)
    angles = place[:, None] * inv_freq[None, :]
    cosine = np.cos(angles.astype(np.float64)).astype(np.float32)
    sine = np.sin(angles.astype(np.float64)).astype(np.float32)
    return (
        np.concatenate([cosine] * 4, axis=1),
        np.concatenate([-sine, sine, -sine, sine], axis=1),
    )


def qkv_kernel(far_ref, near_ref, own_ref, gain_ref, bias_ref, w_ref, cos_ref, sin_ref,
               q_ref, kv_ref, hi_ref, lo_ref):
    step = pl.program_id(0)
    rows = own_ref.shape[0]
    third = pl.num_programs(0) // 3
    halo = hi_ref.shape[0] - rows

    @pl.when(step == 0)
    def _():
        for at, ref in enumerate((far_ref, near_ref, own_ref)):
            xhat, _ = norm_stats(ref[...])
            high, low = split(xhat * gain_ref[...] + bias_ref[...])
            hi_ref[at * rows:(at + 1) * rows] = high
            lo_ref[at * rows:(at + 1) * rows] = low

    weights = split(w_ref[...])

    @pl.when(step < third)
    def _():
        got = three(dot_nn, (hi_ref[halo:], lo_ref[halo:]), weights)
        for at in range(0, got.shape[1], 128):
            q_ref[:, at:at + 128] = rotate(got[:, at:at + 128], cos_ref[halo:], sin_ref[halo:])

    @pl.when((step >= third) & (step < 2 * third))
    def _():
        got = three(dot_nn, (hi_ref[...], lo_ref[...]), weights)
        for at in range(0, got.shape[1], 128):
            kv_ref[:, at:at + 128] = rotate(got[:, at:at + 128], cos_ref[...], sin_ref[...])

    @pl.when(step >= 2 * third)
    def _():
        kv_ref[...] = three(dot_nn, (hi_ref[...], lo_ref[...]), weights)


def project(far, near, own, gain, bias, w_full, cosine, sine):
    rows, model = own.shape
    total = 3 * rows
    wide = 256
    third = model // wide
    whole = lambda shape: pl.BlockSpec(shape, lambda j: (0, 0))
    return pl.pallas_call(
        qkv_kernel,
        grid=(3 * third,),
        in_specs=[
            whole((rows, model)), whole((rows, model)), whole((rows, model)),
            whole((1, model)), whole((1, model)),
            pl.BlockSpec((model, wide), lambda j: (0, j)),
            whole((total, 128)), whole((total, 128)),
        ],
        out_specs=[
            pl.BlockSpec((rows, wide), lambda j: (0, jnp.minimum(j, third - 1))),
            pl.BlockSpec((total, wide), lambda j: (0, jnp.maximum(j - third, 0))),
            whole((total, model)), whole((total, model)),
        ],
        out_shape=[
            jax.ShapeDtypeStruct((rows, model), F32),
            jax.ShapeDtypeStruct((total, 2 * model), F32),
            jax.ShapeDtypeStruct((total, model), BF16),
            jax.ShapeDtypeStruct((total, model), BF16),
        ],
        cost_estimate=cost(20),
        compiler_params=params(),
    )(far, near, own, gain, bias, w_full, cosine, sine)


def own_pair(values, head):
    lane = lax.broadcasted_iota(jnp.int32, values.shape, 1)
    other = pltpu.roll(values, 64, 1)
    return jnp.where((lane < 64) == (head == 0), values, other)


def outer_form(values, head):
    high, low = split(own_pair(values, head))
    return jnp.concatenate([high, low], axis=1)


def mixed(values, head):
    pair = own_pair(values, head)
    lane = lax.broadcasted_iota(jnp.int32, pair.shape, 1)
    high = pair.astype(BF16).astype(F32)
    return jnp.where(lane < 64, high, pair - high).astype(BF16)


def inner_form(values, head):
    half = mixed(values, head)
    return jnp.concatenate([half, half], axis=1)


def fold(values):
    return values + pltpu.roll(values, 64, 1)


def attend_kernel(q_ref, k_ref, v_ref, segq_ref, segk_ref, out_ref, bias_ref):
    rows = q_ref.shape[0]
    halo = k_ref.shape[0] - rows
    span = halo + BLK

    @pl.when(pl.program_id(0) == 0)
    def _():
        for at in range(0, rows, BLK):
            row = lax.broadcasted_iota(jnp.int32, (BLK, span), 0)
            col = lax.broadcasted_iota(jnp.int32, (BLK, span), 1)
            same = segq_ref[at:at + BLK, :1] == segk_ref[:1, at:at + span]
            bias_ref[at:at + BLK] = jnp.where(same & (col - halo <= row), 0.0, NEG)

    lane = lax.broadcasted_iota(jnp.int32, (BLK, 128), 1)
    scaled = q_ref[...] * (SCALE * LOG2E)
    results = []
    for head in range(2):
        left = inner_form(scaled, head)
        right = outer_form(k_ref[...], head)
        vals = mixed(v_ref[...], head)
        outs = []
        for at in range(0, rows, BLK):
            scores = dot_nt(left[at:at + BLK], right[at:at + span]) + bias_ref[at:at + BLK]
            top = jnp.max(scores, axis=1, keepdims=True)
            expo = jnp.exp2(scores - top)
            total = jnp.sum(expo, axis=1, keepdims=True)
            high, low = split(expo)
            got = dot_nn(high, vals[at:at + span]) + dot_nn(low, vals[at:at + span])
            outs.append(fold(got) / total)
        results.append(outs)
    for at in range(0, rows, BLK):
        out_ref[at:at + BLK] = jnp.where(
            lane < 64, results[0][at // BLK], results[1][at // BLK]
        )


def attend(q_rot, kv, seg_q, seg_k):
    rows, model = q_rot.shape
    total = kv.shape[0]
    pairs = model // 128
    return pl.pallas_call(
        attend_kernel,
        grid=(pairs,),
        in_specs=[
            pl.BlockSpec((rows, 128), lambda p: (0, p)),
            pl.BlockSpec((total, 128), lambda p: (0, p)),
            pl.BlockSpec((total, 128), lambda p: (0, pairs + p)),
            pl.BlockSpec((rows, 128), lambda p: (0, 0)),
            pl.BlockSpec((8, total), lambda p: (0, 0)),
        ],
        out_specs=pl.BlockSpec((rows, 128), lambda p: (0, p)),
        out_shape=jax.ShapeDtypeStruct((rows, model), F32),
        scratch_shapes=[pltpu.VMEM((rows, total - rows + BLK), F32)],
        cost_estimate=cost(24),
        compiler_params=params(),
    )(q_rot, kv, kv, seg_q, seg_k)


def attend_back_kernel(q_ref, k_ref, v_ref, g_ref, segq_ref, segk_ref, cos_ref, sin_ref, *refs):
    dq_ref, dk_ref, dv_ref, bias_ref = refs[-4:]
    rows = q_ref.shape[0]
    halo = k_ref.shape[0] - rows
    span = halo + BLK

    @pl.when(pl.program_id(0) == 0)
    def _():
        for at in range(0, rows, BLK):
            key = lax.broadcasted_iota(jnp.int32, (span, BLK), 0)
            query = lax.broadcasted_iota(jnp.int32, (span, BLK), 1)
            same = segk_ref[at:at + span, :1] == segq_ref[:1, at:at + BLK]
            bias_ref[:, at:at + BLK] = jnp.where(same & (key - halo <= query), 0.0, NEG)

    scaled = q_ref[...] * (SCALE * LOG2E)
    dq, dk, dv = [], [], []
    for head in range(2):
        q_in = inner_form(scaled, head)
        g_in = inner_form(g_ref[...], head)
        k_out = outer_form(k_ref[...], head)
        v_out = outer_form(v_ref[...], head)
        q_mix = mixed(q_ref[...], head)
        g_mix = mixed(g_ref[...], head)
        k_mix = mixed(k_ref[...], head)
        dq_head = []
        dk_head = jnp.zeros((halo + rows, 128), F32)
        dv_head = jnp.zeros((halo + rows, 128), F32)
        dk_parts, dv_parts = [], []
        for at in range(0, rows, BLK):
            scores = dot_nt(k_out[at:at + span], q_in[at:at + BLK]) + bias_ref[:, at:at + BLK]
            top = jnp.max(scores, axis=0, keepdims=True)
            expo = jnp.exp2(scores - top)
            inverse = 1.0 / jnp.sum(expo, axis=0, keepdims=True)
            grad_probs = dot_nt(v_out[at:at + span], g_in[at:at + BLK])
            probs = expo * inverse
            delta = jnp.sum(probs * grad_probs, axis=0, keepdims=True)
            grad_scores = probs * (grad_probs - delta)
            probs_cat = jnp.concatenate(split(probs), axis=1)
            scores_cat = jnp.concatenate(split(grad_scores), axis=1)
            g_two = jnp.concatenate([g_mix[at:at + BLK]] * 2, axis=0)
            q_two = jnp.concatenate([q_mix[at:at + BLK]] * 2, axis=0)
            dv_parts.append(dot_nn(probs_cat, g_two))
            dk_parts.append(dot_nn(scores_cat, q_two))
            got = dot_tn(scores_cat, k_mix[at:at + span])
            dq_head.append(fold(got[:BLK] + got[BLK:]))
        for parts, full in ((dk_parts, dk), (dv_parts, dv)):
            pieces = []
            for kb in range((halo + rows) // BLK):
                terms = [
                    parts[qb][(kb - qb) * BLK:(kb - qb + 1) * BLK]
                    for qb in range(rows // BLK)
                    if 0 <= kb - qb < span // BLK
                ]
                pieces.append(fold(functools.reduce(lambda a, b: a + b, terms)))
            full.append(pieces)
        dq.append(dq_head)
    lane = lax.broadcasted_iota(jnp.int32, (BLK, 128), 1)
    for qb in range(rows // BLK):
        rng = slice(qb * BLK, (qb + 1) * BLK)
        far = slice(halo + qb * BLK, halo + (qb + 1) * BLK)
        both = jnp.where(lane < 64, dq[0][qb], dq[1][qb]) * SCALE
        dq_ref[rng] = unrotate(both, cos_ref[far], sin_ref[far])
    for kb in range((halo + rows) // BLK):
        rng = slice(kb * BLK, (kb + 1) * BLK)
        both = jnp.where(lane < 64, dk[0][kb], dk[1][kb]) * SCALE
        dk_ref[rng] = unrotate(both, cos_ref[rng], sin_ref[rng])
        dv_ref[rng] = jnp.where(lane < 64, dv[0][kb], dv[1][kb])


def attend_back(first, count, q_rot, kv, grad, seg_q, seg_k, cosine, sine, before=()):
    rows, model = q_rot.shape
    total = kv.shape[0]
    pairs = model // 128
    fixed = lambda shape: pl.BlockSpec(shape, lambda p: (0, 0))
    return pl.pallas_call(
        attend_back_kernel,
        grid=(count,),
        in_specs=[
            pl.BlockSpec((rows, 128), lambda p: (0, first + p)),
            pl.BlockSpec((total, 128), lambda p: (0, first + p)),
            pl.BlockSpec((total, 128), lambda p: (0, pairs + first + p)),
            pl.BlockSpec((rows, 128), lambda p: (0, first + p)),
            fixed((8, rows)), fixed((total, 128)),
            fixed((total, 128)), fixed((total, 128)),
        ] + [pl.BlockSpec(memory_space=pl.ANY)] * len(before),
        out_specs=[
            pl.BlockSpec((rows, 128), lambda p: (0, first + p)),
            pl.BlockSpec((total, 128), lambda p: (0, first + p)),
            pl.BlockSpec((total, 128), lambda p: (0, first + p)),
        ],
        out_shape=[
            jax.ShapeDtypeStruct((rows, model), F32),
            jax.ShapeDtypeStruct((total, model), F32),
            jax.ShapeDtypeStruct((total, model), F32),
        ],
        scratch_shapes=[pltpu.VMEM((total - rows + BLK, rows), F32)],
        input_output_aliases={8 + i: i for i in range(len(before))},
        cost_estimate=cost(7 * count),
        compiler_params=params(),
    )(q_rot, kv, kv, grad, seg_q, seg_k, cosine, sine, *before)


def mlp_kernel(count, begun, chip_ref, resid_ref, other_ref, cot_ref, cot_other_ref, gain_ref, bias_ref,
               scale_ref, *refs):
    up_refs, down_refs = refs[:count], refs[count:2 * count]
    refs = refs[2 * count:]
    so_far, refs = refs[:4 * begun], refs[4 * begun:]
    sums, grad_ref = refs[:4], refs[4]
    (x_hi, x_lo, xt_hi, xt_lo, g_hi, g_lo, up_hi, up_lo, down_hi, down_lo) = refs[5:]
    step = pl.program_id(0)
    rows = resid_ref.shape[0]

    @pl.when(step == 0)
    def _():
        for at, source, cot in ((0, resid_ref, cot_ref), (rows, other_ref, cot_other_ref)):
            xhat, _ = norm_stats(source[...])
            normed = xhat * gain_ref[...] + bias_ref[...]
            x_hi[at:at + rows], x_lo[at:at + rows] = split(normed)
            xt_hi[:, at:at + rows], xt_lo[:, at:at + rows] = split(normed.T)
            g_hi[at:at + rows], g_lo[at:at + rows] = split(cot[...] * scale_ref[0, 0])
        for at, ref in enumerate(sums):
            ref[...] = so_far[at][...] if begun else jnp.zeros_like(ref)

    for at in range(count):
        spot = (chip_ref[0] ^ at) if count > 1 else 0
        up_rows = up_refs[at].shape[0]
        high, low = split(up_refs[at][...])
        here = pl.ds(pl.multiple_of(spot * up_rows, up_rows), up_rows)
        up_hi[here], up_lo[here] = high, low
        block = down_refs[at][...]
        block = block.reshape(-1, block.shape[-1])
        high, low = split(block)
        here = pl.ds(pl.multiple_of(spot * block.shape[0], block.shape[0]), block.shape[0])
        down_hi[here], down_lo[here] = high, low

    chips, _, tall, width = grad_ref.shape
    up_tall = up_hi.shape[0] // chips
    deep = down_hi.shape[0] // chips
    up = (up_hi[...], up_lo[...])
    down = (down_hi[...], down_lo[...])
    normed = (x_hi[...], x_lo[...])
    normed_t = (xt_hi[...], xt_lo[...])
    grad_block = (g_hi[...], g_lo[...])
    pre = three(dot_nn, normed, up)
    grad_act = three(dot_nt, grad_block, down)
    inner = 0.7978845608028654 * (pre + 0.044715 * pre * pre * pre)
    bent = jnp.tanh(inner)
    act = 0.5 * pre * (1.0 + bent)
    slope = 0.5 * (1.0 + bent) + 0.5 * pre * (1.0 - bent * bent) * (
        0.7978845608028654 * (1.0 + 3.0 * 0.044715 * pre * pre)
    )
    act2 = split(act)
    grad_pre = split(grad_act * slope)
    for at, total in enumerate((three(dot_nn, act2, down), three(dot_nt, grad_pre, up))):
        sums[2 * at][...] += total[:rows]
        sums[2 * at + 1][...] += total[rows:]
    gup = three(dot_nn, normed_t, grad_pre)
    gdown = three(dot_tn, act2, grad_block)
    half = deep // 2
    for chip in range(chips):
        grad_ref[chip, 0, :up_tall] = gup[chip * up_tall:(chip + 1) * up_tall]
        part = gdown[chip * deep:(chip + 1) * deep]
        grad_ref[chip, 0, up_tall:up_tall + deep] = part[:, :width]
        grad_ref[chip, 0, up_tall + deep:] = jnp.concatenate(
            [part[:half, width:], part[half:, width:]], axis=1
        )


def mlp(first, steps, so_far, chip, chips, resid, other, cot, cot_other, gain, bias, scale, ups, downs):
    rows, model = resid.shape
    width = 512
    up_tall = model // chips
    deep = width // chips
    fixed = lambda shape: pl.BlockSpec(shape, lambda j, c: (0, 0))
    if len(ups) > 1:
        down_spec = pl.BlockSpec((deep, model), lambda j, c: (first + j, 0))
    else:
        downs = [downs[0].reshape(chips, -1, model)]
        down_spec = pl.BlockSpec((chips, deep, model), lambda j, c: (0, first + j, 0))
    tall = up_tall + deep + deep // 2
    grid_spec = pltpu.PrefetchScalarGridSpec(
        num_scalar_prefetch=1,
        grid=(steps,),
        in_specs=[fixed((rows, model))] * 4 + [fixed((1, model))] * 2
        + [pl.BlockSpec(memory_space=pltpu.SMEM)]
        + [pl.BlockSpec((up.shape[0], width), lambda j, c: (0, first + j)) for up in ups]
        + [down_spec] * len(downs)
        + [fixed((rows, model))] * len(so_far),
        out_specs=[
            *[fixed((rows, model))] * 4,
            pl.BlockSpec((chips, 1, tall, width), lambda j, c: (0, j, 0, 0)),
        ],
        scratch_shapes=[
            pltpu.VMEM((2 * rows, model), BF16), pltpu.VMEM((2 * rows, model), BF16),
            pltpu.VMEM((model, 2 * rows), BF16), pltpu.VMEM((model, 2 * rows), BF16),
            pltpu.VMEM((2 * rows, model), BF16), pltpu.VMEM((2 * rows, model), BF16),
            pltpu.VMEM((model, width), BF16), pltpu.VMEM((model, width), BF16),
            pltpu.VMEM((width, model), BF16), pltpu.VMEM((width, model), BF16),
        ],
    )
    return pl.pallas_call(
        functools.partial(mlp_kernel, len(ups), len(so_far) // 4),
        grid_spec=grid_spec,
        out_shape=[
            *[jax.ShapeDtypeStruct((rows, model), F32)] * 4,
            jax.ShapeDtypeStruct((chips, steps, tall, width), F32),
        ],
        cost_estimate=cost(18 * steps),
        compiler_params=params(),
    )(chip, resid, other, cot, cot_other, gain, bias, scale, *ups, *downs, *so_far)


def unpack_grads(up, down, sibling_swap, core, chips):
    steps, up_tall, width = up.shape
    deep = up_tall * 2 // 3
    half = up_tall // 2
    mine = jnp.where(core == 0, up[:, :half], up[:, half:])
    other = sibling_swap(jnp.where(core == 0, up[:, half:], up[:, :half]))
    by_core = jnp.stack(
        [jnp.where(core == 0, mine, other), jnp.where(core == 0, other, mine)], axis=0
    )
    by_core = by_core.reshape(2, steps, half, chips, width // chips)
    grad_up = jnp.transpose(by_core, (2, 3, 0, 1, 4)).reshape(half, -1)
    quarter = width // 2
    tail = down[:, deep:]
    right = jnp.concatenate([tail[:, :, :quarter], tail[:, :, quarter:]], axis=1)
    grad_down = jnp.concatenate([down[:, :deep], right], axis=2).reshape(steps * deep, -1)
    return grad_up, grad_down


def resid_back_kernel(part_ref, given_ref, resid_ref, cot_ref, gain_ref, scale_ref, w_ref,
                      grad_ref, att_ref, sums_ref):
    grad = part_ref[...] + given_ref[...]
    xhat, rate = norm_stats(resid_ref[...])
    grad_resid = cot_ref[...] * scale_ref[0, 0] + norm_back(grad, gain_ref[...], xhat, rate)
    grad_ref[...] = grad_resid
    att_ref[...] = three(dot_nt, split(grad_resid), split(w_ref[...]))
    gain_sum = jnp.sum(grad * xhat, axis=0, keepdims=True)
    bias_sum = jnp.sum(grad, axis=0, keepdims=True)
    sums_ref[...] = jnp.concatenate(
        [gain_sum, bias_sum, jnp.zeros((6, gain_sum.shape[1]), F32)], axis=0
    )


def resid_back(part, given, resid, cot, gain, scale, w_full):
    rows, model = resid.shape
    fixed = lambda shape: pl.BlockSpec(shape, lambda j: (0, 0))
    return pl.pallas_call(
        resid_back_kernel,
        grid=(1,),
        in_specs=[fixed((rows, model))] * 4 + [fixed((1, model))]
        + [pl.BlockSpec(memory_space=pltpu.SMEM), fixed((model, model))],
        out_specs=[fixed((rows, model)), fixed((rows, model)), fixed((8, model))],
        out_shape=[
            jax.ShapeDtypeStruct((rows, model), F32),
            jax.ShapeDtypeStruct((rows, model), F32),
            jax.ShapeDtypeStruct((8, model), F32),
        ],
        cost_estimate=cost(6),
        compiler_params=params(),
    )(part, given, resid, cot, gain, scale, w_full)


def place_rows(core_ref, out_refs, got):
    chips, tall = out_refs[0].shape[:2]

    def store(core):
        for block in range(2 * chips):
            ref = out_refs[(block & 1) ^ core]
            ref[block // 2] = got[block * tall:(block + 1) * tall]

    for core in range(2):
        pl.when(core_ref[0] == core)(functools.partial(store, core))


def weights_qk_kernel(core_ref, hi_ref, lo_ref, dq_ref, dk_ref, own_ref, sib_ref, nt_hi, nt_lo):
    out_ref = (own_ref, sib_ref)
    step = pl.program_id(0)
    part = pl.num_programs(0) // 2
    halo = hi_ref.shape[0] - dq_ref.shape[0]

    @pl.when(step == 0)
    def _():
        nt_hi[...] = hi_ref[...].T
        nt_lo[...] = lo_ref[...].T

    @pl.when(step < part)
    def _():
        left = (nt_hi[:, halo:], nt_lo[:, halo:])
        place_rows(core_ref, out_ref, three(dot_nn, left, split(dq_ref[...])))

    @pl.when(step >= part)
    def _():
        left = (nt_hi[...], nt_lo[...])
        place_rows(core_ref, out_ref, three(dot_nn, left, split(dk_ref[...])))


def weights_vo_kernel(core_ref, hi_ref, lo_ref, dv_ref, att_ref, res_ref, own_ref, sib_ref,
                      nt_hi, nt_lo, at_hi, at_lo):
    out_ref = (own_ref, sib_ref)
    step = pl.program_id(0)
    part = pl.num_programs(0) // 2

    @pl.when(step == 0)
    def _():
        nt_hi[...] = hi_ref[...].T
        nt_lo[...] = lo_ref[...].T
        at_hi[...], at_lo[...] = split(att_ref[...].T)

    @pl.when(step < part)
    def _():
        left = (nt_hi[...], nt_lo[...])
        place_rows(core_ref, out_ref, three(dot_nn, left, split(dv_ref[...])))

    @pl.when(step >= part)
    def _():
        left = (at_hi[...], at_lo[...])
        place_rows(core_ref, out_ref, three(dot_nn, left, split(res_ref[...])))


def weight_call(kernel, micros, core, chips, fixed_args, pieces, scratch):
    model = fixed_args[0].shape[1]
    wide = 256
    part = model // wide
    tall = model // chips // 2
    fixed = lambda v: pl.BlockSpec(v.shape, lambda j, c: (0, 0))
    piece = lambda v, at: pl.BlockSpec(
        (v.shape[0], wide), lambda j, c: (0, jnp.clip(j - at * part, 0, part - 1))
    )
    specs, args = [], []
    for value, at in pieces:
        args.append(value)
        specs.append(fixed(value) if at is None else piece(value, at))
    return pl.pallas_call(
        kernel,
        grid_spec=pltpu.PrefetchScalarGridSpec(
            num_scalar_prefetch=1,
            grid=(2 * part,),
            in_specs=[fixed(v) for v in fixed_args] + specs,
            out_specs=[pl.BlockSpec((chips, tall, wide), lambda j, c: (0, 0, j))] * 2,
            scratch_shapes=[pltpu.VMEM((model, n), BF16) for n in scratch],
        ),
        out_shape=[jax.ShapeDtypeStruct((chips, tall, 2 * model), F32)] * 2,
        cost_estimate=cost(micros),
        compiler_params=params(),
    )(core, *fixed_args, *args)


def matmul(left, right):
    return jnp.dot(left, right, precision=HIGH)


def inner_rows(left, right):
    return lax.dot_general(left, right, (((0,), (0,)), ((), ())), precision=HIGH)


def outer_cols(left, right):
    return lax.dot_general(left, right, (((1,), (1,)), ((), ())), precision=HIGH)


def body(
    block_input,
    embedding,
    earlier_outs,
    dwa_weights,
    ln1_gain,
    ln1_bias,
    w_qkv,
    w_out,
    ln2_gain,
    ln2_bias,
    w_up,
    w_down,
    segments,
    cotangent,
):
    groups = lax.axis_size("seq")
    rows, model = block_input.shape
    length = rows * groups
    halo = 2 * rows
    place = lax.axis_index("seq")
    ahead = [(i, i + 1) for i in range(groups - 1)]
    behind = [(i + 1, i) for i in range(groups - 1)]
    gain1, bias1 = ln1_gain[None], ln1_bias[None]
    gain2, bias2 = ln2_gain[None], ln2_bias[None]

    devices = lax.axis_size("dp")
    chips = devices // 2
    spot = lax.axis_index("dp")
    core = spot % 2
    chip = (spot // 2).reshape(1).astype(jnp.int32)
    same_core = [[2 * i + c for i in range(chips)] for c in range(2)]
    exchange = lambda v, bit: lax.ppermute(v, "dp", [(i, i ^ bit) for i in range(devices)])
    swap = lambda v: exchange(v, 1)

    gather = lambda v: lax.all_gather(v, "dp", axis=0, tiled=True)
    qkv_full = gather(w_qkv)

    shard = w_down.shape[0]
    third = shard // 3
    by_core = w_up.reshape(w_up.shape[0], chips, 2, 3, third)
    by_core = jnp.transpose(by_core, (2, 0, 3, 1, 4)).reshape(2, w_up.shape[0], -1)
    mine = jnp.where(core == 0, by_core[0], by_core[1])
    given = swap(jnp.where(core == 0, by_core[1], by_core[0]))
    up_chip = jnp.concatenate(
        [jnp.where(core == 0, mine, given), jnp.where(core == 0, given, mine)], axis=0
    )
    if chips == 4:
        up_x, down_x = exchange(up_chip, 2), exchange(w_down, 2)
        up_y, down_y = exchange(up_chip, 4), exchange(w_down, 4)
        ups = [up_chip, up_x, up_y, exchange(up_y, 2)]
        downs = [w_down, down_x, down_y, exchange(down_x, 4)]
    else:
        ups, downs = (
            [lax.all_gather(v, "dp", axis=0, tiled=True, axis_index_groups=same_core)]
            for v in (up_chip, w_down)
        )

    seg_own = segments + 1
    near = lax.ppermute(block_input, "seq", ahead)
    seg_near = lax.ppermute(seg_own, "seq", ahead)
    far = lax.ppermute(near, "seq", ahead)
    seg_far = lax.ppermute(seg_near, "seq", ahead)
    seg_all = jnp.concatenate([seg_far, seg_near, seg_own], axis=1)
    seg_k_row = jnp.broadcast_to(seg_all, (8, halo + rows))
    seg_k_col = jnp.broadcast_to(seg_all.reshape(-1, 1), (halo + rows, 128))
    seg_q_row = seg_k_row[:, halo:]
    seg_q_col = seg_k_col[halo:]

    cos_all, sin_all = rotary_tables(length, halo)
    cosine = lax.dynamic_slice_in_dim(jnp.asarray(cos_all), place * rows, halo + rows, 0)
    sine = lax.dynamic_slice_in_dim(jnp.asarray(sin_all), place * rows, halo + rows, 0)

    earlier = (embedding, earlier_outs[0], earlier_outs[1], earlier_outs[2])
    base = sum(dwa_weights[i] * value for i, value in enumerate(earlier))
    dots = jnp.stack([jnp.sum(cotangent * value) for value in earlier])
    far, base, dots = lax.optimization_barrier((far, base, dots))

    q_rot, kv, normed_hi, normed_lo = project(
        far, near, block_input, gain1, bias1, qkv_full, cosine, sine
    )
    attended = attend(q_rot, kv, seg_q_col, seg_k_row)

    out_full = gather(w_out)
    resid = block_input + matmul(attended, out_full)
    resid_other = swap(resid)
    cot_other = swap(cotangent)
    scale = dwa_weights[4].reshape(1, 1)
    call = functools.partial(
        mlp, chip=chip, chips=chips, resid=resid, other=resid_other, cot=cotangent,
        cot_other=cot_other, gain=gain2, bias=bias2, scale=scale, ups=ups, downs=downs,
    )
    scatter = lambda v: lax.psum_scatter(v, "dp", scatter_dimension=0, tiled=True)
    scatter_chips = lambda v: lax.psum_scatter(
        v, "dp", scatter_dimension=0, tiled=True, axis_index_groups=same_core
    )
    so_far, shards = (), []
    for third_at in range(3):
        *so_far, grads = call(third_at, 1, tuple(so_far))
        shards.append(scatter_chips(grads)[0])
    out_own, out_part, gnorm_own, gnorm_part = so_far
    given = swap(gnorm_part)

    shift = lambda v, bit: lax.ppermute(v, "seq", [(i, i ^ bit) for i in range(groups)])
    even = place % 2 == 0

    def line_start(shard):
        tall = shard.shape[1] // 2
        halves = (shard[:, :tall], shard[:, tall:])
        kept = jnp.where(even, halves[0], halves[1])
        return kept + shift(jnp.where(even, halves[1], halves[0]), 1)

    def line_middle(kept):
        bit = 2
        while bit < groups:
            kept = kept + shift(kept, bit)
            bit *= 2
        return kept

    def line_end(kept):
        other = shift(kept, 1)
        return jnp.where(even, kept, other), jnp.where(even, other, kept)

    together = lax.optimization_barrier
    shards[0], given = together((shards[0], given))
    line_a = line_start(shards[0])
    grad_resid, grad_attended, sums_two = resid_back(
        gnorm_own, given, resid, cotangent, gain2, scale, out_full
    )

    back_args = (q_rot, kv, grad_attended, seg_q_row, seg_k_col, cosine, sine)
    pairs = model // 128
    line_a, back_args = together((line_a, back_args))
    line_a = line_middle(line_a)
    first_half = attend_back(0, pairs // 2, *back_args)
    line_a, shards[1], back_args, first_half = together(
        (line_a, shards[1], back_args, first_half)
    )
    line_b = line_start(shards[1])
    ends_a = line_end(line_a)
    dq, dk, dv = attend_back(pairs // 2, pairs - pairs // 2, *back_args, before=first_half)
    line_b, ends_a, dq, dk, dv = together((line_b, ends_a, dq, dk, dv))
    line_b = line_middle(line_b)
    core_at = core.reshape(1).astype(jnp.int32)
    normed_parts = (normed_hi, normed_lo)
    grads_qk = weight_call(
        weights_qk_kernel, 9, core_at, chips, normed_parts, [(dq, 0), (dk, 1)], [halo + rows] * 2
    )
    given_qk = swap(grads_qk[1])
    line_b, shards[2], dv, grad_resid = together((line_b, shards[2], dv, grad_resid))
    ends_b = line_end(line_b)
    line_c = line_start(shards[2])
    grads_vo = weight_call(
        weights_vo_kernel, 9, core_at, chips, normed_parts,
        [(dv, 0), (attended, None), (grad_resid, 1)], [halo + rows] * 2 + [rows] * 2,
    )
    line_c, ends_b, grads_vo = together((line_c, ends_b, grads_vo))
    line_c = line_middle(line_c)
    grads_c = jnp.concatenate([grads_qk[0] + given_qk, grads_vo[0] + swap(grads_vo[1])], axis=2)
    grads_c, out_part = together((grads_c, out_part))
    shard_c = scatter_chips(grads_c)[0]
    out_sib = swap(out_part)

    block_out = resid + out_own + out_sib
    output = base + dwa_weights[4] * block_out
    dwa_local = jnp.concatenate([dots, jnp.sum(cotangent * block_out)[None]])

    wq, wk, wv = (qkv_full[:, i * model:(i + 1) * model] for i in range(3))
    part_far = outer_cols(dk[:rows], wk) + outer_cols(dv[:rows], wv)
    dk_rest, dv_rest, far, near, part_far = together((dk[rows:], dv[rows:], far, near, part_far))
    given_near = lax.ppermute(part_far, "seq", behind)
    part_rest = outer_cols(dk_rest, wk) + outer_cols(dv_rest, wv)
    own_part = part_rest[rows:] + outer_cols(dq, wq)
    line_c, part_rest = together((line_c, part_rest))
    ends_c = line_end(line_c)
    (near_rows,) = together((part_rest[:rows],))
    back_near = near_rows + given_near

    xhat1, rate1 = norm_stats(block_input)
    terms = (
        (norm_stats(far)[0], part_far),
        (norm_stats(near)[0], part_rest[:rows]),
        (xhat1, own_part),
    )
    grad_gain_one = sum(jnp.sum(xhat * part, axis=0) for xhat, part in terms)
    grad_bias_one = sum(jnp.sum(part, axis=0) for _, part in terms)

    small = jnp.concatenate(
        [
            grad_gain_one[None], grad_bias_one[None], sums_two[:2],
            jnp.pad(dwa_local, (0, model - 5))[None], jnp.zeros((3, model), F32),
        ],
        axis=0,
    )
    bit = 1
    while bit < devices:
        small = small + exchange(small, bit)
        bit *= 2
    shard_c, back_near, small = together((shard_c, back_near, small))
    last = line_middle(line_start(shard_c[None]))
    given_back = lax.ppermute(back_near, "seq", behind)
    grad_up, grad_down = unpack_grads(
        *(
            jnp.concatenate(parts, axis=0)
            for parts in zip(ends_a, ends_b, ends_c)
        ),
        swap, core, chips,
    )
    last, grad_up, grad_down, small, given_back = together(
        (last, grad_up, grad_down, small, given_back)
    )
    bit = 1
    while bit < groups:
        small = small + shift(small, bit)
        bit *= 2
    gain_one, bias_one, gain_two, bias_two = small[0], small[1], small[2], small[3]
    grad_dwa = small[4, :5]
    last = jnp.concatenate(line_end(last), axis=1)[0]
    grad_qkv, grad_wout = last[:, :3 * model], last[:, 3 * model:]
    grad_normed_one = own_part + given_back
    grad_input = grad_resid + norm_back(grad_normed_one, gain1, xhat1, rate1)
    return (
        output,
        grad_input,
        grad_dwa,
        gain_one,
        bias_one,
        grad_qkv,
        grad_wout,
        gain_two,
        bias_two,
        grad_up,
        grad_down,
    )


def solution(mesh):
    in_specs = (
        P(("dp", "seq"), None),
        P(("dp", "seq"), None),
        P(None, ("dp", "seq"), None),
        P(),
        P(),
        P(),
        P("dp", None),
        P("dp", None),
        P(),
        P(),
        P("dp", None),
        P("dp", None),
        P("dp", "seq"),
        P(("dp", "seq"), None),
    )
    out_specs = (
        P(("dp", "seq"), None),
        P(("dp", "seq"), None),
        P(),
        P(),
        P(),
        P("dp", None),
        P("dp", None),
        P(),
        P(),
        P("dp", None),
        P("dp", None),
    )
    return jax.shard_map(body, mesh=mesh, in_specs=in_specs, out_specs=out_specs, check_vma=False)
```

```python
import functools
import math

import jax
import jax.numpy as jnp
import numpy as np
from jax import lax
from jax.experimental import pallas as pl
from jax.experimental.pallas import tpu as pltpu
from jax.sharding import PartitionSpec as P

HD = 64
DOC_MOST = 768
LOG2E = math.log2(math.e)
SCALE = 1.0 / math.sqrt(HD)
NEG = -1e30
F32 = jnp.float32
BF16 = jnp.bfloat16
HIGH = lax.Precision.HIGH
VMEM_LIMIT = 56 * 1024 * 1024
BLK = 128


def cost(micros):
    return pl.CostEstimate(
        flops=int(micros * 1.1e9), bytes_accessed=1 << 20, transcendentals=0
    )


def params():
    return pltpu.CompilerParams(
        dimension_semantics=("arbitrary",), vmem_limit_bytes=VMEM_LIMIT
    )


def split(values):
    high = values.astype(BF16)
    return high, (values - high.astype(F32)).astype(BF16)


def dot_nn(left, right):
    return lax.dot_general(left, right, (((1,), (0,)), ((), ())), preferred_element_type=F32)


def dot_nt(left, right):
    return lax.dot_general(left, right, (((1,), (1,)), ((), ())), preferred_element_type=F32)


def dot_tn(left, right):
    return lax.dot_general(left, right, (((0,), (0,)), ((), ())), preferred_element_type=F32)


def three(dot, left, right):
    return (
        dot(left[0], right[0]) + dot(left[0], right[1]) + dot(left[1], right[0])
    )


def norm_stats(values):
    row_mean = jnp.mean(values, axis=-1, keepdims=True)
    centred = values - row_mean
    row_var = jnp.mean(centred * centred, axis=-1, keepdims=True)
    rate = lax.rsqrt(row_var + 1e-05)
    return centred * rate, rate


def norm_back(grad, gain, xhat, rate):
    scaled = grad * gain
    return rate * (
        scaled
        - jnp.mean(scaled, axis=-1, keepdims=True)
        - xhat * jnp.mean(scaled * xhat, axis=-1, keepdims=True)
    )


def turned(values):
    lane = lax.broadcasted_iota(jnp.int32, values.shape, 1)
    return jnp.where(
        (lane & 63) < 32, pltpu.roll(values, 96, 1), pltpu.roll(values, 32, 1)
    )


def rotate(values, cosine, sine):
    return values * cosine + turned(values) * sine


def unrotate(values, cosine, sine):
    return values * cosine - turned(values) * sine


def rotary_tables(length, halo):
    half = HD // 2
    inv_freq = (10000.0 ** (-(np.arange(half, dtype=np.float32) * 2.0 / HD))).astype(np.float32)
    place = np.arange(-halo, length, dtype=np.float32)
    angles = place[:, None] * inv_freq[None, :]
    cosine = np.cos(angles.astype(np.float64)).astype(np.float32)
    sine = np.sin(angles.astype(np.float64)).astype(np.float32)
    return (
        np.concatenate([cosine] * 4, axis=1),
        np.concatenate([-sine, sine, -sine, sine], axis=1),
    )


def qkv_kernel(far_ref, near_ref, own_ref, gain_ref, bias_ref, w_ref, cos_ref, sin_ref,
               q_ref, kv_ref, hi_ref, lo_ref):
    step = pl.program_id(0)
    rows = own_ref.shape[0]
    third = pl.num_programs(0) // 3
    halo = hi_ref.shape[0] - rows

    @pl.when(step == 0)
    def _():
        for at, ref in enumerate((far_ref, near_ref, own_ref)):
            xhat, _ = norm_stats(ref[...])
            high, low = split(xhat * gain_ref[...] + bias_ref[...])
            hi_ref[at * rows:(at + 1) * rows] = high
            lo_ref[at * rows:(at + 1) * rows] = low

    weights = split(w_ref[...])

    @pl.when(step < third)
    def _():
        got = three(dot_nn, (hi_ref[halo:], lo_ref[halo:]), weights)
        for at in range(0, got.shape[1], 128):
            q_ref[:, at:at + 128] = rotate(got[:, at:at + 128], cos_ref[halo:], sin_ref[halo:])

    @pl.when((step >= third) & (step < 2 * third))
    def _():
        got = three(dot_nn, (hi_ref[...], lo_ref[...]), weights)
        for at in range(0, got.shape[1], 128):
            kv_ref[:, at:at + 128] = rotate(got[:, at:at + 128], cos_ref[...], sin_ref[...])

    @pl.when(step >= 2 * third)
    def _():
        kv_ref[...] = three(dot_nn, (hi_ref[...], lo_ref[...]), weights)


def project(far, near, own, gain, bias, w_full, cosine, sine):
    rows, model = own.shape
    total = 3 * rows
    wide = 256
    third = model // wide
    whole = lambda shape: pl.BlockSpec(shape, lambda j: (0, 0))
    return pl.pallas_call(
        qkv_kernel,
        grid=(3 * third,),
        in_specs=[
            whole((rows, model)), whole((rows, model)), whole((rows, model)),
            whole((1, model)), whole((1, model)),
            pl.BlockSpec((model, wide), lambda j: (0, j)),
            whole((total, 128)), whole((total, 128)),
        ],
        out_specs=[
            pl.BlockSpec((rows, wide), lambda j: (0, jnp.minimum(j, third - 1))),
            pl.BlockSpec((total, wide), lambda j: (0, jnp.maximum(j - third, 0))),
            whole((total, model)), whole((total, model)),
        ],
        out_shape=[
            jax.ShapeDtypeStruct((rows, model), F32),
            jax.ShapeDtypeStruct((total, 2 * model), F32),
            jax.ShapeDtypeStruct((total, model), BF16),
            jax.ShapeDtypeStruct((total, model), BF16),
        ],
        cost_estimate=cost(20),
        compiler_params=params(),
    )(far, near, own, gain, bias, w_full, cosine, sine)


def own_pair(values, head):
    lane = lax.broadcasted_iota(jnp.int32, values.shape, 1)
    other = pltpu.roll(values, 64, 1)
    return jnp.where((lane < 64) == (head == 0), values, other)


def outer_form(values, head):
    high, low = split(own_pair(values, head))
    return jnp.concatenate([high, low], axis=1)


def mixed(values, head):
    pair = own_pair(values, head)
    lane = lax.broadcasted_iota(jnp.int32, pair.shape, 1)
    high = pair.astype(BF16).astype(F32)
    return jnp.where(lane < 64, high, pair - high).astype(BF16)


def inner_form(values, head):
    half = mixed(values, head)
    return jnp.concatenate([half, half], axis=1)


def fold(values):
    return values + pltpu.roll(values, 64, 1)


def attend_kernel(q_ref, k_ref, v_ref, segq_ref, segk_ref, out_ref, bias_ref):
    rows = q_ref.shape[0]
    halo = k_ref.shape[0] - rows
    span = halo + BLK

    @pl.when(pl.program_id(0) == 0)
    def _():
        for at in range(0, rows, BLK):
            row = lax.broadcasted_iota(jnp.int32, (BLK, span), 0)
            col = lax.broadcasted_iota(jnp.int32, (BLK, span), 1)
            same = segq_ref[at:at + BLK, :1] == segk_ref[:1, at:at + span]
            bias_ref[at:at + BLK] = jnp.where(same & (col - halo <= row), 0.0, NEG)

    lane = lax.broadcasted_iota(jnp.int32, (BLK, 128), 1)
    scaled = q_ref[...] * (SCALE * LOG2E)
    results = []
    for head in range(2):
        left = inner_form(scaled, head)
        right = outer_form(k_ref[...], head)
        vals = mixed(v_ref[...], head)
        outs = []
        for at in range(0, rows, BLK):
            scores = dot_nt(left[at:at + BLK], right[at:at + span]) + bias_ref[at:at + BLK]
            top = jnp.max(scores, axis=1, keepdims=True)
            expo = jnp.exp2(scores - top)
            total = jnp.sum(expo, axis=1, keepdims=True)
            high, low = split(expo)
            got = dot_nn(high, vals[at:at + span]) + dot_nn(low, vals[at:at + span])
            outs.append(fold(got) / total)
        results.append(outs)
    for at in range(0, rows, BLK):
        out_ref[at:at + BLK] = jnp.where(
            lane < 64, results[0][at // BLK], results[1][at // BLK]
        )


def attend(q_rot, kv, seg_q, seg_k):
    rows, model = q_rot.shape
    total = kv.shape[0]
    pairs = model // 128
    return pl.pallas_call(
        attend_kernel,
        grid=(pairs,),
        in_specs=[
            pl.BlockSpec((rows, 128), lambda p: (0, p)),
            pl.BlockSpec((total, 128), lambda p: (0, p)),
            pl.BlockSpec((total, 128), lambda p: (0, pairs + p)),
            pl.BlockSpec((rows, 128), lambda p: (0, 0)),
            pl.BlockSpec((8, total), lambda p: (0, 0)),
        ],
        out_specs=pl.BlockSpec((rows, 128), lambda p: (0, p)),
        out_shape=jax.ShapeDtypeStruct((rows, model), F32),
        scratch_shapes=[pltpu.VMEM((rows, total - rows + BLK), F32)],
        cost_estimate=cost(24),
        compiler_params=params(),
    )(q_rot, kv, kv, seg_q, seg_k)


def attend_back_kernel(q_ref, k_ref, v_ref, g_ref, segq_ref, segk_ref, cos_ref, sin_ref, *refs):
    dq_ref, dk_ref, dv_ref, bias_ref = refs[-4:]
    rows = q_ref.shape[0]
    halo = k_ref.shape[0] - rows
    span = halo + BLK

    @pl.when(pl.program_id(0) == 0)
    def _():
        for at in range(0, rows, BLK):
            key = lax.broadcasted_iota(jnp.int32, (span, BLK), 0)
            query = lax.broadcasted_iota(jnp.int32, (span, BLK), 1)
            same = segk_ref[at:at + span, :1] == segq_ref[:1, at:at + BLK]
            bias_ref[:, at:at + BLK] = jnp.where(same & (key - halo <= query), 0.0, NEG)

    scaled = q_ref[...] * (SCALE * LOG2E)
    dq, dk, dv = [], [], []
    for head in range(2):
        q_in = inner_form(scaled, head)
        g_in = inner_form(g_ref[...], head)
        k_out = outer_form(k_ref[...], head)
        v_out = outer_form(v_ref[...], head)
        q_mix = mixed(q_ref[...], head)
        g_mix = mixed(g_ref[...], head)
        k_mix = mixed(k_ref[...], head)
        dq_head = []
        dk_head = jnp.zeros((halo + rows, 128), F32)
        dv_head = jnp.zeros((halo + rows, 128), F32)
        dk_parts, dv_parts = [], []
        for at in range(0, rows, BLK):
            scores = dot_nt(k_out[at:at + span], q_in[at:at + BLK]) + bias_ref[:, at:at + BLK]
            top = jnp.max(scores, axis=0, keepdims=True)
            expo = jnp.exp2(scores - top)
            inverse = 1.0 / jnp.sum(expo, axis=0, keepdims=True)
            grad_probs = dot_nt(v_out[at:at + span], g_in[at:at + BLK])
            probs = expo * inverse
            delta = jnp.sum(probs * grad_probs, axis=0, keepdims=True)
            grad_scores = probs * (grad_probs - delta)
            probs_cat = jnp.concatenate(split(probs), axis=1)
            scores_cat = jnp.concatenate(split(grad_scores), axis=1)
            g_two = jnp.concatenate([g_mix[at:at + BLK]] * 2, axis=0)
            q_two = jnp.concatenate([q_mix[at:at + BLK]] * 2, axis=0)
            dv_parts.append(dot_nn(probs_cat, g_two))
            dk_parts.append(dot_nn(scores_cat, q_two))
            got = dot_tn(scores_cat, k_mix[at:at + span])
            dq_head.append(fold(got[:BLK] + got[BLK:]))
        for parts, full in ((dk_parts, dk), (dv_parts, dv)):
            pieces = []
            for kb in range((halo + rows) // BLK):
                terms = [
                    parts[qb][(kb - qb) * BLK:(kb - qb + 1) * BLK]
                    for qb in range(rows // BLK)
                    if 0 <= kb - qb < span // BLK
                ]
                pieces.append(fold(functools.reduce(lambda a, b: a + b, terms)))
            full.append(pieces)
        dq.append(dq_head)
    lane = lax.broadcasted_iota(jnp.int32, (BLK, 128), 1)
    for qb in range(rows // BLK):
        rng = slice(qb * BLK, (qb + 1) * BLK)
        far = slice(halo + qb * BLK, halo + (qb + 1) * BLK)
        both = jnp.where(lane < 64, dq[0][qb], dq[1][qb]) * SCALE
        dq_ref[rng] = unrotate(both, cos_ref[far], sin_ref[far])
    for kb in range((halo + rows) // BLK):
        rng = slice(kb * BLK, (kb + 1) * BLK)
        both = jnp.where(lane < 64, dk[0][kb], dk[1][kb]) * SCALE
        dk_ref[rng] = unrotate(both, cos_ref[rng], sin_ref[rng])
        dv_ref[rng] = jnp.where(lane < 64, dv[0][kb], dv[1][kb])


def attend_back(first, count, q_rot, kv, grad, seg_q, seg_k, cosine, sine, before=()):
    rows, model = q_rot.shape
    total = kv.shape[0]
    pairs = model // 128
    fixed = lambda shape: pl.BlockSpec(shape, lambda p: (0, 0))
    return pl.pallas_call(
        attend_back_kernel,
        grid=(count,),
        in_specs=[
            pl.BlockSpec((rows, 128), lambda p: (0, first + p)),
            pl.BlockSpec((total, 128), lambda p: (0, first + p)),
            pl.BlockSpec((total, 128), lambda p: (0, pairs + first + p)),
            pl.BlockSpec((rows, 128), lambda p: (0, first + p)),
            fixed((8, rows)), fixed((total, 128)),
            fixed((total, 128)), fixed((total, 128)),
        ] + [pl.BlockSpec(memory_space=pl.ANY)] * len(before),
        out_specs=[
            pl.BlockSpec((rows, 128), lambda p: (0, first + p)),
            pl.BlockSpec((total, 128), lambda p: (0, first + p)),
            pl.BlockSpec((total, 128), lambda p: (0, first + p)),
        ],
        out_shape=[
            jax.ShapeDtypeStruct((rows, model), F32),
            jax.ShapeDtypeStruct((total, model), F32),
            jax.ShapeDtypeStruct((total, model), F32),
        ],
        scratch_shapes=[pltpu.VMEM((total - rows + BLK, rows), F32)],
        input_output_aliases={8 + i: i for i in range(len(before))},
        cost_estimate=cost(7 * count),
        compiler_params=params(),
    )(q_rot, kv, kv, grad, seg_q, seg_k, cosine, sine, *before)


def mlp_kernel(count, begun, chip_ref, resid_ref, other_ref, cot_ref, cot_other_ref, gain_ref, bias_ref,
               scale_ref, *refs):
    up_refs, down_refs = refs[:count], refs[count:2 * count]
    refs = refs[2 * count:]
    so_far, refs = refs[:2 * begun], refs[2 * begun:]
    out_ref, gnorm_ref, grad_ref = refs[:3]
    (x_hi, x_lo, xt_hi, xt_lo, g_hi, g_lo, up_hi, up_lo, down_hi, down_lo) = refs[3:]
    step = pl.program_id(0)
    rows = resid_ref.shape[0]

    @pl.when(step == 0)
    def _():
        for at, source, cot in ((0, resid_ref, cot_ref), (rows, other_ref, cot_other_ref)):
            xhat, _ = norm_stats(source[...])
            normed = xhat * gain_ref[...] + bias_ref[...]
            x_hi[at:at + rows], x_lo[at:at + rows] = split(normed)
            xt_hi[:, at:at + rows], xt_lo[:, at:at + rows] = split(normed.T)
            g_hi[at:at + rows], g_lo[at:at + rows] = split(cot[...] * scale_ref[0, 0])
        if begun:
            out_ref[...] = so_far[0][...]
            gnorm_ref[...] = so_far[1][...]
        else:
            out_ref[...] = jnp.zeros_like(out_ref)
            gnorm_ref[...] = jnp.zeros_like(gnorm_ref)

    for at in range(count):
        spot = (chip_ref[0] ^ at) if count > 1 else 0
        up_rows = up_refs[at].shape[0]
        high, low = split(up_refs[at][...])
        here = pl.ds(pl.multiple_of(spot * up_rows, up_rows), up_rows)
        up_hi[here], up_lo[here] = high, low
        block = down_refs[at][...]
        block = block.reshape(-1, block.shape[-1])
        high, low = split(block)
        here = pl.ds(pl.multiple_of(spot * block.shape[0], block.shape[0]), block.shape[0])
        down_hi[here], down_lo[here] = high, low

    chips, _, tall, width = grad_ref.shape
    up_tall = up_hi.shape[0] // chips
    deep = down_hi.shape[0] // chips
    up = (up_hi[...], up_lo[...])
    down = (down_hi[...], down_lo[...])
    normed = (x_hi[...], x_lo[...])
    normed_t = (xt_hi[...], xt_lo[...])
    grad_block = (g_hi[...], g_lo[...])
    pre = three(dot_nn, normed, up)
    grad_act = three(dot_nt, grad_block, down)
    inner = 0.7978845608028654 * (pre + 0.044715 * pre * pre * pre)
    bent = jnp.tanh(inner)
    act = 0.5 * pre * (1.0 + bent)
    slope = 0.5 * (1.0 + bent) + 0.5 * pre * (1.0 - bent * bent) * (
        0.7978845608028654 * (1.0 + 3.0 * 0.044715 * pre * pre)
    )
    act2 = split(act)
    grad_pre = split(grad_act * slope)
    out_ref[...] += three(dot_nn, act2, down)
    gnorm_ref[...] += three(dot_nt, grad_pre, up)
    gup = three(dot_nn, normed_t, grad_pre)
    gdown = three(dot_tn, act2, grad_block)
    half = deep // 2
    for chip in range(chips):
        grad_ref[chip, 0, :up_tall] = gup[chip * up_tall:(chip + 1) * up_tall]
        part = gdown[chip * deep:(chip + 1) * deep]
        grad_ref[chip, 0, up_tall:up_tall + deep] = part[:, :width]
        grad_ref[chip, 0, up_tall + deep:] = jnp.concatenate(
            [part[:half, width:], part[half:, width:]], axis=1
        )


def mlp(first, steps, so_far, chip, chips, resid, other, cot, cot_other, gain, bias, scale, ups, downs):
    rows, model = resid.shape
    width = 512
    up_tall = model // chips
    deep = width // chips
    fixed = lambda shape: pl.BlockSpec(shape, lambda j, c: (0, 0))
    if len(ups) > 1:
        down_spec = pl.BlockSpec((deep, model), lambda j, c: (first + j, 0))
    else:
        downs = [downs[0].reshape(chips, -1, model)]
        down_spec = pl.BlockSpec((chips, deep, model), lambda j, c: (0, first + j, 0))
    tall = up_tall + deep + deep // 2
    grid_spec = pltpu.PrefetchScalarGridSpec(
        num_scalar_prefetch=1,
        grid=(steps,),
        in_specs=[fixed((rows, model))] * 4 + [fixed((1, model))] * 2
        + [pl.BlockSpec(memory_space=pltpu.SMEM)]
        + [pl.BlockSpec((up.shape[0], width), lambda j, c: (0, first + j)) for up in ups]
        + [down_spec] * len(downs)
        + [fixed((2 * rows, model))] * len(so_far),
        out_specs=[
            fixed((2 * rows, model)), fixed((2 * rows, model)),
            pl.BlockSpec((chips, 1, tall, width), lambda j, c: (0, j, 0, 0)),
        ],
        scratch_shapes=[
            pltpu.VMEM((2 * rows, model), BF16), pltpu.VMEM((2 * rows, model), BF16),
            pltpu.VMEM((model, 2 * rows), BF16), pltpu.VMEM((model, 2 * rows), BF16),
            pltpu.VMEM((2 * rows, model), BF16), pltpu.VMEM((2 * rows, model), BF16),
            pltpu.VMEM((model, width), BF16), pltpu.VMEM((model, width), BF16),
            pltpu.VMEM((width, model), BF16), pltpu.VMEM((width, model), BF16),
        ],
    )
    return pl.pallas_call(
        functools.partial(mlp_kernel, len(ups), len(so_far) // 2),
        grid_spec=grid_spec,
        out_shape=[
            jax.ShapeDtypeStruct((2 * rows, model), F32),
            jax.ShapeDtypeStruct((2 * rows, model), F32),
            jax.ShapeDtypeStruct((chips, steps, tall, width), F32),
        ],
        cost_estimate=cost(18 * steps),
        compiler_params=params(),
    )(chip, resid, other, cot, cot_other, gain, bias, scale, *ups, *downs, *so_far)


def unpack_grads(up, down, sibling_swap, core, chips):
    steps, up_tall, width = up.shape
    deep = up_tall * 2 // 3
    half = up_tall // 2
    mine = jnp.where(core == 0, up[:, :half], up[:, half:])
    other = sibling_swap(jnp.where(core == 0, up[:, half:], up[:, :half]))
    by_core = jnp.stack(
        [jnp.where(core == 0, mine, other), jnp.where(core == 0, other, mine)], axis=0
    )
    by_core = by_core.reshape(2, steps, half, chips, width // chips)
    grad_up = jnp.transpose(by_core, (2, 3, 0, 1, 4)).reshape(half, -1)
    quarter = width // 2
    tail = down[:, deep:]
    right = jnp.concatenate([tail[:, :, :quarter], tail[:, :, quarter:]], axis=1)
    grad_down = jnp.concatenate([down[:, :deep], right], axis=2).reshape(steps * deep, -1)
    return grad_up, grad_down


def resid_back_kernel(part_ref, given_ref, resid_ref, cot_ref, gain_ref, scale_ref, w_ref,
                      grad_ref, att_ref, sums_ref):
    grad = part_ref[...] + given_ref[...]
    xhat, rate = norm_stats(resid_ref[...])
    grad_resid = cot_ref[...] * scale_ref[0, 0] + norm_back(grad, gain_ref[...], xhat, rate)
    grad_ref[...] = grad_resid
    att_ref[...] = three(dot_nt, split(grad_resid), split(w_ref[...]))
    gain_sum = jnp.sum(grad * xhat, axis=0, keepdims=True)
    bias_sum = jnp.sum(grad, axis=0, keepdims=True)
    sums_ref[...] = jnp.concatenate(
        [gain_sum, bias_sum, jnp.zeros((6, gain_sum.shape[1]), F32)], axis=0
    )


def resid_back(part, given, resid, cot, gain, scale, w_full):
    rows, model = resid.shape
    fixed = lambda shape: pl.BlockSpec(shape, lambda j: (0, 0))
    return pl.pallas_call(
        resid_back_kernel,
        grid=(1,),
        in_specs=[fixed((rows, model))] * 4 + [fixed((1, model))]
        + [pl.BlockSpec(memory_space=pltpu.SMEM), fixed((model, model))],
        out_specs=[fixed((rows, model)), fixed((rows, model)), fixed((8, model))],
        out_shape=[
            jax.ShapeDtypeStruct((rows, model), F32),
            jax.ShapeDtypeStruct((rows, model), F32),
            jax.ShapeDtypeStruct((8, model), F32),
        ],
        cost_estimate=cost(6),
        compiler_params=params(),
    )(part, given, resid, cot, gain, scale, w_full)


def place_rows(core_ref, out_refs, got):
    chips, tall = out_refs[0].shape[:2]

    def store(core):
        for block in range(2 * chips):
            ref = out_refs[(block & 1) ^ core]
            ref[block // 2] = got[block * tall:(block + 1) * tall]

    for core in range(2):
        pl.when(core_ref[0] == core)(functools.partial(store, core))


def weights_qk_kernel(core_ref, hi_ref, lo_ref, dq_ref, dk_ref, own_ref, sib_ref, nt_hi, nt_lo):
    out_ref = (own_ref, sib_ref)
    step = pl.program_id(0)
    part = pl.num_programs(0) // 2
    halo = hi_ref.shape[0] - dq_ref.shape[0]

    @pl.when(step == 0)
    def _():
        nt_hi[...] = hi_ref[...].T
        nt_lo[...] = lo_ref[...].T

    @pl.when(step < part)
    def _():
        left = (nt_hi[:, halo:], nt_lo[:, halo:])
        place_rows(core_ref, out_ref, three(dot_nn, left, split(dq_ref[...])))

    @pl.when(step >= part)
    def _():
        left = (nt_hi[...], nt_lo[...])
        place_rows(core_ref, out_ref, three(dot_nn, left, split(dk_ref[...])))


def weights_vo_kernel(core_ref, hi_ref, lo_ref, dv_ref, att_ref, res_ref, own_ref, sib_ref,
                      nt_hi, nt_lo, at_hi, at_lo):
    out_ref = (own_ref, sib_ref)
    step = pl.program_id(0)
    part = pl.num_programs(0) // 2

    @pl.when(step == 0)
    def _():
        nt_hi[...] = hi_ref[...].T
        nt_lo[...] = lo_ref[...].T
        at_hi[...], at_lo[...] = split(att_ref[...].T)

    @pl.when(step < part)
    def _():
        left = (nt_hi[...], nt_lo[...])
        place_rows(core_ref, out_ref, three(dot_nn, left, split(dv_ref[...])))

    @pl.when(step >= part)
    def _():
        left = (at_hi[...], at_lo[...])
        place_rows(core_ref, out_ref, three(dot_nn, left, split(res_ref[...])))


def weight_call(kernel, micros, core, chips, fixed_args, pieces, scratch):
    model = fixed_args[0].shape[1]
    wide = 256
    part = model // wide
    tall = model // chips // 2
    fixed = lambda v: pl.BlockSpec(v.shape, lambda j, c: (0, 0))
    piece = lambda v, at: pl.BlockSpec(
        (v.shape[0], wide), lambda j, c: (0, jnp.clip(j - at * part, 0, part - 1))
    )
    specs, args = [], []
    for value, at in pieces:
        args.append(value)
        specs.append(fixed(value) if at is None else piece(value, at))
    return pl.pallas_call(
        kernel,
        grid_spec=pltpu.PrefetchScalarGridSpec(
            num_scalar_prefetch=1,
            grid=(2 * part,),
            in_specs=[fixed(v) for v in fixed_args] + specs,
            out_specs=[pl.BlockSpec((chips, tall, wide), lambda j, c: (0, 0, j))] * 2,
            scratch_shapes=[pltpu.VMEM((model, n), BF16) for n in scratch],
        ),
        out_shape=[jax.ShapeDtypeStruct((chips, tall, 2 * model), F32)] * 2,
        cost_estimate=cost(micros),
        compiler_params=params(),
    )(core, *fixed_args, *args)


def matmul(left, right):
    return jnp.dot(left, right, precision=HIGH)


def inner_rows(left, right):
    return lax.dot_general(left, right, (((0,), (0,)), ((), ())), precision=HIGH)


def outer_cols(left, right):
    return lax.dot_general(left, right, (((1,), (1,)), ((), ())), precision=HIGH)


def body(
    block_input,
    embedding,
    earlier_outs,
    dwa_weights,
    ln1_gain,
    ln1_bias,
    w_qkv,
    w_out,
    ln2_gain,
    ln2_bias,
    w_up,
    w_down,
    segments,
    cotangent,
):
    groups = lax.axis_size("seq")
    rows, model = block_input.shape
    length = rows * groups
    halo = 2 * rows
    place = lax.axis_index("seq")
    ahead = [(i, i + 1) for i in range(groups - 1)]
    behind = [(i + 1, i) for i in range(groups - 1)]
    gain1, bias1 = ln1_gain[None], ln1_bias[None]
    gain2, bias2 = ln2_gain[None], ln2_bias[None]

    devices = lax.axis_size("dp")
    chips = devices // 2
    spot = lax.axis_index("dp")
    core = spot % 2
    chip = (spot // 2).reshape(1).astype(jnp.int32)
    same_core = [[2 * i + c for i in range(chips)] for c in range(2)]
    exchange = lambda v, bit: lax.ppermute(v, "dp", [(i, i ^ bit) for i in range(devices)])
    swap = lambda v: exchange(v, 1)

    gather = lambda v: lax.all_gather(v, "dp", axis=0, tiled=True)
    qkv_full = gather(w_qkv)

    shard = w_down.shape[0]
    third = shard // 3
    by_core = w_up.reshape(w_up.shape[0], chips, 2, 3, third)
    by_core = jnp.transpose(by_core, (2, 0, 3, 1, 4)).reshape(2, w_up.shape[0], -1)
    mine = jnp.where(core == 0, by_core[0], by_core[1])
    given = swap(jnp.where(core == 0, by_core[1], by_core[0]))
    up_chip = jnp.concatenate(
        [jnp.where(core == 0, mine, given), jnp.where(core == 0, given, mine)], axis=0
    )
    if chips == 4:
        up_x, down_x = exchange(up_chip, 2), exchange(w_down, 2)
        up_y, down_y = exchange(up_chip, 4), exchange(w_down, 4)
        ups = [up_chip, up_x, up_y, exchange(up_y, 2)]
        downs = [w_down, down_x, down_y, exchange(down_x, 4)]
    else:
        ups, downs = (
            [lax.all_gather(v, "dp", axis=0, tiled=True, axis_index_groups=same_core)]
            for v in (up_chip, w_down)
        )

    seg_own = segments + 1
    near = lax.ppermute(block_input, "seq", ahead)
    seg_near = lax.ppermute(seg_own, "seq", ahead)
    far = lax.ppermute(near, "seq", ahead)
    seg_far = lax.ppermute(seg_near, "seq", ahead)
    seg_all = jnp.concatenate([seg_far, seg_near, seg_own], axis=1)
    seg_k_row = jnp.broadcast_to(seg_all, (8, halo + rows))
    seg_k_col = jnp.broadcast_to(seg_all.reshape(-1, 1), (halo + rows, 128))
    seg_q_row = seg_k_row[:, halo:]
    seg_q_col = seg_k_col[halo:]

    cos_all, sin_all = rotary_tables(length, halo)
    cosine = lax.dynamic_slice_in_dim(jnp.asarray(cos_all), place * rows, halo + rows, 0)
    sine = lax.dynamic_slice_in_dim(jnp.asarray(sin_all), place * rows, halo + rows, 0)

    earlier = (embedding, earlier_outs[0], earlier_outs[1], earlier_outs[2])
    base = sum(dwa_weights[i] * value for i, value in enumerate(earlier))
    dots = jnp.stack([jnp.sum(cotangent * value) for value in earlier])
    far, base, dots = lax.optimization_barrier((far, base, dots))

    q_rot, kv, normed_hi, normed_lo = project(
        far, near, block_input, gain1, bias1, qkv_full, cosine, sine
    )
    attended = attend(q_rot, kv, seg_q_col, seg_k_row)

    out_full = gather(w_out)
    resid = block_input + matmul(attended, out_full)
    resid_other = swap(resid)
    cot_other = swap(cotangent)
    scale = dwa_weights[4].reshape(1, 1)
    call = functools.partial(
        mlp, chip=chip, chips=chips, resid=resid, other=resid_other, cot=cotangent,
        cot_other=cot_other, gain=gain2, bias=bias2, scale=scale, ups=ups, downs=downs,
    )
    scatter = lambda v: lax.psum_scatter(v, "dp", scatter_dimension=0, tiled=True)
    scatter_chips = lambda v: lax.psum_scatter(
        v, "dp", scatter_dimension=0, tiled=True, axis_index_groups=same_core
    )
    so_far, shards = (), []
    for third_at in range(3):
        out_part, gnorm_part, grads = call(third_at, 1, so_far)
        so_far = (out_part, gnorm_part)
        shards.append(scatter_chips(grads)[0])
    given = swap(gnorm_part[rows:])

    shift = lambda v, bit: lax.ppermute(v, "seq", [(i, i ^ bit) for i in range(groups)])
    even = place % 2 == 0

    def line_start(shard):
        tall = shard.shape[1] // 2
        halves = (shard[:, :tall], shard[:, tall:])
        kept = jnp.where(even, halves[0], halves[1])
        return kept + shift(jnp.where(even, halves[1], halves[0]), 1)

    def line_middle(kept):
        bit = 2
        while bit < groups:
            kept = kept + shift(kept, bit)
            bit *= 2
        return kept

    def line_end(kept):
        other = shift(kept, 1)
        return jnp.where(even, kept, other), jnp.where(even, other, kept)

    together = lax.optimization_barrier
    shards[0], given = together((shards[0], given))
    line_a = line_start(shards[0])
    grad_resid, grad_attended, sums_two = resid_back(
        gnorm_part, given, resid, cotangent, gain2, scale, out_full
    )

    back_args = (q_rot, kv, grad_attended, seg_q_row, seg_k_col, cosine, sine)
    pairs = model // 128
    line_a, back_args = together((line_a, back_args))
    line_a = line_middle(line_a)
    first_half = attend_back(0, pairs // 2, *back_args)
    line_a, shards[1], back_args, first_half = together(
        (line_a, shards[1], back_args, first_half)
    )
    line_b = line_start(shards[1])
    ends_a = line_end(line_a)
    dq, dk, dv = attend_back(pairs // 2, pairs - pairs // 2, *back_args, before=first_half)
    line_b, ends_a, dq, dk, dv = together((line_b, ends_a, dq, dk, dv))
    line_b = line_middle(line_b)
    core_at = core.reshape(1).astype(jnp.int32)
    normed_parts = (normed_hi, normed_lo)
    grads_qk = weight_call(
        weights_qk_kernel, 9, core_at, chips, normed_parts, [(dq, 0), (dk, 1)], [halo + rows] * 2
    )
    given_qk = swap(grads_qk[1])
    line_b, shards[2], dv, grad_resid = together((line_b, shards[2], dv, grad_resid))
    ends_b = line_end(line_b)
    line_c = line_start(shards[2])
    grads_vo = weight_call(
        weights_vo_kernel, 9, core_at, chips, normed_parts,
        [(dv, 0), (attended, None), (grad_resid, 1)], [halo + rows] * 2 + [rows] * 2,
    )
    line_c, ends_b, grads_vo = together((line_c, ends_b, grads_vo))
    line_c = line_middle(line_c)
    grads_c = jnp.concatenate([grads_qk[0] + given_qk, grads_vo[0] + swap(grads_vo[1])], axis=2)
    grads_c, out_part = together((grads_c, out_part))
    shard_c = scatter_chips(grads_c)[0]
    out_sib = swap(out_part[rows:])

    block_out = resid + out_part[:rows] + out_sib
    output = base + dwa_weights[4] * block_out
    dwa_local = jnp.concatenate([dots, jnp.sum(cotangent * block_out)[None]])

    wq, wk, wv = (qkv_full[:, i * model:(i + 1) * model] for i in range(3))
    line_c, dk = together((line_c, dk))
    ends_c = line_end(line_c)
    part_far = outer_cols(dk[:rows], wk) + outer_cols(dv[:rows], wv)
    dk_rest, dv_rest, far, near, part_far = together((dk[rows:], dv[rows:], far, near, part_far))
    given_near = lax.ppermute(part_far, "seq", behind)
    part_rest = outer_cols(dk_rest, wk) + outer_cols(dv_rest, wv)
    own_part = part_rest[rows:] + outer_cols(dq, wq)
    (near_rows,) = together((part_rest[:rows],))
    back_near = near_rows + given_near

    xhat1, rate1 = norm_stats(block_input)
    terms = (
        (norm_stats(far)[0], part_far),
        (norm_stats(near)[0], part_rest[:rows]),
        (xhat1, own_part),
    )
    grad_gain_one = sum(jnp.sum(xhat * part, axis=0) for xhat, part in terms)
    grad_bias_one = sum(jnp.sum(part, axis=0) for _, part in terms)

    small = jnp.concatenate(
        [
            grad_gain_one[None], grad_bias_one[None], sums_two[:2],
            jnp.pad(dwa_local, (0, model - 5))[None], jnp.zeros((3, model), F32),
        ],
        axis=0,
    )
    bit = 1
    while bit < devices:
        small = small + exchange(small, bit)
        bit *= 2
    shard_c, back_near, small = together((shard_c, back_near, small))
    last = line_middle(line_start(shard_c[None]))
    given_back = lax.ppermute(back_near, "seq", behind)
    grad_up, grad_down = unpack_grads(
        *(
            jnp.concatenate(parts, axis=0)
            for parts in zip(ends_a, ends_b, ends_c)
        ),
        swap, core, chips,
    )
    last, grad_up, grad_down, small, given_back = together(
        (last, grad_up, grad_down, small, given_back)
    )
    bit = 1
    while bit < groups:
        small = small + shift(small, bit)
        bit *= 2
    gain_one, bias_one, gain_two, bias_two = small[0], small[1], small[2], small[3]
    grad_dwa = small[4, :5]
    last = jnp.concatenate(line_end(last), axis=1)[0]
    grad_qkv, grad_wout = last[:, :3 * model], last[:, 3 * model:]
    grad_normed_one = own_part + given_back
    grad_input = grad_resid + norm_back(grad_normed_one, gain1, xhat1, rate1)
    return (
        output,
        grad_input,
        grad_dwa,
        gain_one,
        bias_one,
        grad_qkv,
        grad_wout,
        gain_two,
        bias_two,
        grad_up,
        grad_down,
    )


def solution(mesh):
    in_specs = (
        P(("dp", "seq"), None),
        P(("dp", "seq"), None),
        P(None, ("dp", "seq"), None),
        P(),
        P(),
        P(),
        P("dp", None),
        P("dp", None),
        P(),
        P(),
        P("dp", None),
        P("dp", None),
        P("dp", "seq"),
        P(("dp", "seq"), None),
    )
    out_specs = (
        P(("dp", "seq"), None),
        P(("dp", "seq"), None),
        P(),
        P(),
        P(),
        P("dp", None),
        P("dp", None),
        P(),
        P(),
        P("dp", None),
        P("dp", None),
    )
    return jax.shard_map(body, mesh=mesh, in_specs=in_specs, out_specs=out_specs, check_vma=False)
```

```python
import functools
import math

import jax
import jax.numpy as jnp
import numpy as np
from jax import lax
from jax.experimental import pallas as pl
from jax.experimental.pallas import tpu as pltpu
from jax.sharding import PartitionSpec as P

HD = 64
DOC_MOST = 768
LOG2E = math.log2(math.e)
SCALE = 1.0 / math.sqrt(HD)
NEG = -1e30
F32 = jnp.float32
BF16 = jnp.bfloat16
HIGH = lax.Precision.HIGH
VMEM_LIMIT = 56 * 1024 * 1024
BLK = 128


def cost(micros):
    return pl.CostEstimate(
        flops=int(micros * 1.1e9), bytes_accessed=1 << 20, transcendentals=0
    )


def params():
    return pltpu.CompilerParams(
        dimension_semantics=("arbitrary",), vmem_limit_bytes=VMEM_LIMIT
    )


def split(values):
    high = values.astype(BF16)
    return high, (values - high.astype(F32)).astype(BF16)


def dot_nn(left, right):
    return lax.dot_general(left, right, (((1,), (0,)), ((), ())), preferred_element_type=F32)


def dot_nt(left, right):
    return lax.dot_general(left, right, (((1,), (1,)), ((), ())), preferred_element_type=F32)


def dot_tn(left, right):
    return lax.dot_general(left, right, (((0,), (0,)), ((), ())), preferred_element_type=F32)


def three(dot, left, right):
    return (
        dot(left[0], right[0]) + dot(left[0], right[1]) + dot(left[1], right[0])
    )


def norm_stats(values):
    row_mean = jnp.mean(values, axis=-1, keepdims=True)
    centred = values - row_mean
    row_var = jnp.mean(centred * centred, axis=-1, keepdims=True)
    rate = lax.rsqrt(row_var + 1e-05)
    return centred * rate, rate


def norm_back(grad, gain, xhat, rate):
    scaled = grad * gain
    return rate * (
        scaled
        - jnp.mean(scaled, axis=-1, keepdims=True)
        - xhat * jnp.mean(scaled * xhat, axis=-1, keepdims=True)
    )


def turned(values):
    lane = lax.broadcasted_iota(jnp.int32, values.shape, 1)
    return jnp.where(
        (lane & 63) < 32, pltpu.roll(values, 96, 1), pltpu.roll(values, 32, 1)
    )


def rotate(values, cosine, sine):
    return values * cosine + turned(values) * sine


def unrotate(values, cosine, sine):
    return values * cosine - turned(values) * sine


def rotary_tables(length, halo):
    half = HD // 2
    inv_freq = (10000.0 ** (-(np.arange(half, dtype=np.float32) * 2.0 / HD))).astype(np.float32)
    place = np.arange(-halo, length, dtype=np.float32)
    angles = place[:, None] * inv_freq[None, :]
    cosine = np.cos(angles.astype(np.float64)).astype(np.float32)
    sine = np.sin(angles.astype(np.float64)).astype(np.float32)
    return (
        np.concatenate([cosine] * 4, axis=1),
        np.concatenate([-sine, sine, -sine, sine], axis=1),
    )


def qkv_kernel(far_ref, near_ref, own_ref, gain_ref, bias_ref, w_ref, cos_ref, sin_ref,
               q_ref, kv_ref, hi_ref, lo_ref):
    step = pl.program_id(0)
    rows = own_ref.shape[0]
    third = pl.num_programs(0) // 3
    halo = hi_ref.shape[0] - rows

    @pl.when(step == 0)
    def _():
        for at, ref in enumerate((far_ref, near_ref, own_ref)):
            xhat, _ = norm_stats(ref[...])
            high, low = split(xhat * gain_ref[...] + bias_ref[...])
            hi_ref[at * rows:(at + 1) * rows] = high
            lo_ref[at * rows:(at + 1) * rows] = low

    weights = split(w_ref[...])

    @pl.when(step < third)
    def _():
        got = three(dot_nn, (hi_ref[halo:], lo_ref[halo:]), weights)
        for at in range(0, got.shape[1], 128):
            q_ref[:, at:at + 128] = rotate(got[:, at:at + 128], cos_ref[halo:], sin_ref[halo:])

    @pl.when((step >= third) & (step < 2 * third))
    def _():
        got = three(dot_nn, (hi_ref[...], lo_ref[...]), weights)
        for at in range(0, got.shape[1], 128):
            kv_ref[:, at:at + 128] = rotate(got[:, at:at + 128], cos_ref[...], sin_ref[...])

    @pl.when(step >= 2 * third)
    def _():
        kv_ref[...] = three(dot_nn, (hi_ref[...], lo_ref[...]), weights)


def project(far, near, own, gain, bias, w_full, cosine, sine):
    rows, model = own.shape
    total = 3 * rows
    wide = 256
    third = model // wide
    whole = lambda shape: pl.BlockSpec(shape, lambda j: (0, 0))
    return pl.pallas_call(
        qkv_kernel,
        grid=(3 * third,),
        in_specs=[
            whole((rows, model)), whole((rows, model)), whole((rows, model)),
            whole((1, model)), whole((1, model)),
            pl.BlockSpec((model, wide), lambda j: (0, j)),
            whole((total, 128)), whole((total, 128)),
        ],
        out_specs=[
            pl.BlockSpec((rows, wide), lambda j: (0, jnp.minimum(j, third - 1))),
            pl.BlockSpec((total, wide), lambda j: (0, jnp.maximum(j - third, 0))),
            whole((total, model)), whole((total, model)),
        ],
        out_shape=[
            jax.ShapeDtypeStruct((rows, model), F32),
            jax.ShapeDtypeStruct((total, 2 * model), F32),
            jax.ShapeDtypeStruct((total, model), BF16),
            jax.ShapeDtypeStruct((total, model), BF16),
        ],
        cost_estimate=cost(20),
        compiler_params=params(),
    )(far, near, own, gain, bias, w_full, cosine, sine)


def own_pair(values, head):
    lane = lax.broadcasted_iota(jnp.int32, values.shape, 1)
    other = pltpu.roll(values, 64, 1)
    return jnp.where((lane < 64) == (head == 0), values, other)


def outer_form(values, head):
    high, low = split(own_pair(values, head))
    return jnp.concatenate([high, low], axis=1)


def mixed(values, head):
    pair = own_pair(values, head)
    lane = lax.broadcasted_iota(jnp.int32, pair.shape, 1)
    high = pair.astype(BF16).astype(F32)
    return jnp.where(lane < 64, high, pair - high).astype(BF16)


def inner_form(values, head):
    half = mixed(values, head)
    return jnp.concatenate([half, half], axis=1)


def fold(values):
    return values + pltpu.roll(values, 64, 1)


def attend_kernel(q_ref, k_ref, v_ref, segq_ref, segk_ref, out_ref, bias_ref):
    rows = q_ref.shape[0]
    halo = k_ref.shape[0] - rows
    span = halo + BLK

    @pl.when(pl.program_id(0) == 0)
    def _():
        for at in range(0, rows, BLK):
            row = lax.broadcasted_iota(jnp.int32, (BLK, span), 0)
            col = lax.broadcasted_iota(jnp.int32, (BLK, span), 1)
            same = segq_ref[at:at + BLK, :1] == segk_ref[:1, at:at + span]
            bias_ref[at:at + BLK] = jnp.where(same & (col - halo <= row), 0.0, NEG)

    lane = lax.broadcasted_iota(jnp.int32, (BLK, 128), 1)
    scaled = q_ref[...] * (SCALE * LOG2E)
    results = []
    for head in range(2):
        left = inner_form(scaled, head)
        right = outer_form(k_ref[...], head)
        vals = mixed(v_ref[...], head)
        outs = []
        for at in range(0, rows, BLK):
            scores = dot_nt(left[at:at + BLK], right[at:at + span]) + bias_ref[at:at + BLK]
            top = jnp.max(scores, axis=1, keepdims=True)
            expo = jnp.exp2(scores - top)
            total = jnp.sum(expo, axis=1, keepdims=True)
            high, low = split(expo)
            got = dot_nn(high, vals[at:at + span]) + dot_nn(low, vals[at:at + span])
            outs.append(fold(got) / total)
        results.append(outs)
    for at in range(0, rows, BLK):
        out_ref[at:at + BLK] = jnp.where(
            lane < 64, results[0][at // BLK], results[1][at // BLK]
        )


def attend(q_rot, kv, seg_q, seg_k):
    rows, model = q_rot.shape
    total = kv.shape[0]
    pairs = model // 128
    return pl.pallas_call(
        attend_kernel,
        grid=(pairs,),
        in_specs=[
            pl.BlockSpec((rows, 128), lambda p: (0, p)),
            pl.BlockSpec((total, 128), lambda p: (0, p)),
            pl.BlockSpec((total, 128), lambda p: (0, pairs + p)),
            pl.BlockSpec((rows, 128), lambda p: (0, 0)),
            pl.BlockSpec((8, total), lambda p: (0, 0)),
        ],
        out_specs=pl.BlockSpec((rows, 128), lambda p: (0, p)),
        out_shape=jax.ShapeDtypeStruct((rows, model), F32),
        scratch_shapes=[pltpu.VMEM((rows, total - rows + BLK), F32)],
        cost_estimate=cost(24),
        compiler_params=params(),
    )(q_rot, kv, kv, seg_q, seg_k)


def attend_back_kernel(q_ref, k_ref, v_ref, g_ref, segq_ref, segk_ref, cos_ref, sin_ref, *refs):
    dq_ref, dk_ref, dv_ref, bias_ref = refs[-4:]
    rows = q_ref.shape[0]
    halo = k_ref.shape[0] - rows
    span = halo + BLK

    @pl.when(pl.program_id(0) == 0)
    def _():
        for at in range(0, rows, BLK):
            key = lax.broadcasted_iota(jnp.int32, (span, BLK), 0)
            query = lax.broadcasted_iota(jnp.int32, (span, BLK), 1)
            same = segk_ref[at:at + span, :1] == segq_ref[:1, at:at + BLK]
            bias_ref[:, at:at + BLK] = jnp.where(same & (key - halo <= query), 0.0, NEG)

    scaled = q_ref[...] * (SCALE * LOG2E)
    dq, dk, dv = [], [], []
    for head in range(2):
        q_in = inner_form(scaled, head)
        g_in = inner_form(g_ref[...], head)
        k_out = outer_form(k_ref[...], head)
        v_out = outer_form(v_ref[...], head)
        q_mix = mixed(q_ref[...], head)
        g_mix = mixed(g_ref[...], head)
        k_mix = mixed(k_ref[...], head)
        dq_head = []
        dk_head = jnp.zeros((halo + rows, 128), F32)
        dv_head = jnp.zeros((halo + rows, 128), F32)
        dk_parts, dv_parts = [], []
        for at in range(0, rows, BLK):
            scores = dot_nt(k_out[at:at + span], q_in[at:at + BLK]) + bias_ref[:, at:at + BLK]
            top = jnp.max(scores, axis=0, keepdims=True)
            expo = jnp.exp2(scores - top)
            inverse = 1.0 / jnp.sum(expo, axis=0, keepdims=True)
            grad_probs = dot_nt(v_out[at:at + span], g_in[at:at + BLK])
            probs = expo * inverse
            delta = jnp.sum(probs * grad_probs, axis=0, keepdims=True)
            grad_scores = probs * (grad_probs - delta)
            probs_cat = jnp.concatenate(split(probs), axis=1)
            scores_cat = jnp.concatenate(split(grad_scores), axis=1)
            g_two = jnp.concatenate([g_mix[at:at + BLK]] * 2, axis=0)
            q_two = jnp.concatenate([q_mix[at:at + BLK]] * 2, axis=0)
            dv_parts.append(dot_nn(probs_cat, g_two))
            dk_parts.append(dot_nn(scores_cat, q_two))
            got = dot_tn(scores_cat, k_mix[at:at + span])
            dq_head.append(fold(got[:BLK] + got[BLK:]))
        for parts, full in ((dk_parts, dk), (dv_parts, dv)):
            pieces = []
            for kb in range((halo + rows) // BLK):
                terms = [
                    parts[qb][(kb - qb) * BLK:(kb - qb + 1) * BLK]
                    for qb in range(rows // BLK)
                    if 0 <= kb - qb < span // BLK
                ]
                pieces.append(fold(functools.reduce(lambda a, b: a + b, terms)))
            full.append(pieces)
        dq.append(dq_head)
    lane = lax.broadcasted_iota(jnp.int32, (BLK, 128), 1)
    for qb in range(rows // BLK):
        rng = slice(qb * BLK, (qb + 1) * BLK)
        far = slice(halo + qb * BLK, halo + (qb + 1) * BLK)
        both = jnp.where(lane < 64, dq[0][qb], dq[1][qb]) * SCALE
        dq_ref[rng] = unrotate(both, cos_ref[far], sin_ref[far])
    for kb in range((halo + rows) // BLK):
        rng = slice(kb * BLK, (kb + 1) * BLK)
        both = jnp.where(lane < 64, dk[0][kb], dk[1][kb]) * SCALE
        dk_ref[rng] = unrotate(both, cos_ref[rng], sin_ref[rng])
        dv_ref[rng] = jnp.where(lane < 64, dv[0][kb], dv[1][kb])


def attend_back(first, count, q_rot, kv, grad, seg_q, seg_k, cosine, sine, before=()):
    rows, model = q_rot.shape
    total = kv.shape[0]
    pairs = model // 128
    fixed = lambda shape: pl.BlockSpec(shape, lambda p: (0, 0))
    return pl.pallas_call(
        attend_back_kernel,
        grid=(count,),
        in_specs=[
            pl.BlockSpec((rows, 128), lambda p: (0, first + p)),
            pl.BlockSpec((total, 128), lambda p: (0, first + p)),
            pl.BlockSpec((total, 128), lambda p: (0, pairs + first + p)),
            pl.BlockSpec((rows, 128), lambda p: (0, first + p)),
            fixed((8, rows)), fixed((total, 128)),
            fixed((total, 128)), fixed((total, 128)),
        ] + [pl.BlockSpec(memory_space=pl.ANY)] * len(before),
        out_specs=[
            pl.BlockSpec((rows, 128), lambda p: (0, first + p)),
            pl.BlockSpec((total, 128), lambda p: (0, first + p)),
            pl.BlockSpec((total, 128), lambda p: (0, first + p)),
        ],
        out_shape=[
            jax.ShapeDtypeStruct((rows, model), F32),
            jax.ShapeDtypeStruct((total, model), F32),
            jax.ShapeDtypeStruct((total, model), F32),
        ],
        scratch_shapes=[pltpu.VMEM((total - rows + BLK, rows), F32)],
        input_output_aliases={8 + i: i for i in range(len(before))},
        cost_estimate=cost(7 * count),
        compiler_params=params(),
    )(q_rot, kv, kv, grad, seg_q, seg_k, cosine, sine, *before)


def mlp_kernel(count, begun, chip_ref, resid_ref, other_ref, cot_ref, cot_other_ref, gain_ref, bias_ref,
               scale_ref, *refs):
    up_refs, down_refs = refs[:count], refs[count:2 * count]
    refs = refs[2 * count:]
    so_far, refs = refs[:2 * begun], refs[2 * begun:]
    out_ref, gnorm_ref, grad_ref = refs[:3]
    (x_hi, x_lo, xt_hi, xt_lo, g_hi, g_lo, up_hi, up_lo, down_hi, down_lo) = refs[3:]
    step = pl.program_id(0)
    rows = resid_ref.shape[0]

    @pl.when(step == 0)
    def _():
        for at, source, cot in ((0, resid_ref, cot_ref), (rows, other_ref, cot_other_ref)):
            xhat, _ = norm_stats(source[...])
            normed = xhat * gain_ref[...] + bias_ref[...]
            x_hi[at:at + rows], x_lo[at:at + rows] = split(normed)
            xt_hi[:, at:at + rows], xt_lo[:, at:at + rows] = split(normed.T)
            g_hi[at:at + rows], g_lo[at:at + rows] = split(cot[...] * scale_ref[0, 0])
        if begun:
            out_ref[...] = so_far[0][...]
            gnorm_ref[...] = so_far[1][...]
        else:
            out_ref[...] = jnp.zeros_like(out_ref)
            gnorm_ref[...] = jnp.zeros_like(gnorm_ref)

    for at in range(count):
        spot = (chip_ref[0] ^ at) if count > 1 else 0
        up_rows = up_refs[at].shape[0]
        high, low = split(up_refs[at][...])
        here = pl.ds(pl.multiple_of(spot * up_rows, up_rows), up_rows)
        up_hi[here], up_lo[here] = high, low
        block = down_refs[at][...]
        block = block.reshape(-1, block.shape[-1])
        high, low = split(block)
        here = pl.ds(pl.multiple_of(spot * block.shape[0], block.shape[0]), block.shape[0])
        down_hi[here], down_lo[here] = high, low

    chips, _, tall, width = grad_ref.shape
    up_tall = up_hi.shape[0] // chips
    deep = down_hi.shape[0] // chips
    up = (up_hi[...], up_lo[...])
    down = (down_hi[...], down_lo[...])
    normed = (x_hi[...], x_lo[...])
    normed_t = (xt_hi[...], xt_lo[...])
    grad_block = (g_hi[...], g_lo[...])
    pre = three(dot_nn, normed, up)
    grad_act = three(dot_nt, grad_block, down)
    inner = 0.7978845608028654 * (pre + 0.044715 * pre * pre * pre)
    bent = jnp.tanh(inner)
    act = 0.5 * pre * (1.0 + bent)
    slope = 0.5 * (1.0 + bent) + 0.5 * pre * (1.0 - bent * bent) * (
        0.7978845608028654 * (1.0 + 3.0 * 0.044715 * pre * pre)
    )
    act2 = split(act)
    grad_pre = split(grad_act * slope)
    out_ref[...] += three(dot_nn, act2, down)
    gnorm_ref[...] += three(dot_nt, grad_pre, up)
    gup = three(dot_nn, normed_t, grad_pre)
    gdown = three(dot_tn, act2, grad_block)
    half = deep // 2
    for chip in range(chips):
        grad_ref[chip, 0, :up_tall] = gup[chip * up_tall:(chip + 1) * up_tall]
        part = gdown[chip * deep:(chip + 1) * deep]
        grad_ref[chip, 0, up_tall:up_tall + deep] = part[:, :width]
        grad_ref[chip, 0, up_tall + deep:] = jnp.concatenate(
            [part[:half, width:], part[half:, width:]], axis=1
        )


def mlp(first, steps, so_far, chip, chips, resid, other, cot, cot_other, gain, bias, scale, ups, downs):
    rows, model = resid.shape
    width = 512
    up_tall = model // chips
    deep = width // chips
    fixed = lambda shape: pl.BlockSpec(shape, lambda j, c: (0, 0))
    if len(ups) > 1:
        down_spec = pl.BlockSpec((deep, model), lambda j, c: (first + j, 0))
    else:
        downs = [downs[0].reshape(chips, -1, model)]
        down_spec = pl.BlockSpec((chips, deep, model), lambda j, c: (0, first + j, 0))
    tall = up_tall + deep + deep // 2
    grid_spec = pltpu.PrefetchScalarGridSpec(
        num_scalar_prefetch=1,
        grid=(steps,),
        in_specs=[fixed((rows, model))] * 4 + [fixed((1, model))] * 2
        + [pl.BlockSpec(memory_space=pltpu.SMEM)]
        + [pl.BlockSpec((up.shape[0], width), lambda j, c: (0, first + j)) for up in ups]
        + [down_spec] * len(downs)
        + [fixed((2 * rows, model))] * len(so_far),
        out_specs=[
            fixed((2 * rows, model)), fixed((2 * rows, model)),
            pl.BlockSpec((chips, 1, tall, width), lambda j, c: (0, j, 0, 0)),
        ],
        scratch_shapes=[
            pltpu.VMEM((2 * rows, model), BF16), pltpu.VMEM((2 * rows, model), BF16),
            pltpu.VMEM((model, 2 * rows), BF16), pltpu.VMEM((model, 2 * rows), BF16),
            pltpu.VMEM((2 * rows, model), BF16), pltpu.VMEM((2 * rows, model), BF16),
            pltpu.VMEM((model, width), BF16), pltpu.VMEM((model, width), BF16),
            pltpu.VMEM((width, model), BF16), pltpu.VMEM((width, model), BF16),
        ],
    )
    return pl.pallas_call(
        functools.partial(mlp_kernel, len(ups), len(so_far) // 2),
        grid_spec=grid_spec,
        out_shape=[
            jax.ShapeDtypeStruct((2 * rows, model), F32),
            jax.ShapeDtypeStruct((2 * rows, model), F32),
            jax.ShapeDtypeStruct((chips, steps, tall, width), F32),
        ],
        cost_estimate=cost(18 * steps),
        compiler_params=params(),
    )(chip, resid, other, cot, cot_other, gain, bias, scale, *ups, *downs, *so_far)


def unpack_grads(up, down, sibling_swap, core, chips):
    steps, up_tall, width = up.shape
    deep = up_tall * 2 // 3
    half = up_tall // 2
    mine = jnp.where(core == 0, up[:, :half], up[:, half:])
    other = sibling_swap(jnp.where(core == 0, up[:, half:], up[:, :half]))
    by_core = jnp.stack(
        [jnp.where(core == 0, mine, other), jnp.where(core == 0, other, mine)], axis=0
    )
    by_core = by_core.reshape(2, steps, half, chips, width // chips)
    grad_up = jnp.transpose(by_core, (2, 3, 0, 1, 4)).reshape(half, -1)
    quarter = width // 2
    tail = down[:, deep:]
    right = jnp.concatenate([tail[:, :, :quarter], tail[:, :, quarter:]], axis=1)
    grad_down = jnp.concatenate([down[:, :deep], right], axis=2).reshape(steps * deep, -1)
    return grad_up, grad_down


def resid_back_kernel(part_ref, given_ref, resid_ref, cot_ref, gain_ref, scale_ref, w_ref,
                      grad_ref, att_ref, sums_ref):
    grad = part_ref[...] + given_ref[...]
    xhat, rate = norm_stats(resid_ref[...])
    grad_resid = cot_ref[...] * scale_ref[0, 0] + norm_back(grad, gain_ref[...], xhat, rate)
    grad_ref[...] = grad_resid
    att_ref[...] = three(dot_nt, split(grad_resid), split(w_ref[...]))
    gain_sum = jnp.sum(grad * xhat, axis=0, keepdims=True)
    bias_sum = jnp.sum(grad, axis=0, keepdims=True)
    sums_ref[...] = jnp.concatenate(
        [gain_sum, bias_sum, jnp.zeros((6, gain_sum.shape[1]), F32)], axis=0
    )


def resid_back(part, given, resid, cot, gain, scale, w_full):
    rows, model = resid.shape
    fixed = lambda shape: pl.BlockSpec(shape, lambda j: (0, 0))
    return pl.pallas_call(
        resid_back_kernel,
        grid=(1,),
        in_specs=[fixed((rows, model))] * 4 + [fixed((1, model))]
        + [pl.BlockSpec(memory_space=pltpu.SMEM), fixed((model, model))],
        out_specs=[fixed((rows, model)), fixed((rows, model)), fixed((8, model))],
        out_shape=[
            jax.ShapeDtypeStruct((rows, model), F32),
            jax.ShapeDtypeStruct((rows, model), F32),
            jax.ShapeDtypeStruct((8, model), F32),
        ],
        cost_estimate=cost(6),
        compiler_params=params(),
    )(part, given, resid, cot, gain, scale, w_full)


def place_rows(core_ref, out_refs, got):
    chips, tall = out_refs[0].shape[:2]

    def store(core):
        for block in range(2 * chips):
            ref = out_refs[(block & 1) ^ core]
            ref[block // 2] = got[block * tall:(block + 1) * tall]

    for core in range(2):
        pl.when(core_ref[0] == core)(functools.partial(store, core))


def weights_qk_kernel(core_ref, hi_ref, lo_ref, dq_ref, dk_ref, own_ref, sib_ref, nt_hi, nt_lo):
    out_ref = (own_ref, sib_ref)
    step = pl.program_id(0)
    part = pl.num_programs(0) // 2
    halo = hi_ref.shape[0] - dq_ref.shape[0]

    @pl.when(step == 0)
    def _():
        nt_hi[...] = hi_ref[...].T
        nt_lo[...] = lo_ref[...].T

    @pl.when(step < part)
    def _():
        left = (nt_hi[:, halo:], nt_lo[:, halo:])
        place_rows(core_ref, out_ref, three(dot_nn, left, split(dq_ref[...])))

    @pl.when(step >= part)
    def _():
        left = (nt_hi[...], nt_lo[...])
        place_rows(core_ref, out_ref, three(dot_nn, left, split(dk_ref[...])))


def weights_vo_kernel(core_ref, hi_ref, lo_ref, dv_ref, att_ref, res_ref, own_ref, sib_ref,
                      nt_hi, nt_lo, at_hi, at_lo):
    out_ref = (own_ref, sib_ref)
    step = pl.program_id(0)
    part = pl.num_programs(0) // 2

    @pl.when(step == 0)
    def _():
        nt_hi[...] = hi_ref[...].T
        nt_lo[...] = lo_ref[...].T
        at_hi[...], at_lo[...] = split(att_ref[...].T)

    @pl.when(step < part)
    def _():
        left = (nt_hi[...], nt_lo[...])
        place_rows(core_ref, out_ref, three(dot_nn, left, split(dv_ref[...])))

    @pl.when(step >= part)
    def _():
        left = (at_hi[...], at_lo[...])
        place_rows(core_ref, out_ref, three(dot_nn, left, split(res_ref[...])))


def weight_call(kernel, micros, core, chips, fixed_args, pieces, scratch):
    model = fixed_args[0].shape[1]
    wide = 256
    part = model // wide
    tall = model // chips // 2
    fixed = lambda v: pl.BlockSpec(v.shape, lambda j, c: (0, 0))
    piece = lambda v, at: pl.BlockSpec(
        (v.shape[0], wide), lambda j, c: (0, jnp.clip(j - at * part, 0, part - 1))
    )
    specs, args = [], []
    for value, at in pieces:
        args.append(value)
        specs.append(fixed(value) if at is None else piece(value, at))
    return pl.pallas_call(
        kernel,
        grid_spec=pltpu.PrefetchScalarGridSpec(
            num_scalar_prefetch=1,
            grid=(2 * part,),
            in_specs=[fixed(v) for v in fixed_args] + specs,
            out_specs=[pl.BlockSpec((chips, tall, wide), lambda j, c: (0, 0, j))] * 2,
            scratch_shapes=[pltpu.VMEM((model, n), BF16) for n in scratch],
        ),
        out_shape=[jax.ShapeDtypeStruct((chips, tall, 2 * model), F32)] * 2,
        cost_estimate=cost(micros),
        compiler_params=params(),
    )(core, *fixed_args, *args)


def partial_kernel(count, *refs):
    grads, w_ref, out_ref = refs[:count], refs[count], refs[count + 1]
    held = refs[count + 2:]
    model = grads[0].shape[1]
    first = 3 - count

    @pl.when(pl.program_id(0) == 0)
    def _():
        for at, ref in enumerate(grads):
            held[2 * at][...], held[2 * at + 1][...] = split(ref[...])

    total = None
    for at in range(count):
        weights = split(w_ref[:, (first + at) * model:(first + at + 1) * model])
        term = three(dot_nt, (held[2 * at][...], held[2 * at + 1][...]), weights)
        total = term if total is None else total + term
    out_ref[...] = total


def partial_rows(block, grads, w_full):
    model = w_full.shape[0]
    rows = grads[0].shape[0] if len(grads) == 3 else grads[0].shape[0] // 3
    wide = 256
    specs = [pl.BlockSpec((rows, model), lambda j: (block, 0))] * 2
    if len(grads) == 3:
        specs = [pl.BlockSpec((rows, model), lambda j: (0, 0))] + specs
    return pl.pallas_call(
        functools.partial(partial_kernel, len(grads)),
        grid=(model // wide,),
        in_specs=specs + [pl.BlockSpec((wide, 3 * model), lambda j: (j, 0))],
        out_specs=pl.BlockSpec((rows, wide), lambda j: (0, j)),
        out_shape=jax.ShapeDtypeStruct((rows, model), F32),
        scratch_shapes=[pltpu.VMEM((rows, model), BF16)] * (2 * len(grads)),
        cost_estimate=cost(6),
        compiler_params=params(),
    )(*grads, w_full)


def matmul(left, right):
    return jnp.dot(left, right, precision=HIGH)


def inner_rows(left, right):
    return lax.dot_general(left, right, (((0,), (0,)), ((), ())), precision=HIGH)


def outer_cols(left, right):
    return lax.dot_general(left, right, (((1,), (1,)), ((), ())), precision=HIGH)


def body(
    block_input,
    embedding,
    earlier_outs,
    dwa_weights,
    ln1_gain,
    ln1_bias,
    w_qkv,
    w_out,
    ln2_gain,
    ln2_bias,
    w_up,
    w_down,
    segments,
    cotangent,
):
    groups = lax.axis_size("seq")
    rows, model = block_input.shape
    length = rows * groups
    halo = 2 * rows
    place = lax.axis_index("seq")
    ahead = [(i, i + 1) for i in range(groups - 1)]
    behind = [(i + 1, i) for i in range(groups - 1)]
    gain1, bias1 = ln1_gain[None], ln1_bias[None]
    gain2, bias2 = ln2_gain[None], ln2_bias[None]

    devices = lax.axis_size("dp")
    chips = devices // 2
    spot = lax.axis_index("dp")
    core = spot % 2
    chip = (spot // 2).reshape(1).astype(jnp.int32)
    same_core = [[2 * i + c for i in range(chips)] for c in range(2)]
    exchange = lambda v, bit: lax.ppermute(v, "dp", [(i, i ^ bit) for i in range(devices)])
    swap = lambda v: exchange(v, 1)

    gather = lambda v: lax.all_gather(v, "dp", axis=0, tiled=True)
    qkv_full = gather(w_qkv)

    shard = w_down.shape[0]
    third = shard // 3
    by_core = w_up.reshape(w_up.shape[0], chips, 2, 3, third)
    by_core = jnp.transpose(by_core, (2, 0, 3, 1, 4)).reshape(2, w_up.shape[0], -1)
    mine = jnp.where(core == 0, by_core[0], by_core[1])
    given = swap(jnp.where(core == 0, by_core[1], by_core[0]))
    up_chip = jnp.concatenate(
        [jnp.where(core == 0, mine, given), jnp.where(core == 0, given, mine)], axis=0
    )
    if chips == 4:
        up_x, down_x = exchange(up_chip, 2), exchange(w_down, 2)
        up_y, down_y = exchange(up_chip, 4), exchange(w_down, 4)
        ups = [up_chip, up_x, up_y, exchange(up_y, 2)]
        downs = [w_down, down_x, down_y, exchange(down_x, 4)]
    else:
        ups, downs = (
            [lax.all_gather(v, "dp", axis=0, tiled=True, axis_index_groups=same_core)]
            for v in (up_chip, w_down)
        )

    seg_own = segments + 1
    near = lax.ppermute(block_input, "seq", ahead)
    seg_near = lax.ppermute(seg_own, "seq", ahead)
    far = lax.ppermute(near, "seq", ahead)
    seg_far = lax.ppermute(seg_near, "seq", ahead)
    seg_all = jnp.concatenate([seg_far, seg_near, seg_own], axis=1)
    seg_k_row = jnp.broadcast_to(seg_all, (8, halo + rows))
    seg_k_col = jnp.broadcast_to(seg_all.reshape(-1, 1), (halo + rows, 128))
    seg_q_row = seg_k_row[:, halo:]
    seg_q_col = seg_k_col[halo:]

    cos_all, sin_all = rotary_tables(length, halo)
    cosine = lax.dynamic_slice_in_dim(jnp.asarray(cos_all), place * rows, halo + rows, 0)
    sine = lax.dynamic_slice_in_dim(jnp.asarray(sin_all), place * rows, halo + rows, 0)

    earlier = (embedding, earlier_outs[0], earlier_outs[1], earlier_outs[2])
    base = sum(dwa_weights[i] * value for i, value in enumerate(earlier))
    dots = jnp.stack([jnp.sum(cotangent * value) for value in earlier])
    far, base, dots = lax.optimization_barrier((far, base, dots))

    q_rot, kv, normed_hi, normed_lo = project(
        far, near, block_input, gain1, bias1, qkv_full, cosine, sine
    )
    attended = attend(q_rot, kv, seg_q_col, seg_k_row)

    out_full = gather(w_out)
    resid = block_input + matmul(attended, out_full)
    resid_other = swap(resid)
    cot_other = swap(cotangent)
    scale = dwa_weights[4].reshape(1, 1)
    call = functools.partial(
        mlp, chip=chip, chips=chips, resid=resid, other=resid_other, cot=cotangent,
        cot_other=cot_other, gain=gain2, bias=bias2, scale=scale, ups=ups, downs=downs,
    )
    scatter = lambda v: lax.psum_scatter(v, "dp", scatter_dimension=0, tiled=True)
    scatter_chips = lambda v: lax.psum_scatter(
        v, "dp", scatter_dimension=0, tiled=True, axis_index_groups=same_core
    )
    so_far, shards = (), []
    for third_at in range(3):
        out_part, gnorm_part, grads = call(third_at, 1, so_far)
        so_far = (out_part, gnorm_part)
        shards.append(scatter_chips(grads)[0])
    given = swap(gnorm_part[rows:])

    shift = lambda v, bit: lax.ppermute(v, "seq", [(i, i ^ bit) for i in range(groups)])
    even = place % 2 == 0

    def line_start(shard):
        tall = shard.shape[1] // 2
        halves = (shard[:, :tall], shard[:, tall:])
        kept = jnp.where(even, halves[0], halves[1])
        return kept + shift(jnp.where(even, halves[1], halves[0]), 1)

    def line_middle(kept):
        bit = 2
        while bit < groups:
            kept = kept + shift(kept, bit)
            bit *= 2
        return kept

    def line_end(kept):
        other = shift(kept, 1)
        return jnp.where(even, kept, other), jnp.where(even, other, kept)

    together = lax.optimization_barrier
    shards[0], given = together((shards[0], given))
    line_a = line_start(shards[0])
    grad_resid, grad_attended, sums_two = resid_back(
        gnorm_part, given, resid, cotangent, gain2, scale, out_full
    )

    back_args = (q_rot, kv, grad_attended, seg_q_row, seg_k_col, cosine, sine)
    pairs = model // 128
    line_a, back_args = together((line_a, back_args))
    line_a = line_middle(line_a)
    first_half = attend_back(0, pairs // 2, *back_args)
    line_a, shards[1], back_args, first_half = together(
        (line_a, shards[1], back_args, first_half)
    )
    line_b = line_start(shards[1])
    ends_a = line_end(line_a)
    dq, dk, dv = attend_back(pairs // 2, pairs - pairs // 2, *back_args, before=first_half)
    line_b, ends_a, dq, dk, dv = together((line_b, ends_a, dq, dk, dv))
    line_b = line_middle(line_b)
    core_at = core.reshape(1).astype(jnp.int32)
    normed_parts = (normed_hi, normed_lo)
    grads_qk = weight_call(
        weights_qk_kernel, 9, core_at, chips, normed_parts, [(dq, 0), (dk, 1)], [halo + rows] * 2
    )
    given_qk = swap(grads_qk[1])
    line_b, shards[2], dv, grad_resid = together((line_b, shards[2], dv, grad_resid))
    ends_b = line_end(line_b)
    line_c = line_start(shards[2])
    grads_vo = weight_call(
        weights_vo_kernel, 9, core_at, chips, normed_parts,
        [(dv, 0), (attended, None), (grad_resid, 1)], [halo + rows] * 2 + [rows] * 2,
    )
    line_c, ends_b, grads_vo = together((line_c, ends_b, grads_vo))
    line_c = line_middle(line_c)
    grads_c = jnp.concatenate([grads_qk[0] + given_qk, grads_vo[0] + swap(grads_vo[1])], axis=2)
    grads_c, out_part = together((grads_c, out_part))
    shard_c = scatter_chips(grads_c)[0]
    out_sib = swap(out_part[rows:])

    block_out = resid + out_part[:rows] + out_sib
    output = base + dwa_weights[4] * block_out
    dwa_local = jnp.concatenate([dots, jnp.sum(cotangent * block_out)[None]])

    part_far = partial_rows(0, (dk, dv), qkv_full)
    given_near = lax.ppermute(part_far, "seq", behind)
    dk, far, near, line_c, part_far = together((dk, far, near, line_c, part_far))
    ends_c = line_end(line_c)
    part_near = partial_rows(1, (dk, dv), qkv_full)
    own_part = partial_rows(2, (dq, dk, dv), qkv_full)
    own_part, ends_c = together((own_part, ends_c))
    (sent,) = together((part_near,))
    back_near = sent + given_near

    xhat1, rate1 = norm_stats(block_input)
    terms = (
        (norm_stats(far)[0], part_far),
        (norm_stats(near)[0], part_near),
        (xhat1, own_part),
    )
    grad_gain_one = sum(jnp.sum(xhat * part, axis=0) for xhat, part in terms)
    grad_bias_one = sum(jnp.sum(part, axis=0) for _, part in terms)

    small = jnp.concatenate(
        [
            grad_gain_one[None], grad_bias_one[None], sums_two[:2],
            jnp.pad(dwa_local, (0, model - 5))[None], jnp.zeros((3, model), F32),
        ],
        axis=0,
    )
    bit = 1
    while bit < devices:
        small = small + exchange(small, bit)
        bit *= 2
    shard_c, back_near, small = together((shard_c, back_near, small))
    last = line_middle(line_start(shard_c[None]))
    given_back = lax.ppermute(back_near, "seq", behind)
    grad_up, grad_down = unpack_grads(
        *(
            jnp.concatenate(parts, axis=0)
            for parts in zip(ends_a, ends_b, ends_c)
        ),
        swap, core, chips,
    )
    last, grad_up, grad_down, small, given_back = together(
        (last, grad_up, grad_down, small, given_back)
    )
    bit = 1
    while bit < groups:
        small = small + shift(small, bit)
        bit *= 2
    gain_one, bias_one, gain_two, bias_two = small[0], small[1], small[2], small[3]
    grad_dwa = small[4, :5]
    last = jnp.concatenate(line_end(last), axis=1)[0]
    grad_qkv, grad_wout = last[:, :3 * model], last[:, 3 * model:]
    grad_normed_one = own_part + given_back
    grad_input = grad_resid + norm_back(grad_normed_one, gain1, xhat1, rate1)
    return (
        output,
        grad_input,
        grad_dwa,
        gain_one,
        bias_one,
        grad_qkv,
        grad_wout,
        gain_two,
        bias_two,
        grad_up,
        grad_down,
    )


def solution(mesh):
    in_specs = (
        P(("dp", "seq"), None),
        P(("dp", "seq"), None),
        P(None, ("dp", "seq"), None),
        P(),
        P(),
        P(),
        P("dp", None),
        P("dp", None),
        P(),
        P(),
        P("dp", None),
        P("dp", None),
        P("dp", "seq"),
        P(("dp", "seq"), None),
    )
    out_specs = (
        P(("dp", "seq"), None),
        P(("dp", "seq"), None),
        P(),
        P(),
        P(),
        P("dp", None),
        P("dp", None),
        P(),
        P(),
        P("dp", None),
        P("dp", None),
    )
    return jax.shard_map(body, mesh=mesh, in_specs=in_specs, out_specs=out_specs, check_vma=False)
```

```python
import functools
import math

import jax
import jax.numpy as jnp
import numpy as np
from jax import lax
from jax.experimental import pallas as pl
from jax.experimental.pallas import tpu as pltpu
from jax.sharding import PartitionSpec as P

HD = 64
DOC_MOST = 768
LOG2E = math.log2(math.e)
SCALE = 1.0 / math.sqrt(HD)
NEG = -1e30
F32 = jnp.float32
BF16 = jnp.bfloat16
HIGH = lax.Precision.HIGH
VMEM_LIMIT = 56 * 1024 * 1024
BLK = 128


def cost(micros):
    return pl.CostEstimate(
        flops=int(micros * 1.1e9), bytes_accessed=1 << 20, transcendentals=0
    )


def params():
    return pltpu.CompilerParams(
        dimension_semantics=("arbitrary",), vmem_limit_bytes=VMEM_LIMIT
    )


def split(values):
    high = values.astype(BF16)
    return high, (values - high.astype(F32)).astype(BF16)


def dot_nn(left, right):
    return lax.dot_general(left, right, (((1,), (0,)), ((), ())), preferred_element_type=F32)


def dot_nt(left, right):
    return lax.dot_general(left, right, (((1,), (1,)), ((), ())), preferred_element_type=F32)


def dot_tn(left, right):
    return lax.dot_general(left, right, (((0,), (0,)), ((), ())), preferred_element_type=F32)


def three(dot, left, right):
    return (
        dot(left[0], right[0]) + dot(left[0], right[1]) + dot(left[1], right[0])
    )


def norm_stats(values):
    row_mean = jnp.mean(values, axis=-1, keepdims=True)
    centred = values - row_mean
    row_var = jnp.mean(centred * centred, axis=-1, keepdims=True)
    rate = lax.rsqrt(row_var + 1e-05)
    return centred * rate, rate


def norm_back(grad, gain, xhat, rate):
    scaled = grad * gain
    return rate * (
        scaled
        - jnp.mean(scaled, axis=-1, keepdims=True)
        - xhat * jnp.mean(scaled * xhat, axis=-1, keepdims=True)
    )


def turned(values):
    lane = lax.broadcasted_iota(jnp.int32, values.shape, 1)
    return jnp.where(
        (lane & 63) < 32, pltpu.roll(values, 96, 1), pltpu.roll(values, 32, 1)
    )


def rotate(values, cosine, sine):
    return values * cosine + turned(values) * sine


def unrotate(values, cosine, sine):
    return values * cosine - turned(values) * sine


def rotary_tables(length, halo):
    half = HD // 2
    inv_freq = (10000.0 ** (-(np.arange(half, dtype=np.float32) * 2.0 / HD))).astype(np.float32)
    place = np.arange(-halo, length, dtype=np.float32)
    angles = place[:, None] * inv_freq[None, :]
    cosine = np.cos(angles.astype(np.float64)).astype(np.float32)
    sine = np.sin(angles.astype(np.float64)).astype(np.float32)
    return (
        np.concatenate([cosine] * 4, axis=1),
        np.concatenate([-sine, sine, -sine, sine], axis=1),
    )


def qkv_kernel(far_ref, near_ref, own_ref, gain_ref, bias_ref, w_ref, cos_ref, sin_ref,
               q_ref, kv_ref, hi_ref, lo_ref):
    step = pl.program_id(0)
    rows = own_ref.shape[0]
    third = pl.num_programs(0) // 3
    halo = hi_ref.shape[0] - rows

    @pl.when(step == 0)
    def _():
        for at, ref in enumerate((far_ref, near_ref, own_ref)):
            xhat, _ = norm_stats(ref[...])
            high, low = split(xhat * gain_ref[...] + bias_ref[...])
            hi_ref[at * rows:(at + 1) * rows] = high
            lo_ref[at * rows:(at + 1) * rows] = low

    weights = split(w_ref[...])

    @pl.when(step < third)
    def _():
        got = three(dot_nn, (hi_ref[halo:], lo_ref[halo:]), weights)
        for at in range(0, got.shape[1], 128):
            q_ref[:, at:at + 128] = rotate(got[:, at:at + 128], cos_ref[halo:], sin_ref[halo:])

    @pl.when((step >= third) & (step < 2 * third))
    def _():
        got = three(dot_nn, (hi_ref[...], lo_ref[...]), weights)
        for at in range(0, got.shape[1], 128):
            kv_ref[:, at:at + 128] = rotate(got[:, at:at + 128], cos_ref[...], sin_ref[...])

    @pl.when(step >= 2 * third)
    def _():
        kv_ref[...] = three(dot_nn, (hi_ref[...], lo_ref[...]), weights)


def project(far, near, own, gain, bias, w_full, cosine, sine):
    rows, model = own.shape
    total = 3 * rows
    wide = 256
    third = model // wide
    whole = lambda shape: pl.BlockSpec(shape, lambda j: (0, 0))
    return pl.pallas_call(
        qkv_kernel,
        grid=(3 * third,),
        in_specs=[
            whole((rows, model)), whole((rows, model)), whole((rows, model)),
            whole((1, model)), whole((1, model)),
            pl.BlockSpec((model, wide), lambda j: (0, j)),
            whole((total, 128)), whole((total, 128)),
        ],
        out_specs=[
            pl.BlockSpec((rows, wide), lambda j: (0, jnp.minimum(j, third - 1))),
            pl.BlockSpec((total, wide), lambda j: (0, jnp.maximum(j - third, 0))),
            whole((total, model)), whole((total, model)),
        ],
        out_shape=[
            jax.ShapeDtypeStruct((rows, model), F32),
            jax.ShapeDtypeStruct((total, 2 * model), F32),
            jax.ShapeDtypeStruct((total, model), BF16),
            jax.ShapeDtypeStruct((total, model), BF16),
        ],
        cost_estimate=cost(0.5),
        compiler_params=params(),
    )(far, near, own, gain, bias, w_full, cosine, sine)


def own_pair(values, head):
    lane = lax.broadcasted_iota(jnp.int32, values.shape, 1)
    other = pltpu.roll(values, 64, 1)
    return jnp.where((lane < 64) == (head == 0), values, other)


def outer_form(values, head):
    high, low = split(own_pair(values, head))
    return jnp.concatenate([high, low], axis=1)


def mixed(values, head):
    pair = own_pair(values, head)
    lane = lax.broadcasted_iota(jnp.int32, pair.shape, 1)
    high = pair.astype(BF16).astype(F32)
    return jnp.where(lane < 64, high, pair - high).astype(BF16)


def inner_form(values, head):
    half = mixed(values, head)
    return jnp.concatenate([half, half], axis=1)


def fold(values):
    return values + pltpu.roll(values, 64, 1)


def attend_kernel(q_ref, k_ref, v_ref, segq_ref, segk_ref, out_ref, bias_ref):
    rows = q_ref.shape[0]
    halo = k_ref.shape[0] - rows
    span = halo + BLK

    @pl.when(pl.program_id(0) == 0)
    def _():
        for at in range(0, rows, BLK):
            row = lax.broadcasted_iota(jnp.int32, (BLK, span), 0)
            col = lax.broadcasted_iota(jnp.int32, (BLK, span), 1)
            same = segq_ref[at:at + BLK, :1] == segk_ref[:1, at:at + span]
            bias_ref[at:at + BLK] = jnp.where(same & (col - halo <= row), 0.0, NEG)

    lane = lax.broadcasted_iota(jnp.int32, (BLK, 128), 1)
    scaled = q_ref[...] * (SCALE * LOG2E)
    results = []
    for head in range(2):
        left = inner_form(scaled, head)
        right = outer_form(k_ref[...], head)
        vals = mixed(v_ref[...], head)
        outs = []
        for at in range(0, rows, BLK):
            scores = dot_nt(left[at:at + BLK], right[at:at + span]) + bias_ref[at:at + BLK]
            top = jnp.max(scores, axis=1, keepdims=True)
            expo = jnp.exp2(scores - top)
            total = jnp.sum(expo, axis=1, keepdims=True)
            high, low = split(expo)
            got = dot_nn(high, vals[at:at + span]) + dot_nn(low, vals[at:at + span])
            outs.append(fold(got) / total)
        results.append(outs)
    for at in range(0, rows, BLK):
        out_ref[at:at + BLK] = jnp.where(
            lane < 64, results[0][at // BLK], results[1][at // BLK]
        )


def attend(q_rot, kv, seg_q, seg_k):
    rows, model = q_rot.shape
    total = kv.shape[0]
    pairs = model // 128
    return pl.pallas_call(
        attend_kernel,
        grid=(pairs,),
        in_specs=[
            pl.BlockSpec((rows, 128), lambda p: (0, p)),
            pl.BlockSpec((total, 128), lambda p: (0, p)),
            pl.BlockSpec((total, 128), lambda p: (0, pairs + p)),
            pl.BlockSpec((rows, 128), lambda p: (0, 0)),
            pl.BlockSpec((8, total), lambda p: (0, 0)),
        ],
        out_specs=pl.BlockSpec((rows, 128), lambda p: (0, p)),
        out_shape=jax.ShapeDtypeStruct((rows, model), F32),
        scratch_shapes=[pltpu.VMEM((rows, total - rows + BLK), F32)],
        cost_estimate=cost(0.5),
        compiler_params=params(),
    )(q_rot, kv, kv, seg_q, seg_k)


def attend_back_kernel(q_ref, k_ref, v_ref, g_ref, segq_ref, segk_ref, cos_ref, sin_ref, *refs):
    dq_ref, dk_ref, dv_ref, bias_ref = refs[-4:]
    rows = q_ref.shape[0]
    halo = k_ref.shape[0] - rows
    span = halo + BLK

    @pl.when(pl.program_id(0) == 0)
    def _():
        for at in range(0, rows, BLK):
            key = lax.broadcasted_iota(jnp.int32, (span, BLK), 0)
            query = lax.broadcasted_iota(jnp.int32, (span, BLK), 1)
            same = segk_ref[at:at + span, :1] == segq_ref[:1, at:at + BLK]
            bias_ref[:, at:at + BLK] = jnp.where(same & (key - halo <= query), 0.0, NEG)

    scaled = q_ref[...] * (SCALE * LOG2E)
    dq, dk, dv = [], [], []
    for head in range(2):
        q_in = inner_form(scaled, head)
        g_in = inner_form(g_ref[...], head)
        k_out = outer_form(k_ref[...], head)
        v_out = outer_form(v_ref[...], head)
        q_mix = mixed(q_ref[...], head)
        g_mix = mixed(g_ref[...], head)
        k_mix = mixed(k_ref[...], head)
        dq_head = []
        dk_head = jnp.zeros((halo + rows, 128), F32)
        dv_head = jnp.zeros((halo + rows, 128), F32)
        dk_parts, dv_parts = [], []
        for at in range(0, rows, BLK):
            scores = dot_nt(k_out[at:at + span], q_in[at:at + BLK]) + bias_ref[:, at:at + BLK]
            top = jnp.max(scores, axis=0, keepdims=True)
            expo = jnp.exp2(scores - top)
            inverse = 1.0 / jnp.sum(expo, axis=0, keepdims=True)
            grad_probs = dot_nt(v_out[at:at + span], g_in[at:at + BLK])
            probs = expo * inverse
            delta = jnp.sum(probs * grad_probs, axis=0, keepdims=True)
            grad_scores = probs * (grad_probs - delta)
            probs_cat = jnp.concatenate(split(probs), axis=1)
            scores_cat = jnp.concatenate(split(grad_scores), axis=1)
            g_two = jnp.concatenate([g_mix[at:at + BLK]] * 2, axis=0)
            q_two = jnp.concatenate([q_mix[at:at + BLK]] * 2, axis=0)
            dv_parts.append(dot_nn(probs_cat, g_two))
            dk_parts.append(dot_nn(scores_cat, q_two))
            got = dot_tn(scores_cat, k_mix[at:at + span])
            dq_head.append(fold(got[:BLK] + got[BLK:]))
        for parts, full in ((dk_parts, dk), (dv_parts, dv)):
            pieces = []
            for kb in range((halo + rows) // BLK):
                terms = [
                    parts[qb][(kb - qb) * BLK:(kb - qb + 1) * BLK]
                    for qb in range(rows // BLK)
                    if 0 <= kb - qb < span // BLK
                ]
                pieces.append(fold(functools.reduce(lambda a, b: a + b, terms)))
            full.append(pieces)
        dq.append(dq_head)
    lane = lax.broadcasted_iota(jnp.int32, (BLK, 128), 1)
    for qb in range(rows // BLK):
        rng = slice(qb * BLK, (qb + 1) * BLK)
        far = slice(halo + qb * BLK, halo + (qb + 1) * BLK)
        both = jnp.where(lane < 64, dq[0][qb], dq[1][qb]) * SCALE
        dq_ref[rng] = unrotate(both, cos_ref[far], sin_ref[far])
    for kb in range((halo + rows) // BLK):
        rng = slice(kb * BLK, (kb + 1) * BLK)
        both = jnp.where(lane < 64, dk[0][kb], dk[1][kb]) * SCALE
        dk_ref[rng] = unrotate(both, cos_ref[rng], sin_ref[rng])
        dv_ref[rng] = jnp.where(lane < 64, dv[0][kb], dv[1][kb])


def attend_back(first, count, q_rot, kv, grad, seg_q, seg_k, cosine, sine, before=()):
    rows, model = q_rot.shape
    total = kv.shape[0]
    pairs = model // 128
    fixed = lambda shape: pl.BlockSpec(shape, lambda p: (0, 0))
    return pl.pallas_call(
        attend_back_kernel,
        grid=(count,),
        in_specs=[
            pl.BlockSpec((rows, 128), lambda p: (0, first + p)),
            pl.BlockSpec((total, 128), lambda p: (0, first + p)),
            pl.BlockSpec((total, 128), lambda p: (0, pairs + first + p)),
            pl.BlockSpec((rows, 128), lambda p: (0, first + p)),
            fixed((8, rows)), fixed((total, 128)),
            fixed((total, 128)), fixed((total, 128)),
        ] + [pl.BlockSpec(memory_space=pl.ANY)] * len(before),
        out_specs=[
            pl.BlockSpec((rows, 128), lambda p: (0, first + p)),
            pl.BlockSpec((total, 128), lambda p: (0, first + p)),
            pl.BlockSpec((total, 128), lambda p: (0, first + p)),
        ],
        out_shape=[
            jax.ShapeDtypeStruct((rows, model), F32),
            jax.ShapeDtypeStruct((total, model), F32),
            jax.ShapeDtypeStruct((total, model), F32),
        ],
        scratch_shapes=[pltpu.VMEM((total - rows + BLK, rows), F32)],
        input_output_aliases={8 + i: i for i in range(len(before))},
        cost_estimate=cost(7 * count),
        compiler_params=params(),
    )(q_rot, kv, kv, grad, seg_q, seg_k, cosine, sine, *before)


def mlp_kernel(count, begun, chip_ref, resid_ref, other_ref, cot_ref, cot_other_ref, gain_ref, bias_ref,
               scale_ref, *refs):
    weight_refs, refs = refs[:max(1, 2 * count)], refs[max(1, 2 * count):]
    so_far, refs = refs[:2 * begun], refs[2 * begun:]
    out_ref, gnorm_ref, grad_ref = refs[:3]
    (x_hi, x_lo, xt_hi, xt_lo, g_hi, g_lo, up_hi, up_lo, down_hi, down_lo) = refs[3:]
    step = pl.program_id(0)
    rows = resid_ref.shape[0]

    @pl.when(step == 0)
    def _():
        for at, source, cot in ((0, resid_ref, cot_ref), (rows, other_ref, cot_other_ref)):
            xhat, _ = norm_stats(source[...])
            normed = xhat * gain_ref[...] + bias_ref[...]
            x_hi[at:at + rows], x_lo[at:at + rows] = split(normed)
            xt_hi[:, at:at + rows], xt_lo[:, at:at + rows] = split(normed.T)
            g_hi[at:at + rows], g_lo[at:at + rows] = split(cot[...] * scale_ref[0, 0])
        if begun:
            out_ref[...] = so_far[0][...]
            gnorm_ref[...] = so_far[1][...]
        else:
            out_ref[...] = jnp.zeros_like(out_ref)
            gnorm_ref[...] = jnp.zeros_like(gnorm_ref)

    chips, _, tall, width = grad_ref.shape
    up_tall = up_hi.shape[0] // chips
    deep = down_hi.shape[0] // chips
    half = deep // 2

    def place(spot, values, targets, folded):
        for part, target in zip(split(values), targets):
            if folded:
                here = pl.ds(pl.multiple_of(spot * deep, deep), deep)
                target[here, :width] = part[:deep]
                target[here, width:] = jnp.concatenate(
                    [part[deep:, :width // 2], part[deep:, width // 2:]], axis=0
                )
            else:
                target[pl.ds(pl.multiple_of(spot * up_tall, up_tall), up_tall)] = part

    for at in range(count):
        place(chip_ref[0] ^ at, weight_refs[at][...], (up_hi, up_lo), False)
        place(chip_ref[0] ^ at, weight_refs[count + at][...], (down_hi, down_lo), True)
    if count == 0:
        for at in range(chips):
            place(at, weight_refs[0][at, :up_tall], (up_hi, up_lo), False)
            place(at, weight_refs[0][at, up_tall:], (down_hi, down_lo), True)
    up = (up_hi[...], up_lo[...])
    down = (down_hi[...], down_lo[...])
    normed = (x_hi[...], x_lo[...])
    normed_t = (xt_hi[...], xt_lo[...])
    grad_block = (g_hi[...], g_lo[...])
    pre = three(dot_nn, normed, up)
    grad_act = three(dot_nt, grad_block, down)
    inner = 0.7978845608028654 * (pre + 0.044715 * pre * pre * pre)
    bent = jnp.tanh(inner)
    act = 0.5 * pre * (1.0 + bent)
    slope = 0.5 * (1.0 + bent) + 0.5 * pre * (1.0 - bent * bent) * (
        0.7978845608028654 * (1.0 + 3.0 * 0.044715 * pre * pre)
    )
    act2 = split(act)
    grad_pre = split(grad_act * slope)
    out_ref[...] += three(dot_nn, act2, down)
    gnorm_ref[...] += three(dot_nt, grad_pre, up)
    gup = three(dot_nn, normed_t, grad_pre)
    gdown = three(dot_tn, act2, grad_block)
    for chip in range(chips):
        grad_ref[chip, 0, :up_tall] = gup[chip * up_tall:(chip + 1) * up_tall]
        part = gdown[chip * deep:(chip + 1) * deep]
        grad_ref[chip, 0, up_tall:up_tall + deep] = part[:, :width]
        grad_ref[chip, 0, up_tall + deep:] = jnp.concatenate(
            [part[:half, width:], part[half:, width:]], axis=1
        )


def mlp(so_far, weights, chip, chips, resid, other, cot, cot_other, gain, bias, scale):
    rows, model = resid.shape
    width = 512
    up_tall = model // chips
    deep = width // chips
    fixed = lambda shape: pl.BlockSpec(shape, lambda j, c: (0, 0))
    if len(weights) > 1:
        specs = [
            pl.BlockSpec((up_tall, width), lambda j, c, at=at: (at, 0)) for _, at in weights
        ]
        weights = [value for value, _ in weights]
    else:
        specs = [pl.BlockSpec(weights[0].shape, lambda j, c: (0, 0, 0))]
    count = len(weights) // 2
    tall = up_tall + deep + deep // 2
    grid_spec = pltpu.PrefetchScalarGridSpec(
        num_scalar_prefetch=1,
        grid=(1,),
        in_specs=[fixed((rows, model))] * 4 + [fixed((1, model))] * 2
        + [pl.BlockSpec(memory_space=pltpu.SMEM)]
        + specs
        + [fixed((2 * rows, model))] * len(so_far),
        out_specs=[
            fixed((2 * rows, model)), fixed((2 * rows, model)),
            pl.BlockSpec((chips, 1, tall, width), lambda j, c: (0, j, 0, 0)),
        ],
        scratch_shapes=[
            pltpu.VMEM((2 * rows, model), BF16), pltpu.VMEM((2 * rows, model), BF16),
            pltpu.VMEM((model, 2 * rows), BF16), pltpu.VMEM((model, 2 * rows), BF16),
            pltpu.VMEM((2 * rows, model), BF16), pltpu.VMEM((2 * rows, model), BF16),
            pltpu.VMEM((model, width), BF16), pltpu.VMEM((model, width), BF16),
            pltpu.VMEM((width, model), BF16), pltpu.VMEM((width, model), BF16),
        ],
    )
    return pl.pallas_call(
        functools.partial(mlp_kernel, count, len(so_far) // 2),
        grid_spec=grid_spec,
        out_shape=[
            jax.ShapeDtypeStruct((2 * rows, model), F32),
            jax.ShapeDtypeStruct((2 * rows, model), F32),
            jax.ShapeDtypeStruct((chips, 1, tall, width), F32),
        ],
        cost_estimate=cost(18),
        compiler_params=params(),
    )(chip, resid, other, cot, cot_other, gain, bias, scale, *weights, *so_far)


def fold_rows(values, width):
    rows = values.shape[0]
    right = values[:, width:]
    return jnp.concatenate(
        [
            values[:, :width],
            jnp.concatenate([right[:rows // 2], right[rows // 2:]], axis=1),
        ],
        axis=0,
    )


def unpack_grads(up, down, sibling_swap, core, chips):
    steps, up_tall, width = up.shape
    deep = up_tall * 2 // 3
    half = up_tall // 2
    mine = jnp.where(core == 0, up[:, :half], up[:, half:])
    other = sibling_swap(jnp.where(core == 0, up[:, half:], up[:, :half]))
    by_core = jnp.stack(
        [jnp.where(core == 0, mine, other), jnp.where(core == 0, other, mine)], axis=0
    )
    by_core = by_core.reshape(2, steps, half, chips, width // chips)
    grad_up = jnp.transpose(by_core, (2, 3, 0, 1, 4)).reshape(half, -1)
    quarter = width // 2
    tail = down[:, deep:]
    right = jnp.concatenate([tail[:, :, :quarter], tail[:, :, quarter:]], axis=1)
    grad_down = jnp.concatenate([down[:, :deep], right], axis=2).reshape(steps * deep, -1)
    return grad_up, grad_down


def resid_back_kernel(part_ref, given_ref, resid_ref, cot_ref, gain_ref, scale_ref, w_ref,
                      grad_ref, att_ref, sums_ref):
    grad = part_ref[...] + given_ref[...]
    xhat, rate = norm_stats(resid_ref[...])
    grad_resid = cot_ref[...] * scale_ref[0, 0] + norm_back(grad, gain_ref[...], xhat, rate)
    grad_ref[...] = grad_resid
    att_ref[...] = three(dot_nt, split(grad_resid), split(w_ref[...]))
    gain_sum = jnp.sum(grad * xhat, axis=0, keepdims=True)
    bias_sum = jnp.sum(grad, axis=0, keepdims=True)
    sums_ref[...] = jnp.concatenate(
        [gain_sum, bias_sum, jnp.zeros((6, gain_sum.shape[1]), F32)], axis=0
    )


def resid_back(part, given, resid, cot, gain, scale, w_full):
    rows, model = resid.shape
    fixed = lambda shape: pl.BlockSpec(shape, lambda j: (0, 0))
    return pl.pallas_call(
        resid_back_kernel,
        grid=(1,),
        in_specs=[fixed((rows, model))] * 4 + [fixed((1, model))]
        + [pl.BlockSpec(memory_space=pltpu.SMEM), fixed((model, model))],
        out_specs=[fixed((rows, model)), fixed((rows, model)), fixed((8, model))],
        out_shape=[
            jax.ShapeDtypeStruct((rows, model), F32),
            jax.ShapeDtypeStruct((rows, model), F32),
            jax.ShapeDtypeStruct((8, model), F32),
        ],
        cost_estimate=cost(6),
        compiler_params=params(),
    )(part, given, resid, cot, gain, scale, w_full)


def place_rows(core_ref, out_refs, got):
    chips, tall = out_refs[0].shape[:2]

    def store(core):
        for block in range(2 * chips):
            ref = out_refs[(block & 1) ^ core]
            ref[block // 2] = got[block * tall:(block + 1) * tall]

    for core in range(2):
        pl.when(core_ref[0] == core)(functools.partial(store, core))


def weights_qk_kernel(core_ref, hi_ref, lo_ref, dq_ref, dk_ref, own_ref, sib_ref, nt_hi, nt_lo):
    out_ref = (own_ref, sib_ref)
    step = pl.program_id(0)
    part = pl.num_programs(0) // 2
    halo = hi_ref.shape[0] - dq_ref.shape[0]

    @pl.when(step == 0)
    def _():
        nt_hi[...] = hi_ref[...].T
        nt_lo[...] = lo_ref[...].T

    @pl.when(step < part)
    def _():
        left = (nt_hi[:, halo:], nt_lo[:, halo:])
        place_rows(core_ref, out_ref, three(dot_nn, left, split(dq_ref[...])))

    @pl.when(step >= part)
    def _():
        left = (nt_hi[...], nt_lo[...])
        place_rows(core_ref, out_ref, three(dot_nn, left, split(dk_ref[...])))


def weights_vo_kernel(core_ref, hi_ref, lo_ref, dv_ref, att_ref, res_ref, own_ref, sib_ref,
                      nt_hi, nt_lo, at_hi, at_lo):
    out_ref = (own_ref, sib_ref)
    step = pl.program_id(0)
    part = pl.num_programs(0) // 2

    @pl.when(step == 0)
    def _():
        nt_hi[...] = hi_ref[...].T
        nt_lo[...] = lo_ref[...].T
        at_hi[...], at_lo[...] = split(att_ref[...].T)

    @pl.when(step < part)
    def _():
        left = (nt_hi[...], nt_lo[...])
        place_rows(core_ref, out_ref, three(dot_nn, left, split(dv_ref[...])))

    @pl.when(step >= part)
    def _():
        left = (at_hi[...], at_lo[...])
        place_rows(core_ref, out_ref, three(dot_nn, left, split(res_ref[...])))


def weight_call(kernel, micros, core, chips, fixed_args, pieces, scratch):
    model = fixed_args[0].shape[1]
    wide = 256
    part = model // wide
    tall = model // chips // 2
    fixed = lambda v: pl.BlockSpec(v.shape, lambda j, c: (0, 0))
    piece = lambda v, at: pl.BlockSpec(
        (v.shape[0], wide), lambda j, c: (0, jnp.clip(j - at * part, 0, part - 1))
    )
    specs, args = [], []
    for value, at in pieces:
        args.append(value)
        specs.append(fixed(value) if at is None else piece(value, at))
    return pl.pallas_call(
        kernel,
        grid_spec=pltpu.PrefetchScalarGridSpec(
            num_scalar_prefetch=1,
            grid=(2 * part,),
            in_specs=[fixed(v) for v in fixed_args] + specs,
            out_specs=[pl.BlockSpec((chips, tall, wide), lambda j, c: (0, 0, j))] * 2,
            scratch_shapes=[pltpu.VMEM((model, n), BF16) for n in scratch],
        ),
        out_shape=[jax.ShapeDtypeStruct((chips, tall, 2 * model), F32)] * 2,
        cost_estimate=cost(micros),
        compiler_params=params(),
    )(core, *fixed_args, *args)


def partial_kernel(count, *refs):
    grads, w_ref, out_ref = refs[:count], refs[count], refs[count + 1]
    held = refs[count + 2:]
    model = grads[0].shape[1]
    first = 3 - count

    @pl.when(pl.program_id(0) == 0)
    def _():
        for at, ref in enumerate(grads):
            held[2 * at][...], held[2 * at + 1][...] = split(ref[...])

    total = None
    for at in range(count):
        weights = split(w_ref[:, (first + at) * model:(first + at + 1) * model])
        term = three(dot_nt, (held[2 * at][...], held[2 * at + 1][...]), weights)
        total = term if total is None else total + term
    out_ref[...] = total


def partial_rows(block, grads, w_full):
    model = w_full.shape[0]
    rows = grads[0].shape[0] if len(grads) == 3 else grads[0].shape[0] // 3
    wide = 256
    specs = [pl.BlockSpec((rows, model), lambda j: (block, 0))] * 2
    if len(grads) == 3:
        specs = [pl.BlockSpec((rows, model), lambda j: (0, 0))] + specs
    return pl.pallas_call(
        functools.partial(partial_kernel, len(grads)),
        grid=(model // wide,),
        in_specs=specs + [pl.BlockSpec((wide, 3 * model), lambda j: (j, 0))],
        out_specs=pl.BlockSpec((rows, wide), lambda j: (0, j)),
        out_shape=jax.ShapeDtypeStruct((rows, model), F32),
        scratch_shapes=[pltpu.VMEM((rows, model), BF16)] * (2 * len(grads)),
        cost_estimate=cost(6),
        compiler_params=params(),
    )(*grads, w_full)


def matmul(left, right):
    return jnp.dot(left, right, precision=HIGH)


def inner_rows(left, right):
    return lax.dot_general(left, right, (((0,), (0,)), ((), ())), precision=HIGH)


def outer_cols(left, right):
    return lax.dot_general(left, right, (((1,), (1,)), ((), ())), precision=HIGH)


def body(
    block_input,
    embedding,
    earlier_outs,
    dwa_weights,
    ln1_gain,
    ln1_bias,
    w_qkv,
    w_out,
    ln2_gain,
    ln2_bias,
    w_up,
    w_down,
    segments,
    cotangent,
):
    groups = lax.axis_size("seq")
    rows, model = block_input.shape
    length = rows * groups
    halo = 2 * rows
    place = lax.axis_index("seq")
    ahead = [(i, i + 1) for i in range(groups - 1)]
    behind = [(i + 1, i) for i in range(groups - 1)]
    gain1, bias1 = ln1_gain[None], ln1_bias[None]
    gain2, bias2 = ln2_gain[None], ln2_bias[None]

    devices = lax.axis_size("dp")
    chips = devices // 2
    spot = lax.axis_index("dp")
    core = spot % 2
    chip = (spot // 2).reshape(1).astype(jnp.int32)
    same_core = [[2 * i + c for i in range(chips)] for c in range(2)]
    exchange = lambda v, bit: lax.ppermute(v, "dp", [(i, i ^ bit) for i in range(devices)])
    swap = lambda v: exchange(v, 1)

    gather = lambda v: lax.all_gather(v, "dp", axis=0, tiled=True)
    qkv_full = gather(w_qkv)

    shard = w_down.shape[0]
    third = shard // 3
    by_core = w_up.reshape(w_up.shape[0], chips, 2, 3, third)
    by_core = jnp.transpose(by_core, (2, 0, 3, 1, 4)).reshape(2, w_up.shape[0], -1)
    mine = jnp.where(core == 0, by_core[0], by_core[1])
    given = swap(jnp.where(core == 0, by_core[1], by_core[0]))
    up_chip = jnp.concatenate(
        [jnp.where(core == 0, mine, given), jnp.where(core == 0, given, mine)], axis=0
    )
    width = up_chip.shape[1] // 3
    together = lax.optimization_barrier
    thirds = [
        (up_chip[:, i * width:(i + 1) * width], fold_rows(w_down[i * third:(i + 1) * third], width))
        for i in range(3)
    ]
    first_own = jnp.concatenate(thirds[0], axis=0)
    rest_own = jnp.concatenate([thirds[1][0], thirds[2][0], thirds[1][1], thirds[2][1]], axis=0)

    def sides_of(own):
        return [exchange(own, 2), exchange(own, 4)] if chips == 4 else []

    def diagonal_of(sides):
        if chips != 4:
            return []
        middle = sides[0].shape[0] // 2
        return [exchange(sides[1][:middle], 2), exchange(sides[0][middle:], 4)]

    def pieces(own, sides, diagonal, at):
        if chips != 4:
            own = own.reshape(2, -1, up_chip.shape[0], width)[:, at].reshape(-1, width)
            return [
                lax.all_gather(own, "dp", axis=0, axis_index_groups=same_core)
            ]
        below = own.shape[0] // up_chip.shape[0] // 2
        ups = [(own, at), (sides[0], at), (sides[1], at), (diagonal[0], at)]
        downs = [(value, below + at) for value in (own, *sides)] + [(diagonal[1], at)]
        return ups + downs

    numbers = jnp.pad((segments + 1).astype(F32), ((0, 7), (0, model - rows)))
    near = lax.ppermute(jnp.concatenate([block_input, numbers], axis=0), "seq", ahead)
    far = lax.ppermute(near, "seq", ahead)
    seg_all = jnp.concatenate(
        [far[rows:rows + 1, :rows], near[rows:rows + 1, :rows], numbers[:1, :rows]], axis=1
    ).astype(jnp.int32)
    seg_k_row = jnp.broadcast_to(seg_all, (8, halo + rows))
    seg_k_col = jnp.broadcast_to(seg_all.reshape(-1, 1), (halo + rows, 128))

    cos_all, sin_all = rotary_tables(length, halo)
    cosine = lax.dynamic_slice_in_dim(jnp.asarray(cos_all), place * rows, halo + rows, 0)
    sine = lax.dynamic_slice_in_dim(jnp.asarray(sin_all), place * rows, halo + rows, 0)

    earlier = (embedding, earlier_outs[0], earlier_outs[1], earlier_outs[2])
    base = sum(dwa_weights[i] * value for i, value in enumerate(earlier))
    dots = jnp.stack([jnp.sum(cotangent * value) for value in earlier])
    tables = (cosine, sine, seg_k_row, seg_k_col)
    far, base, dots, qkv_full, first_own, rest_own, tables = together(
        (far, base, dots, qkv_full, first_own, rest_own, tables)
    )
    cosine, sine, seg_k_row, seg_k_col = tables
    seg_q_row, seg_q_col = seg_k_row[:, halo:], seg_k_col[halo:]
    first_sides, rest_sides = sides_of(first_own), sides_of(rest_own)

    q_rot, kv, normed_hi, normed_lo = project(
        far, near, block_input, gain1, bias1, qkv_full, cosine, sine
    )
    attended = attend(q_rot, kv, seg_q_col, seg_k_row)
    attended, first_sides = together((attended, first_sides))
    first_diagonal = diagonal_of(first_sides)

    out_full = gather(w_out)
    resid = block_input + matmul(attended, out_full)
    resid, rest_sides, first_diagonal = together((resid, rest_sides, first_diagonal))
    rest_diagonal = diagonal_of(rest_sides)
    resid_other = swap(resid)
    cot_other = swap(cotangent)
    scale = dwa_weights[4].reshape(1, 1)
    call = functools.partial(
        mlp, chip=chip, chips=chips, resid=resid, other=resid_other, cot=cotangent,
        cot_other=cot_other, gain=gain2, bias=bias2, scale=scale,
    )
    scatter = lambda v: lax.psum_scatter(v, "dp", scatter_dimension=0, tiled=True)
    scatter_chips = lambda v: lax.psum_scatter(
        v, "dp", scatter_dimension=0, tiled=True, axis_index_groups=same_core
    )
    so_far, shards = (), []
    for third_at in range(3):
        if third_at == 0:
            weights = pieces(first_own, first_sides, first_diagonal, 0)
        else:
            weights = pieces(rest_own, rest_sides, rest_diagonal, third_at - 1)
        out_part, gnorm_part, grads = call(so_far, weights)
        if third_at == 0:
            grads, rest_diagonal = together((grads, rest_diagonal))
        so_far = (out_part, gnorm_part)
        shards.append(scatter_chips(grads)[0])
    given = swap(gnorm_part[rows:])

    shift = lambda v, bit: lax.ppermute(v, "seq", [(i, i ^ bit) for i in range(groups)])
    even = place % 2 == 0

    def line_start(shard):
        tall = shard.shape[1] // 2
        halves = (shard[:, :tall], shard[:, tall:])
        kept = jnp.where(even, halves[0], halves[1])
        return kept + shift(jnp.where(even, halves[1], halves[0]), 1)

    def line_middle(kept):
        bit = 2
        while bit < groups:
            kept = kept + shift(kept, bit)
            bit *= 2
        return kept

    def line_end(kept):
        other = shift(kept, 1)
        return jnp.where(even, kept, other), jnp.where(even, other, kept)

    shards[0], given = together((shards[0], given))
    line_a = line_start(shards[0])
    grad_resid, grad_attended, sums_two = resid_back(
        gnorm_part, given, resid, cotangent, gain2, scale, out_full
    )

    back_args = (q_rot, kv, grad_attended, seg_q_row, seg_k_col, cosine, sine)
    pairs = model // 128
    line_a, back_args = together((line_a, back_args))
    line_a = line_middle(line_a)
    first_half = attend_back(0, pairs // 2, *back_args)
    line_a, shards[1], back_args, first_half = together(
        (line_a, shards[1], back_args, first_half)
    )
    line_b = line_start(shards[1])
    ends_a = line_end(line_a)
    dq, dk, dv = attend_back(pairs // 2, pairs - pairs // 2, *back_args, before=first_half)
    line_b, ends_a, dq, dk, dv = together((line_b, ends_a, dq, dk, dv))
    line_b = line_middle(line_b)
    core_at = core.reshape(1).astype(jnp.int32)
    normed_parts = (normed_hi, normed_lo)
    grads_qk = weight_call(
        weights_qk_kernel, 9, core_at, chips, normed_parts, [(dq, 0), (dk, 1)], [halo + rows] * 2
    )
    given_qk = swap(grads_qk[1])
    line_b, shards[2], dv, grad_resid = together((line_b, shards[2], dv, grad_resid))
    ends_b = line_end(line_b)
    line_c = line_start(shards[2])
    grads_vo = weight_call(
        weights_vo_kernel, 9, core_at, chips, normed_parts,
        [(dv, 0), (attended, None), (grad_resid, 1)], [halo + rows] * 2 + [rows] * 2,
    )
    line_c, ends_b, grads_vo = together((line_c, ends_b, grads_vo))
    line_c = line_middle(line_c)
    grads_c = jnp.concatenate([grads_qk[0] + given_qk, grads_vo[0] + swap(grads_vo[1])], axis=2)
    grads_c, out_part = together((grads_c, out_part))
    shard_c = scatter_chips(grads_c)[0]
    out_sib = swap(out_part[rows:])

    block_out = resid + out_part[:rows] + out_sib
    output = base + dwa_weights[4] * block_out
    dwa_local = jnp.concatenate([dots, jnp.sum(cotangent * block_out)[None]])

    part_far = partial_rows(0, (dk, dv), qkv_full)
    given_near = lax.ppermute(part_far, "seq", behind)
    dk, far, near, line_c, part_far = together((dk, far, near, line_c, part_far))
    ends_c = line_end(line_c)
    part_near = partial_rows(1, (dk, dv), qkv_full)
    own_part = partial_rows(2, (dq, dk, dv), qkv_full)
    own_part, ends_c = together((own_part, ends_c))
    (sent,) = together((part_near,))
    back_near = sent + given_near

    xhat1, rate1 = norm_stats(block_input)
    terms = (
        (norm_stats(far[:rows])[0], part_far),
        (norm_stats(near[:rows])[0], part_near),
        (xhat1, own_part),
    )
    grad_gain_one = sum(jnp.sum(xhat * part, axis=0) for xhat, part in terms)
    grad_bias_one = sum(jnp.sum(part, axis=0) for _, part in terms)

    small = jnp.concatenate(
        [
            grad_gain_one[None], grad_bias_one[None], sums_two[:2],
            jnp.pad(dwa_local, (0, model - 5))[None], jnp.zeros((3, model), F32),
        ],
        axis=0,
    )
    bit = 1
    while bit < devices:
        small = small + exchange(small, bit)
        bit *= 2
    shard_c, back_near, small = together((shard_c, back_near, small))
    last = line_middle(line_start(shard_c[None]))
    given_back = lax.ppermute(back_near, "seq", behind)
    grad_up, grad_down = unpack_grads(
        *(
            jnp.concatenate(parts, axis=0)
            for parts in zip(ends_a, ends_b, ends_c)
        ),
        swap, core, chips,
    )
    last, grad_up, grad_down, small, given_back = together(
        (last, grad_up, grad_down, small, given_back)
    )
    bit = 1
    while bit < groups:
        small = small + shift(small, bit)
        bit *= 2
    gain_one, bias_one, gain_two, bias_two = small[0], small[1], small[2], small[3]
    grad_dwa = small[4, :5]
    last = jnp.concatenate(line_end(last), axis=1)[0]
    grad_qkv, grad_wout = last[:, :3 * model], last[:, 3 * model:]
    grad_normed_one = own_part + given_back
    grad_input = grad_resid + norm_back(grad_normed_one, gain1, xhat1, rate1)
    return (
        output,
        grad_input,
        grad_dwa,
        gain_one,
        bias_one,
        grad_qkv,
        grad_wout,
        gain_two,
        bias_two,
        grad_up,
        grad_down,
    )


def solution(mesh):
    in_specs = (
        P(("dp", "seq"), None),
        P(("dp", "seq"), None),
        P(None, ("dp", "seq"), None),
        P(),
        P(),
        P(),
        P("dp", None),
        P("dp", None),
        P(),
        P(),
        P("dp", None),
        P("dp", None),
        P("dp", "seq"),
        P(("dp", "seq"), None),
    )
    out_specs = (
        P(("dp", "seq"), None),
        P(("dp", "seq"), None),
        P(),
        P(),
        P(),
        P("dp", None),
        P("dp", None),
        P(),
        P(),
        P("dp", None),
        P("dp", None),
    )
    return jax.shard_map(body, mesh=mesh, in_specs=in_specs, out_specs=out_specs, check_vma=False)
```

```python
import functools
import math

import jax
import jax.numpy as jnp
import numpy as np
from jax import lax
from jax.experimental import pallas as pl
from jax.experimental.pallas import tpu as pltpu
from jax.sharding import PartitionSpec as P

HD = 64
DOC_MOST = 768
LOG2E = math.log2(math.e)
SCALE = 1.0 / math.sqrt(HD)
NEG = -1e30
F32 = jnp.float32
BF16 = jnp.bfloat16
HIGH = lax.Precision.HIGH
VMEM_LIMIT = 56 * 1024 * 1024
BLK = 128


def cost(micros):
    return pl.CostEstimate(
        flops=int(micros * 1.1e9), bytes_accessed=1 << 20, transcendentals=0
    )


def params():
    return pltpu.CompilerParams(
        dimension_semantics=("arbitrary",), vmem_limit_bytes=VMEM_LIMIT
    )


def split(values):
    high = values.astype(BF16)
    return high, (values - high.astype(F32)).astype(BF16)


def dot_nn(left, right):
    return lax.dot_general(left, right, (((1,), (0,)), ((), ())), preferred_element_type=F32)


def dot_nt(left, right):
    return lax.dot_general(left, right, (((1,), (1,)), ((), ())), preferred_element_type=F32)


def dot_tn(left, right):
    return lax.dot_general(left, right, (((0,), (0,)), ((), ())), preferred_element_type=F32)


def three(dot, left, right):
    return (
        dot(left[0], right[0]) + dot(left[0], right[1]) + dot(left[1], right[0])
    )


def norm_stats(values):
    row_mean = jnp.mean(values, axis=-1, keepdims=True)
    centred = values - row_mean
    row_var = jnp.mean(centred * centred, axis=-1, keepdims=True)
    rate = lax.rsqrt(row_var + 1e-05)
    return centred * rate, rate


def norm_back(grad, gain, xhat, rate):
    scaled = grad * gain
    return rate * (
        scaled
        - jnp.mean(scaled, axis=-1, keepdims=True)
        - xhat * jnp.mean(scaled * xhat, axis=-1, keepdims=True)
    )


def turned(values):
    lane = lax.broadcasted_iota(jnp.int32, values.shape, 1)
    return jnp.where(
        (lane & 63) < 32, pltpu.roll(values, 96, 1), pltpu.roll(values, 32, 1)
    )


def rotate(values, cosine, sine):
    return values * cosine + turned(values) * sine


def unrotate(values, cosine, sine):
    return values * cosine - turned(values) * sine


def rotary_tables(length, halo):
    half = HD // 2
    inv_freq = (10000.0 ** (-(np.arange(half, dtype=np.float32) * 2.0 / HD))).astype(np.float32)
    place = np.arange(-halo, length, dtype=np.float32)
    angles = place[:, None] * inv_freq[None, :]
    cosine = np.cos(angles.astype(np.float64)).astype(np.float32)
    sine = np.sin(angles.astype(np.float64)).astype(np.float32)
    return (
        np.concatenate([cosine] * 4, axis=1),
        np.concatenate([-sine, sine, -sine, sine], axis=1),
    )


def qkv_kernel(far_ref, near_ref, own_ref, gain_ref, bias_ref, w_ref, cos_ref, sin_ref,
               q_ref, kv_ref, hi_ref, lo_ref):
    step = pl.program_id(0)
    rows = own_ref.shape[0]
    third = pl.num_programs(0) // 3
    halo = hi_ref.shape[0] - rows

    @pl.when(step == 0)
    def _():
        for at, ref in enumerate((far_ref, near_ref, own_ref)):
            xhat, _ = norm_stats(ref[...])
            high, low = split(xhat * gain_ref[...] + bias_ref[...])
            hi_ref[at * rows:(at + 1) * rows] = high
            lo_ref[at * rows:(at + 1) * rows] = low

    weights = split(w_ref[...])

    @pl.when(step < third)
    def _():
        got = three(dot_nn, (hi_ref[halo:], lo_ref[halo:]), weights)
        for at in range(0, got.shape[1], 128):
            q_ref[:, at:at + 128] = rotate(got[:, at:at + 128], cos_ref[halo:], sin_ref[halo:])

    @pl.when((step >= third) & (step < 2 * third))
    def _():
        got = three(dot_nn, (hi_ref[...], lo_ref[...]), weights)
        for at in range(0, got.shape[1], 128):
            kv_ref[:, at:at + 128] = rotate(got[:, at:at + 128], cos_ref[...], sin_ref[...])

    @pl.when(step >= 2 * third)
    def _():
        kv_ref[...] = three(dot_nn, (hi_ref[...], lo_ref[...]), weights)


def project(far, near, own, gain, bias, w_full, cosine, sine):
    rows, model = own.shape
    total = 3 * rows
    wide = 256
    third = model // wide
    whole = lambda shape: pl.BlockSpec(shape, lambda j: (0, 0))
    return pl.pallas_call(
        qkv_kernel,
        grid=(3 * third,),
        in_specs=[
            whole((rows, model)), whole((rows, model)), whole((rows, model)),
            whole((1, model)), whole((1, model)),
            pl.BlockSpec((model, wide), lambda j: (0, j)),
            whole((total, 128)), whole((total, 128)),
        ],
        out_specs=[
            pl.BlockSpec((rows, wide), lambda j: (0, jnp.minimum(j, third - 1))),
            pl.BlockSpec((total, wide), lambda j: (0, jnp.maximum(j - third, 0))),
            whole((total, model)), whole((total, model)),
        ],
        out_shape=[
            jax.ShapeDtypeStruct((rows, model), F32),
            jax.ShapeDtypeStruct((total, 2 * model), F32),
            jax.ShapeDtypeStruct((total, model), BF16),
            jax.ShapeDtypeStruct((total, model), BF16),
        ],
        cost_estimate=cost(20),
        compiler_params=params(),
    )(far, near, own, gain, bias, w_full, cosine, sine)


def own_pair(values, head):
    lane = lax.broadcasted_iota(jnp.int32, values.shape, 1)
    other = pltpu.roll(values, 64, 1)
    return jnp.where((lane < 64) == (head == 0), values, other)


def outer_form(values, head):
    high, low = split(own_pair(values, head))
    return jnp.concatenate([high, low], axis=1)


def mixed(values, head):
    pair = own_pair(values, head)
    lane = lax.broadcasted_iota(jnp.int32, pair.shape, 1)
    high = pair.astype(BF16).astype(F32)
    return jnp.where(lane < 64, high, pair - high).astype(BF16)


def inner_form(values, head):
    half = mixed(values, head)
    return jnp.concatenate([half, half], axis=1)


def fold(values):
    return values + pltpu.roll(values, 64, 1)


def attend_kernel(q_ref, k_ref, v_ref, segq_ref, segk_ref, out_ref, bias_ref):
    rows = q_ref.shape[0]
    halo = k_ref.shape[0] - rows
    span = halo + BLK

    @pl.when(pl.program_id(0) == 0)
    def _():
        for at in range(0, rows, BLK):
            row = lax.broadcasted_iota(jnp.int32, (BLK, span), 0)
            col = lax.broadcasted_iota(jnp.int32, (BLK, span), 1)
            same = segq_ref[at:at + BLK, :1] == segk_ref[:1, at:at + span]
            bias_ref[at:at + BLK] = jnp.where(same & (col - halo <= row), 0.0, NEG)

    lane = lax.broadcasted_iota(jnp.int32, (BLK, 128), 1)
    scaled = q_ref[...] * (SCALE * LOG2E)
    results = []
    for head in range(2):
        left = inner_form(scaled, head)
        right = outer_form(k_ref[...], head)
        vals = mixed(v_ref[...], head)
        outs = []
        for at in range(0, rows, BLK):
            scores = dot_nt(left[at:at + BLK], right[at:at + span]) + bias_ref[at:at + BLK]
            top = jnp.max(scores, axis=1, keepdims=True)
            expo = jnp.exp2(scores - top)
            total = jnp.sum(expo, axis=1, keepdims=True)
            high, low = split(expo)
            got = dot_nn(high, vals[at:at + span]) + dot_nn(low, vals[at:at + span])
            outs.append(fold(got) / total)
        results.append(outs)
    for at in range(0, rows, BLK):
        out_ref[at:at + BLK] = jnp.where(
            lane < 64, results[0][at // BLK], results[1][at // BLK]
        )


def attend(q_rot, kv, seg_q, seg_k):
    rows, model = q_rot.shape
    total = kv.shape[0]
    pairs = model // 128
    return pl.pallas_call(
        attend_kernel,
        grid=(pairs,),
        in_specs=[
            pl.BlockSpec((rows, 128), lambda p: (0, p)),
            pl.BlockSpec((total, 128), lambda p: (0, p)),
            pl.BlockSpec((total, 128), lambda p: (0, pairs + p)),
            pl.BlockSpec((rows, 128), lambda p: (0, 0)),
            pl.BlockSpec((8, total), lambda p: (0, 0)),
        ],
        out_specs=pl.BlockSpec((rows, 128), lambda p: (0, p)),
        out_shape=jax.ShapeDtypeStruct((rows, model), F32),
        scratch_shapes=[pltpu.VMEM((rows, total - rows + BLK), F32)],
        cost_estimate=cost(24),
        compiler_params=params(),
    )(q_rot, kv, kv, seg_q, seg_k)


def attend_back_kernel(q_ref, k_ref, v_ref, g_ref, segq_ref, segk_ref, cos_ref, sin_ref, *refs):
    dq_ref, dk_ref, dv_ref, bias_ref = refs[-4:]
    rows = q_ref.shape[0]
    halo = k_ref.shape[0] - rows
    span = halo + BLK

    @pl.when(pl.program_id(0) == 0)
    def _():
        for at in range(0, rows, BLK):
            key = lax.broadcasted_iota(jnp.int32, (span, BLK), 0)
            query = lax.broadcasted_iota(jnp.int32, (span, BLK), 1)
            same = segk_ref[at:at + span, :1] == segq_ref[:1, at:at + BLK]
            bias_ref[:, at:at + BLK] = jnp.where(same & (key - halo <= query), 0.0, NEG)

    scaled = q_ref[...] * (SCALE * LOG2E)
    dq, dk, dv = [], [], []
    for head in range(2):
        q_in = inner_form(scaled, head)
        g_in = inner_form(g_ref[...], head)
        k_out = outer_form(k_ref[...], head)
        v_out = outer_form(v_ref[...], head)
        q_mix = mixed(q_ref[...], head)
        g_mix = mixed(g_ref[...], head)
        k_mix = mixed(k_ref[...], head)
        dq_head = []
        dk_head = jnp.zeros((halo + rows, 128), F32)
        dv_head = jnp.zeros((halo + rows, 128), F32)
        dk_parts, dv_parts = [], []
        for at in range(0, rows, BLK):
            scores = dot_nt(k_out[at:at + span], q_in[at:at + BLK]) + bias_ref[:, at:at + BLK]
            top = jnp.max(scores, axis=0, keepdims=True)
            expo = jnp.exp2(scores - top)
            inverse = 1.0 / jnp.sum(expo, axis=0, keepdims=True)
            grad_probs = dot_nt(v_out[at:at + span], g_in[at:at + BLK])
            probs = expo * inverse
            delta = jnp.sum(probs * grad_probs, axis=0, keepdims=True)
            grad_scores = probs * (grad_probs - delta)
            probs_cat = jnp.concatenate(split(probs), axis=1)
            scores_cat = jnp.concatenate(split(grad_scores), axis=1)
            g_two = jnp.concatenate([g_mix[at:at + BLK]] * 2, axis=0)
            q_two = jnp.concatenate([q_mix[at:at + BLK]] * 2, axis=0)
            dv_parts.append(dot_nn(probs_cat, g_two))
            dk_parts.append(dot_nn(scores_cat, q_two))
            got = dot_tn(scores_cat, k_mix[at:at + span])
            dq_head.append(fold(got[:BLK] + got[BLK:]))
        for parts, full in ((dk_parts, dk), (dv_parts, dv)):
            pieces = []
            for kb in range((halo + rows) // BLK):
                terms = [
                    parts[qb][(kb - qb) * BLK:(kb - qb + 1) * BLK]
                    for qb in range(rows // BLK)
                    if 0 <= kb - qb < span // BLK
                ]
                pieces.append(fold(functools.reduce(lambda a, b: a + b, terms)))
            full.append(pieces)
        dq.append(dq_head)
    lane = lax.broadcasted_iota(jnp.int32, (BLK, 128), 1)
    for qb in range(rows // BLK):
        rng = slice(qb * BLK, (qb + 1) * BLK)
        far = slice(halo + qb * BLK, halo + (qb + 1) * BLK)
        both = jnp.where(lane < 64, dq[0][qb], dq[1][qb]) * SCALE
        dq_ref[rng] = unrotate(both, cos_ref[far], sin_ref[far])
    for kb in range((halo + rows) // BLK):
        rng = slice(kb * BLK, (kb + 1) * BLK)
        both = jnp.where(lane < 64, dk[0][kb], dk[1][kb]) * SCALE
        dk_ref[rng] = unrotate(both, cos_ref[rng], sin_ref[rng])
        dv_ref[rng] = jnp.where(lane < 64, dv[0][kb], dv[1][kb])


def attend_back(first, count, q_rot, kv, grad, seg_q, seg_k, cosine, sine, before=()):
    rows, model = q_rot.shape
    total = kv.shape[0]
    pairs = model // 128
    fixed = lambda shape: pl.BlockSpec(shape, lambda p: (0, 0))
    return pl.pallas_call(
        attend_back_kernel,
        grid=(count,),
        in_specs=[
            pl.BlockSpec((rows, 128), lambda p: (0, first + p)),
            pl.BlockSpec((total, 128), lambda p: (0, first + p)),
            pl.BlockSpec((total, 128), lambda p: (0, pairs + first + p)),
            pl.BlockSpec((rows, 128), lambda p: (0, first + p)),
            fixed((8, rows)), fixed((total, 128)),
            fixed((total, 128)), fixed((total, 128)),
        ] + [pl.BlockSpec(memory_space=pl.ANY)] * len(before),
        out_specs=[
            pl.BlockSpec((rows, 128), lambda p: (0, first + p)),
            pl.BlockSpec((total, 128), lambda p: (0, first + p)),
            pl.BlockSpec((total, 128), lambda p: (0, first + p)),
        ],
        out_shape=[
            jax.ShapeDtypeStruct((rows, model), F32),
            jax.ShapeDtypeStruct((total, model), F32),
            jax.ShapeDtypeStruct((total, model), F32),
        ],
        scratch_shapes=[pltpu.VMEM((total - rows + BLK, rows), F32)],
        input_output_aliases={8 + i: i for i in range(len(before))},
        cost_estimate=cost(7 * count),
        compiler_params=params(),
    )(q_rot, kv, kv, grad, seg_q, seg_k, cosine, sine, *before)


def mlp_kernel(count, begun, chip_ref, resid_ref, other_ref, cot_ref, cot_other_ref, gain_ref, bias_ref,
               scale_ref, *refs):
    up_refs, down_refs = refs[:count], refs[count:2 * count]
    refs = refs[2 * count:]
    so_far, refs = refs[:2 * begun], refs[2 * begun:]
    out_ref, gnorm_ref, grad_ref = refs[:3]
    (x_hi, x_lo, xt_hi, xt_lo, g_hi, g_lo, up_hi, up_lo, down_hi, down_lo) = refs[3:]
    step = pl.program_id(0)
    rows = resid_ref.shape[0]

    @pl.when(step == 0)
    def _():
        for at, source, cot in ((0, resid_ref, cot_ref), (rows, other_ref, cot_other_ref)):
            xhat, _ = norm_stats(source[...])
            normed = xhat * gain_ref[...] + bias_ref[...]
            x_hi[at:at + rows], x_lo[at:at + rows] = split(normed)
            xt_hi[:, at:at + rows], xt_lo[:, at:at + rows] = split(normed.T)
            g_hi[at:at + rows], g_lo[at:at + rows] = split(cot[...] * scale_ref[0, 0])
        if begun:
            out_ref[...] = so_far[0][...]
            gnorm_ref[...] = so_far[1][...]
        else:
            out_ref[...] = jnp.zeros_like(out_ref)
            gnorm_ref[...] = jnp.zeros_like(gnorm_ref)

    for at in range(count):
        spot = (chip_ref[0] ^ at) if count > 1 else 0
        up_rows = up_refs[at].shape[0]
        high, low = split(up_refs[at][...])
        here = pl.ds(pl.multiple_of(spot * up_rows, up_rows), up_rows)
        up_hi[here], up_lo[here] = high, low
        block = down_refs[at][...]
        block = block.reshape(-1, block.shape[-1])
        high, low = split(block)
        here = pl.ds(pl.multiple_of(spot * block.shape[0], block.shape[0]), block.shape[0])
        down_hi[here], down_lo[here] = high, low

    chips, _, tall, width = grad_ref.shape
    up_tall = up_hi.shape[0] // chips
    deep = down_hi.shape[0] // chips
    up = (up_hi[...], up_lo[...])
    down = (down_hi[...], down_lo[...])
    normed = (x_hi[...], x_lo[...])
    normed_t = (xt_hi[...], xt_lo[...])
    grad_block = (g_hi[...], g_lo[...])
    pre = three(dot_nn, normed, up)
    grad_act = three(dot_nt, grad_block, down)
    inner = 0.7978845608028654 * (pre + 0.044715 * pre * pre * pre)
    bent = jnp.tanh(inner)
    act = 0.5 * pre * (1.0 + bent)
    slope = 0.5 * (1.0 + bent) + 0.5 * pre * (1.0 - bent * bent) * (
        0.7978845608028654 * (1.0 + 3.0 * 0.044715 * pre * pre)
    )
    act2 = split(act)
    grad_pre = split(grad_act * slope)
    out_ref[...] += three(dot_nn, act2, down)
    gnorm_ref[...] += three(dot_nt, grad_pre, up)
    gup = three(dot_nn, normed_t, grad_pre)
    gdown = three(dot_tn, act2, grad_block)
    half = deep // 2
    for chip in range(chips):
        grad_ref[chip, 0, :up_tall] = gup[chip * up_tall:(chip + 1) * up_tall]
        part = gdown[chip * deep:(chip + 1) * deep]
        grad_ref[chip, 0, up_tall:up_tall + deep] = part[:, :width]
        grad_ref[chip, 0, up_tall + deep:] = jnp.concatenate(
            [part[:half, width:], part[half:, width:]], axis=1
        )


def mlp(first, steps, so_far, chip, chips, resid, other, cot, cot_other, gain, bias, scale, ups, downs):
    rows, model = resid.shape
    width = 512
    up_tall = model // chips
    deep = width // chips
    fixed = lambda shape: pl.BlockSpec(shape, lambda j, c: (0, 0))
    if len(ups) > 1:
        down_spec = pl.BlockSpec((deep, model), lambda j, c: (first + j, 0))
    else:
        downs = [downs[0].reshape(chips, -1, model)]
        down_spec = pl.BlockSpec((chips, deep, model), lambda j, c: (0, first + j, 0))
    tall = up_tall + deep + deep // 2
    grid_spec = pltpu.PrefetchScalarGridSpec(
        num_scalar_prefetch=1,
        grid=(steps,),
        in_specs=[fixed((rows, model))] * 4 + [fixed((1, model))] * 2
        + [pl.BlockSpec(memory_space=pltpu.SMEM)]
        + [pl.BlockSpec((up.shape[0], width), lambda j, c: (0, first + j)) for up in ups]
        + [down_spec] * len(downs)
        + [fixed((2 * rows, model))] * len(so_far),
        out_specs=[
            fixed((2 * rows, model)), fixed((2 * rows, model)),
            pl.BlockSpec((chips, 1, tall, width), lambda j, c: (0, j, 0, 0)),
        ],
        scratch_shapes=[
            pltpu.VMEM((2 * rows, model), BF16), pltpu.VMEM((2 * rows, model), BF16),
            pltpu.VMEM((model, 2 * rows), BF16), pltpu.VMEM((model, 2 * rows), BF16),
            pltpu.VMEM((2 * rows, model), BF16), pltpu.VMEM((2 * rows, model), BF16),
            pltpu.VMEM((model, width), BF16), pltpu.VMEM((model, width), BF16),
            pltpu.VMEM((width, model), BF16), pltpu.VMEM((width, model), BF16),
        ],
    )
    return pl.pallas_call(
        functools.partial(mlp_kernel, len(ups), len(so_far) // 2),
        grid_spec=grid_spec,
        out_shape=[
            jax.ShapeDtypeStruct((2 * rows, model), F32),
            jax.ShapeDtypeStruct((2 * rows, model), F32),
            jax.ShapeDtypeStruct((chips, steps, tall, width), F32),
        ],
        cost_estimate=cost(18 * steps),
        compiler_params=params(),
    )(chip, resid, other, cot, cot_other, gain, bias, scale, *ups, *downs, *so_far)


def unpack_grads(up, down, sibling_swap, core, chips):
    steps, up_tall, width = up.shape
    deep = up_tall * 2 // 3
    half = up_tall // 2
    mine = jnp.where(core == 0, up[:, :half], up[:, half:])
    other = sibling_swap(jnp.where(core == 0, up[:, half:], up[:, :half]))
    by_core = jnp.stack(
        [jnp.where(core == 0, mine, other), jnp.where(core == 0, other, mine)], axis=0
    )
    by_core = by_core.reshape(2, steps, half, chips, width // chips)
    grad_up = jnp.transpose(by_core, (2, 3, 0, 1, 4)).reshape(half, -1)
    quarter = width // 2
    tail = down[:, deep:]
    right = jnp.concatenate([tail[:, :, :quarter], tail[:, :, quarter:]], axis=1)
    grad_down = jnp.concatenate([down[:, :deep], right], axis=2).reshape(steps * deep, -1)
    return grad_up, grad_down


def resid_back_kernel(part_ref, given_ref, resid_ref, cot_ref, gain_ref, scale_ref, w_ref,
                      grad_ref, att_ref, sums_ref):
    grad = part_ref[...] + given_ref[...]
    xhat, rate = norm_stats(resid_ref[...])
    grad_resid = cot_ref[...] * scale_ref[0, 0] + norm_back(grad, gain_ref[...], xhat, rate)
    grad_ref[...] = grad_resid
    att_ref[...] = three(dot_nt, split(grad_resid), split(w_ref[...]))
    gain_sum = jnp.sum(grad * xhat, axis=0, keepdims=True)
    bias_sum = jnp.sum(grad, axis=0, keepdims=True)
    sums_ref[...] = jnp.concatenate(
        [gain_sum, bias_sum, jnp.zeros((6, gain_sum.shape[1]), F32)], axis=0
    )


def resid_back(part, given, resid, cot, gain, scale, w_full):
    rows, model = resid.shape
    fixed = lambda shape: pl.BlockSpec(shape, lambda j: (0, 0))
    return pl.pallas_call(
        resid_back_kernel,
        grid=(1,),
        in_specs=[fixed((rows, model))] * 4 + [fixed((1, model))]
        + [pl.BlockSpec(memory_space=pltpu.SMEM), fixed((model, model))],
        out_specs=[fixed((rows, model)), fixed((rows, model)), fixed((8, model))],
        out_shape=[
            jax.ShapeDtypeStruct((rows, model), F32),
            jax.ShapeDtypeStruct((rows, model), F32),
            jax.ShapeDtypeStruct((8, model), F32),
        ],
        cost_estimate=cost(6),
        compiler_params=params(),
    )(part, given, resid, cot, gain, scale, w_full)


def place_rows(core_ref, out_refs, got):
    chips, tall = out_refs[0].shape[:2]

    def store(core):
        for block in range(2 * chips):
            ref = out_refs[(block & 1) ^ core]
            ref[block // 2] = got[block * tall:(block + 1) * tall]

    for core in range(2):
        pl.when(core_ref[0] == core)(functools.partial(store, core))


def weights_qk_kernel(core_ref, hi_ref, lo_ref, dq_ref, dk_ref, own_ref, sib_ref, nt_hi, nt_lo):
    out_ref = (own_ref, sib_ref)
    step = pl.program_id(0)
    part = pl.num_programs(0) // 2
    halo = hi_ref.shape[0] - dq_ref.shape[0]

    @pl.when(step == 0)
    def _():
        nt_hi[...] = hi_ref[...].T
        nt_lo[...] = lo_ref[...].T

    @pl.when(step < part)
    def _():
        left = (nt_hi[:, halo:], nt_lo[:, halo:])
        place_rows(core_ref, out_ref, three(dot_nn, left, split(dq_ref[...])))

    @pl.when(step >= part)
    def _():
        left = (nt_hi[...], nt_lo[...])
        place_rows(core_ref, out_ref, three(dot_nn, left, split(dk_ref[...])))


def weights_vo_kernel(core_ref, hi_ref, lo_ref, dv_ref, att_ref, res_ref, own_ref, sib_ref,
                      nt_hi, nt_lo, at_hi, at_lo):
    out_ref = (own_ref, sib_ref)
    step = pl.program_id(0)
    part = pl.num_programs(0) // 2

    @pl.when(step == 0)
    def _():
        nt_hi[...] = hi_ref[...].T
        nt_lo[...] = lo_ref[...].T
        at_hi[...], at_lo[...] = split(att_ref[...].T)

    @pl.when(step < part)
    def _():
        left = (nt_hi[...], nt_lo[...])
        place_rows(core_ref, out_ref, three(dot_nn, left, split(dv_ref[...])))

    @pl.when(step >= part)
    def _():
        left = (at_hi[...], at_lo[...])
        place_rows(core_ref, out_ref, three(dot_nn, left, split(res_ref[...])))


def weight_call(kernel, micros, core, chips, fixed_args, pieces, scratch):
    model = fixed_args[0].shape[1]
    wide = 256
    part = model // wide
    tall = model // chips // 2
    fixed = lambda v: pl.BlockSpec(v.shape, lambda j, c: (0, 0))
    piece = lambda v, at: pl.BlockSpec(
        (v.shape[0], wide), lambda j, c: (0, jnp.clip(j - at * part, 0, part - 1))
    )
    specs, args = [], []
    for value, at in pieces:
        args.append(value)
        specs.append(fixed(value) if at is None else piece(value, at))
    return pl.pallas_call(
        kernel,
        grid_spec=pltpu.PrefetchScalarGridSpec(
            num_scalar_prefetch=1,
            grid=(2 * part,),
            in_specs=[fixed(v) for v in fixed_args] + specs,
            out_specs=[pl.BlockSpec((chips, tall, wide), lambda j, c: (0, 0, j))] * 2,
            scratch_shapes=[pltpu.VMEM((model, n), BF16) for n in scratch],
        ),
        out_shape=[jax.ShapeDtypeStruct((chips, tall, 2 * model), F32)] * 2,
        cost_estimate=cost(micros),
        compiler_params=params(),
    )(core, *fixed_args, *args)


def partial_kernel(count, *refs):
    grads, w_ref, out_ref = refs[:count], refs[count], refs[count + 1]
    held = refs[count + 2:]
    model = grads[0].shape[1]
    first = 3 - count

    @pl.when(pl.program_id(0) == 0)
    def _():
        for at, ref in enumerate(grads):
            held[2 * at][...], held[2 * at + 1][...] = split(ref[...])

    total = None
    for at in range(count):
        weights = split(w_ref[:, (first + at) * model:(first + at + 1) * model])
        term = three(dot_nt, (held[2 * at][...], held[2 * at + 1][...]), weights)
        total = term if total is None else total + term
    out_ref[...] = total


def partial_rows(block, grads, w_full):
    model = w_full.shape[0]
    rows = grads[0].shape[0] if len(grads) == 3 else grads[0].shape[0] // 3
    wide = 256
    specs = [pl.BlockSpec((rows, model), lambda j: (block, 0))] * 2
    if len(grads) == 3:
        specs = [pl.BlockSpec((rows, model), lambda j: (0, 0))] + specs
    return pl.pallas_call(
        functools.partial(partial_kernel, len(grads)),
        grid=(model // wide,),
        in_specs=specs + [pl.BlockSpec((wide, 3 * model), lambda j: (j, 0))],
        out_specs=pl.BlockSpec((rows, wide), lambda j: (0, j)),
        out_shape=jax.ShapeDtypeStruct((rows, model), F32),
        scratch_shapes=[pltpu.VMEM((rows, model), BF16)] * (2 * len(grads)),
        cost_estimate=cost(6),
        compiler_params=params(),
    )(*grads, w_full)


def matmul(left, right):
    return jnp.dot(left, right, precision=HIGH)


def inner_rows(left, right):
    return lax.dot_general(left, right, (((0,), (0,)), ((), ())), precision=HIGH)


def outer_cols(left, right):
    return lax.dot_general(left, right, (((1,), (1,)), ((), ())), precision=HIGH)


def body(
    block_input,
    embedding,
    earlier_outs,
    dwa_weights,
    ln1_gain,
    ln1_bias,
    w_qkv,
    w_out,
    ln2_gain,
    ln2_bias,
    w_up,
    w_down,
    segments,
    cotangent,
):
    groups = lax.axis_size("seq")
    rows, model = block_input.shape
    length = rows * groups
    halo = 2 * rows
    place = lax.axis_index("seq")
    ahead = [(i, i + 1) for i in range(groups - 1)]
    behind = [(i + 1, i) for i in range(groups - 1)]
    gain1, bias1 = ln1_gain[None], ln1_bias[None]
    gain2, bias2 = ln2_gain[None], ln2_bias[None]

    devices = lax.axis_size("dp")
    chips = devices // 2
    spot = lax.axis_index("dp")
    core = spot % 2
    chip = (spot // 2).reshape(1).astype(jnp.int32)
    same_core = [[2 * i + c for i in range(chips)] for c in range(2)]
    exchange = lambda v, bit: lax.ppermute(v, "dp", [(i, i ^ bit) for i in range(devices)])
    swap = lambda v: exchange(v, 1)

    gather = lambda v: lax.all_gather(v, "dp", axis=0, tiled=True)
    qkv_full = gather(w_qkv)

    shard = w_down.shape[0]
    third = shard // 3
    by_core = w_up.reshape(w_up.shape[0], chips, 2, 3, third)
    by_core = jnp.transpose(by_core, (2, 0, 3, 1, 4)).reshape(2, w_up.shape[0], -1)
    mine = jnp.where(core == 0, by_core[0], by_core[1])
    given = swap(jnp.where(core == 0, by_core[1], by_core[0]))
    up_chip = jnp.concatenate(
        [jnp.where(core == 0, mine, given), jnp.where(core == 0, given, mine)], axis=0
    )
    if chips == 4:
        up_x, down_x = exchange(up_chip, 2), exchange(w_down, 2)
        up_y, down_y = exchange(up_chip, 4), exchange(w_down, 4)
        ups = [up_chip, up_x, up_y, exchange(up_y, 2)]
        downs = [w_down, down_x, down_y, exchange(down_x, 4)]
    else:
        ups, downs = (
            [lax.all_gather(v, "dp", axis=0, tiled=True, axis_index_groups=same_core)]
            for v in (up_chip, w_down)
        )

    seg_own = segments + 1
    near = lax.ppermute(block_input, "seq", ahead)
    seg_near = lax.ppermute(seg_own, "seq", ahead)
    far = lax.ppermute(near, "seq", ahead)
    seg_far = lax.ppermute(seg_near, "seq", ahead)
    seg_all = jnp.concatenate([seg_far, seg_near, seg_own], axis=1)
    seg_k_row = jnp.broadcast_to(seg_all, (8, halo + rows))
    seg_k_col = jnp.broadcast_to(seg_all.reshape(-1, 1), (halo + rows, 128))
    seg_q_row = seg_k_row[:, halo:]
    seg_q_col = seg_k_col[halo:]

    cos_all, sin_all = rotary_tables(length, halo)
    cosine = lax.dynamic_slice_in_dim(jnp.asarray(cos_all), place * rows, halo + rows, 0)
    sine = lax.dynamic_slice_in_dim(jnp.asarray(sin_all), place * rows, halo + rows, 0)

    earlier = (embedding, earlier_outs[0], earlier_outs[1], earlier_outs[2])
    base = sum(dwa_weights[i] * value for i, value in enumerate(earlier))
    dots = jnp.stack([jnp.sum(cotangent * value) for value in earlier])
    far, base, dots = lax.optimization_barrier((far, base, dots))

    q_rot, kv, normed_hi, normed_lo = project(
        far, near, block_input, gain1, bias1, qkv_full, cosine, sine
    )
    attended = attend(q_rot, kv, seg_q_col, seg_k_row)

    out_full = gather(w_out)
    resid = block_input + matmul(attended, out_full)
    resid_other = swap(resid)
    cot_other = swap(cotangent)
    scale = dwa_weights[4].reshape(1, 1)
    call = functools.partial(
        mlp, chip=chip, chips=chips, resid=resid, other=resid_other, cot=cotangent,
        cot_other=cot_other, gain=gain2, bias=bias2, scale=scale, ups=ups, downs=downs,
    )
    scatter = lambda v: lax.psum_scatter(v, "dp", scatter_dimension=0, tiled=True)
    scatter_chips = lambda v: lax.psum_scatter(
        v, "dp", scatter_dimension=0, tiled=True, axis_index_groups=same_core
    )
    so_far, shards = (), []
    for third_at in range(3):
        out_part, gnorm_part, grads = call(third_at, 1, so_far)
        so_far = (out_part, gnorm_part)
        shards.append(scatter_chips(grads)[0])
    given = swap(gnorm_part[rows:])

    shift = lambda v, bit: lax.ppermute(v, "seq", [(i, i ^ bit) for i in range(groups)])
    even = place % 2 == 0

    def line_start(shard):
        tall = shard.shape[1] // 2
        halves = (shard[:, :tall], shard[:, tall:])
        kept = jnp.where(even, halves[0], halves[1])
        return kept + shift(jnp.where(even, halves[1], halves[0]), 1)

    def line_middle(kept):
        bit = 2
        while bit < groups:
            kept = kept + shift(kept, bit)
            bit *= 2
        return kept

    def line_end(kept):
        other = shift(kept, 1)
        return jnp.where(even, kept, other), jnp.where(even, other, kept)

    together = lax.optimization_barrier
    shards[0], given = together((shards[0], given))
    line_a = line_start(shards[0])
    grad_resid, grad_attended, sums_two = resid_back(
        gnorm_part, given, resid, cotangent, gain2, scale, out_full
    )

    back_args = (q_rot, kv, grad_attended, seg_q_row, seg_k_col, cosine, sine)
    pairs = model // 128
    line_a, back_args = together((line_a, back_args))
    line_a = line_middle(line_a)
    first_half = attend_back(0, pairs // 2, *back_args)
    line_a, shards[1], back_args, first_half = together(
        (line_a, shards[1], back_args, first_half)
    )
    line_b = line_start(shards[1])
    ends_a = line_end(line_a)
    dq, dk, dv = attend_back(pairs // 2, pairs - pairs // 2, *back_args, before=first_half)
    line_b, ends_a, dq, dk, dv = together((line_b, ends_a, dq, dk, dv))
    line_b = line_middle(line_b)
    core_at = core.reshape(1).astype(jnp.int32)
    normed_parts = (normed_hi, normed_lo)
    grads_qk = weight_call(
        weights_qk_kernel, 9, core_at, chips, normed_parts, [(dq, 0), (dk, 1)], [halo + rows] * 2
    )
    given_qk = swap(grads_qk[1])
    line_b, shards[2], dv, grad_resid = together((line_b, shards[2], dv, grad_resid))
    ends_b = line_end(line_b)
    line_c = line_start(shards[2])
    grads_vo = weight_call(
        weights_vo_kernel, 9, core_at, chips, normed_parts,
        [(dv, 0), (attended, None), (grad_resid, 1)], [halo + rows] * 2 + [rows] * 2,
    )
    line_c, ends_b, grads_vo, dk = together((line_c, ends_b, grads_vo, dk))
    part_far = partial_rows(0, (dk, dv), qkv_full)
    line_c = line_middle(line_c)
    grads_c = jnp.concatenate([grads_qk[0] + given_qk, grads_vo[0] + swap(grads_vo[1])], axis=2)
    grads_c, out_part, line_c, part_far = together((grads_c, out_part, line_c, part_far))
    shard_c = scatter_chips(grads_c)[0]
    out_sib = swap(out_part[rows:])

    block_out = resid + out_part[:rows] + out_sib
    output = base + dwa_weights[4] * block_out
    dwa_local = jnp.concatenate([dots, jnp.sum(cotangent * block_out)[None]])

    given_near = lax.ppermute(part_far, "seq", behind)
    ends_c = line_end(line_c)
    part_near = partial_rows(1, (dk, dv), qkv_full)
    given_near, dq = together((given_near, dq))
    own_part = partial_rows(2, (dq, dk, dv), qkv_full)
    own_part, ends_c = together((own_part, ends_c))
    (sent,) = together((part_near,))
    back_near = sent + given_near

    xhat1, rate1 = norm_stats(block_input)
    terms = (
        (norm_stats(far)[0], part_far),
        (norm_stats(near)[0], part_near),
        (xhat1, own_part),
    )
    grad_gain_one = sum(jnp.sum(xhat * part, axis=0) for xhat, part in terms)
    grad_bias_one = sum(jnp.sum(part, axis=0) for _, part in terms)

    small = jnp.concatenate(
        [
            grad_gain_one[None], grad_bias_one[None], sums_two[:2],
            jnp.pad(dwa_local, (0, model - 5))[None], jnp.zeros((3, model), F32),
        ],
        axis=0,
    )
    bit = 1
    while bit < devices:
        small = small + exchange(small, bit)
        bit *= 2
    given_back = lax.ppermute(back_near, "seq", behind)
    shard_c, given_back, small = together((shard_c, given_back, small))
    last = line_middle(line_start(shard_c[None]))
    grad_normed_one = own_part + given_back
    grad_input = grad_resid + norm_back(grad_normed_one, gain1, xhat1, rate1)
    grad_up, grad_down = unpack_grads(
        *(
            jnp.concatenate(parts, axis=0)
            for parts in zip(ends_a, ends_b, ends_c)
        ),
        swap, core, chips,
    )
    last, grad_up, grad_down, small, grad_input = together(
        (last, grad_up, grad_down, small, grad_input)
    )
    bit = 1
    while bit < groups:
        small = small + shift(small, bit)
        bit *= 2
    gain_one, bias_one, gain_two, bias_two = small[0], small[1], small[2], small[3]
    grad_dwa = small[4, :5]
    last = jnp.concatenate(line_end(last), axis=1)[0]
    grad_qkv, grad_wout = last[:, :3 * model], last[:, 3 * model:]
    return (
        output,
        grad_input,
        grad_dwa,
        gain_one,
        bias_one,
        grad_qkv,
        grad_wout,
        gain_two,
        bias_two,
        grad_up,
        grad_down,
    )


def solution(mesh):
    in_specs = (
        P(("dp", "seq"), None),
        P(("dp", "seq"), None),
        P(None, ("dp", "seq"), None),
        P(),
        P(),
        P(),
        P("dp", None),
        P("dp", None),
        P(),
        P(),
        P("dp", None),
        P("dp", None),
        P("dp", "seq"),
        P(("dp", "seq"), None),
    )
    out_specs = (
        P(("dp", "seq"), None),
        P(("dp", "seq"), None),
        P(),
        P(),
        P(),
        P("dp", None),
        P("dp", None),
        P(),
        P(),
        P("dp", None),
        P("dp", None),
    )
    return jax.shard_map(body, mesh=mesh, in_specs=in_specs, out_specs=out_specs, check_vma=False)
```

```python
import functools
import math

import jax
import jax.numpy as jnp
import numpy as np
from jax import lax
from jax.experimental import pallas as pl
from jax.experimental.pallas import tpu as pltpu
from jax.sharding import PartitionSpec as P

HD = 64
DOC_MOST = 768
LOG2E = math.log2(math.e)
SCALE = 1.0 / math.sqrt(HD)
NEG = -1e30
F32 = jnp.float32
BF16 = jnp.bfloat16
HIGH = lax.Precision.HIGH
VMEM_LIMIT = 56 * 1024 * 1024
BLK = 128


def cost(micros):
    return pl.CostEstimate(
        flops=int(micros * 1.1e9), bytes_accessed=1 << 20, transcendentals=0
    )


def params():
    return pltpu.CompilerParams(
        dimension_semantics=("arbitrary",), vmem_limit_bytes=VMEM_LIMIT
    )


def split(values):
    high = values.astype(BF16)
    return high, (values - high.astype(F32)).astype(BF16)


def dot_nn(left, right):
    return lax.dot_general(left, right, (((1,), (0,)), ((), ())), preferred_element_type=F32)


def dot_nt(left, right):
    return lax.dot_general(left, right, (((1,), (1,)), ((), ())), preferred_element_type=F32)


def dot_tn(left, right):
    return lax.dot_general(left, right, (((0,), (0,)), ((), ())), preferred_element_type=F32)


def three(dot, left, right):
    return (
        dot(left[0], right[0]) + dot(left[0], right[1]) + dot(left[1], right[0])
    )


def norm_stats(values):
    row_mean = jnp.mean(values, axis=-1, keepdims=True)
    centred = values - row_mean
    row_var = jnp.mean(centred * centred, axis=-1, keepdims=True)
    rate = lax.rsqrt(row_var + 1e-05)
    return centred * rate, rate


def norm_back(grad, gain, xhat, rate):
    scaled = grad * gain
    return rate * (
        scaled
        - jnp.mean(scaled, axis=-1, keepdims=True)
        - xhat * jnp.mean(scaled * xhat, axis=-1, keepdims=True)
    )


def turned(values):
    lane = lax.broadcasted_iota(jnp.int32, values.shape, 1)
    return jnp.where(
        (lane & 63) < 32, pltpu.roll(values, 96, 1), pltpu.roll(values, 32, 1)
    )


def rotate(values, cosine, sine):
    return values * cosine + turned(values) * sine


def unrotate(values, cosine, sine):
    return values * cosine - turned(values) * sine


def rotary_tables(length, halo):
    half = HD // 2
    inv_freq = (10000.0 ** (-(np.arange(half, dtype=np.float32) * 2.0 / HD))).astype(np.float32)
    place = np.arange(-halo, length, dtype=np.float32)
    angles = place[:, None] * inv_freq[None, :]
    cosine = np.cos(angles.astype(np.float64)).astype(np.float32)
    sine = np.sin(angles.astype(np.float64)).astype(np.float32)
    return (
        np.concatenate([cosine] * 4, axis=1),
        np.concatenate([-sine, sine, -sine, sine], axis=1),
    )


def qkv_kernel(far_ref, near_ref, own_ref, gain_ref, bias_ref, w_ref, cos_ref, sin_ref,
               q_ref, kv_ref, hi_ref, lo_ref):
    step = pl.program_id(0)
    rows = own_ref.shape[0]
    third = pl.num_programs(0) // 3
    halo = hi_ref.shape[0] - rows

    @pl.when(step == 0)
    def _():
        for at, ref in enumerate((far_ref, near_ref, own_ref)):
            xhat, _ = norm_stats(ref[...])
            high, low = split(xhat * gain_ref[...] + bias_ref[...])
            hi_ref[at * rows:(at + 1) * rows] = high
            lo_ref[at * rows:(at + 1) * rows] = low

    weights = split(w_ref[...])

    @pl.when(step < third)
    def _():
        got = three(dot_nn, (hi_ref[halo:], lo_ref[halo:]), weights)
        for at in range(0, got.shape[1], 128):
            q_ref[:, at:at + 128] = rotate(got[:, at:at + 128], cos_ref[halo:], sin_ref[halo:])

    @pl.when((step >= third) & (step < 2 * third))
    def _():
        got = three(dot_nn, (hi_ref[...], lo_ref[...]), weights)
        for at in range(0, got.shape[1], 128):
            kv_ref[:, at:at + 128] = rotate(got[:, at:at + 128], cos_ref[...], sin_ref[...])

    @pl.when(step >= 2 * third)
    def _():
        kv_ref[...] = three(dot_nn, (hi_ref[...], lo_ref[...]), weights)


def project(far, near, own, gain, bias, w_full, cosine, sine):
    rows, model = own.shape
    total = 3 * rows
    wide = 256
    third = model // wide
    whole = lambda shape: pl.BlockSpec(shape, lambda j: (0, 0))
    return pl.pallas_call(
        qkv_kernel,
        grid=(3 * third,),
        in_specs=[
            whole((rows, model)), whole((rows, model)), whole((rows, model)),
            whole((1, model)), whole((1, model)),
            pl.BlockSpec((model, wide), lambda j: (0, j)),
            whole((total, 128)), whole((total, 128)),
        ],
        out_specs=[
            pl.BlockSpec((rows, wide), lambda j: (0, jnp.minimum(j, third - 1))),
            pl.BlockSpec((total, wide), lambda j: (0, jnp.maximum(j - third, 0))),
            whole((total, model)), whole((total, model)),
        ],
        out_shape=[
            jax.ShapeDtypeStruct((rows, model), F32),
            jax.ShapeDtypeStruct((total, 2 * model), F32),
            jax.ShapeDtypeStruct((total, model), BF16),
            jax.ShapeDtypeStruct((total, model), BF16),
        ],
        cost_estimate=cost(20),
        compiler_params=params(),
    )(far, near, own, gain, bias, w_full, cosine, sine)


def own_pair(values, head):
    lane = lax.broadcasted_iota(jnp.int32, values.shape, 1)
    other = pltpu.roll(values, 64, 1)
    return jnp.where((lane < 64) == (head == 0), values, other)


def outer_form(values, head):
    high, low = split(own_pair(values, head))
    return jnp.concatenate([high, low], axis=1)


def mixed(values, head):
    pair = own_pair(values, head)
    lane = lax.broadcasted_iota(jnp.int32, pair.shape, 1)
    high = pair.astype(BF16).astype(F32)
    return jnp.where(lane < 64, high, pair - high).astype(BF16)


def inner_form(values, head):
    half = mixed(values, head)
    return jnp.concatenate([half, half], axis=1)


def fold(values):
    return values + pltpu.roll(values, 64, 1)


def attend_kernel(q_ref, k_ref, v_ref, segq_ref, segk_ref, out_ref, bias_ref):
    rows = q_ref.shape[0]
    halo = k_ref.shape[0] - rows
    span = halo + BLK

    @pl.when(pl.program_id(0) == 0)
    def _():
        for at in range(0, rows, BLK):
            row = lax.broadcasted_iota(jnp.int32, (BLK, span), 0)
            col = lax.broadcasted_iota(jnp.int32, (BLK, span), 1)
            same = segq_ref[at:at + BLK, :1] == segk_ref[:1, at:at + span]
            bias_ref[at:at + BLK] = jnp.where(same & (col - halo <= row), 0.0, NEG)

    lane = lax.broadcasted_iota(jnp.int32, (BLK, 128), 1)
    scaled = q_ref[...] * (SCALE * LOG2E)
    results = []
    for head in range(2):
        left = inner_form(scaled, head)
        right = outer_form(k_ref[...], head)
        vals = mixed(v_ref[...], head)
        outs = []
        for at in range(0, rows, BLK):
            scores = dot_nt(left[at:at + BLK], right[at:at + span]) + bias_ref[at:at + BLK]
            top = jnp.max(scores, axis=1, keepdims=True)
            expo = jnp.exp2(scores - top)
            total = jnp.sum(expo, axis=1, keepdims=True)
            high, low = split(expo)
            got = dot_nn(high, vals[at:at + span]) + dot_nn(low, vals[at:at + span])
            outs.append(fold(got) / total)
        results.append(outs)
    for at in range(0, rows, BLK):
        out_ref[at:at + BLK] = jnp.where(
            lane < 64, results[0][at // BLK], results[1][at // BLK]
        )


def attend(q_rot, kv, seg_q, seg_k):
    rows, model = q_rot.shape
    total = kv.shape[0]
    pairs = model // 128
    return pl.pallas_call(
        attend_kernel,
        grid=(pairs,),
        in_specs=[
            pl.BlockSpec((rows, 128), lambda p: (0, p)),
            pl.BlockSpec((total, 128), lambda p: (0, p)),
            pl.BlockSpec((total, 128), lambda p: (0, pairs + p)),
            pl.BlockSpec((rows, 128), lambda p: (0, 0)),
            pl.BlockSpec((8, total), lambda p: (0, 0)),
        ],
        out_specs=pl.BlockSpec((rows, 128), lambda p: (0, p)),
        out_shape=jax.ShapeDtypeStruct((rows, model), F32),
        scratch_shapes=[pltpu.VMEM((rows, total - rows + BLK), F32)],
        cost_estimate=cost(24),
        compiler_params=params(),
    )(q_rot, kv, kv, seg_q, seg_k)


def attend_back_kernel(q_ref, k_ref, v_ref, g_ref, segq_ref, segk_ref, cos_ref, sin_ref, *refs):
    dq_ref, dk_ref, dv_ref, bias_ref = refs[-4:]
    rows = q_ref.shape[0]
    halo = k_ref.shape[0] - rows
    span = halo + BLK

    @pl.when(pl.program_id(0) == 0)
    def _():
        for at in range(0, rows, BLK):
            key = lax.broadcasted_iota(jnp.int32, (span, BLK), 0)
            query = lax.broadcasted_iota(jnp.int32, (span, BLK), 1)
            same = segk_ref[at:at + span, :1] == segq_ref[:1, at:at + BLK]
            bias_ref[:, at:at + BLK] = jnp.where(same & (key - halo <= query), 0.0, NEG)

    scaled = q_ref[...] * (SCALE * LOG2E)
    dq, dk, dv = [], [], []
    for head in range(2):
        q_in = inner_form(scaled, head)
        g_in = inner_form(g_ref[...], head)
        k_out = outer_form(k_ref[...], head)
        v_out = outer_form(v_ref[...], head)
        q_mix = mixed(q_ref[...], head)
        g_mix = mixed(g_ref[...], head)
        k_mix = mixed(k_ref[...], head)
        dq_head = []
        dk_head = jnp.zeros((halo + rows, 128), F32)
        dv_head = jnp.zeros((halo + rows, 128), F32)
        dk_parts, dv_parts = [], []
        for at in range(0, rows, BLK):
            scores = dot_nt(k_out[at:at + span], q_in[at:at + BLK]) + bias_ref[:, at:at + BLK]
            top = jnp.max(scores, axis=0, keepdims=True)
            expo = jnp.exp2(scores - top)
            inverse = 1.0 / jnp.sum(expo, axis=0, keepdims=True)
            grad_probs = dot_nt(v_out[at:at + span], g_in[at:at + BLK])
            probs = expo * inverse
            delta = jnp.sum(probs * grad_probs, axis=0, keepdims=True)
            grad_scores = probs * (grad_probs - delta)
            probs_cat = jnp.concatenate(split(probs), axis=1)
            scores_cat = jnp.concatenate(split(grad_scores), axis=1)
            g_two = jnp.concatenate([g_mix[at:at + BLK]] * 2, axis=0)
            q_two = jnp.concatenate([q_mix[at:at + BLK]] * 2, axis=0)
            dv_parts.append(dot_nn(probs_cat, g_two))
            dk_parts.append(dot_nn(scores_cat, q_two))
            got = dot_tn(scores_cat, k_mix[at:at + span])
            dq_head.append(fold(got[:BLK] + got[BLK:]))
        for parts, full in ((dk_parts, dk), (dv_parts, dv)):
            pieces = []
            for kb in range((halo + rows) // BLK):
                terms = [
                    parts[qb][(kb - qb) * BLK:(kb - qb + 1) * BLK]
                    for qb in range(rows // BLK)
                    if 0 <= kb - qb < span // BLK
                ]
                pieces.append(fold(functools.reduce(lambda a, b: a + b, terms)))
            full.append(pieces)
        dq.append(dq_head)
    lane = lax.broadcasted_iota(jnp.int32, (BLK, 128), 1)
    for qb in range(rows // BLK):
        rng = slice(qb * BLK, (qb + 1) * BLK)
        far = slice(halo + qb * BLK, halo + (qb + 1) * BLK)
        both = jnp.where(lane < 64, dq[0][qb], dq[1][qb]) * SCALE
        dq_ref[rng] = unrotate(both, cos_ref[far], sin_ref[far])
    for kb in range((halo + rows) // BLK):
        rng = slice(kb * BLK, (kb + 1) * BLK)
        both = jnp.where(lane < 64, dk[0][kb], dk[1][kb]) * SCALE
        dk_ref[rng] = unrotate(both, cos_ref[rng], sin_ref[rng])
        dv_ref[rng] = jnp.where(lane < 64, dv[0][kb], dv[1][kb])


def attend_back(first, count, q_rot, kv, grad, seg_q, seg_k, cosine, sine, before=()):
    rows, model = q_rot.shape
    total = kv.shape[0]
    pairs = model // 128
    fixed = lambda shape: pl.BlockSpec(shape, lambda p: (0, 0))
    return pl.pallas_call(
        attend_back_kernel,
        grid=(count,),
        in_specs=[
            pl.BlockSpec((rows, 128), lambda p: (0, first + p)),
            pl.BlockSpec((total, 128), lambda p: (0, first + p)),
            pl.BlockSpec((total, 128), lambda p: (0, pairs + first + p)),
            pl.BlockSpec((rows, 128), lambda p: (0, first + p)),
            fixed((8, rows)), fixed((total, 128)),
            fixed((total, 128)), fixed((total, 128)),
        ] + [pl.BlockSpec(memory_space=pl.ANY)] * len(before),
        out_specs=[
            pl.BlockSpec((rows, 128), lambda p: (0, first + p)),
            pl.BlockSpec((total, 128), lambda p: (0, first + p)),
            pl.BlockSpec((total, 128), lambda p: (0, first + p)),
        ],
        out_shape=[
            jax.ShapeDtypeStruct((rows, model), F32),
            jax.ShapeDtypeStruct((total, model), F32),
            jax.ShapeDtypeStruct((total, model), F32),
        ],
        scratch_shapes=[pltpu.VMEM((total - rows + BLK, rows), F32)],
        input_output_aliases={8 + i: i for i in range(len(before))},
        cost_estimate=cost(7 * count),
        compiler_params=params(),
    )(q_rot, kv, kv, grad, seg_q, seg_k, cosine, sine, *before)


def mlp_kernel(count, begun, chip_ref, resid_ref, other_ref, cot_ref, cot_other_ref, gain_ref, bias_ref,
               scale_ref, *refs):
    up_refs, down_refs = refs[:count], refs[count:2 * count]
    refs = refs[2 * count:]
    so_far, refs = refs[:2 * begun], refs[2 * begun:]
    out_ref, gnorm_ref, grad_ref = refs[:3]
    (x_hi, x_lo, xt_hi, xt_lo, g_hi, g_lo, up_hi, up_lo, down_hi, down_lo) = refs[3:]
    step = pl.program_id(0)
    rows = resid_ref.shape[0]

    @pl.when(step == 0)
    def _():
        for at, source, cot in ((0, resid_ref, cot_ref), (rows, other_ref, cot_other_ref)):
            xhat, _ = norm_stats(source[...])
            normed = xhat * gain_ref[...] + bias_ref[...]
            x_hi[at:at + rows], x_lo[at:at + rows] = split(normed)
            xt_hi[:, at:at + rows], xt_lo[:, at:at + rows] = split(normed.T)
            g_hi[at:at + rows], g_lo[at:at + rows] = split(cot[...] * scale_ref[0, 0])
        if begun:
            out_ref[...] = so_far[0][...]
            gnorm_ref[...] = so_far[1][...]
        else:
            out_ref[...] = jnp.zeros_like(out_ref)
            gnorm_ref[...] = jnp.zeros_like(gnorm_ref)

    for at in range(count):
        spot = (chip_ref[0] ^ at) if count > 1 else 0
        up_rows = up_refs[at].shape[0]
        high, low = split(up_refs[at][...])
        here = pl.ds(pl.multiple_of(spot * up_rows, up_rows), up_rows)
        up_hi[here], up_lo[here] = high, low
        block = down_refs[at][...]
        block = block.reshape(-1, block.shape[-1])
        high, low = split(block)
        here = pl.ds(pl.multiple_of(spot * block.shape[0], block.shape[0]), block.shape[0])
        down_hi[here], down_lo[here] = high, low

    chips, _, tall, width = grad_ref.shape
    up_tall = up_hi.shape[0] // chips
    deep = down_hi.shape[0] // chips
    up = (up_hi[...], up_lo[...])
    down = (down_hi[...], down_lo[...])
    normed = (x_hi[...], x_lo[...])
    normed_t = (xt_hi[...], xt_lo[...])
    grad_block = (g_hi[...], g_lo[...])
    pre = three(dot_nn, normed, up)
    grad_act = three(dot_nt, grad_block, down)
    inner = 0.7978845608028654 * (pre + 0.044715 * pre * pre * pre)
    bent = jnp.tanh(inner)
    act = 0.5 * pre * (1.0 + bent)
    slope = 0.5 * (1.0 + bent) + 0.5 * pre * (1.0 - bent * bent) * (
        0.7978845608028654 * (1.0 + 3.0 * 0.044715 * pre * pre)
    )
    act2 = split(act)
    grad_pre = split(grad_act * slope)
    out_ref[...] += three(dot_nn, act2, down)
    gnorm_ref[...] += three(dot_nt, grad_pre, up)
    gup = three(dot_nn, normed_t, grad_pre)
    gdown = three(dot_tn, act2, grad_block)
    half = deep // 2
    for chip in range(chips):
        grad_ref[chip, 0, :up_tall] = gup[chip * up_tall:(chip + 1) * up_tall]
        part = gdown[chip * deep:(chip + 1) * deep]
        grad_ref[chip, 0, up_tall:up_tall + deep] = part[:, :width]
        grad_ref[chip, 0, up_tall + deep:] = jnp.concatenate(
            [part[:half, width:], part[half:, width:]], axis=1
        )


def mlp(first, steps, so_far, chip, chips, resid, other, cot, cot_other, gain, bias, scale, ups, downs):
    rows, model = resid.shape
    width = 512
    up_tall = model // chips
    deep = width // chips
    fixed = lambda shape: pl.BlockSpec(shape, lambda j, c: (0, 0))
    if len(ups) > 1:
        down_spec = pl.BlockSpec((deep, model), lambda j, c: (first + j, 0))
    else:
        downs = [downs[0].reshape(chips, -1, model)]
        down_spec = pl.BlockSpec((chips, deep, model), lambda j, c: (0, first + j, 0))
    tall = up_tall + deep + deep // 2
    grid_spec = pltpu.PrefetchScalarGridSpec(
        num_scalar_prefetch=1,
        grid=(steps,),
        in_specs=[fixed((rows, model))] * 4 + [fixed((1, model))] * 2
        + [pl.BlockSpec(memory_space=pltpu.SMEM)]
        + [pl.BlockSpec((up.shape[0], width), lambda j, c: (0, first + j)) for up in ups]
        + [down_spec] * len(downs)
        + [fixed((2 * rows, model))] * len(so_far),
        out_specs=[
            fixed((2 * rows, model)), fixed((2 * rows, model)),
            pl.BlockSpec((chips, 1, tall, width), lambda j, c: (0, j, 0, 0)),
        ],
        scratch_shapes=[
            pltpu.VMEM((2 * rows, model), BF16), pltpu.VMEM((2 * rows, model), BF16),
            pltpu.VMEM((model, 2 * rows), BF16), pltpu.VMEM((model, 2 * rows), BF16),
            pltpu.VMEM((2 * rows, model), BF16), pltpu.VMEM((2 * rows, model), BF16),
            pltpu.VMEM((model, width), BF16), pltpu.VMEM((model, width), BF16),
            pltpu.VMEM((width, model), BF16), pltpu.VMEM((width, model), BF16),
        ],
    )
    return pl.pallas_call(
        functools.partial(mlp_kernel, len(ups), len(so_far) // 2),
        grid_spec=grid_spec,
        out_shape=[
            jax.ShapeDtypeStruct((2 * rows, model), F32),
            jax.ShapeDtypeStruct((2 * rows, model), F32),
            jax.ShapeDtypeStruct((chips, steps, tall, width), F32),
        ],
        cost_estimate=cost(18 * steps),
        compiler_params=params(),
    )(chip, resid, other, cot, cot_other, gain, bias, scale, *ups, *downs, *so_far)


def unpack_grads(up, down, sibling_swap, core, chips):
    steps, up_tall, width = up.shape
    deep = up_tall * 2 // 3
    half = up_tall // 2
    mine = jnp.where(core == 0, up[:, :half], up[:, half:])
    other = sibling_swap(jnp.where(core == 0, up[:, half:], up[:, :half]))
    by_core = jnp.stack(
        [jnp.where(core == 0, mine, other), jnp.where(core == 0, other, mine)], axis=0
    )
    by_core = by_core.reshape(2, steps, half, chips, width // chips)
    grad_up = jnp.transpose(by_core, (2, 3, 0, 1, 4)).reshape(half, -1)
    quarter = width // 2
    tail = down[:, deep:]
    right = jnp.concatenate([tail[:, :, :quarter], tail[:, :, quarter:]], axis=1)
    grad_down = jnp.concatenate([down[:, :deep], right], axis=2).reshape(steps * deep, -1)
    return grad_up, grad_down


def resid_back_kernel(part_ref, given_ref, resid_ref, cot_ref, gain_ref, scale_ref, w_ref,
                      grad_ref, att_ref, sums_ref):
    grad = part_ref[...] + given_ref[...]
    xhat, rate = norm_stats(resid_ref[...])
    grad_resid = cot_ref[...] * scale_ref[0, 0] + norm_back(grad, gain_ref[...], xhat, rate)
    grad_ref[...] = grad_resid
    att_ref[...] = three(dot_nt, split(grad_resid), split(w_ref[...]))
    gain_sum = jnp.sum(grad * xhat, axis=0, keepdims=True)
    bias_sum = jnp.sum(grad, axis=0, keepdims=True)
    sums_ref[...] = jnp.concatenate(
        [gain_sum, bias_sum, jnp.zeros((6, gain_sum.shape[1]), F32)], axis=0
    )


def resid_back(part, given, resid, cot, gain, scale, w_full):
    rows, model = resid.shape
    fixed = lambda shape: pl.BlockSpec(shape, lambda j: (0, 0))
    return pl.pallas_call(
        resid_back_kernel,
        grid=(1,),
        in_specs=[fixed((rows, model))] * 4 + [fixed((1, model))]
        + [pl.BlockSpec(memory_space=pltpu.SMEM), fixed((model, model))],
        out_specs=[fixed((rows, model)), fixed((rows, model)), fixed((8, model))],
        out_shape=[
            jax.ShapeDtypeStruct((rows, model), F32),
            jax.ShapeDtypeStruct((rows, model), F32),
            jax.ShapeDtypeStruct((8, model), F32),
        ],
        cost_estimate=cost(6),
        compiler_params=params(),
    )(part, given, resid, cot, gain, scale, w_full)


def place_rows(core_ref, out_refs, got):
    chips, tall = out_refs[0].shape[:2]

    def store(core):
        for block in range(2 * chips):
            ref = out_refs[(block & 1) ^ core]
            ref[block // 2] = got[block * tall:(block + 1) * tall]

    for core in range(2):
        pl.when(core_ref[0] == core)(functools.partial(store, core))


def weights_qk_kernel(core_ref, hi_ref, lo_ref, dq_ref, dk_ref, own_ref, sib_ref, nt_hi, nt_lo):
    out_ref = (own_ref, sib_ref)
    step = pl.program_id(0)
    part = pl.num_programs(0) // 2
    halo = hi_ref.shape[0] - dq_ref.shape[0]

    @pl.when(step == 0)
    def _():
        nt_hi[...] = hi_ref[...].T
        nt_lo[...] = lo_ref[...].T

    @pl.when(step < part)
    def _():
        left = (nt_hi[:, halo:], nt_lo[:, halo:])
        place_rows(core_ref, out_ref, three(dot_nn, left, split(dq_ref[...])))

    @pl.when(step >= part)
    def _():
        left = (nt_hi[...], nt_lo[...])
        place_rows(core_ref, out_ref, three(dot_nn, left, split(dk_ref[...])))


def weights_vo_kernel(core_ref, hi_ref, lo_ref, dv_ref, att_ref, res_ref, own_ref, sib_ref,
                      nt_hi, nt_lo, at_hi, at_lo):
    out_ref = (own_ref, sib_ref)
    step = pl.program_id(0)
    part = pl.num_programs(0) // 2

    @pl.when(step == 0)
    def _():
        nt_hi[...] = hi_ref[...].T
        nt_lo[...] = lo_ref[...].T
        at_hi[...], at_lo[...] = split(att_ref[...].T)

    @pl.when(step < part)
    def _():
        left = (nt_hi[...], nt_lo[...])
        place_rows(core_ref, out_ref, three(dot_nn, left, split(dv_ref[...])))

    @pl.when(step >= part)
    def _():
        left = (at_hi[...], at_lo[...])
        place_rows(core_ref, out_ref, three(dot_nn, left, split(res_ref[...])))


def weight_call(kernel, micros, core, chips, fixed_args, pieces, scratch):
    model = fixed_args[0].shape[1]
    wide = 256
    part = model // wide
    tall = model // chips // 2
    fixed = lambda v: pl.BlockSpec(v.shape, lambda j, c: (0, 0))
    piece = lambda v, at: pl.BlockSpec(
        (v.shape[0], wide), lambda j, c: (0, jnp.clip(j - at * part, 0, part - 1))
    )
    specs, args = [], []
    for value, at in pieces:
        args.append(value)
        specs.append(fixed(value) if at is None else piece(value, at))
    return pl.pallas_call(
        kernel,
        grid_spec=pltpu.PrefetchScalarGridSpec(
            num_scalar_prefetch=1,
            grid=(2 * part,),
            in_specs=[fixed(v) for v in fixed_args] + specs,
            out_specs=[pl.BlockSpec((chips, tall, wide), lambda j, c: (0, 0, j))] * 2,
            scratch_shapes=[pltpu.VMEM((model, n), BF16) for n in scratch],
        ),
        out_shape=[jax.ShapeDtypeStruct((chips, tall, 2 * model), F32)] * 2,
        cost_estimate=cost(micros),
        compiler_params=params(),
    )(core, *fixed_args, *args)


def partial_kernel(count, *refs):
    grads, w_ref, out_ref = refs[:count], refs[count], refs[count + 1]
    held = refs[count + 2:]
    model = grads[0].shape[1]
    first = 3 - count

    @pl.when(pl.program_id(0) == 0)
    def _():
        for at, ref in enumerate(grads):
            held[2 * at][...], held[2 * at + 1][...] = split(ref[...])

    total = None
    for at in range(count):
        weights = split(w_ref[:, (first + at) * model:(first + at + 1) * model])
        term = three(dot_nt, (held[2 * at][...], held[2 * at + 1][...]), weights)
        total = term if total is None else total + term
    out_ref[...] = total


def partial_rows(block, grads, w_full):
    model = w_full.shape[0]
    rows = grads[0].shape[0] if len(grads) == 3 else grads[0].shape[0] // 3
    wide = 256
    specs = [pl.BlockSpec((rows, model), lambda j: (block, 0))] * 2
    if len(grads) == 3:
        specs = [pl.BlockSpec((rows, model), lambda j: (0, 0))] + specs
    return pl.pallas_call(
        functools.partial(partial_kernel, len(grads)),
        grid=(model // wide,),
        in_specs=specs + [pl.BlockSpec((wide, 3 * model), lambda j: (j, 0))],
        out_specs=pl.BlockSpec((rows, wide), lambda j: (0, j)),
        out_shape=jax.ShapeDtypeStruct((rows, model), F32),
        scratch_shapes=[pltpu.VMEM((rows, model), BF16)] * (2 * len(grads)),
        cost_estimate=cost(6),
        compiler_params=params(),
    )(*grads, w_full)


def matmul(left, right):
    return jnp.dot(left, right, precision=HIGH)


def inner_rows(left, right):
    return lax.dot_general(left, right, (((0,), (0,)), ((), ())), precision=HIGH)


def outer_cols(left, right):
    return lax.dot_general(left, right, (((1,), (1,)), ((), ())), precision=HIGH)


def body(
    block_input,
    embedding,
    earlier_outs,
    dwa_weights,
    ln1_gain,
    ln1_bias,
    w_qkv,
    w_out,
    ln2_gain,
    ln2_bias,
    w_up,
    w_down,
    segments,
    cotangent,
):
    groups = lax.axis_size("seq")
    rows, model = block_input.shape
    length = rows * groups
    halo = 2 * rows
    place = lax.axis_index("seq")
    ahead = [(i, i + 1) for i in range(groups - 1)]
    behind = [(i + 1, i) for i in range(groups - 1)]
    gain1, bias1 = ln1_gain[None], ln1_bias[None]
    gain2, bias2 = ln2_gain[None], ln2_bias[None]

    devices = lax.axis_size("dp")
    chips = devices // 2
    spot = lax.axis_index("dp")
    core = spot % 2
    chip = (spot // 2).reshape(1).astype(jnp.int32)
    same_core = [[2 * i + c for i in range(chips)] for c in range(2)]
    exchange = lambda v, bit: lax.ppermute(v, "dp", [(i, i ^ bit) for i in range(devices)])
    swap = lambda v: exchange(v, 1)

    gather = lambda v: lax.all_gather(v, "dp", axis=0, tiled=True)
    qkv_full = gather(w_qkv)

    shard = w_down.shape[0]
    third = shard // 3
    by_core = w_up.reshape(w_up.shape[0], chips, 2, 3, third)
    by_core = jnp.transpose(by_core, (2, 0, 3, 1, 4)).reshape(2, w_up.shape[0], -1)
    mine = jnp.where(core == 0, by_core[0], by_core[1])
    given = swap(jnp.where(core == 0, by_core[1], by_core[0]))
    up_chip = jnp.concatenate(
        [jnp.where(core == 0, mine, given), jnp.where(core == 0, given, mine)], axis=0
    )
    if chips == 4:
        up_x, down_x = exchange(up_chip, 2), exchange(w_down, 2)
        up_y, down_y = exchange(up_chip, 4), exchange(w_down, 4)
        ups = [up_chip, up_x, up_y, exchange(up_y, 2)]
        downs = [w_down, down_x, down_y, exchange(down_x, 4)]
    else:
        ups, downs = (
            [lax.all_gather(v, "dp", axis=0, tiled=True, axis_index_groups=same_core)]
            for v in (up_chip, w_down)
        )

    seg_own = segments + 1
    near = lax.ppermute(block_input, "seq", ahead)
    seg_near = lax.ppermute(seg_own, "seq", ahead)
    far = lax.ppermute(near, "seq", ahead)
    seg_far = lax.ppermute(seg_near, "seq", ahead)
    seg_all = jnp.concatenate([seg_far, seg_near, seg_own], axis=1)
    seg_k_row = jnp.broadcast_to(seg_all, (8, halo + rows))
    seg_k_col = jnp.broadcast_to(seg_all.reshape(-1, 1), (halo + rows, 128))
    seg_q_row = seg_k_row[:, halo:]
    seg_q_col = seg_k_col[halo:]

    cos_all, sin_all = rotary_tables(length, halo)
    cosine = lax.dynamic_slice_in_dim(jnp.asarray(cos_all), place * rows, halo + rows, 0)
    sine = lax.dynamic_slice_in_dim(jnp.asarray(sin_all), place * rows, halo + rows, 0)

    earlier = (embedding, earlier_outs[0], earlier_outs[1], earlier_outs[2])
    base = sum(dwa_weights[i] * value for i, value in enumerate(earlier))
    dots = jnp.stack([jnp.sum(cotangent * value) for value in earlier])
    far, base, dots = lax.optimization_barrier((far, base, dots))

    q_rot, kv, normed_hi, normed_lo = project(
        far, near, block_input, gain1, bias1, qkv_full, cosine, sine
    )
    attended = attend(q_rot, kv, seg_q_col, seg_k_row)

    out_full = gather(w_out)
    resid = block_input + matmul(attended, out_full)
    resid_other = swap(resid)
    cot_other = swap(cotangent)
    scale = dwa_weights[4].reshape(1, 1)
    call = functools.partial(
        mlp, chip=chip, chips=chips, resid=resid, other=resid_other, cot=cotangent,
        cot_other=cot_other, gain=gain2, bias=bias2, scale=scale, ups=ups, downs=downs,
    )
    scatter = lambda v: lax.psum_scatter(v, "dp", scatter_dimension=0, tiled=True)
    scatter_chips = lambda v: lax.psum_scatter(
        v, "dp", scatter_dimension=0, tiled=True, axis_index_groups=same_core
    )
    so_far, shards = (), []
    for third_at in range(3):
        out_part, gnorm_part, grads = call(third_at, 1, so_far)
        so_far = (out_part, gnorm_part)
        shards.append(scatter_chips(grads)[0])
    given = swap(gnorm_part[rows:])

    shift = lambda v, bit: lax.ppermute(v, "seq", [(i, i ^ bit) for i in range(groups)])
    even = place % 2 == 0

    def line_start(shard):
        tall = shard.shape[1] // 2
        halves = (shard[:, :tall], shard[:, tall:])
        kept = jnp.where(even, halves[0], halves[1])
        return kept + shift(jnp.where(even, halves[1], halves[0]), 1)

    def line_middle(kept):
        bit = 2
        while bit < groups:
            kept = kept + shift(kept, bit)
            bit *= 2
        return kept

    def line_end(kept):
        other = shift(kept, 1)
        return jnp.where(even, kept, other), jnp.where(even, other, kept)

    together = lax.optimization_barrier
    shards[0], given = together((shards[0], given))
    line_a = line_start(shards[0])
    grad_resid, grad_attended, sums_two = resid_back(
        gnorm_part, given, resid, cotangent, gain2, scale, out_full
    )

    back_args = (q_rot, kv, grad_attended, seg_q_row, seg_k_col, cosine, sine)
    pairs = model // 128
    line_a, back_args = together((line_a, back_args))
    line_a = line_middle(line_a)
    first_half = attend_back(0, pairs // 2, *back_args)
    line_a, shards[1], back_args, first_half = together(
        (line_a, shards[1], back_args, first_half)
    )
    line_b = line_start(shards[1])
    ends_a = line_end(line_a)
    dq, dk, dv = attend_back(pairs // 2, pairs - pairs // 2, *back_args, before=first_half)
    line_b, ends_a, dq, dk, dv = together((line_b, ends_a, dq, dk, dv))
    line_b = line_middle(line_b)
    core_at = core.reshape(1).astype(jnp.int32)
    normed_parts = (normed_hi, normed_lo)
    grads_qk = weight_call(
        weights_qk_kernel, 9, core_at, chips, normed_parts, [(dq, 0), (dk, 1)], [halo + rows] * 2
    )
    given_qk = swap(grads_qk[1])
    line_b, shards[2], dv, grad_resid = together((line_b, shards[2], dv, grad_resid))
    ends_b = line_end(line_b)
    line_c = line_start(shards[2])
    grads_vo = weight_call(
        weights_vo_kernel, 9, core_at, chips, normed_parts,
        [(dv, 0), (attended, None), (grad_resid, 1)], [halo + rows] * 2 + [rows] * 2,
    )
    line_c, ends_b, grads_vo, dk = together((line_c, ends_b, grads_vo, dk))
    part_far = partial_rows(0, (dk, dv), qkv_full)
    line_c = line_middle(line_c)
    grads_c = jnp.concatenate([grads_qk[0] + given_qk, grads_vo[0] + swap(grads_vo[1])], axis=2)
    grads_c, out_part, part_far = together((grads_c, out_part, part_far))
    shard_c = scatter_chips(grads_c)[0]
    out_sib = swap(out_part[rows:])

    block_out = resid + out_part[:rows] + out_sib
    output = base + dwa_weights[4] * block_out
    dwa_local = jnp.concatenate([dots, jnp.sum(cotangent * block_out)[None]])

    given_near = lax.ppermute(part_far, "seq", behind)
    part_near = partial_rows(1, (dk, dv), qkv_full)
    given_near, line_c, dq, far, near = together((given_near, line_c, dq, far, near))
    ends_c = line_end(line_c)
    own_part = partial_rows(2, (dq, dk, dv), qkv_full)
    own_part, ends_c = together((own_part, ends_c))
    (sent,) = together((part_near,))
    back_near = sent + given_near

    xhat1, rate1 = norm_stats(block_input)
    terms = (
        (norm_stats(far)[0], part_far),
        (norm_stats(near)[0], part_near),
        (xhat1, own_part),
    )
    grad_gain_one = sum(jnp.sum(xhat * part, axis=0) for xhat, part in terms)
    grad_bias_one = sum(jnp.sum(part, axis=0) for _, part in terms)

    small = jnp.concatenate(
        [
            grad_gain_one[None], grad_bias_one[None], sums_two[:2],
            jnp.pad(dwa_local, (0, model - 5))[None], jnp.zeros((3, model), F32),
        ],
        axis=0,
    )
    bit = 1
    while bit < devices:
        small = small + exchange(small, bit)
        bit *= 2
    given_back = lax.ppermute(back_near, "seq", behind)
    shard_c, given_back, small = together((shard_c, given_back, small))
    last = line_middle(line_start(shard_c[None]))
    grad_normed_one = own_part + given_back
    grad_input = grad_resid + norm_back(grad_normed_one, gain1, xhat1, rate1)
    grad_up, grad_down = unpack_grads(
        *(
            jnp.concatenate(parts, axis=0)
            for parts in zip(ends_a, ends_b, ends_c)
        ),
        swap, core, chips,
    )
    last, grad_up, grad_down, small, grad_input = together(
        (last, grad_up, grad_down, small, grad_input)
    )
    bit = 1
    while bit < groups:
        small = small + shift(small, bit)
        bit *= 2
    gain_one, bias_one, gain_two, bias_two = small[0], small[1], small[2], small[3]
    grad_dwa = small[4, :5]
    last = jnp.concatenate(line_end(last), axis=1)[0]
    grad_qkv, grad_wout = last[:, :3 * model], last[:, 3 * model:]
    return (
        output,
        grad_input,
        grad_dwa,
        gain_one,
        bias_one,
        grad_qkv,
        grad_wout,
        gain_two,
        bias_two,
        grad_up,
        grad_down,
    )


def solution(mesh):
    in_specs = (
        P(("dp", "seq"), None),
        P(("dp", "seq"), None),
        P(None, ("dp", "seq"), None),
        P(),
        P(),
        P(),
        P("dp", None),
        P("dp", None),
        P(),
        P(),
        P("dp", None),
        P("dp", None),
        P("dp", "seq"),
        P(("dp", "seq"), None),
    )
    out_specs = (
        P(("dp", "seq"), None),
        P(("dp", "seq"), None),
        P(),
        P(),
        P(),
        P("dp", None),
        P("dp", None),
        P(),
        P(),
        P("dp", None),
        P("dp", None),
    )
    return jax.shard_map(body, mesh=mesh, in_specs=in_specs, out_specs=out_specs, check_vma=False)
```

```python
import functools
import math

import jax
import jax.numpy as jnp
import numpy as np
from jax import lax
from jax.experimental import pallas as pl
from jax.experimental.pallas import tpu as pltpu
from jax.sharding import PartitionSpec as P

HD = 64
DOC_MOST = 768
LOG2E = math.log2(math.e)
SCALE = 1.0 / math.sqrt(HD)
NEG = -1e30
F32 = jnp.float32
BF16 = jnp.bfloat16
HIGH = lax.Precision.HIGH
VMEM_LIMIT = 56 * 1024 * 1024
BLK = 128


def cost(micros):
    return pl.CostEstimate(
        flops=int(micros * 1.1e9), bytes_accessed=1 << 20, transcendentals=0
    )


def params(fused=False):
    return pltpu.CompilerParams(
        dimension_semantics=("arbitrary",),
        vmem_limit_bytes=VMEM_LIMIT,
        fuse_transposed_lhs_in_matmul=fused,
    )


def split(values):
    high = values.astype(BF16)
    return high, (values - high.astype(F32)).astype(BF16)


def dot_nn(left, right):
    return lax.dot_general(left, right, (((1,), (0,)), ((), ())), preferred_element_type=F32)


def dot_nt(left, right):
    return lax.dot_general(left, right, (((1,), (1,)), ((), ())), preferred_element_type=F32)


def dot_tn(left, right):
    return lax.dot_general(left, right, (((0,), (0,)), ((), ())), preferred_element_type=F32)


def three(dot, left, right):
    return (
        dot(left[0], right[0]) + dot(left[0], right[1]) + dot(left[1], right[0])
    )


def norm_stats(values):
    row_mean = jnp.mean(values, axis=-1, keepdims=True)
    centred = values - row_mean
    row_var = jnp.mean(centred * centred, axis=-1, keepdims=True)
    rate = lax.rsqrt(row_var + 1e-05)
    return centred * rate, rate


def norm_back(grad, gain, xhat, rate):
    scaled = grad * gain
    return rate * (
        scaled
        - jnp.mean(scaled, axis=-1, keepdims=True)
        - xhat * jnp.mean(scaled * xhat, axis=-1, keepdims=True)
    )


def turned(values):
    lane = lax.broadcasted_iota(jnp.int32, values.shape, 1)
    return jnp.where(
        (lane & 63) < 32, pltpu.roll(values, 96, 1), pltpu.roll(values, 32, 1)
    )


def rotate(values, cosine, sine):
    return values * cosine + turned(values) * sine


def unrotate(values, cosine, sine):
    return values * cosine - turned(values) * sine


def rotary_tables(length, halo):
    half = HD // 2
    inv_freq = (10000.0 ** (-(np.arange(half, dtype=np.float32) * 2.0 / HD))).astype(np.float32)
    place = np.arange(-halo, length, dtype=np.float32)
    angles = place[:, None] * inv_freq[None, :]
    cosine = np.cos(angles.astype(np.float64)).astype(np.float32)
    sine = np.sin(angles.astype(np.float64)).astype(np.float32)
    return (
        np.concatenate([cosine] * 4, axis=1),
        np.concatenate([-sine, sine, -sine, sine], axis=1),
    )


def qkv_kernel(far_ref, near_ref, own_ref, gain_ref, bias_ref, w_ref, cos_ref, sin_ref,
               q_ref, kv_ref, hi_ref, lo_ref):
    step = pl.program_id(0)
    rows = own_ref.shape[0]
    third = pl.num_programs(0) // 3
    halo = hi_ref.shape[0] - rows

    @pl.when(step == 0)
    def _():
        for at, ref in enumerate((far_ref, near_ref, own_ref)):
            xhat, _ = norm_stats(ref[...])
            high, low = split(xhat * gain_ref[...] + bias_ref[...])
            hi_ref[at * rows:(at + 1) * rows] = high
            lo_ref[at * rows:(at + 1) * rows] = low

    weights = split(w_ref[...])

    @pl.when(step < third)
    def _():
        got = three(dot_nn, (hi_ref[halo:], lo_ref[halo:]), weights)
        for at in range(0, got.shape[1], 128):
            q_ref[:, at:at + 128] = rotate(got[:, at:at + 128], cos_ref[halo:], sin_ref[halo:])

    @pl.when((step >= third) & (step < 2 * third))
    def _():
        got = three(dot_nn, (hi_ref[...], lo_ref[...]), weights)
        for at in range(0, got.shape[1], 128):
            kv_ref[:, at:at + 128] = rotate(got[:, at:at + 128], cos_ref[...], sin_ref[...])

    @pl.when(step >= 2 * third)
    def _():
        kv_ref[...] = three(dot_nn, (hi_ref[...], lo_ref[...]), weights)


def project(far, near, own, gain, bias, w_full, cosine, sine):
    rows, model = own.shape
    total = 3 * rows
    wide = 256
    third = model // wide
    whole = lambda shape: pl.BlockSpec(shape, lambda j: (0, 0))
    return pl.pallas_call(
        qkv_kernel,
        grid=(3 * third,),
        in_specs=[
            whole((rows, model)), whole((rows, model)), whole((rows, model)),
            whole((1, model)), whole((1, model)),
            pl.BlockSpec((model, wide), lambda j: (0, j)),
            whole((total, 128)), whole((total, 128)),
        ],
        out_specs=[
            pl.BlockSpec((rows, wide), lambda j: (0, jnp.minimum(j, third - 1))),
            pl.BlockSpec((total, wide), lambda j: (0, jnp.maximum(j - third, 0))),
            whole((total, model)), whole((total, model)),
        ],
        out_shape=[
            jax.ShapeDtypeStruct((rows, model), F32),
            jax.ShapeDtypeStruct((total, 2 * model), F32),
            jax.ShapeDtypeStruct((total, model), BF16),
            jax.ShapeDtypeStruct((total, model), BF16),
        ],
        cost_estimate=cost(20),
        compiler_params=params(),
    )(far, near, own, gain, bias, w_full, cosine, sine)


def own_pair(values, head):
    lane = lax.broadcasted_iota(jnp.int32, values.shape, 1)
    other = pltpu.roll(values, 64, 1)
    return jnp.where((lane < 64) == (head == 0), values, other)


def outer_form(values, head):
    high, low = split(own_pair(values, head))
    return jnp.concatenate([high, low], axis=1)


def mixed(values, head):
    pair = own_pair(values, head)
    lane = lax.broadcasted_iota(jnp.int32, pair.shape, 1)
    high = pair.astype(BF16).astype(F32)
    return jnp.where(lane < 64, high, pair - high).astype(BF16)


def inner_form(values, head):
    half = mixed(values, head)
    return jnp.concatenate([half, half], axis=1)


def fold(values):
    return values + pltpu.roll(values, 64, 1)


def attend_kernel(q_ref, k_ref, v_ref, segq_ref, segk_ref, out_ref, bias_ref):
    rows = q_ref.shape[0]
    halo = k_ref.shape[0] - rows
    span = halo + BLK

    @pl.when(pl.program_id(0) == 0)
    def _():
        for at in range(0, rows, BLK):
            row = lax.broadcasted_iota(jnp.int32, (BLK, span), 0)
            col = lax.broadcasted_iota(jnp.int32, (BLK, span), 1)
            same = segq_ref[at:at + BLK, :1] == segk_ref[:1, at:at + span]
            bias_ref[at:at + BLK] = jnp.where(same & (col - halo <= row), 0.0, NEG)

    lane = lax.broadcasted_iota(jnp.int32, (BLK, 128), 1)
    scaled = q_ref[...] * (SCALE * LOG2E)
    results = []
    for head in range(2):
        left = inner_form(scaled, head)
        right = outer_form(k_ref[...], head)
        vals = mixed(v_ref[...], head)
        outs = []
        for at in range(0, rows, BLK):
            scores = dot_nt(left[at:at + BLK], right[at:at + span]) + bias_ref[at:at + BLK]
            top = jnp.max(scores, axis=1, keepdims=True)
            expo = jnp.exp2(scores - top)
            total = jnp.sum(expo, axis=1, keepdims=True)
            high, low = split(expo)
            got = dot_nn(high, vals[at:at + span]) + dot_nn(low, vals[at:at + span])
            outs.append(fold(got) / total)
        results.append(outs)
    for at in range(0, rows, BLK):
        out_ref[at:at + BLK] = jnp.where(
            lane < 64, results[0][at // BLK], results[1][at // BLK]
        )


def attend(q_rot, kv, seg_q, seg_k):
    rows, model = q_rot.shape
    total = kv.shape[0]
    pairs = model // 128
    return pl.pallas_call(
        attend_kernel,
        grid=(pairs,),
        in_specs=[
            pl.BlockSpec((rows, 128), lambda p: (0, p)),
            pl.BlockSpec((total, 128), lambda p: (0, p)),
            pl.BlockSpec((total, 128), lambda p: (0, pairs + p)),
            pl.BlockSpec((rows, 128), lambda p: (0, 0)),
            pl.BlockSpec((8, total), lambda p: (0, 0)),
        ],
        out_specs=pl.BlockSpec((rows, 128), lambda p: (0, p)),
        out_shape=jax.ShapeDtypeStruct((rows, model), F32),
        scratch_shapes=[pltpu.VMEM((rows, total - rows + BLK), F32)],
        cost_estimate=cost(24),
        compiler_params=params(),
    )(q_rot, kv, kv, seg_q, seg_k)


def attend_back_kernel(q_ref, k_ref, v_ref, g_ref, segq_ref, segk_ref, cos_ref, sin_ref, *refs):
    dq_ref, dk_ref, dv_ref, bias_ref = refs[-4:]
    rows = q_ref.shape[0]
    halo = k_ref.shape[0] - rows
    span = halo + BLK

    @pl.when(pl.program_id(0) == 0)
    def _():
        for at in range(0, rows, BLK):
            key = lax.broadcasted_iota(jnp.int32, (span, BLK), 0)
            query = lax.broadcasted_iota(jnp.int32, (span, BLK), 1)
            same = segk_ref[at:at + span, :1] == segq_ref[:1, at:at + BLK]
            bias_ref[:, at:at + BLK] = jnp.where(same & (key - halo <= query), 0.0, NEG)

    scaled = q_ref[...] * (SCALE * LOG2E)
    dq, dk, dv = [], [], []
    for head in range(2):
        q_in = inner_form(scaled, head)
        g_in = inner_form(g_ref[...], head)
        k_out = outer_form(k_ref[...], head)
        v_out = outer_form(v_ref[...], head)
        q_mix = mixed(q_ref[...], head)
        g_mix = mixed(g_ref[...], head)
        k_mix = mixed(k_ref[...], head)
        dq_head = []
        dk_head = jnp.zeros((halo + rows, 128), F32)
        dv_head = jnp.zeros((halo + rows, 128), F32)
        dk_parts, dv_parts = [], []
        for at in range(0, rows, BLK):
            scores = dot_nt(k_out[at:at + span], q_in[at:at + BLK]) + bias_ref[:, at:at + BLK]
            top = jnp.max(scores, axis=0, keepdims=True)
            expo = jnp.exp2(scores - top)
            inverse = 1.0 / jnp.sum(expo, axis=0, keepdims=True)
            grad_probs = dot_nt(v_out[at:at + span], g_in[at:at + BLK])
            probs = expo * inverse
            delta = jnp.sum(probs * grad_probs, axis=0, keepdims=True)
            grad_scores = probs * (grad_probs - delta)
            probs_cat = jnp.concatenate(split(probs), axis=1)
            scores_cat = jnp.concatenate(split(grad_scores), axis=1)
            g_two = jnp.concatenate([g_mix[at:at + BLK]] * 2, axis=0)
            q_two = jnp.concatenate([q_mix[at:at + BLK]] * 2, axis=0)
            dv_parts.append(dot_nn(probs_cat, g_two))
            dk_parts.append(dot_nn(scores_cat, q_two))
            got = dot_tn(scores_cat, k_mix[at:at + span])
            dq_head.append(fold(got[:BLK] + got[BLK:]))
        for parts, full in ((dk_parts, dk), (dv_parts, dv)):
            pieces = []
            for kb in range((halo + rows) // BLK):
                terms = [
                    parts[qb][(kb - qb) * BLK:(kb - qb + 1) * BLK]
                    for qb in range(rows // BLK)
                    if 0 <= kb - qb < span // BLK
                ]
                pieces.append(fold(functools.reduce(lambda a, b: a + b, terms)))
            full.append(pieces)
        dq.append(dq_head)
    lane = lax.broadcasted_iota(jnp.int32, (BLK, 128), 1)
    for qb in range(rows // BLK):
        rng = slice(qb * BLK, (qb + 1) * BLK)
        far = slice(halo + qb * BLK, halo + (qb + 1) * BLK)
        both = jnp.where(lane < 64, dq[0][qb], dq[1][qb]) * SCALE
        dq_ref[rng] = unrotate(both, cos_ref[far], sin_ref[far])
    for kb in range((halo + rows) // BLK):
        rng = slice(kb * BLK, (kb + 1) * BLK)
        both = jnp.where(lane < 64, dk[0][kb], dk[1][kb]) * SCALE
        dk_ref[rng] = unrotate(both, cos_ref[rng], sin_ref[rng])
        dv_ref[rng] = jnp.where(lane < 64, dv[0][kb], dv[1][kb])


def attend_back(first, count, q_rot, kv, grad, seg_q, seg_k, cosine, sine, before=()):
    rows, model = q_rot.shape
    total = kv.shape[0]
    pairs = model // 128
    fixed = lambda shape: pl.BlockSpec(shape, lambda p: (0, 0))
    return pl.pallas_call(
        attend_back_kernel,
        grid=(count,),
        in_specs=[
            pl.BlockSpec((rows, 128), lambda p: (0, first + p)),
            pl.BlockSpec((total, 128), lambda p: (0, first + p)),
            pl.BlockSpec((total, 128), lambda p: (0, pairs + first + p)),
            pl.BlockSpec((rows, 128), lambda p: (0, first + p)),
            fixed((8, rows)), fixed((total, 128)),
            fixed((total, 128)), fixed((total, 128)),
        ] + [pl.BlockSpec(memory_space=pl.ANY)] * len(before),
        out_specs=[
            pl.BlockSpec((rows, 128), lambda p: (0, first + p)),
            pl.BlockSpec((total, 128), lambda p: (0, first + p)),
            pl.BlockSpec((total, 128), lambda p: (0, first + p)),
        ],
        out_shape=[
            jax.ShapeDtypeStruct((rows, model), F32),
            jax.ShapeDtypeStruct((total, model), F32),
            jax.ShapeDtypeStruct((total, model), F32),
        ],
        scratch_shapes=[pltpu.VMEM((total - rows + BLK, rows), F32)],
        input_output_aliases={8 + i: i for i in range(len(before))},
        cost_estimate=cost(7 * count),
        compiler_params=params(True),
    )(q_rot, kv, kv, grad, seg_q, seg_k, cosine, sine, *before)


def mlp_kernel(count, begun, chip_ref, resid_ref, other_ref, cot_ref, cot_other_ref, gain_ref, bias_ref,
               scale_ref, *refs):
    up_refs, down_refs = refs[:count], refs[count:2 * count]
    refs = refs[2 * count:]
    so_far, refs = refs[:2 * begun], refs[2 * begun:]
    out_ref, gnorm_ref, grad_ref = refs[:3]
    (x_hi, x_lo, xt_hi, xt_lo, g_hi, g_lo, up_hi, up_lo, down_hi, down_lo) = refs[3:]
    step = pl.program_id(0)
    rows = resid_ref.shape[0]

    @pl.when(step == 0)
    def _():
        for at, source, cot in ((0, resid_ref, cot_ref), (rows, other_ref, cot_other_ref)):
            xhat, _ = norm_stats(source[...])
            normed = xhat * gain_ref[...] + bias_ref[...]
            x_hi[at:at + rows], x_lo[at:at + rows] = split(normed)
            xt_hi[:, at:at + rows], xt_lo[:, at:at + rows] = split(normed.T)
            g_hi[at:at + rows], g_lo[at:at + rows] = split(cot[...] * scale_ref[0, 0])
        if begun:
            out_ref[...] = so_far[0][...]
            gnorm_ref[...] = so_far[1][...]
        else:
            out_ref[...] = jnp.zeros_like(out_ref)
            gnorm_ref[...] = jnp.zeros_like(gnorm_ref)

    for at in range(count):
        spot = (chip_ref[0] ^ at) if count > 1 else 0
        up_rows = up_refs[at].shape[0]
        high, low = split(up_refs[at][...])
        here = pl.ds(pl.multiple_of(spot * up_rows, up_rows), up_rows)
        up_hi[here], up_lo[here] = high, low
        block = down_refs[at][...]
        block = block.reshape(-1, block.shape[-1])
        high, low = split(block)
        here = pl.ds(pl.multiple_of(spot * block.shape[0], block.shape[0]), block.shape[0])
        down_hi[here], down_lo[here] = high, low

    chips, _, tall, width = grad_ref.shape
    up_tall = up_hi.shape[0] // chips
    deep = down_hi.shape[0] // chips
    up = (up_hi[...], up_lo[...])
    down = (down_hi[...], down_lo[...])
    normed = (x_hi[...], x_lo[...])
    normed_t = (xt_hi[...], xt_lo[...])
    grad_block = (g_hi[...], g_lo[...])
    pre = three(dot_nn, normed, up)
    grad_act = three(dot_nt, grad_block, down)
    inner = 0.7978845608028654 * (pre + 0.044715 * pre * pre * pre)
    bent = jnp.tanh(inner)
    act = 0.5 * pre * (1.0 + bent)
    slope = 0.5 * (1.0 + bent) + 0.5 * pre * (1.0 - bent * bent) * (
        0.7978845608028654 * (1.0 + 3.0 * 0.044715 * pre * pre)
    )
    act2 = split(act)
    grad_pre = split(grad_act * slope)
    out_ref[...] += three(dot_nn, act2, down)
    gnorm_ref[...] += three(dot_nt, grad_pre, up)
    gup = three(dot_nn, normed_t, grad_pre)
    gdown = three(dot_tn, act2, grad_block)
    half = deep // 2
    for chip in range(chips):
        grad_ref[chip, 0, :up_tall] = gup[chip * up_tall:(chip + 1) * up_tall]
        part = gdown[chip * deep:(chip + 1) * deep]
        grad_ref[chip, 0, up_tall:up_tall + deep] = part[:, :width]
        grad_ref[chip, 0, up_tall + deep:] = jnp.concatenate(
            [part[:half, width:], part[half:, width:]], axis=1
        )


def mlp(first, steps, so_far, chip, chips, resid, other, cot, cot_other, gain, bias, scale, ups, downs):
    rows, model = resid.shape
    width = 512
    up_tall = model // chips
    deep = width // chips
    fixed = lambda shape: pl.BlockSpec(shape, lambda j, c: (0, 0))
    if len(ups) > 1:
        down_spec = pl.BlockSpec((deep, model), lambda j, c: (first + j, 0))
    else:
        downs = [downs[0].reshape(chips, -1, model)]
        down_spec = pl.BlockSpec((chips, deep, model), lambda j, c: (0, first + j, 0))
    tall = up_tall + deep + deep // 2
    grid_spec = pltpu.PrefetchScalarGridSpec(
        num_scalar_prefetch=1,
        grid=(steps,),
        in_specs=[fixed((rows, model))] * 4 + [fixed((1, model))] * 2
        + [pl.BlockSpec(memory_space=pltpu.SMEM)]
        + [pl.BlockSpec((up.shape[0], width), lambda j, c: (0, first + j)) for up in ups]
        + [down_spec] * len(downs)
        + [fixed((2 * rows, model))] * len(so_far),
        out_specs=[
            fixed((2 * rows, model)), fixed((2 * rows, model)),
            pl.BlockSpec((chips, 1, tall, width), lambda j, c: (0, j, 0, 0)),
        ],
        scratch_shapes=[
            pltpu.VMEM((2 * rows, model), BF16), pltpu.VMEM((2 * rows, model), BF16),
            pltpu.VMEM((model, 2 * rows), BF16), pltpu.VMEM((model, 2 * rows), BF16),
            pltpu.VMEM((2 * rows, model), BF16), pltpu.VMEM((2 * rows, model), BF16),
            pltpu.VMEM((model, width), BF16), pltpu.VMEM((model, width), BF16),
            pltpu.VMEM((width, model), BF16), pltpu.VMEM((width, model), BF16),
        ],
    )
    return pl.pallas_call(
        functools.partial(mlp_kernel, len(ups), len(so_far) // 2),
        grid_spec=grid_spec,
        out_shape=[
            jax.ShapeDtypeStruct((2 * rows, model), F32),
            jax.ShapeDtypeStruct((2 * rows, model), F32),
            jax.ShapeDtypeStruct((chips, steps, tall, width), F32),
        ],
        cost_estimate=cost(18 * steps),
        compiler_params=params(True),
    )(chip, resid, other, cot, cot_other, gain, bias, scale, *ups, *downs, *so_far)


def unpack_grads(up, down, sibling_swap, core, chips):
    steps, up_tall, width = up.shape
    deep = up_tall * 2 // 3
    half = up_tall // 2
    mine = jnp.where(core == 0, up[:, :half], up[:, half:])
    other = sibling_swap(jnp.where(core == 0, up[:, half:], up[:, :half]))
    by_core = jnp.stack(
        [jnp.where(core == 0, mine, other), jnp.where(core == 0, other, mine)], axis=0
    )
    by_core = by_core.reshape(2, steps, half, chips, width // chips)
    grad_up = jnp.transpose(by_core, (2, 3, 0, 1, 4)).reshape(half, -1)
    quarter = width // 2
    tail = down[:, deep:]
    right = jnp.concatenate([tail[:, :, :quarter], tail[:, :, quarter:]], axis=1)
    grad_down = jnp.concatenate([down[:, :deep], right], axis=2).reshape(steps * deep, -1)
    return grad_up, grad_down


def resid_back_kernel(part_ref, given_ref, resid_ref, cot_ref, gain_ref, scale_ref, w_ref,
                      grad_ref, att_ref, sums_ref):
    grad = part_ref[...] + given_ref[...]
    xhat, rate = norm_stats(resid_ref[...])
    grad_resid = cot_ref[...] * scale_ref[0, 0] + norm_back(grad, gain_ref[...], xhat, rate)
    grad_ref[...] = grad_resid
    att_ref[...] = three(dot_nt, split(grad_resid), split(w_ref[...]))
    gain_sum = jnp.sum(grad * xhat, axis=0, keepdims=True)
    bias_sum = jnp.sum(grad, axis=0, keepdims=True)
    sums_ref[...] = jnp.concatenate(
        [gain_sum, bias_sum, jnp.zeros((6, gain_sum.shape[1]), F32)], axis=0
    )


def resid_back(part, given, resid, cot, gain, scale, w_full):
    rows, model = resid.shape
    fixed = lambda shape: pl.BlockSpec(shape, lambda j: (0, 0))
    return pl.pallas_call(
        resid_back_kernel,
        grid=(1,),
        in_specs=[fixed((rows, model))] * 4 + [fixed((1, model))]
        + [pl.BlockSpec(memory_space=pltpu.SMEM), fixed((model, model))],
        out_specs=[fixed((rows, model)), fixed((rows, model)), fixed((8, model))],
        out_shape=[
            jax.ShapeDtypeStruct((rows, model), F32),
            jax.ShapeDtypeStruct((rows, model), F32),
            jax.ShapeDtypeStruct((8, model), F32),
        ],
        cost_estimate=cost(6),
        compiler_params=params(),
    )(part, given, resid, cot, gain, scale, w_full)


def place_rows(core_ref, out_refs, got):
    chips, tall = out_refs[0].shape[:2]

    def store(core):
        for block in range(2 * chips):
            ref = out_refs[(block & 1) ^ core]
            ref[block // 2] = got[block * tall:(block + 1) * tall]

    for core in range(2):
        pl.when(core_ref[0] == core)(functools.partial(store, core))


def weights_qk_kernel(core_ref, hi_ref, lo_ref, dq_ref, dk_ref, own_ref, sib_ref, nt_hi, nt_lo):
    out_ref = (own_ref, sib_ref)
    step = pl.program_id(0)
    part = pl.num_programs(0) // 2
    halo = hi_ref.shape[0] - dq_ref.shape[0]

    @pl.when(step == 0)
    def _():
        nt_hi[...] = hi_ref[...].T
        nt_lo[...] = lo_ref[...].T

    @pl.when(step < part)
    def _():
        left = (nt_hi[:, halo:], nt_lo[:, halo:])
        place_rows(core_ref, out_ref, three(dot_nn, left, split(dq_ref[...])))

    @pl.when(step >= part)
    def _():
        left = (nt_hi[...], nt_lo[...])
        place_rows(core_ref, out_ref, three(dot_nn, left, split(dk_ref[...])))


def weights_vo_kernel(core_ref, hi_ref, lo_ref, dv_ref, att_ref, res_ref, own_ref, sib_ref,
                      nt_hi, nt_lo, at_hi, at_lo):
    out_ref = (own_ref, sib_ref)
    step = pl.program_id(0)
    part = pl.num_programs(0) // 2

    @pl.when(step == 0)
    def _():
        nt_hi[...] = hi_ref[...].T
        nt_lo[...] = lo_ref[...].T
        at_hi[...], at_lo[...] = split(att_ref[...].T)

    @pl.when(step < part)
    def _():
        left = (nt_hi[...], nt_lo[...])
        place_rows(core_ref, out_ref, three(dot_nn, left, split(dv_ref[...])))

    @pl.when(step >= part)
    def _():
        left = (at_hi[...], at_lo[...])
        place_rows(core_ref, out_ref, three(dot_nn, left, split(res_ref[...])))


def weight_call(kernel, micros, core, chips, fixed_args, pieces, scratch):
    model = fixed_args[0].shape[1]
    wide = 256
    part = model // wide
    tall = model // chips // 2
    fixed = lambda v: pl.BlockSpec(v.shape, lambda j, c: (0, 0))
    piece = lambda v, at: pl.BlockSpec(
        (v.shape[0], wide), lambda j, c: (0, jnp.clip(j - at * part, 0, part - 1))
    )
    specs, args = [], []
    for value, at in pieces:
        args.append(value)
        specs.append(fixed(value) if at is None else piece(value, at))
    return pl.pallas_call(
        kernel,
        grid_spec=pltpu.PrefetchScalarGridSpec(
            num_scalar_prefetch=1,
            grid=(2 * part,),
            in_specs=[fixed(v) for v in fixed_args] + specs,
            out_specs=[pl.BlockSpec((chips, tall, wide), lambda j, c: (0, 0, j))] * 2,
            scratch_shapes=[pltpu.VMEM((model, n), BF16) for n in scratch],
        ),
        out_shape=[jax.ShapeDtypeStruct((chips, tall, 2 * model), F32)] * 2,
        cost_estimate=cost(micros),
        compiler_params=params(),
    )(core, *fixed_args, *args)


def partial_kernel(count, *refs):
    grads, w_ref, out_ref = refs[:count], refs[count], refs[count + 1]
    held = refs[count + 2:]
    model = grads[0].shape[1]
    first = 3 - count

    @pl.when(pl.program_id(0) == 0)
    def _():
        for at, ref in enumerate(grads):
            held[2 * at][...], held[2 * at + 1][...] = split(ref[...])

    total = None
    for at in range(count):
        weights = split(w_ref[:, (first + at) * model:(first + at + 1) * model])
        term = three(dot_nt, (held[2 * at][...], held[2 * at + 1][...]), weights)
        total = term if total is None else total + term
    out_ref[...] = total


def partial_rows(block, grads, w_full):
    model = w_full.shape[0]
    rows = grads[0].shape[0] if len(grads) == 3 else grads[0].shape[0] // 3
    wide = 256
    specs = [pl.BlockSpec((rows, model), lambda j: (block, 0))] * 2
    if len(grads) == 3:
        specs = [pl.BlockSpec((rows, model), lambda j: (0, 0))] + specs
    return pl.pallas_call(
        functools.partial(partial_kernel, len(grads)),
        grid=(model // wide,),
        in_specs=specs + [pl.BlockSpec((wide, 3 * model), lambda j: (j, 0))],
        out_specs=pl.BlockSpec((rows, wide), lambda j: (0, j)),
        out_shape=jax.ShapeDtypeStruct((rows, model), F32),
        scratch_shapes=[pltpu.VMEM((rows, model), BF16)] * (2 * len(grads)),
        cost_estimate=cost(6),
        compiler_params=params(),
    )(*grads, w_full)


def matmul(left, right):
    return jnp.dot(left, right, precision=HIGH)


def inner_rows(left, right):
    return lax.dot_general(left, right, (((0,), (0,)), ((), ())), precision=HIGH)


def outer_cols(left, right):
    return lax.dot_general(left, right, (((1,), (1,)), ((), ())), precision=HIGH)


def body(
    block_input,
    embedding,
    earlier_outs,
    dwa_weights,
    ln1_gain,
    ln1_bias,
    w_qkv,
    w_out,
    ln2_gain,
    ln2_bias,
    w_up,
    w_down,
    segments,
    cotangent,
):
    groups = lax.axis_size("seq")
    rows, model = block_input.shape
    length = rows * groups
    halo = 2 * rows
    place = lax.axis_index("seq")
    ahead = [(i, i + 1) for i in range(groups - 1)]
    behind = [(i + 1, i) for i in range(groups - 1)]
    gain1, bias1 = ln1_gain[None], ln1_bias[None]
    gain2, bias2 = ln2_gain[None], ln2_bias[None]

    devices = lax.axis_size("dp")
    chips = devices // 2
    spot = lax.axis_index("dp")
    core = spot % 2
    chip = (spot // 2).reshape(1).astype(jnp.int32)
    same_core = [[2 * i + c for i in range(chips)] for c in range(2)]
    exchange = lambda v, bit: lax.ppermute(v, "dp", [(i, i ^ bit) for i in range(devices)])
    swap = lambda v: exchange(v, 1)

    gather = lambda v: lax.all_gather(v, "dp", axis=0, tiled=True)
    qkv_full = gather(w_qkv)

    shard = w_down.shape[0]
    third = shard // 3
    by_core = w_up.reshape(w_up.shape[0], chips, 2, 3, third)
    by_core = jnp.transpose(by_core, (2, 0, 3, 1, 4)).reshape(2, w_up.shape[0], -1)
    mine = jnp.where(core == 0, by_core[0], by_core[1])
    given = swap(jnp.where(core == 0, by_core[1], by_core[0]))
    up_chip = jnp.concatenate(
        [jnp.where(core == 0, mine, given), jnp.where(core == 0, given, mine)], axis=0
    )
    if chips == 4:
        up_x, down_x = exchange(up_chip, 2), exchange(w_down, 2)
        up_y, down_y = exchange(up_chip, 4), exchange(w_down, 4)
        ups = [up_chip, up_x, up_y, exchange(up_y, 2)]
        downs = [w_down, down_x, down_y, exchange(down_x, 4)]
    else:
        ups, downs = (
            [lax.all_gather(v, "dp", axis=0, tiled=True, axis_index_groups=same_core)]
            for v in (up_chip, w_down)
        )

    seg_own = segments + 1
    near = lax.ppermute(block_input, "seq", ahead)
    seg_near = lax.ppermute(seg_own, "seq", ahead)
    far = lax.ppermute(near, "seq", ahead)
    seg_far = lax.ppermute(seg_near, "seq", ahead)
    seg_all = jnp.concatenate([seg_far, seg_near, seg_own], axis=1)
    seg_k_row = jnp.broadcast_to(seg_all, (8, halo + rows))
    seg_k_col = jnp.broadcast_to(seg_all.reshape(-1, 1), (halo + rows, 128))
    seg_q_row = seg_k_row[:, halo:]
    seg_q_col = seg_k_col[halo:]

    cos_all, sin_all = rotary_tables(length, halo)
    cosine = lax.dynamic_slice_in_dim(jnp.asarray(cos_all), place * rows, halo + rows, 0)
    sine = lax.dynamic_slice_in_dim(jnp.asarray(sin_all), place * rows, halo + rows, 0)

    earlier = (embedding, earlier_outs[0], earlier_outs[1], earlier_outs[2])
    base = sum(dwa_weights[i] * value for i, value in enumerate(earlier))
    dots = jnp.stack([jnp.sum(cotangent * value) for value in earlier])
    far, base, dots = lax.optimization_barrier((far, base, dots))

    q_rot, kv, normed_hi, normed_lo = project(
        far, near, block_input, gain1, bias1, qkv_full, cosine, sine
    )
    attended = attend(q_rot, kv, seg_q_col, seg_k_row)

    out_full = gather(w_out)
    resid = block_input + matmul(attended, out_full)
    resid_other = swap(resid)
    cot_other = swap(cotangent)
    scale = dwa_weights[4].reshape(1, 1)
    call = functools.partial(
        mlp, chip=chip, chips=chips, resid=resid, other=resid_other, cot=cotangent,
        cot_other=cot_other, gain=gain2, bias=bias2, scale=scale, ups=ups, downs=downs,
    )
    scatter = lambda v: lax.psum_scatter(v, "dp", scatter_dimension=0, tiled=True)
    scatter_chips = lambda v: lax.psum_scatter(
        v, "dp", scatter_dimension=0, tiled=True, axis_index_groups=same_core
    )
    so_far, shards = (), []
    for third_at in range(3):
        out_part, gnorm_part, grads = call(third_at, 1, so_far)
        so_far = (out_part, gnorm_part)
        shards.append(scatter_chips(grads)[0])
    given = swap(gnorm_part[rows:])

    shift = lambda v, bit: lax.ppermute(v, "seq", [(i, i ^ bit) for i in range(groups)])
    even = place % 2 == 0

    def line_start(shard):
        tall = shard.shape[1] // 2
        halves = (shard[:, :tall], shard[:, tall:])
        kept = jnp.where(even, halves[0], halves[1])
        return kept + shift(jnp.where(even, halves[1], halves[0]), 1)

    def line_middle(kept):
        bit = 2
        while bit < groups:
            kept = kept + shift(kept, bit)
            bit *= 2
        return kept

    def line_end(kept):
        other = shift(kept, 1)
        return jnp.where(even, kept, other), jnp.where(even, other, kept)

    together = lax.optimization_barrier
    shards[0], given = together((shards[0], given))
    line_a = line_start(shards[0])
    grad_resid, grad_attended, sums_two = resid_back(
        gnorm_part, given, resid, cotangent, gain2, scale, out_full
    )

    back_args = (q_rot, kv, grad_attended, seg_q_row, seg_k_col, cosine, sine)
    pairs = model // 128
    line_a, back_args = together((line_a, back_args))
    line_a = line_middle(line_a)
    first_half = attend_back(0, pairs // 2, *back_args)
    line_a, shards[1], back_args, first_half = together(
        (line_a, shards[1], back_args, first_half)
    )
    line_b = line_start(shards[1])
    ends_a = line_end(line_a)
    dq, dk, dv = attend_back(pairs // 2, pairs - pairs // 2, *back_args, before=first_half)
    line_b, ends_a, dq, dk, dv = together((line_b, ends_a, dq, dk, dv))
    line_b = line_middle(line_b)
    core_at = core.reshape(1).astype(jnp.int32)
    normed_parts = (normed_hi, normed_lo)
    grads_qk = weight_call(
        weights_qk_kernel, 9, core_at, chips, normed_parts, [(dq, 0), (dk, 1)], [halo + rows] * 2
    )
    given_qk = swap(grads_qk[1])
    line_b, shards[2], dv, grad_resid = together((line_b, shards[2], dv, grad_resid))
    ends_b = line_end(line_b)
    line_c = line_start(shards[2])
    grads_vo = weight_call(
        weights_vo_kernel, 9, core_at, chips, normed_parts,
        [(dv, 0), (attended, None), (grad_resid, 1)], [halo + rows] * 2 + [rows] * 2,
    )
    line_c, ends_b, grads_vo = together((line_c, ends_b, grads_vo))
    line_c = line_middle(line_c)
    grads_c = jnp.concatenate([grads_qk[0] + given_qk, grads_vo[0] + swap(grads_vo[1])], axis=2)
    grads_c, out_part = together((grads_c, out_part))
    shard_c = scatter_chips(grads_c)[0]
    out_sib = swap(out_part[rows:])

    block_out = resid + out_part[:rows] + out_sib
    output = base + dwa_weights[4] * block_out
    dwa_local = jnp.concatenate([dots, jnp.sum(cotangent * block_out)[None]])

    part_far = partial_rows(0, (dk, dv), qkv_full)
    given_near = lax.ppermute(part_far, "seq", behind)
    dk, far, near, line_c, part_far = together((dk, far, near, line_c, part_far))
    ends_c = line_end(line_c)
    part_near = partial_rows(1, (dk, dv), qkv_full)
    own_part = partial_rows(2, (dq, dk, dv), qkv_full)
    (sent,) = together((part_near,))
    back_near = sent + given_near

    xhat1, rate1 = norm_stats(block_input)
    terms = (
        (norm_stats(far)[0], part_far),
        (norm_stats(near)[0], part_near),
        (xhat1, own_part),
    )
    grad_gain_one = sum(jnp.sum(xhat * part, axis=0) for xhat, part in terms)
    grad_bias_one = sum(jnp.sum(part, axis=0) for _, part in terms)

    small = jnp.concatenate(
        [
            grad_gain_one[None], grad_bias_one[None], sums_two[:2],
            jnp.pad(dwa_local, (0, model - 5))[None], jnp.zeros((3, model), F32),
        ],
        axis=0,
    )
    bit = 1
    while bit < devices:
        small = small + exchange(small, bit)
        bit *= 2
    shard_c, back_near, small = together((shard_c, back_near, small))
    last = line_middle(line_start(shard_c[None]))
    given_back = lax.ppermute(back_near, "seq", behind)
    grad_up, grad_down = unpack_grads(
        *(
            jnp.concatenate(parts, axis=0)
            for parts in zip(ends_a, ends_b, ends_c)
        ),
        swap, core, chips,
    )
    last, grad_up, grad_down, small, given_back = together(
        (last, grad_up, grad_down, small, given_back)
    )
    bit = 1
    while bit < groups:
        small = small + shift(small, bit)
        bit *= 2
    gain_one, bias_one, gain_two, bias_two = small[0], small[1], small[2], small[3]
    grad_dwa = small[4, :5]
    last = jnp.concatenate(line_end(last), axis=1)[0]
    grad_qkv, grad_wout = last[:, :3 * model], last[:, 3 * model:]
    grad_normed_one = own_part + given_back
    grad_input = grad_resid + norm_back(grad_normed_one, gain1, xhat1, rate1)
    return (
        output,
        grad_input,
        grad_dwa,
        gain_one,
        bias_one,
        grad_qkv,
        grad_wout,
        gain_two,
        bias_two,
        grad_up,
        grad_down,
    )


def solution(mesh):
    in_specs = (
        P(("dp", "seq"), None),
        P(("dp", "seq"), None),
        P(None, ("dp", "seq"), None),
        P(),
        P(),
        P(),
        P("dp", None),
        P("dp", None),
        P(),
        P(),
        P("dp", None),
        P("dp", None),
        P("dp", "seq"),
        P(("dp", "seq"), None),
    )
    out_specs = (
        P(("dp", "seq"), None),
        P(("dp", "seq"), None),
        P(),
        P(),
        P(),
        P("dp", None),
        P("dp", None),
        P(),
        P(),
        P("dp", None),
        P("dp", None),
    )
    return jax.shard_map(body, mesh=mesh, in_specs=in_specs, out_specs=out_specs, check_vma=False)
```

```python
import functools
import math

import jax
import jax.numpy as jnp
import numpy as np
from jax import lax
from jax.experimental import pallas as pl
from jax.experimental.pallas import tpu as pltpu
from jax.sharding import PartitionSpec as P

HD = 64
DOC_MOST = 768
LOG2E = math.log2(math.e)
SCALE = 1.0 / math.sqrt(HD)
NEG = -1e30
F32 = jnp.float32
BF16 = jnp.bfloat16
HIGH = lax.Precision.HIGH
VMEM_LIMIT = 56 * 1024 * 1024
BLK = 128


def cost(micros):
    return pl.CostEstimate(
        flops=int(micros * 1.1e9), bytes_accessed=1 << 20, transcendentals=0
    )


def params():
    return pltpu.CompilerParams(
        dimension_semantics=("arbitrary",), vmem_limit_bytes=VMEM_LIMIT
    )


def split(values):
    high = values.astype(BF16)
    return high, (values - high.astype(F32)).astype(BF16)


def dot_nn(left, right):
    return lax.dot_general(left, right, (((1,), (0,)), ((), ())), preferred_element_type=F32)


def dot_nt(left, right):
    return lax.dot_general(left, right, (((1,), (1,)), ((), ())), preferred_element_type=F32)


def dot_tn(left, right):
    return lax.dot_general(left, right, (((0,), (0,)), ((), ())), preferred_element_type=F32)


def three(dot, left, right):
    return (
        dot(left[0], right[0]) + dot(left[0], right[1]) + dot(left[1], right[0])
    )


def norm_stats(values):
    row_mean = jnp.mean(values, axis=-1, keepdims=True)
    centred = values - row_mean
    row_var = jnp.mean(centred * centred, axis=-1, keepdims=True)
    rate = lax.rsqrt(row_var + 1e-05)
    return centred * rate, rate


def norm_back(grad, gain, xhat, rate):
    scaled = grad * gain
    return rate * (
        scaled
        - jnp.mean(scaled, axis=-1, keepdims=True)
        - xhat * jnp.mean(scaled * xhat, axis=-1, keepdims=True)
    )


def turned(values):
    lane = lax.broadcasted_iota(jnp.int32, values.shape, 1)
    return jnp.where(
        (lane & 63) < 32, pltpu.roll(values, 96, 1), pltpu.roll(values, 32, 1)
    )


def rotate(values, cosine, sine):
    return values * cosine + turned(values) * sine


def unrotate(values, cosine, sine):
    return values * cosine - turned(values) * sine


def rotary_tables(length, halo):
    half = HD // 2
    inv_freq = (10000.0 ** (-(np.arange(half, dtype=np.float32) * 2.0 / HD))).astype(np.float32)
    place = np.arange(-halo, length, dtype=np.float32)
    angles = place[:, None] * inv_freq[None, :]
    cosine = np.cos(angles.astype(np.float64)).astype(np.float32)
    sine = np.sin(angles.astype(np.float64)).astype(np.float32)
    return (
        np.concatenate([cosine] * 4, axis=1),
        np.concatenate([-sine, sine, -sine, sine], axis=1),
    )


def qkv_kernel(far_ref, near_ref, own_ref, gain_ref, bias_ref, w_ref, cos_ref, sin_ref,
               q_ref, kv_ref, hi_ref, lo_ref):
    step = pl.program_id(0)
    rows = own_ref.shape[0]
    third = pl.num_programs(0) // 3
    halo = hi_ref.shape[0] - rows

    @pl.when(step == 0)
    def _():
        for at, ref in enumerate((far_ref, near_ref, own_ref)):
            xhat, _ = norm_stats(ref[...])
            high, low = split(xhat * gain_ref[...] + bias_ref[...])
            hi_ref[at * rows:(at + 1) * rows] = high
            lo_ref[at * rows:(at + 1) * rows] = low

    weights = split(w_ref[...])

    @pl.when(step < third)
    def _():
        got = three(dot_nn, (hi_ref[halo:], lo_ref[halo:]), weights)
        for at in range(0, got.shape[1], 128):
            q_ref[:, at:at + 128] = rotate(got[:, at:at + 128], cos_ref[halo:], sin_ref[halo:])

    @pl.when((step >= third) & (step < 2 * third))
    def _():
        got = three(dot_nn, (hi_ref[...], lo_ref[...]), weights)
        for at in range(0, got.shape[1], 128):
            kv_ref[:, at:at + 128] = rotate(got[:, at:at + 128], cos_ref[...], sin_ref[...])

    @pl.when(step >= 2 * third)
    def _():
        kv_ref[...] = three(dot_nn, (hi_ref[...], lo_ref[...]), weights)


def project(far, near, own, gain, bias, w_full, cosine, sine):
    rows, model = own.shape
    total = 3 * rows
    wide = 256
    third = model // wide
    whole = lambda shape: pl.BlockSpec(shape, lambda j: (0, 0))
    return pl.pallas_call(
        qkv_kernel,
        grid=(3 * third,),
        in_specs=[
            whole((rows, model)), whole((rows, model)), whole((rows, model)),
            whole((1, model)), whole((1, model)),
            pl.BlockSpec((model, wide), lambda j: (0, j)),
            whole((total, 128)), whole((total, 128)),
        ],
        out_specs=[
            pl.BlockSpec((rows, wide), lambda j: (0, jnp.minimum(j, third - 1))),
            pl.BlockSpec((total, wide), lambda j: (0, jnp.maximum(j - third, 0))),
            whole((total, model)), whole((total, model)),
        ],
        out_shape=[
            jax.ShapeDtypeStruct((rows, model), F32),
            jax.ShapeDtypeStruct((total, 2 * model), F32),
            jax.ShapeDtypeStruct((total, model), BF16),
            jax.ShapeDtypeStruct((total, model), BF16),
        ],
        cost_estimate=cost(20),
        compiler_params=params(),
    )(far, near, own, gain, bias, w_full, cosine, sine)


def own_pair(values, head):
    lane = lax.broadcasted_iota(jnp.int32, values.shape, 1)
    other = pltpu.roll(values, 64, 1)
    return jnp.where((lane < 64) == (head == 0), values, other)


def outer_form(values, head):
    high, low = split(own_pair(values, head))
    return jnp.concatenate([high, low], axis=1)


def mixed(values, head):
    pair = own_pair(values, head)
    lane = lax.broadcasted_iota(jnp.int32, pair.shape, 1)
    high = pair.astype(BF16).astype(F32)
    return jnp.where(lane < 64, high, pair - high).astype(BF16)


def inner_form(values, head):
    half = mixed(values, head)
    return jnp.concatenate([half, half], axis=1)


def fold(values):
    return values + pltpu.roll(values, 64, 1)


def attend_kernel(q_ref, k_ref, v_ref, segq_ref, segk_ref, out_ref, bias_ref):
    rows = q_ref.shape[0]
    halo = k_ref.shape[0] - rows
    span = halo + BLK

    @pl.when(pl.program_id(0) == 0)
    def _():
        for at in range(0, rows, BLK):
            row = lax.broadcasted_iota(jnp.int32, (BLK, span), 0)
            col = lax.broadcasted_iota(jnp.int32, (BLK, span), 1)
            same = segq_ref[at:at + BLK, :1] == segk_ref[:1, at:at + span]
            bias_ref[at:at + BLK] = jnp.where(same & (col - halo <= row), 0.0, NEG)

    lane = lax.broadcasted_iota(jnp.int32, (BLK, 128), 1)
    scaled = q_ref[...] * (SCALE * LOG2E)
    results = []
    for head in range(2):
        left = inner_form(scaled, head)
        right = outer_form(k_ref[...], head)
        vals = mixed(v_ref[...], head)
        outs = []
        for at in range(0, rows, BLK):
            scores = dot_nt(left[at:at + BLK], right[at:at + span]) + bias_ref[at:at + BLK]
            top = jnp.max(scores, axis=1, keepdims=True)
            expo = jnp.exp2(scores - top)
            total = jnp.sum(expo, axis=1, keepdims=True)
            high, low = split(expo)
            got = dot_nn(high, vals[at:at + span]) + dot_nn(low, vals[at:at + span])
            outs.append(fold(got) / total)
        results.append(outs)
    for at in range(0, rows, BLK):
        out_ref[at:at + BLK] = jnp.where(
            lane < 64, results[0][at // BLK], results[1][at // BLK]
        )


def attend(q_rot, kv, seg_q, seg_k):
    rows, model = q_rot.shape
    total = kv.shape[0]
    pairs = model // 128
    return pl.pallas_call(
        attend_kernel,
        grid=(pairs,),
        in_specs=[
            pl.BlockSpec((rows, 128), lambda p: (0, p)),
            pl.BlockSpec((total, 128), lambda p: (0, p)),
            pl.BlockSpec((total, 128), lambda p: (0, pairs + p)),
            pl.BlockSpec((rows, 128), lambda p: (0, 0)),
            pl.BlockSpec((8, total), lambda p: (0, 0)),
        ],
        out_specs=pl.BlockSpec((rows, 128), lambda p: (0, p)),
        out_shape=jax.ShapeDtypeStruct((rows, model), F32),
        scratch_shapes=[pltpu.VMEM((rows, total - rows + BLK), F32)],
        cost_estimate=cost(24),
        compiler_params=params(),
    )(q_rot, kv, kv, seg_q, seg_k)


def attend_back_kernel(q_ref, k_ref, v_ref, g_ref, segq_ref, segk_ref, cos_ref, sin_ref, *refs):
    dq_ref, dk_ref, dv_ref, bias_ref = refs[-4:]
    rows = q_ref.shape[0]
    halo = k_ref.shape[0] - rows
    span = halo + BLK

    @pl.when(pl.program_id(0) == 0)
    def _():
        for at in range(0, rows, BLK):
            key = lax.broadcasted_iota(jnp.int32, (span, BLK), 0)
            query = lax.broadcasted_iota(jnp.int32, (span, BLK), 1)
            same = segk_ref[at:at + span, :1] == segq_ref[:1, at:at + BLK]
            bias_ref[:, at:at + BLK] = jnp.where(same & (key - halo <= query), 0.0, NEG)

    scaled = q_ref[...] * (SCALE * LOG2E)
    dq, dk, dv = [], [], []
    for head in range(2):
        q_in = inner_form(scaled, head)
        g_in = inner_form(g_ref[...], head)
        k_out = outer_form(k_ref[...], head)
        v_out = outer_form(v_ref[...], head)
        q_mix = mixed(q_ref[...], head)
        g_mix = mixed(g_ref[...], head)
        k_mix = mixed(k_ref[...], head)
        dq_head = []
        dk_head = jnp.zeros((halo + rows, 128), F32)
        dv_head = jnp.zeros((halo + rows, 128), F32)
        dk_parts, dv_parts = [], []
        for at in range(0, rows, BLK):
            scores = dot_nt(k_out[at:at + span], q_in[at:at + BLK]) + bias_ref[:, at:at + BLK]
            top = jnp.max(scores, axis=0, keepdims=True)
            expo = jnp.exp2(scores - top)
            inverse = 1.0 / jnp.sum(expo, axis=0, keepdims=True)
            grad_probs = dot_nt(v_out[at:at + span], g_in[at:at + BLK])
            probs = expo * inverse
            delta = jnp.sum(probs * grad_probs, axis=0, keepdims=True)
            grad_scores = probs * (grad_probs - delta)
            probs_cat = jnp.concatenate(split(probs), axis=1)
            scores_cat = jnp.concatenate(split(grad_scores), axis=1)
            g_two = jnp.concatenate([g_mix[at:at + BLK]] * 2, axis=0)
            q_two = jnp.concatenate([q_mix[at:at + BLK]] * 2, axis=0)
            dv_parts.append(dot_nn(probs_cat, g_two))
            dk_parts.append(dot_nn(scores_cat, q_two))
            got = dot_tn(scores_cat, k_mix[at:at + span])
            dq_head.append(fold(got[:BLK] + got[BLK:]))
        for parts, full in ((dk_parts, dk), (dv_parts, dv)):
            pieces = []
            for kb in range((halo + rows) // BLK):
                terms = [
                    parts[qb][(kb - qb) * BLK:(kb - qb + 1) * BLK]
                    for qb in range(rows // BLK)
                    if 0 <= kb - qb < span // BLK
                ]
                pieces.append(fold(functools.reduce(lambda a, b: a + b, terms)))
            full.append(pieces)
        dq.append(dq_head)
    lane = lax.broadcasted_iota(jnp.int32, (BLK, 128), 1)
    for qb in range(rows // BLK):
        rng = slice(qb * BLK, (qb + 1) * BLK)
        far = slice(halo + qb * BLK, halo + (qb + 1) * BLK)
        both = jnp.where(lane < 64, dq[0][qb], dq[1][qb]) * SCALE
        dq_ref[rng] = unrotate(both, cos_ref[far], sin_ref[far])
    for kb in range((halo + rows) // BLK):
        rng = slice(kb * BLK, (kb + 1) * BLK)
        both = jnp.where(lane < 64, dk[0][kb], dk[1][kb]) * SCALE
        dk_ref[rng] = unrotate(both, cos_ref[rng], sin_ref[rng])
        dv_ref[rng] = jnp.where(lane < 64, dv[0][kb], dv[1][kb])


def attend_back(first, count, q_rot, kv, grad, seg_q, seg_k, cosine, sine, before=()):
    rows, model = q_rot.shape
    total = kv.shape[0]
    pairs = model // 128
    fixed = lambda shape: pl.BlockSpec(shape, lambda p: (0, 0))
    return pl.pallas_call(
        attend_back_kernel,
        grid=(count,),
        in_specs=[
            pl.BlockSpec((rows, 128), lambda p: (0, first + p)),
            pl.BlockSpec((total, 128), lambda p: (0, first + p)),
            pl.BlockSpec((total, 128), lambda p: (0, pairs + first + p)),
            pl.BlockSpec((rows, 128), lambda p: (0, first + p)),
            fixed((8, rows)), fixed((total, 128)),
            fixed((total, 128)), fixed((total, 128)),
        ] + [pl.BlockSpec(memory_space=pl.ANY)] * len(before),
        out_specs=[
            pl.BlockSpec((rows, 128), lambda p: (0, first + p)),
            pl.BlockSpec((total, 128), lambda p: (0, first + p)),
            pl.BlockSpec((total, 128), lambda p: (0, first + p)),
        ],
        out_shape=[
            jax.ShapeDtypeStruct((rows, model), F32),
            jax.ShapeDtypeStruct((total, model), F32),
            jax.ShapeDtypeStruct((total, model), F32),
        ],
        scratch_shapes=[pltpu.VMEM((total - rows + BLK, rows), F32)],
        input_output_aliases={8 + i: i for i in range(len(before))},
        cost_estimate=cost(7 * count),
        compiler_params=params(),
    )(q_rot, kv, kv, grad, seg_q, seg_k, cosine, sine, *before)


def mlp_kernel(count, begun, chip_ref, resid_ref, other_ref, cot_ref, cot_other_ref, gain_ref, bias_ref,
               scale_ref, *refs):
    up_refs, down_refs = refs[:count], refs[count:2 * count]
    refs = refs[2 * count:]
    so_far, refs = refs[:2 * begun], refs[2 * begun:]
    out_ref, gnorm_ref, grad_ref = refs[:3]
    (x_hi, x_lo, xt_hi, xt_lo, g_hi, g_lo, up_hi, up_lo, down_hi, down_lo) = refs[3:]
    step = pl.program_id(0)
    rows = resid_ref.shape[0]

    @pl.when(step == 0)
    def _():
        for at, source, cot in ((0, resid_ref, cot_ref), (rows, other_ref, cot_other_ref)):
            xhat, _ = norm_stats(source[...])
            normed = xhat * gain_ref[...] + bias_ref[...]
            x_hi[at:at + rows], x_lo[at:at + rows] = split(normed)
            xt_hi[:, at:at + rows], xt_lo[:, at:at + rows] = split(normed.T)
            g_hi[at:at + rows], g_lo[at:at + rows] = split(cot[...] * scale_ref[0, 0])
        if begun:
            out_ref[...] = so_far[0][...]
            gnorm_ref[...] = so_far[1][...]
        else:
            out_ref[...] = jnp.zeros_like(out_ref)
            gnorm_ref[...] = jnp.zeros_like(gnorm_ref)

    for at in range(count):
        spot = (chip_ref[0] ^ at) if count > 1 else 0
        up_rows = up_refs[at].shape[0]
        high, low = split(up_refs[at][...])
        here = pl.ds(pl.multiple_of(spot * up_rows, up_rows), up_rows)
        up_hi[here], up_lo[here] = high, low
        block = down_refs[at][...]
        block = block.reshape(-1, block.shape[-1])
        high, low = split(block)
        here = pl.ds(pl.multiple_of(spot * block.shape[0], block.shape[0]), block.shape[0])
        down_hi[here], down_lo[here] = high, low

    chips, _, tall, width = grad_ref.shape
    up_tall = up_hi.shape[0] // chips
    deep = down_hi.shape[0] // chips
    up = (up_hi[...], up_lo[...])
    down = (down_hi[...], down_lo[...])
    normed = (x_hi[...], x_lo[...])
    normed_t = (xt_hi[...], xt_lo[...])
    grad_block = (g_hi[...], g_lo[...])
    pre = three(dot_nn, normed, up)
    grad_act = three(dot_nt, grad_block, down)
    inner = 0.7978845608028654 * (pre + 0.044715 * pre * pre * pre)
    bent = jnp.tanh(inner)
    act = 0.5 * pre * (1.0 + bent)
    slope = 0.5 * (1.0 + bent) + 0.5 * pre * (1.0 - bent * bent) * (
        0.7978845608028654 * (1.0 + 3.0 * 0.044715 * pre * pre)
    )
    act2 = split(act)
    grad_pre = split(grad_act * slope)
    out_ref[...] += three(dot_nn, act2, down)
    gnorm_ref[...] += three(dot_nt, grad_pre, up)
    gup = three(dot_nn, normed_t, grad_pre)
    gdown = three(dot_tn, act2, grad_block)
    half = deep // 2
    for chip in range(chips):
        grad_ref[chip, 0, :up_tall] = gup[chip * up_tall:(chip + 1) * up_tall]
        part = gdown[chip * deep:(chip + 1) * deep]
        grad_ref[chip, 0, up_tall:up_tall + deep] = part[:, :width]
        grad_ref[chip, 0, up_tall + deep:] = jnp.concatenate(
            [part[:half, width:], part[half:, width:]], axis=1
        )


def mlp(first, steps, so_far, chip, chips, resid, other, cot, cot_other, gain, bias, scale, ups, downs):
    rows, model = resid.shape
    width = 512
    up_tall = model // chips
    deep = width // chips
    fixed = lambda shape: pl.BlockSpec(shape, lambda j, c: (0, 0))
    if len(ups) > 1:
        down_spec = pl.BlockSpec((deep, model), lambda j, c: (first + j, 0))
    else:
        downs = [downs[0].reshape(chips, -1, model)]
        down_spec = pl.BlockSpec((chips, deep, model), lambda j, c: (0, first + j, 0))
    tall = up_tall + deep + deep // 2
    grid_spec = pltpu.PrefetchScalarGridSpec(
        num_scalar_prefetch=1,
        grid=(steps,),
        in_specs=[fixed((rows, model))] * 4 + [fixed((1, model))] * 2
        + [pl.BlockSpec(memory_space=pltpu.SMEM)]
        + [pl.BlockSpec((up.shape[0], width), lambda j, c: (0, first + j)) for up in ups]
        + [down_spec] * len(downs)
        + [fixed((2 * rows, model))] * len(so_far),
        out_specs=[
            fixed((2 * rows, model)), fixed((2 * rows, model)),
            pl.BlockSpec((chips, 1, tall, width), lambda j, c: (0, j, 0, 0)),
        ],
        scratch_shapes=[
            pltpu.VMEM((2 * rows, model), BF16), pltpu.VMEM((2 * rows, model), BF16),
            pltpu.VMEM((model, 2 * rows), BF16), pltpu.VMEM((model, 2 * rows), BF16),
            pltpu.VMEM((2 * rows, model), BF16), pltpu.VMEM((2 * rows, model), BF16),
            pltpu.VMEM((model, width), BF16), pltpu.VMEM((model, width), BF16),
            pltpu.VMEM((width, model), BF16), pltpu.VMEM((width, model), BF16),
        ],
    )
    return pl.pallas_call(
        functools.partial(mlp_kernel, len(ups), len(so_far) // 2),
        grid_spec=grid_spec,
        out_shape=[
            jax.ShapeDtypeStruct((2 * rows, model), F32),
            jax.ShapeDtypeStruct((2 * rows, model), F32),
            jax.ShapeDtypeStruct((chips, steps, tall, width), F32),
        ],
        cost_estimate=cost(18 * steps),
        compiler_params=params(),
    )(chip, resid, other, cot, cot_other, gain, bias, scale, *ups, *downs, *so_far)


def unpack_grads(up, down, sibling_swap, core, chips):
    steps, up_tall, width = up.shape
    deep = up_tall * 2 // 3
    half = up_tall // 2
    mine = jnp.where(core == 0, up[:, :half], up[:, half:])
    other = sibling_swap(jnp.where(core == 0, up[:, half:], up[:, :half]))
    by_core = jnp.stack(
        [jnp.where(core == 0, mine, other), jnp.where(core == 0, other, mine)], axis=0
    )
    by_core = by_core.reshape(2, steps, half, chips, width // chips)
    grad_up = jnp.transpose(by_core, (2, 3, 0, 1, 4)).reshape(half, -1)
    quarter = width // 2
    tail = down[:, deep:]
    right = jnp.concatenate([tail[:, :, :quarter], tail[:, :, quarter:]], axis=1)
    grad_down = jnp.concatenate([down[:, :deep], right], axis=2).reshape(steps * deep, -1)
    return grad_up, grad_down


def resid_back_kernel(part_ref, given_ref, resid_ref, cot_ref, gain_ref, scale_ref, w_ref,
                      grad_ref, att_ref, sums_ref):
    grad = part_ref[...] + given_ref[...]
    xhat, rate = norm_stats(resid_ref[...])
    grad_resid = cot_ref[...] * scale_ref[0, 0] + norm_back(grad, gain_ref[...], xhat, rate)
    grad_ref[...] = grad_resid
    att_ref[...] = three(dot_nt, split(grad_resid), split(w_ref[...]))
    gain_sum = jnp.sum(grad * xhat, axis=0, keepdims=True)
    bias_sum = jnp.sum(grad, axis=0, keepdims=True)
    sums_ref[...] = jnp.concatenate(
        [gain_sum, bias_sum, jnp.zeros((6, gain_sum.shape[1]), F32)], axis=0
    )


def resid_back(part, given, resid, cot, gain, scale, w_full):
    rows, model = resid.shape
    fixed = lambda shape: pl.BlockSpec(shape, lambda j: (0, 0))
    return pl.pallas_call(
        resid_back_kernel,
        grid=(1,),
        in_specs=[fixed((rows, model))] * 4 + [fixed((1, model))]
        + [pl.BlockSpec(memory_space=pltpu.SMEM), fixed((model, model))],
        out_specs=[fixed((rows, model)), fixed((rows, model)), fixed((8, model))],
        out_shape=[
            jax.ShapeDtypeStruct((rows, model), F32),
            jax.ShapeDtypeStruct((rows, model), F32),
            jax.ShapeDtypeStruct((8, model), F32),
        ],
        cost_estimate=cost(6),
        compiler_params=params(),
    )(part, given, resid, cot, gain, scale, w_full)


def place_rows(core_ref, out_refs, got):
    chips, tall = out_refs[0].shape[:2]

    def store(core):
        for block in range(2 * chips):
            ref = out_refs[(block & 1) ^ core]
            ref[block // 2] = got[block * tall:(block + 1) * tall]

    for core in range(2):
        pl.when(core_ref[0] == core)(functools.partial(store, core))


def weights_qk_kernel(core_ref, hi_ref, lo_ref, dq_ref, dk_ref, own_ref, sib_ref, nt_hi, nt_lo):
    out_ref = (own_ref, sib_ref)
    step = pl.program_id(0)
    part = pl.num_programs(0) // 2
    halo = hi_ref.shape[0] - dq_ref.shape[0]

    @pl.when(step == 0)
    def _():
        nt_hi[...] = hi_ref[...].T
        nt_lo[...] = lo_ref[...].T

    @pl.when(step < part)
    def _():
        left = (nt_hi[:, halo:], nt_lo[:, halo:])
        place_rows(core_ref, out_ref, three(dot_nn, left, split(dq_ref[...])))

    @pl.when(step >= part)
    def _():
        left = (nt_hi[...], nt_lo[...])
        place_rows(core_ref, out_ref, three(dot_nn, left, split(dk_ref[...])))


def weights_vo_kernel(core_ref, hi_ref, lo_ref, dv_ref, att_ref, res_ref, own_ref, sib_ref,
                      nt_hi, nt_lo, at_hi, at_lo):
    out_ref = (own_ref, sib_ref)
    step = pl.program_id(0)
    part = pl.num_programs(0) // 2

    @pl.when(step == 0)
    def _():
        nt_hi[...] = hi_ref[...].T
        nt_lo[...] = lo_ref[...].T
        at_hi[...], at_lo[...] = split(att_ref[...].T)

    @pl.when(step < part)
    def _():
        left = (nt_hi[...], nt_lo[...])
        place_rows(core_ref, out_ref, three(dot_nn, left, split(dv_ref[...])))

    @pl.when(step >= part)
    def _():
        left = (at_hi[...], at_lo[...])
        place_rows(core_ref, out_ref, three(dot_nn, left, split(res_ref[...])))


def weight_call(kernel, micros, core, chips, fixed_args, pieces, scratch):
    model = fixed_args[0].shape[1]
    wide = 256
    part = model // wide
    tall = model // chips // 2
    fixed = lambda v: pl.BlockSpec(v.shape, lambda j, c: (0, 0))
    piece = lambda v, at: pl.BlockSpec(
        (v.shape[0], wide), lambda j, c: (0, jnp.clip(j - at * part, 0, part - 1))
    )
    specs, args = [], []
    for value, at in pieces:
        args.append(value)
        specs.append(fixed(value) if at is None else piece(value, at))
    return pl.pallas_call(
        kernel,
        grid_spec=pltpu.PrefetchScalarGridSpec(
            num_scalar_prefetch=1,
            grid=(2 * part,),
            in_specs=[fixed(v) for v in fixed_args] + specs,
            out_specs=[pl.BlockSpec((chips, tall, wide), lambda j, c: (0, 0, j))] * 2,
            scratch_shapes=[pltpu.VMEM((model, n), BF16) for n in scratch],
        ),
        out_shape=[jax.ShapeDtypeStruct((chips, tall, 2 * model), F32)] * 2,
        cost_estimate=cost(micros),
        compiler_params=params(),
    )(core, *fixed_args, *args)


def partial_kernel(count, *refs):
    grads, w_ref, out_ref = refs[:count], refs[count], refs[count + 1]
    held = refs[count + 2:]
    model = grads[0].shape[1]
    first = 3 - count

    @pl.when(pl.program_id(0) == 0)
    def _():
        for at, ref in enumerate(grads):
            held[2 * at][...], held[2 * at + 1][...] = split(ref[...])

    total = None
    for at in range(count):
        weights = split(w_ref[:, (first + at) * model:(first + at + 1) * model])
        term = three(dot_nt, (held[2 * at][...], held[2 * at + 1][...]), weights)
        total = term if total is None else total + term
    out_ref[...] = total


def partial_rows(block, grads, w_full):
    model = w_full.shape[0]
    rows = grads[0].shape[0] if len(grads) == 3 else grads[0].shape[0] // 3
    wide = 256
    specs = [pl.BlockSpec((rows, model), lambda j: (block, 0))] * 2
    if len(grads) == 3:
        specs = [pl.BlockSpec((rows, model), lambda j: (0, 0))] + specs
    return pl.pallas_call(
        functools.partial(partial_kernel, len(grads)),
        grid=(model // wide,),
        in_specs=specs + [pl.BlockSpec((wide, 3 * model), lambda j: (j, 0))],
        out_specs=pl.BlockSpec((rows, wide), lambda j: (0, j)),
        out_shape=jax.ShapeDtypeStruct((rows, model), F32),
        scratch_shapes=[pltpu.VMEM((rows, model), BF16)] * (2 * len(grads)),
        cost_estimate=cost(6),
        compiler_params=params(),
    )(*grads, w_full)


def matmul(left, right):
    return jnp.dot(left, right, precision=HIGH)


def inner_rows(left, right):
    return lax.dot_general(left, right, (((0,), (0,)), ((), ())), precision=HIGH)


def outer_cols(left, right):
    return lax.dot_general(left, right, (((1,), (1,)), ((), ())), precision=HIGH)


def body(
    block_input,
    embedding,
    earlier_outs,
    dwa_weights,
    ln1_gain,
    ln1_bias,
    w_qkv,
    w_out,
    ln2_gain,
    ln2_bias,
    w_up,
    w_down,
    segments,
    cotangent,
):
    groups = lax.axis_size("seq")
    rows, model = block_input.shape
    length = rows * groups
    halo = 2 * rows
    place = lax.axis_index("seq")
    ahead = [(i, i + 1) for i in range(groups - 1)]
    behind = [(i + 1, i) for i in range(groups - 1)]
    gain1, bias1 = ln1_gain[None], ln1_bias[None]
    gain2, bias2 = ln2_gain[None], ln2_bias[None]

    devices = lax.axis_size("dp")
    chips = devices // 2
    spot = lax.axis_index("dp")
    core = spot % 2
    chip = (spot // 2).reshape(1).astype(jnp.int32)
    same_core = [[2 * i + c for i in range(chips)] for c in range(2)]
    exchange = lambda v, bit: lax.ppermute(v, "dp", [(i, i ^ bit) for i in range(devices)])
    swap = lambda v: exchange(v, 1)

    gather = lambda v: lax.all_gather(v, "dp", axis=0, tiled=True)
    qkv_full = gather(w_qkv)

    shard = w_down.shape[0]
    third = shard // 3
    by_core = w_up.reshape(w_up.shape[0], chips, 2, 3, third)
    by_core = jnp.transpose(by_core, (2, 0, 3, 1, 4)).reshape(2, w_up.shape[0], -1)
    mine = jnp.where(core == 0, by_core[0], by_core[1])
    given = swap(jnp.where(core == 0, by_core[1], by_core[0]))
    up_chip = jnp.concatenate(
        [jnp.where(core == 0, mine, given), jnp.where(core == 0, given, mine)], axis=0
    )
    if chips == 4:
        up_x, down_x = exchange(up_chip, 2), exchange(w_down, 2)
        up_y, down_y = exchange(up_chip, 4), exchange(w_down, 4)
        ups = [up_chip, up_x, up_y, exchange(up_y, 2)]
        downs = [w_down, down_x, down_y, exchange(down_x, 4)]
    else:
        ups, downs = (
            [lax.all_gather(v, "dp", axis=0, tiled=True, axis_index_groups=same_core)]
            for v in (up_chip, w_down)
        )

    seg_own = segments + 1
    near = lax.ppermute(block_input, "seq", ahead)
    seg_near = lax.ppermute(seg_own, "seq", ahead)
    far = lax.ppermute(near, "seq", ahead)
    seg_far = lax.ppermute(seg_near, "seq", ahead)
    seg_all = jnp.concatenate([seg_far, seg_near, seg_own], axis=1)
    seg_k_row = jnp.broadcast_to(seg_all, (8, halo + rows))
    seg_k_col = jnp.broadcast_to(seg_all.reshape(-1, 1), (halo + rows, 128))
    seg_q_row = seg_k_row[:, halo:]
    seg_q_col = seg_k_col[halo:]

    cos_all, sin_all = rotary_tables(length, halo)
    cosine = lax.dynamic_slice_in_dim(jnp.asarray(cos_all), place * rows, halo + rows, 0)
    sine = lax.dynamic_slice_in_dim(jnp.asarray(sin_all), place * rows, halo + rows, 0)

    earlier = (embedding, earlier_outs[0], earlier_outs[1], earlier_outs[2])
    base = sum(dwa_weights[i] * value for i, value in enumerate(earlier))
    dots = jnp.stack([jnp.sum(cotangent * value) for value in earlier])
    far, base, dots = lax.optimization_barrier((far, base, dots))

    q_rot, kv, normed_hi, normed_lo = project(
        far, near, block_input, gain1, bias1, qkv_full, cosine, sine
    )
    attended = attend(q_rot, kv, seg_q_col, seg_k_row)

    out_full = gather(w_out)
    resid = block_input + matmul(attended, out_full)
    resid_other = swap(resid)
    cot_other = swap(cotangent)
    scale = dwa_weights[4].reshape(1, 1)
    call = functools.partial(
        mlp, chip=chip, chips=chips, resid=resid, other=resid_other, cot=cotangent,
        cot_other=cot_other, gain=gain2, bias=bias2, scale=scale, ups=ups, downs=downs,
    )
    scatter = lambda v: lax.psum_scatter(v, "dp", scatter_dimension=0, tiled=True)
    scatter_chips = lambda v: lax.psum_scatter(
        v, "dp", scatter_dimension=0, tiled=True, axis_index_groups=same_core
    )
    so_far, shards = (), []
    for third_at in range(3):
        out_part, gnorm_part, grads = call(third_at, 1, so_far)
        so_far = (out_part, gnorm_part)
        shards.append(scatter_chips(grads)[0])
    given = swap(gnorm_part[rows:])

    shift = lambda v, bit: lax.ppermute(v, "seq", [(i, i ^ bit) for i in range(groups)])
    even = place % 2 == 0

    def line_start(shard):
        tall = shard.shape[1] // 2
        halves = (shard[:, :tall], shard[:, tall:])
        kept = jnp.where(even, halves[0], halves[1])
        return kept + shift(jnp.where(even, halves[1], halves[0]), 1)

    def line_middle(kept):
        bit = 2
        while bit < groups:
            kept = kept + shift(kept, bit)
            bit *= 2
        return kept

    def line_end(kept):
        other = shift(kept, 1)
        return jnp.where(even, kept, other), jnp.where(even, other, kept)

    together = lax.optimization_barrier
    shards[0], given = together((shards[0], given))
    line_a = line_start(shards[0])
    grad_resid, grad_attended, sums_two = resid_back(
        gnorm_part, given, resid, cotangent, gain2, scale, out_full
    )

    back_args = (q_rot, kv, grad_attended, seg_q_row, seg_k_col, cosine, sine)
    pairs = model // 128
    line_a, back_args = together((line_a, back_args))
    line_a = line_middle(line_a)
    first_half = attend_back(0, pairs // 2, *back_args)
    line_a, shards[1], back_args, first_half = together(
        (line_a, shards[1], back_args, first_half)
    )
    line_b = line_start(shards[1])
    ends_a = line_end(line_a)
    dq, dk, dv = attend_back(pairs // 2, pairs - pairs // 2, *back_args, before=first_half)
    line_b, ends_a, dq, dk, dv = together((line_b, ends_a, dq, dk, dv))
    line_b = line_middle(line_b)
    core_at = core.reshape(1).astype(jnp.int32)
    normed_parts = (normed_hi, normed_lo)
    grads_qk = weight_call(
        weights_qk_kernel, 9, core_at, chips, normed_parts, [(dq, 0), (dk, 1)], [halo + rows] * 2
    )
    given_qk = swap(grads_qk[1])
    line_b, shards[2], dv, grad_resid = together((line_b, shards[2], dv, grad_resid))
    ends_b = line_end(line_b)
    line_c = line_start(shards[2])
    grads_vo = weight_call(
        weights_vo_kernel, 9, core_at, chips, normed_parts,
        [(dv, 0), (attended, None), (grad_resid, 1)], [halo + rows] * 2 + [rows] * 2,
    )
    line_c, ends_b, grads_vo = together((line_c, ends_b, grads_vo))
    line_c = line_middle(line_c)
    grads_c = jnp.concatenate([grads_qk[0] + given_qk, grads_vo[0] + swap(grads_vo[1])], axis=2)
    grads_c, out_part = together((grads_c, out_part))
    shard_c = scatter_chips(grads_c)[0]
    out_sib = swap(out_part[rows:])

    block_out = resid + out_part[:rows] + out_sib
    output = base + dwa_weights[4] * block_out
    dwa_local = jnp.concatenate([dots, jnp.sum(cotangent * block_out)[None]])

    part_far = partial_rows(0, (dk, dv), qkv_full)
    given_near = lax.ppermute(part_far, "seq", behind)
    dk, far, near, line_c, part_far = together((dk, far, near, line_c, part_far))
    ends_c = line_end(line_c)
    part_near = partial_rows(1, (dk, dv), qkv_full)
    own_part = partial_rows(2, (dq, dk, dv), qkv_full)
    (sent,) = together((part_near,))
    back_near = sent + given_near

    xhat1, rate1 = norm_stats(block_input)
    terms = (
        (norm_stats(far)[0], part_far),
        (norm_stats(near)[0], part_near),
        (xhat1, own_part),
    )
    grad_gain_one = sum(jnp.sum(xhat * part, axis=0) for xhat, part in terms)
    grad_bias_one = sum(jnp.sum(part, axis=0) for _, part in terms)

    small = jnp.concatenate(
        [
            grad_gain_one[None], grad_bias_one[None], sums_two[:2],
            jnp.pad(dwa_local, (0, model - 5))[None], jnp.zeros((3, model), F32),
        ],
        axis=0,
    )
    bit = 1
    while bit < devices:
        small = small + exchange(small, bit)
        bit *= 2
    shard_c, back_near, small = together((shard_c, back_near, small))
    last = line_middle(line_start(shard_c[None]))
    given_back = lax.ppermute(back_near, "seq", behind)
    grad_up, grad_down = unpack_grads(
        *(
            jnp.concatenate(parts, axis=0)
            for parts in zip(ends_a, ends_b, ends_c)
        ),
        swap, core, chips,
    )
    last, grad_up, grad_down, small, given_back = together(
        (last, grad_up, grad_down, small, given_back)
    )
    bit = 1
    while bit < groups:
        small = small + shift(small, bit)
        bit *= 2
    gain_one, bias_one, gain_two, bias_two = small[0], small[1], small[2], small[3]
    grad_dwa = small[4, :5]
    last = jnp.concatenate(line_end(last), axis=1)[0]
    grad_qkv, grad_wout = last[:, :3 * model], last[:, 3 * model:]
    grad_normed_one = own_part + given_back
    grad_input = grad_resid + norm_back(grad_normed_one, gain1, xhat1, rate1)
    return (
        output,
        grad_input,
        grad_dwa,
        gain_one,
        bias_one,
        grad_qkv,
        grad_wout,
        gain_two,
        bias_two,
        grad_up,
        grad_down,
    )


def solution(mesh):
    in_specs = (
        P(("dp", "seq"), None),
        P(("dp", "seq"), None),
        P(None, ("dp", "seq"), None),
        P(),
        P(),
        P(),
        P("dp", None),
        P("dp", None),
        P(),
        P(),
        P("dp", None),
        P("dp", None),
        P("dp", "seq"),
        P(("dp", "seq"), None),
    )
    out_specs = (
        P(("dp", "seq"), None),
        P(("dp", "seq"), None),
        P(),
        P(),
        P(),
        P("dp", None),
        P("dp", None),
        P(),
        P(),
        P("dp", None),
        P("dp", None),
    )
    return jax.shard_map(body, mesh=mesh, in_specs=in_specs, out_specs=out_specs, check_vma=False)
```
